32 devices in a mesh: dp: 4 (over y, core), tensor: 8 (over z, x).
Axes of the slice: x: 2, y: 2, z: 4, core: 2. Of those that a mesh axis runs over, the one named last changes fastest.
Arguments:
- tokens: bfloat16 [4096, 2048], P(('dp', 'tensor')), may hold values from -6 to 6
- lengths: int32 [4, 6], P('dp'), may hold values from 1 to 8, 16 in all within a row
- gain_attn: float32 [2048], replicated, may hold values from 0.25 to 1.75
- w_query: bfloat16 [2048, 2048], P(None, 'tensor'), may hold values from -0.125 to 0.125
- w_kv: bfloat16 [2048, 256], replicated, may hold values from -0.125 to 0.125
- w_attn_out: bfloat16 [2048, 2048], P('tensor'), may hold values from -1 to 1
- gain_mlp: float32 [2048], replicated, may hold values from 0.25 to 1.75
- w_gate: bfloat16 [2048, 5632], P(None, 'tensor'), may hold values from -0.125 to 0.125
- w_up: bfloat16 [2048, 5632], P(None, 'tensor'), may hold values from -0.125 to 0.125
- w_down: bfloat16 [5632, 2048], P('tensor'), may hold values from -0.078125 to 0.078125
- out_grad: bfloat16 [4096, 2048], P(('dp', 'tensor')), may hold values from -6 to 6
- kv_grad: bfloat16 [4096, 256], P(('dp', 'tensor')), may hold values from -6 to 6
Outputs:
- block_out: bfloat16 [4096, 2048], P(('dp', 'tensor'))
- grad_tokens: bfloat16 [4096, 2048], P(('dp', 'tensor'))
- grad_gain_attn: float32 [2048], P(('dp', 'tensor'))
- grad_w_query: float32 [2048, 2048], P('dp', 'tensor')
- grad_w_kv: float32 [2048, 256], P(('dp', 'tensor'))
- grad_w_attn_out: float32 [2048, 2048], P('tensor', 'dp')
- grad_gain_mlp: float32 [2048], P(('dp', 'tensor'))
- grad_w_gate: float32 [2048, 5632], P('dp', 'tensor')
- grad_w_up: float32 [2048, 5632], P('dp', 'tensor')
- grad_w_down: float32 [5632, 2048], P('tensor', 'dp')
The draws below stay inside these ranges and needn't reach their ends.
Inputs may be any that keep to these rules, and one draw needn't show every extreme that they name: Each row of lengths gives the lengths, in units of 64 tokens, of its group's 6 pieces in order; they sum to 16, the largest is exactly 8, and the last piece is padding.
All inputs are finite; a program needn't handle non-finite values.
Results may differ from the reference program's by a relative error of at most 0.024.
Values may be sent and summed in bfloat16 or wider, within the bound.
A program may use at most 128 MiB of HBM per device.

```python
import math
import jax
import jax.numpy as jnp
import numpy as np
from jax import lax

D = 2048
HEADS = 16
HD = 128
FF = 5632
GROUP_TOK = 1024
SPAN = 64
PIECES = 6
UNITS = 16
LONGEST = 8
GROUPS = 4
TOKENS = 4096


def levels(rng, extent, shards, smallest, high):
    def one(dim, shards_of):
        draws = jax.random.uniform(jax.random.fold_in(jax.random.fold_in(rng, 6), dim), (shards_of,), jnp.float32, smallest / len(shards), high / len(shards))
        return jnp.repeat(jnp.exp(draws), extent[dim] // shards_of).reshape((-1,) + (1,) * (len(extent) - dim - 1))

    factor_of = one(*shards[0])
    for cut in shards[1:]:
        factor_of = factor_of * one(*cut)
    return factor_of


def split_up(amount, total, bound, lean):
    portions = [(1 << 20) // math.isqrt(standing ** lean) + 1 for standing in range(2, amount + 1)]
    rest, counts = total - bound - (amount - 1), [1] * (amount - 1)
    while rest > 0:
        free = [i for i in range(amount - 1) if counts[i] < bound]
        mass, budget = sum([portions[i] for i in free]), rest
        for i in free:
            addition = min(bound - counts[i], max(1, budget * portions[i] // mass), rest)
            counts[i] = counts[i] + addition
            rest = rest - addition
    return np.array([bound] + counts)


def uneven_parts(own_key, amount, total, limit, skew):
    if amount == 2:
        one = jax.random.randint(own_key, (), max(1, total - limit), min(limit, total - 1) + 1)
        return jnp.stack([one, total - one])
    tallies = jnp.asarray(split_up(amount, total, limit, skew), jnp.int32)
    twos = (amount - 1) // 2
    giver, receiver = tallies[1:1 + 2 * twos:2], tallies[2:2 + 2 * twos:2]
    room = jnp.minimum(giver - 1, limit - receiver)
    passed = jax.random.randint(jax.random.fold_in(own_key, 1), (twos,), 0, 1 << 20) % (room + 1)
    tallies = tallies.at[1:1 + 2 * twos:2].set(giver - passed).at[2:2 + 2 * twos:2].set(receiver + passed)
    return tallies[jax.random.permutation(jax.random.fold_in(own_key, 2), amount)]


def normal_values(own_key, dims, spread, most, pieces=(), kind=jnp.bfloat16):
    loudness = levels(own_key, dims, pieces, -0.22, 0.18) if pieces else 1.0
    drawn = jax.random.normal(own_key, dims, jnp.float32) * spread * loudness
    return jnp.minimum(jnp.maximum(drawn, -most), most).astype(kind)


def setup_inputs(seed: int = 0) -> dict:
    arg_keys = jax.random.split(jax.random.key(seed), 13)
    return {
        "tokens": normal_values(arg_keys[0], (TOKENS, D), 1.0, 6.0, ((0, 32),)),
        "lengths": jax.vmap(lambda own: uneven_parts(own, PIECES, UNITS, LONGEST, 2))(jax.random.split(arg_keys[1], GROUPS)).reshape((GROUPS, PIECES)).astype(jnp.int32),
        "gain_attn": jnp.clip(1.0 + 0.15 * jax.random.normal(arg_keys[2], (D,), jnp.float32), 0.25, 1.75),
        "w_query": normal_values(arg_keys[3], (D, HEADS * HD), D ** -0.5, 0.125, ((1, 8),)),
        "w_kv": normal_values(arg_keys[4], (D, 2 * HD), D ** -0.5, 0.125),
        "w_attn_out": normal_values(arg_keys[5], (HEADS * HD, D), 32 ** -0.5, 1.0, ((0, 8),)),
        "gain_mlp": jnp.clip(1.0 + 0.15 * jax.random.normal(arg_keys[6], (D,), jnp.float32), 0.25, 1.75),
        "w_gate": normal_values(arg_keys[7], (D, FF), D ** -0.5, 0.125, ((1, 8),)),
        "w_up": normal_values(arg_keys[8], (D, FF), D ** -0.5, 0.125, ((1, 8),)),
        "w_down": normal_values(arg_keys[9], (FF, D), FF ** -0.5, 0.078125, ((0, 8),)),
        "out_grad": normal_values(arg_keys[10], (TOKENS, D), 1.0, 6.0, ((0, 32),)),
        "kv_grad": normal_values(arg_keys[11], (TOKENS, 2 * HD), 1.0, 6.0, ((0, 32),)),
    }


EPSILON = 1e-05
ROTARY_BASE = 10000.0
MASKED = -1e+30
HIGH = lax.Precision.HIGHEST

@jax.custom_vjp
def low(v):
    return lax.optimization_barrier(v.astype(jnp.bfloat16)).astype(jnp.float32)

@jax.custom_vjp
def low_back(v):
    return v

def low_keep(v):
    return (low(v), None)

def low_pass(kept, grad):
    return (grad,)

def back_keep(v):
    return (v, None)

def back_low(kept, grad):
    return (low(grad),)
low.defvjp(low_keep, low_pass)
low_back.defvjp(back_keep, back_low)

def rotary_tables(positions, width):
    half_width = width // 2
    freqs = ROTARY_BASE ** (-jnp.arange(half_width, dtype=jnp.float32) / half_width)
    angles = positions[:, None] * freqs[None, :]
    return (jnp.cos(angles), jnp.sin(angles))

def rotate(values, cosine, sine):
    half_width = values.shape[-1] // 2
    first_half = values[..., :half_width]
    second_half = values[..., half_width:]
    return jnp.concatenate([first_half * cosine - second_half * sine, second_half * cosine + first_half * sine], axis=-1)

def layout(piece_units, rows):
    piece_rows = piece_units.astype(jnp.int32) * SPAN
    ends = jnp.cumsum(piece_rows).astype(jnp.int32)
    starts = ends - piece_rows
    row_steps = jnp.arange(rows, dtype=jnp.int32)
    segment = lax.optimization_barrier(jnp.sum((row_steps[:, None] >= ends[None, :]).astype(jnp.int32), axis=1)).astype(jnp.int32)
    member = segment[:, None] == jnp.arange(piece_units.shape[0], dtype=jnp.int32)[None, :]
    row_start = lax.optimization_barrier(jnp.sum(jnp.where(member, starts[None, :], 0), axis=1)).astype(jnp.int32)
    positions = (row_steps - row_start).astype(jnp.float32)
    keep = (segment < piece_units.shape[0] - 1).astype(jnp.float32)
    return (segment, row_steps, positions, keep)

def attention_block(query_block, keys, values, block_segment, block_steps, segment, row_steps):
    scale = keys.shape[-1] ** (-0.5)
    scores = jnp.einsum('qhd,kd->hqk', query_block, keys, precision=HIGH) * scale
    scores = low_back(scores)
    allowed = (block_segment[:, None] == segment[None, :]) & (row_steps[None, :] <= block_steps[:, None])
    scores = jnp.where(allowed[None], scores, MASKED)
    probs = low(jax.nn.softmax(scores, axis=-1))
    attended = jnp.einsum('hqk,kd->qhd', probs, values, precision=HIGH)
    return low(low_back(attended))

def layer(tokens, params, segment, row_steps, positions, keep):
    gain_attn, w_query, w_kv, w_attn_out, gain_mlp, w_gate, w_up, w_down = params
    rows = tokens.shape[0]
    head_dim = w_kv.shape[1] // 2
    heads = w_query.shape[1] // head_dim
    inv_first = lax.rsqrt(lax.optimization_barrier(jnp.mean(tokens * tokens, axis=-1, keepdims=True)) + EPSILON)
    normed = low(tokens * inv_first * gain_attn)
    cosine, sine = rotary_tables(positions, head_dim)
    queries = low_back(jnp.dot(normed, w_query, precision=HIGH)).reshape(rows, heads, head_dim)
    queries = low(rotate(queries, cosine[:, None, :], sine[:, None, :]))
    kv_raw = low_back(jnp.dot(normed, w_kv, precision=HIGH))
    shared = low(jnp.concatenate([rotate(kv_raw[:, :head_dim], cosine, sine), kv_raw[:, head_dim:]], axis=1))
    keys = shared[:, :head_dim]
    values = shared[:, head_dim:]
    block = min(512, rows)
    count = rows // block

    def one_block(item):
        return attention_block(item[0], keys, values, item[1], item[2], segment, row_steps)
    attended = lax.map(jax.checkpoint(one_block), (queries.reshape(count, block, heads, head_dim), segment.reshape(count, block), row_steps.reshape(count, block)))
    attended = attended.reshape(rows, heads * head_dim)
    mid = tokens + low_back(jnp.dot(attended, w_attn_out, precision=HIGH))
    inv_second = lax.rsqrt(lax.optimization_barrier(jnp.mean(mid * mid, axis=-1, keepdims=True)) + EPSILON)
    normed_mlp = low(mid * inv_second * gain_mlp)
    gate = low_back(jnp.dot(normed_mlp, w_gate, precision=HIGH))
    up = low_back(jnp.dot(normed_mlp, w_up, precision=HIGH))
    hidden = low(jax.nn.silu(gate) * up)
    mlp_out = low_back(jnp.dot(hidden, w_down, precision=HIGH))
    return (keep[:, None] * (mid + mlp_out), keep[:, None] * shared)

def reference(tokens, lengths, gain_attn, w_query, w_kv, w_attn_out, gain_mlp, w_gate, w_up, w_down, out_grad, kv_grad):
    params = tuple((weight.astype(jnp.float32) for weight in (gain_attn, w_query, w_kv, w_attn_out, gain_mlp, w_gate, w_up, w_down)))
    width = tokens.shape[1]

    def one_group(totals, item):
        group_tokens, group_grad, group_kv_grad, piece_units = item
        segment, row_steps, positions, keep = layout(piece_units, GROUP_TOK)

        def forward(inputs, weights):
            return layer(inputs, weights, segment, row_steps, positions, keep)
        outputs, pull = jax.vjp(forward, group_tokens.astype(jnp.float32), params)
        grad_in, grad_params = pull((group_grad.astype(jnp.float32), group_kv_grad.astype(jnp.float32)))
        totals = jax.tree.map(lambda left, right: left + right, totals, grad_params)
        return (totals, (outputs[0].astype(jnp.bfloat16), grad_in.astype(jnp.bfloat16)))
    initial = jax.tree.map(jnp.zeros_like, params)
    totals, results = lax.scan(one_group, initial, (tokens.reshape(GROUPS, GROUP_TOK, width), out_grad.reshape(GROUPS, GROUP_TOK, width), kv_grad.reshape(GROUPS, GROUP_TOK, kv_grad.shape[1]), lengths))
    block_out = results[0].reshape(TOKENS, width)
    grad_tokens = results[1].reshape(TOKENS, width)
    return (block_out, grad_tokens, totals[0], totals[1], totals[2], totals[3], totals[4], totals[5], totals[6], totals[7])
```

```python
import jax
import jax.numpy as jnp
from jax import lax
from jax.sharding import PartitionSpec as P

SPAN = 64


EPSILON = 1e-05
ROTARY_BASE = 10000.0
MASKED = -1e30


def rotary_tables(positions, width):
    half_width = width // 2
    freqs = ROTARY_BASE ** (-jnp.arange(half_width, dtype=jnp.float32) / half_width)
    angles = positions[:, None] * freqs[None, :]
    return (jnp.cos(angles), jnp.sin(angles))


def rotate(values, cosine, sine):
    half_width = values.shape[-1] // 2
    first_half = values[..., :half_width]
    second_half = values[..., half_width:]
    return jnp.concatenate(
        [first_half * cosine - second_half * sine, second_half * cosine + first_half * sine],
        axis=-1,
    )


def unrotate(values, cosine, sine):
    half_width = values.shape[-1] // 2
    first_half = values[..., :half_width]
    second_half = values[..., half_width:]
    return jnp.concatenate(
        [first_half * cosine + second_half * sine, second_half * cosine - first_half * sine],
        axis=-1,
    )


def layout(piece_units, rows):
    piece_rows = piece_units * SPAN
    ends = jnp.cumsum(piece_rows)
    starts = ends - piece_rows
    row_steps = jnp.arange(rows, dtype=jnp.int32)
    segment = jnp.sum((row_steps[:, None] >= ends[None, :]).astype(jnp.int32), axis=1)
    member = segment[:, None] == jnp.arange(piece_units.shape[0], dtype=jnp.int32)[None, :]
    row_start = jnp.sum(jnp.where(member, starts[None, :], 0), axis=1)
    positions = (row_steps - row_start).astype(jnp.float32)
    keep = (segment < piece_units.shape[0] - 1).astype(jnp.float32)
    return (segment, row_steps, positions, keep)


def permitted(block_segment, block_steps, segment, row_steps):
    return (block_segment[:, None] == segment[None, :]) & (
        row_steps[None, :] <= block_steps[:, None]
    )


def spread_rows(values):
    return lax.all_gather(values, "tensor", axis=0, tiled=True)


def spread_grads(values):
    return lax.all_gather(values, "tensor", axis=0, tiled=True)


def per_device(
    tokens,
    lengths,
    gain_attn,
    w_query,
    w_kv,
    w_attn_out,
    gain_mlp,
    w_gate,
    w_up,
    w_down,
    out_grad,
    kv_grad,
):
    local_rows = tokens.shape[0]
    parts = lax.axis_size("tensor")
    total_rows = local_rows * parts
    first_row = lax.axis_index("tensor") * local_rows
    segment, row_steps, positions, keep = layout(lengths[0], total_rows)
    head_dim = w_kv.shape[1] // 2
    local_heads = w_query.shape[1] // head_dim
    scale = head_dim ** (-0.5)
    cosine, sine = rotary_tables(positions, head_dim)
    row_keep = lax.dynamic_slice_in_dim(keep, first_row, local_rows, 0)[:, None]
    row_cosine = lax.dynamic_slice_in_dim(cosine, first_row, local_rows, 0)
    row_sine = lax.dynamic_slice_in_dim(sine, first_row, local_rows, 0)
    tokens_full = tokens.astype(jnp.float32)
    inv_first = lax.rsqrt(jnp.mean(tokens_full * tokens_full, axis=-1, keepdims=True) + EPSILON)
    unit_first = tokens_full * inv_first
    normed_rows = (unit_first * gain_attn).astype(jnp.bfloat16)
    normed = spread_rows(normed_rows)
    queries = jnp.dot(normed, w_query, preferred_element_type=jnp.float32).reshape(
        total_rows, local_heads, head_dim
    )
    queries = rotate(queries, cosine[:, None, :], sine[:, None, :]).astype(jnp.bfloat16)
    kv_raw = jnp.dot(normed, w_kv, preferred_element_type=jnp.float32)
    shared = jnp.concatenate(
        [rotate(kv_raw[:, :head_dim], cosine, sine), kv_raw[:, head_dim:]], axis=1
    ).astype(jnp.bfloat16)
    keys = shared[:, :head_dim]
    values = shared[:, head_dim:]
    block = min(512, total_rows)
    count = total_rows // block
    pieces = []
    log_totals = []
    for number in range(count):
        begin = number * block
        query_block = queries[begin : begin + block]
        allowed = permitted(
            segment[begin : begin + block], row_steps[begin : begin + block], segment, row_steps
        )
        scores = (
            jnp.einsum("qhd,kd->hqk", query_block, keys, preferred_element_type=jnp.float32) * scale
        )
        scores = jnp.where(allowed[None], scores, MASKED)
        row_max = jnp.max(scores, axis=-1, keepdims=True)
        exp_scores = jnp.exp(scores - row_max)
        row_total = jnp.sum(exp_scores, axis=-1, keepdims=True)
        log_totals.append(row_max + jnp.log(row_total))
        weights = (exp_scores / row_total).astype(jnp.bfloat16)
        pieces.append(
            jnp.einsum("hqk,kd->qhd", weights, values, preferred_element_type=jnp.float32).astype(
                jnp.bfloat16
            )
        )
    attended = jnp.concatenate(pieces, axis=0).reshape(total_rows, local_heads * head_dim)
    attn_rows = lax.psum_scatter(
        jnp.dot(attended, w_attn_out, preferred_element_type=jnp.float32).astype(jnp.bfloat16),
        "tensor",
        scatter_dimension=0,
        tiled=True,
    ).astype(jnp.float32)
    mid = tokens_full + attn_rows
    inv_second = lax.rsqrt(jnp.mean(mid * mid, axis=-1, keepdims=True) + EPSILON)
    unit_second = mid * inv_second
    normed_mlp = spread_rows((unit_second * gain_mlp).astype(jnp.bfloat16))
    gate = jnp.dot(normed_mlp, w_gate, preferred_element_type=jnp.float32)
    up = jnp.dot(normed_mlp, w_up, preferred_element_type=jnp.float32)
    sigma = jax.nn.sigmoid(gate)
    active = gate * sigma
    hidden = (active * up).astype(jnp.bfloat16)
    mlp_rows = lax.psum_scatter(
        jnp.dot(hidden, w_down, preferred_element_type=jnp.float32).astype(jnp.bfloat16),
        "tensor",
        scatter_dimension=0,
        tiled=True,
    ).astype(jnp.float32)
    block_out = (row_keep * (mid + mlp_rows)).astype(jnp.bfloat16)
    out_full = row_keep * out_grad.astype(jnp.float32)
    grad_mlp = spread_grads(out_full.astype(jnp.bfloat16))
    g_down = jnp.einsum("rf,rd->fd", hidden, grad_mlp, preferred_element_type=jnp.float32)
    g_hidden = jnp.einsum("rd,fd->rf", grad_mlp, w_down, preferred_element_type=jnp.float32)
    d_gate = (g_hidden * up * sigma * (1.0 + gate * (1.0 - sigma))).astype(jnp.bfloat16)
    d_up = (g_hidden * active).astype(jnp.bfloat16)
    g_gate = jnp.einsum("rd,rf->df", normed_mlp, d_gate, preferred_element_type=jnp.float32)
    g_up = jnp.einsum("rd,rf->df", normed_mlp, d_up, preferred_element_type=jnp.float32)
    back_mlp = lax.psum_scatter(
        (
            jnp.einsum("rf,df->rd", d_gate, w_gate, preferred_element_type=jnp.float32)
            + jnp.einsum("rf,df->rd", d_up, w_up, preferred_element_type=jnp.float32)
        ).astype(jnp.bfloat16),
        "tensor",
        scatter_dimension=0,
        tiled=True,
    ).astype(jnp.float32)
    e_mlp = back_mlp * gain_mlp
    g_gain_mlp = jnp.sum(back_mlp * unit_second, axis=0)
    d_mid = out_full + inv_second * (
        e_mlp - unit_second * jnp.mean(e_mlp * unit_second, axis=-1, keepdims=True)
    )
    grad_attn = spread_grads(d_mid.astype(jnp.bfloat16))
    g_attn_out = jnp.einsum("rh,rd->hd", attended, grad_attn, preferred_element_type=jnp.float32)
    d_att = jnp.einsum(
        "rd,hd->rh", grad_attn, w_attn_out, preferred_element_type=jnp.float32
    ).astype(jnp.bfloat16)
    d_att = d_att.reshape(total_rows, local_heads, head_dim)
    query_pieces = []
    d_keys = jnp.zeros((total_rows, head_dim), jnp.float32)
    d_values = jnp.zeros((total_rows, head_dim), jnp.float32)
    for number in range(count):
        begin = number * block
        query_block = queries[begin : begin + block]
        grad_block = d_att[begin : begin + block]
        allowed = permitted(
            segment[begin : begin + block], row_steps[begin : begin + block], segment, row_steps
        )
        scores = (
            jnp.einsum("qhd,kd->hqk", query_block, keys, preferred_element_type=jnp.float32) * scale
        )
        scores = jnp.where(allowed[None], scores, MASKED)
        probs = jnp.exp(scores - log_totals[number])
        weights = probs.astype(jnp.bfloat16)
        d_probs = jnp.einsum("qhd,kd->hqk", grad_block, values, preferred_element_type=jnp.float32)
        inner = jnp.sum(d_probs * probs, axis=-1, keepdims=True)
        d_scores = (probs * (d_probs - inner)).astype(jnp.bfloat16)
        query_pieces.append(
            jnp.einsum("hqk,kd->qhd", d_scores, keys, preferred_element_type=jnp.float32) * scale
        )
        d_keys = (
            d_keys
            + jnp.einsum("hqk,qhd->kd", d_scores, query_block, preferred_element_type=jnp.float32)
            * scale
        )
        d_values = d_values + jnp.einsum(
            "hqk,qhd->kd", weights, grad_block, preferred_element_type=jnp.float32
        )
    d_queries = jnp.concatenate(query_pieces, axis=0)
    d_queries = unrotate(d_queries, cosine[:, None, :], sine[:, None, :]).astype(jnp.bfloat16)
    d_queries = d_queries.reshape(total_rows, local_heads * head_dim)
    g_query = jnp.einsum("rd,rh->dh", normed, d_queries, preferred_element_type=jnp.float32)
    kv_rows = lax.psum_scatter(
        jnp.concatenate([d_keys, d_values], axis=1).astype(jnp.bfloat16),
        "tensor",
        scatter_dimension=0,
        tiled=True,
    ).astype(jnp.float32)
    kv_rows = kv_rows + row_keep * kv_grad.astype(jnp.float32)
    d_kv = jnp.concatenate(
        [unrotate(kv_rows[:, :head_dim], row_cosine, row_sine), kv_rows[:, head_dim:]], axis=1
    ).astype(jnp.bfloat16)
    d_kv_all = lax.all_gather(d_kv, "tensor", axis=0, tiled=True)
    width = normed.shape[1]
    groups = lax.axis_size("dp")
    own = lax.dynamic_index_in_dim(
        normed.reshape(total_rows, groups, parts, width // (groups * parts)),
        lax.axis_index("tensor"),
        2,
        False,
    ).reshape(total_rows, width // parts)
    g_kv = jnp.einsum("rd,rk->dk", own, d_kv_all, preferred_element_type=jnp.float32)
    back_attn = lax.psum_scatter(
        jnp.einsum("rh,dh->rd", d_queries, w_query, preferred_element_type=jnp.float32).astype(
            jnp.bfloat16
        ),
        "tensor",
        scatter_dimension=0,
        tiled=True,
    ).astype(jnp.float32)
    back_attn = back_attn + jnp.einsum("rk,dk->rd", d_kv, w_kv, preferred_element_type=jnp.float32)
    e_attn = back_attn * gain_attn
    g_gain_attn = jnp.sum(back_attn * unit_first, axis=0)
    grad_tokens = (
        d_mid
        + inv_first * (e_attn - unit_first * jnp.mean(e_attn * unit_first, axis=-1, keepdims=True))
    ).astype(jnp.bfloat16)
    kv_sum = lax.psum_scatter(g_kv, "dp", scatter_dimension=0, tiled=True)
    share = width // (groups * parts)
    first = (lax.axis_index("dp") * parts + lax.axis_index("tensor")) * share
    gain_all = lax.all_gather(jnp.stack([g_gain_attn, g_gain_mlp]), ("dp", "tensor"), axis=0)
    gain_sums = jnp.sum(lax.dynamic_slice_in_dim(gain_all, first, share, 2), axis=0)
    query_sum, out_sum, gate_sum, up_sum, down_sum = (
        lax.psum_scatter(
            g_query.astype(jnp.bfloat16), "dp", scatter_dimension=0, tiled=True
        ).astype(jnp.float32),
        lax.psum_scatter(
            g_attn_out.astype(jnp.bfloat16), "dp", scatter_dimension=1, tiled=True
        ).astype(jnp.float32),
        lax.psum_scatter(g_gate.astype(jnp.bfloat16), "dp", scatter_dimension=0, tiled=True).astype(
            jnp.float32
        ),
        lax.psum_scatter(g_up.astype(jnp.bfloat16), "dp", scatter_dimension=0, tiled=True).astype(
            jnp.float32
        ),
        lax.psum_scatter(g_down.astype(jnp.bfloat16), "dp", scatter_dimension=1, tiled=True).astype(
            jnp.float32
        ),
    )
    return (
        block_out,
        grad_tokens,
        gain_sums[0],
        query_sum,
        kv_sum,
        out_sum,
        gain_sums[1],
        gate_sum,
        up_sum,
        down_sum,
    )


def solution(mesh):
    placed = (
        P(("dp", "tensor"), None),
        P("dp", None),
        P(),
        P(None, "tensor"),
        P(),
        P("tensor", None),
        P(),
        P(None, "tensor"),
        P(None, "tensor"),
        P("tensor", None),
        P(("dp", "tensor"), None),
        P(("dp", "tensor"), None),
    )
    return jax.shard_map(
        per_device,
        mesh=mesh,
        in_specs=placed,
        out_specs=(
            P(("dp", "tensor"), None),
            P(("dp", "tensor"), None),
            P(("dp", "tensor")),
            P("dp", "tensor"),
            P(("dp", "tensor"), None),
            P("tensor", "dp"),
            P(("dp", "tensor")),
            P("dp", "tensor"),
            P("dp", "tensor"),
            P("tensor", "dp"),
        ),
        check_vma=False,
    )
```

```python
import functools
import types

import jax
import jax.numpy as jnp
from jax import lax
from jax.experimental import pallas as pl
from jax.experimental.pallas import tpu as pltpu
from jax.sharding import PartitionSpec as P

SPAN = 64


EPSILON = 1e-05
ROTARY_BASE = 10000.0
MASKED = -1e30


def rotary_tables(positions, width):
    half_width = width // 2
    freqs = ROTARY_BASE ** (-jnp.arange(half_width, dtype=jnp.float32) / half_width)
    angles = positions[:, None] * freqs[None, :]
    return (jnp.cos(angles), jnp.sin(angles))


def rotate(values, cosine, sine):
    half_width = values.shape[-1] // 2
    first_half = values[..., :half_width]
    second_half = values[..., half_width:]
    return jnp.concatenate(
        [first_half * cosine - second_half * sine, second_half * cosine + first_half * sine],
        axis=-1,
    )


def unrotate(values, cosine, sine):
    half_width = values.shape[-1] // 2
    first_half = values[..., :half_width]
    second_half = values[..., half_width:]
    return jnp.concatenate(
        [first_half * cosine + second_half * sine, second_half * cosine - first_half * sine],
        axis=-1,
    )


def layout(piece_units, rows):
    piece_rows = piece_units * SPAN
    ends = jnp.cumsum(piece_rows)
    starts = ends - piece_rows
    row_steps = jnp.arange(rows, dtype=jnp.int32)
    segment = jnp.sum((row_steps[:, None] >= ends[None, :]).astype(jnp.int32), axis=1)
    member = segment[:, None] == jnp.arange(piece_units.shape[0], dtype=jnp.int32)[None, :]
    row_start = jnp.sum(jnp.where(member, starts[None, :], 0), axis=1)
    positions = (row_steps - row_start).astype(jnp.float32)
    keep = (segment < piece_units.shape[0] - 1).astype(jnp.float32)
    return (segment, row_steps, positions, keep)


def permitted(block_segment, block_steps, segment, row_steps):
    return (block_segment[:, None] == segment[None, :]) & (
        row_steps[None, :] <= block_steps[:, None]
    )


def spread_rows(values):
    return lax.all_gather(values, "tensor", axis=0, tiled=True)


def spread_grads(values):
    return lax.all_gather(values, "tensor", axis=0, tiled=True)


def per_device(
    tokens,
    lengths,
    gain_attn,
    w_query,
    w_kv,
    w_attn_out,
    gain_mlp,
    w_gate,
    w_up,
    w_down,
    out_grad,
    kv_grad,
):
    local_rows = tokens.shape[0]
    parts = lax.axis_size("tensor")
    total_rows = local_rows * parts
    first_row = lax.axis_index("tensor") * local_rows
    segment, row_steps, positions, keep = layout(lengths[0], total_rows)
    head_dim = w_kv.shape[1] // 2
    local_heads = w_query.shape[1] // head_dim
    scale = head_dim ** (-0.5)
    cosine, sine = rotary_tables(positions, head_dim)
    row_keep = lax.dynamic_slice_in_dim(keep, first_row, local_rows, 0)[:, None]
    row_cosine = lax.dynamic_slice_in_dim(cosine, first_row, local_rows, 0)
    row_sine = lax.dynamic_slice_in_dim(sine, first_row, local_rows, 0)
    tokens_full = tokens.astype(jnp.float32)
    inv_first = lax.rsqrt(jnp.mean(tokens_full * tokens_full, axis=-1, keepdims=True) + EPSILON)
    unit_first = tokens_full * inv_first
    normed_rows = (unit_first * gain_attn).astype(jnp.bfloat16)
    normed = spread_rows(normed_rows)
    queries = jnp.dot(normed, w_query, preferred_element_type=jnp.float32).reshape(
        total_rows, local_heads, head_dim
    )
    queries = rotate(queries, cosine[:, None, :], sine[:, None, :]).astype(jnp.bfloat16)
    kv_raw = jnp.dot(normed, w_kv, preferred_element_type=jnp.float32)
    shared = jnp.concatenate(
        [rotate(kv_raw[:, :head_dim], cosine, sine), kv_raw[:, head_dim:]], axis=1
    ).astype(jnp.bfloat16)
    keys = shared[:, :head_dim]
    values = shared[:, head_dim:]
    block = min(512, total_rows)
    count = total_rows // block
    pieces = []
    log_totals = []
    for number in range(count):
        begin = number * block
        query_block = queries[begin : begin + block]
        allowed = permitted(
            segment[begin : begin + block], row_steps[begin : begin + block], segment, row_steps
        )
        scores = (
            jnp.einsum("qhd,kd->hqk", query_block, keys, preferred_element_type=jnp.float32) * scale
        )
        scores = jnp.where(allowed[None], scores, MASKED)
        row_max = jnp.max(scores, axis=-1, keepdims=True)
        exp_scores = jnp.exp(scores - row_max)
        row_total = jnp.sum(exp_scores, axis=-1, keepdims=True)
        log_totals.append(row_max + jnp.log(row_total))
        weights = (exp_scores / row_total).astype(jnp.bfloat16)
        pieces.append(
            jnp.einsum("hqk,kd->qhd", weights, values, preferred_element_type=jnp.float32).astype(
                jnp.bfloat16
            )
        )
    attended = jnp.concatenate(pieces, axis=0).reshape(total_rows, local_heads * head_dim)
    attn_rows = lax.psum_scatter(
        jnp.dot(attended, w_attn_out, preferred_element_type=jnp.float32).astype(jnp.bfloat16),
        "tensor",
        scatter_dimension=0,
        tiled=True,
    ).astype(jnp.float32)
    mid = tokens_full + attn_rows
    inv_second = lax.rsqrt(jnp.mean(mid * mid, axis=-1, keepdims=True) + EPSILON)
    unit_second = mid * inv_second
    normed_mlp = spread_rows((unit_second * gain_mlp).astype(jnp.bfloat16))
    gate = jnp.dot(normed_mlp, w_gate, preferred_element_type=jnp.float32)
    up = jnp.dot(normed_mlp, w_up, preferred_element_type=jnp.float32)
    sigma = jax.nn.sigmoid(gate)
    active = gate * sigma
    hidden = (active * up).astype(jnp.bfloat16)
    mlp_rows = lax.psum_scatter(
        jnp.dot(hidden, w_down, preferred_element_type=jnp.float32).astype(jnp.bfloat16),
        "tensor",
        scatter_dimension=0,
        tiled=True,
    ).astype(jnp.float32)
    block_out = (row_keep * (mid + mlp_rows)).astype(jnp.bfloat16)
    out_full = row_keep * out_grad.astype(jnp.float32)
    grad_mlp = spread_grads(out_full.astype(jnp.bfloat16))
    g_down = jnp.einsum("rf,rd->fd", hidden, grad_mlp, preferred_element_type=jnp.float32)
    g_hidden = jnp.einsum("rd,fd->rf", grad_mlp, w_down, preferred_element_type=jnp.float32)
    d_gate = (g_hidden * up * sigma * (1.0 + gate * (1.0 - sigma))).astype(jnp.bfloat16)
    d_up = (g_hidden * active).astype(jnp.bfloat16)
    g_gate = jnp.einsum("rd,rf->df", normed_mlp, d_gate, preferred_element_type=jnp.float32)
    g_up = jnp.einsum("rd,rf->df", normed_mlp, d_up, preferred_element_type=jnp.float32)
    back_mlp = lax.psum_scatter(
        (
            jnp.einsum("rf,df->rd", d_gate, w_gate, preferred_element_type=jnp.float32)
            + jnp.einsum("rf,df->rd", d_up, w_up, preferred_element_type=jnp.float32)
        ).astype(jnp.bfloat16),
        "tensor",
        scatter_dimension=0,
        tiled=True,
    ).astype(jnp.float32)
    e_mlp = back_mlp * gain_mlp
    g_gain_mlp = jnp.sum(back_mlp * unit_second, axis=0)
    d_mid = out_full + inv_second * (
        e_mlp - unit_second * jnp.mean(e_mlp * unit_second, axis=-1, keepdims=True)
    )
    grad_attn = spread_grads(d_mid.astype(jnp.bfloat16))
    g_attn_out = jnp.einsum("rh,rd->hd", attended, grad_attn, preferred_element_type=jnp.float32)
    d_att = jnp.einsum(
        "rd,hd->rh", grad_attn, w_attn_out, preferred_element_type=jnp.float32
    ).astype(jnp.bfloat16)
    d_att = d_att.reshape(total_rows, local_heads, head_dim)
    query_pieces = []
    d_keys = jnp.zeros((total_rows, head_dim), jnp.float32)
    d_values = jnp.zeros((total_rows, head_dim), jnp.float32)
    for number in range(count):
        begin = number * block
        query_block = queries[begin : begin + block]
        grad_block = d_att[begin : begin + block]
        allowed = permitted(
            segment[begin : begin + block], row_steps[begin : begin + block], segment, row_steps
        )
        scores = (
            jnp.einsum("qhd,kd->hqk", query_block, keys, preferred_element_type=jnp.float32) * scale
        )
        scores = jnp.where(allowed[None], scores, MASKED)
        probs = jnp.exp(scores - log_totals[number])
        weights = probs.astype(jnp.bfloat16)
        d_probs = jnp.einsum("qhd,kd->hqk", grad_block, values, preferred_element_type=jnp.float32)
        inner = jnp.sum(d_probs * probs, axis=-1, keepdims=True)
        d_scores = (probs * (d_probs - inner)).astype(jnp.bfloat16)
        query_pieces.append(
            jnp.einsum("hqk,kd->qhd", d_scores, keys, preferred_element_type=jnp.float32) * scale
        )
        d_keys = (
            d_keys
            + jnp.einsum("hqk,qhd->kd", d_scores, query_block, preferred_element_type=jnp.float32)
            * scale
        )
        d_values = d_values + jnp.einsum(
            "hqk,qhd->kd", weights, grad_block, preferred_element_type=jnp.float32
        )
    d_queries = jnp.concatenate(query_pieces, axis=0)
    d_queries = unrotate(d_queries, cosine[:, None, :], sine[:, None, :]).astype(jnp.bfloat16)
    d_queries = d_queries.reshape(total_rows, local_heads * head_dim)
    g_query = jnp.einsum("rd,rh->dh", normed, d_queries, preferred_element_type=jnp.float32)
    kv_rows = lax.psum_scatter(
        jnp.concatenate([d_keys, d_values], axis=1).astype(jnp.bfloat16),
        "tensor",
        scatter_dimension=0,
        tiled=True,
    ).astype(jnp.float32)
    kv_rows = kv_rows + row_keep * kv_grad.astype(jnp.float32)
    d_kv = jnp.concatenate(
        [unrotate(kv_rows[:, :head_dim], row_cosine, row_sine), kv_rows[:, head_dim:]], axis=1
    ).astype(jnp.bfloat16)
    d_kv_all = lax.all_gather(d_kv, "tensor", axis=0, tiled=True)
    width = normed.shape[1]
    groups = lax.axis_size("dp")
    own = lax.dynamic_index_in_dim(
        normed.reshape(total_rows, groups, parts, width // (groups * parts)),
        lax.axis_index("tensor"),
        2,
        False,
    ).reshape(total_rows, width // parts)
    g_kv = jnp.einsum("rd,rk->dk", own, d_kv_all, preferred_element_type=jnp.float32)
    back_attn = lax.psum_scatter(
        jnp.einsum("rh,dh->rd", d_queries, w_query, preferred_element_type=jnp.float32).astype(
            jnp.bfloat16
        ),
        "tensor",
        scatter_dimension=0,
        tiled=True,
    ).astype(jnp.float32)
    back_attn = back_attn + jnp.einsum("rk,dk->rd", d_kv, w_kv, preferred_element_type=jnp.float32)
    e_attn = back_attn * gain_attn
    g_gain_attn = jnp.sum(back_attn * unit_first, axis=0)
    grad_tokens = (
        d_mid
        + inv_first * (e_attn - unit_first * jnp.mean(e_attn * unit_first, axis=-1, keepdims=True))
    ).astype(jnp.bfloat16)
    kv_sum = lax.psum_scatter(g_kv, "dp", scatter_dimension=0, tiled=True)
    share = width // (groups * parts)
    first = (lax.axis_index("dp") * parts + lax.axis_index("tensor")) * share
    gain_all = lax.all_gather(jnp.stack([g_gain_attn, g_gain_mlp]), ("dp", "tensor"), axis=0)
    gain_sums = jnp.sum(lax.dynamic_slice_in_dim(gain_all, first, share, 2), axis=0)
    query_sum, out_sum, gate_sum, up_sum, down_sum = (
        lax.psum_scatter(
            g_query.astype(jnp.bfloat16), "dp", scatter_dimension=0, tiled=True
        ).astype(jnp.float32),
        lax.psum_scatter(
            g_attn_out.astype(jnp.bfloat16), "dp", scatter_dimension=1, tiled=True
        ).astype(jnp.float32),
        lax.psum_scatter(g_gate.astype(jnp.bfloat16), "dp", scatter_dimension=0, tiled=True).astype(
            jnp.float32
        ),
        lax.psum_scatter(g_up.astype(jnp.bfloat16), "dp", scatter_dimension=0, tiled=True).astype(
            jnp.float32
        ),
        lax.psum_scatter(g_down.astype(jnp.bfloat16), "dp", scatter_dimension=1, tiled=True).astype(
            jnp.float32
        ),
    )
    return (
        block_out,
        grad_tokens,
        gain_sums[0],
        query_sum,
        kv_sum,
        out_sum,
        gain_sums[1],
        gate_sum,
        up_sum,
        down_sum,
    )


F32, BF16 = jnp.float32, jnp.bfloat16
MESH = pl.DeviceIdType.MESH
MIB = 1 << 20


def dot(a, b):
    return jnp.dot(a, b, preferred_element_type=F32)


def dot_rows(a, b):
    return lax.dot_general(a, b, (((1,), (1,)), ((), ())), preferred_element_type=F32)


def dot_cols(a, b):
    return lax.dot_general(a, b, (((0,), (0,)), ((), ())), preferred_element_type=F32)


def tiles(width, step):
    return [(at, min(step, width - at)) for at in range(0, width, step)]


GN, GG, GM, GA = range(4)
RO, RB, RD, RQ = range(4)
LEN, TOK, WQ, OG, KVG, WO, WG, WU, WD, BO, GT = range(11)
DOWN, GATE, UP, OUT, QUERY = GRADS = range(5)


def semaphores(nz):
    counts = dict(
        swap=11,
        gz=4 * 2 * nz,
        gc=4 * nz,
        rz=4 * 2 * nz,
        rc=4 * nz,
        stage=20,
        px=20,
        pc=20,
        py=5,
        ld=20,
        st=5,
        kc=nz,
        kz=nz,
        ka=2 * nz,
        kyx=2,
        gains=3 + nz,
        spill=2,
        outs=4,
    )
    firsts, total = {}, 0
    for name, count in counts.items():
        firsts[name] = total
        total += count
    return types.SimpleNamespace(**firsts), total


def block_kernel(nz, pieces, S, R):
    rows, width = R.tokens.shape
    ff = R.w_down.shape[0]
    total = 2 * nz * rows
    pair = 2 * rows
    head = 128
    heads = R.wq.shape[1] // head
    scale = head ** (-0.5)
    DS, DR = R.send, R.recv

    dp, tensor = lax.axis_index("dp"), lax.axis_index("tensor")
    y, c = dp // 2, dp % 2
    z, x = tensor // 2, tensor % 2
    keeper = c == x

    def dev(yy, cc, zz, xx):
        return (2 * yy + cc, 2 * zz + xx)

    sibling = dev(y, 1 - c, z, x)
    partner = dev(y, 1 - c, z, 1 - x)
    across_x = dev(y, c, z, 1 - x)
    across_y = dev(1 - y, c, z, x)

    def send(src, dst, s, r, to):
        return pltpu.make_async_remote_copy(
            src_ref=src,
            dst_ref=dst,
            send_sem=DS.at[s],
            recv_sem=DR.at[r],
            device_id=to,
            device_id_type=MESH,
        )

    def arrived(dst, r):
        pltpu.make_async_copy(dst, dst, DR.at[r]).wait()

    def sent(src, s):
        pltpu.make_async_copy(src, src, DS.at[s]).wait()

    barrier = pltpu.get_barrier_semaphore()
    for to in (across_x, across_y, partner):
        pl.semaphore_signal(barrier, inc=1, device_id=to, device_id_type=MESH)
    for zz in range(nz):
        for cc in range(2):

            @pl.when((zz != z) | (cc != c))
            def _():
                pl.semaphore_signal(
                    barrier, inc=1, device_id=dev(y, cc, zz, x), device_id_type=MESH
                )

    pl.semaphore_wait(barrier, 3 + 2 * nz - 1)

    def swap_start(item, src, dst):
        at = S.swap + item

        @pl.when(keeper)
        def _():
            pltpu.make_async_copy(src, dst, DR.at[at]).start()

        @pl.when(jnp.logical_not(keeper))
        def _():
            send(src, dst, at, at, partner).start()

    def swap_wait(item, dst):
        arrived(dst, S.swap + item)

    def swap_sent(item, src):
        @pl.when(jnp.logical_not(keeper))
        def _():
            sent(src, S.swap + item)

    def piece(ref, chunk, core):
        return ref.at[pl.ds(pl.multiple_of((2 * chunk + core) * rows, rows), rows)]

    def chunk_rows(chunk):
        return pl.ds(pl.multiple_of(chunk * pair, pair), pair)

    own_at = pl.multiple_of((2 * z + c) * rows, rows)

    def gather_start(name, ref):
        own = piece(ref, z, c)

        @pl.when(z < nz - 1)
        def _():
            send(own, own, S.gz + 2 * nz * name + z, S.gz + 2 * nz * name + z, dev(y, c, z + 1, x)).start()

        @pl.when(z > 0)
        def _():
            send(
                own, own, S.gz + 2 * nz * name + nz + z, S.gz + 2 * nz * name + z, dev(y, c, z - 1, x)
            ).start()

        send(own, own, S.gc + nz * name + z, S.gc + nz * name + z, sibling).start()

    def gather_pass(name, ref, step):
        for way in range(2):
            chunk = z - 1 - step if way == 0 else z + 1 + step

            @pl.when((chunk >= 0) & (chunk <= nz - 1))
            def _():
                part = piece(ref, chunk, c)
                arrived(part, S.gz + 2 * nz * name + chunk)
                further = z < nz - 1 if way == 0 else z > 0
                to = dev(y, c, z + 1 - 2 * way, x)

                @pl.when(further)
                def _():
                    send(
                        part,
                        part,
                        S.gz + 2 * nz * name + nz * way + chunk,
                        S.gz + 2 * nz * name + chunk,
                        to,
                    ).start()

                send(
                    part, part, S.gc + nz * name + chunk, S.gc + nz * name + chunk, sibling
                ).start()

    def gather_own(name, ref, work):
        arrived(piece(ref, z, 1 - c), S.gc + nz * name + z)
        if work is not None:
            work(z)

    def gather_use(name, ref, step, work):
        for way in range(2):
            chunk = z - 1 - step if way == 0 else z + 1 + step

            @pl.when((chunk >= 0) & (chunk <= nz - 1))
            def _():
                arrived(piece(ref, chunk, 1 - c), S.gc + nz * name + chunk)
                if work is not None:
                    work(chunk)

    def gather_end(name, ref):
        for chunk in range(nz):
            part = piece(ref, chunk, c)
            sent(part, S.gc + nz * name + chunk)

            @pl.when((z < nz - 1) & (chunk <= z))
            def _():
                sent(part, S.gz + 2 * nz * name + chunk)

            @pl.when((z > 0) & (chunk >= z))
            def _():
                sent(part, S.gz + 2 * nz * name + nz + chunk)

    def half(chunk, core):
        return R.part.at[chunk, pl.ds(pl.multiple_of(core * rows, rows), rows)]

    def z_slot(name, way, chunk, at):
        slot = chunk if way == 0 else jnp.where(chunk == at, nz, chunk)
        return R.from_z.at[name % 2, slot]

    def add_rows(dst, src):
        @pl.loop(0, rows // 32)
        def _(i):
            at = pl.ds(pl.multiple_of(i * 32, 32), 32)
            dst[at, :] = (dst[at, :].astype(F32) + src[at, :].astype(F32)).astype(dst.dtype)

    def scatter_term(name, chunk, work):
        work(chunk)
        send(
            half(chunk, 1 - c),
            R.from_core.at[chunk],
            S.rc + nz * name + chunk,
            S.rc + nz * name + chunk,
            sibling,
        ).start()

    def scatter_slot(step, way):
        if way == 0:
            chunk = nz - 1 + z - step
            return chunk, (step >= z) & (z < nz - 1)
        chunk = step - (nz - 1 - z)
        return chunk, (chunk >= 0) & (z > 0)

    def scatter_step(name, step, work):
        for way in range(2):
            chunk, valid = scatter_slot(step, way)

            @pl.when(valid)
            def _():
                scatter_term(name, chunk, work)

        for way in range(2):
            chunk, valid = scatter_slot(step, way)

            @pl.when(valid)
            def _():
                arrived(R.from_core.at[chunk], S.rc + nz * name + chunk)
                mine = half(chunk, c)
                add_rows(mine, R.from_core.at[chunk])
                earlier = z > 0 if way == 0 else z < nz - 1

                @pl.when(earlier)
                def _():
                    arrived(z_slot(name, way, chunk, z), S.rz + 2 * nz * name + nz * way + chunk)
                    add_rows(mine, z_slot(name, way, chunk, z))

                send(
                    mine,
                    z_slot(name, way, chunk, z + 1 - 2 * way),
                    S.rz + 2 * nz * name + nz * way + chunk,
                    S.rz + 2 * nz * name + nz * way + chunk,
                    dev(y, c, z + 1 - 2 * way, x),
                ).start()

    def scatter_end(name, own_term=True):
        arrived(R.from_core.at[z], S.rc + nz * name + z)
        mine = half(z, c)
        acc = R.acc

        @pl.loop(0, rows // 32)
        def _(i):
            at = pl.ds(pl.multiple_of(i * 32, 32), 32)
            acc[at, :] = mine[at, :].astype(F32) + R.from_core[z, at, :].astype(F32)

        for way in range(2):

            @pl.when(z > 0 if way == 0 else z < nz - 1)
            def _():
                arrived(z_slot(name, way, z, z), S.rz + 2 * nz * name + nz * way + z)
                add_rows(acc, z_slot(name, way, z, z))

    def scatter_sent(name):
        for chunk in range(nz):
            sent(half(chunk, 1 - c), S.rc + nz * name + chunk)
            for way in range(2):

                @pl.when(z < chunk if way == 0 else z > chunk)
                def _():
                    sent(half(chunk, c), S.rz + 2 * nz * name + nz * way + chunk)

    def each_rows(body, step=32):
        @pl.loop(0, rows // step)
        def _(i):
            body(pl.multiple_of(i * step, step), step)

    def keep_of(first, count):
        index = lax.broadcasted_iota(jnp.int32, (count, 1), 0) + (own_at + first)
        return (index.astype(F32) < R.last[0:1, 0:1]).astype(F32)

    def rotary():
        units = R.len[...] * 64.0
        ends, end = [], jnp.zeros((1, 128), F32)
        for p in range(pieces):
            end = end + units[p : p + 1, :]
            ends.append((units[p : p + 1, :], end))
        R.last[...] = jnp.broadcast_to(ends[-2][1], (8, 128))

        @pl.loop(0, total // 128)
        def _(i):
            at = pl.ds(pl.multiple_of(i * 128, 128), 128)
            index = (lax.broadcasted_iota(jnp.int32, (128, 128), 0) + i * 128).astype(F32)
            start = jnp.zeros((128, 128), F32)
            for length, stop in ends[:-1]:
                start = start + jnp.where(stop <= index, length, 0.0)
            R.start[at, :] = start
            angle = (index - start) * R.freq[0:1, :]
            lane = lax.broadcasted_iota(jnp.int32, (128, 128), 1)
            R.cos[at, :] = jnp.cos(angle)
            R.sin[at, :] = jnp.where(lane < 64, -1.0, 1.0) * jnp.sin(angle)

    def turn(value, cosine, sine):
        swapped = jnp.concatenate([value[:, 64:], value[:, :64]], axis=1)
        return value * cosine + swapped * sine

    def project(chunk):
        at = chunk_rows(chunk)
        normed = R.norm[at, :]
        cosine, sine = R.cos[at, :], R.sin[at, :]
        queries = dot(normed, R.wq[...])
        for h in range(heads):
            cols = slice(h * head, (h + 1) * head)
            R.q[at, cols] = turn(queries[:, cols], cosine, sine).astype(BF16)
        kv = dot(normed, R.wkv[...])
        R.kv[at, :head] = turn(kv[:, :head], cosine, sine).astype(BF16)
        R.kv[at, head:] = kv[:, head:].astype(BF16)

    def attend(chunk):
        at = chunk_rows(chunk)
        keys, values = R.kv[:, :head], R.kv[:, head:]
        start = R.start[at, 0:1]
        column = lax.broadcasted_iota(jnp.int32, (pair, total), 1).astype(F32)
        row = (lax.broadcasted_iota(jnp.int32, (pair, 1), 0) + chunk * pair).astype(F32)
        allowed = (column >= start) & (column <= row)
        for h in range(heads):
            cols = slice(h * head, (h + 1) * head)
            scores = dot_rows(R.q[at, cols], keys) * scale
            scores = jnp.where(allowed, scores, -1e30)
            exps = jnp.exp(scores - jnp.max(scores, axis=1, keepdims=True))
            weights = exps * (1.0 / jnp.sum(exps, axis=1, keepdims=True))
            weights = weights.astype(BF16)
            R.probs[h, at, :] = weights
            R.att[at, cols] = dot(weights, values).astype(BF16)

    def out_term(chunk):
        attend(chunk)
        at = chunk_rows(chunk)
        for n, size in tiles(width, 512):
            R.part[chunk, :, n : n + size] = dot(
                R.att[at, :], R.wo[:, n : n + size]
            ).astype(BF16)

    def forward_mlp(chunk):
        at = chunk_rows(chunk)
        for n, size in tiles(ff, 256):
            cols = slice(n, n + size)
            gate = dot_rows(R.nmlp[at, :], R.wg[cols, :])
            up = dot_rows(R.nmlp[at, :], R.wu[cols, :])
            sigma = 1.0 / (1.0 + jnp.exp(-gate))
            active = gate * sigma
            R.hid[at, cols] = (active * up).astype(BF16)
            R.dup[at, cols] = active.astype(BF16)
            R.dgate[at, cols] = (up * (sigma * (1.0 + gate * (1.0 - sigma)))).astype(BF16)

    def backward_mlp(chunk):
        at = chunk_rows(chunk)
        for n, size in tiles(ff, 256):
            cols = slice(n, n + size)
            grad = dot_rows(R.gmlp[at, :], R.wd[cols, :])
            R.dup[at, cols] = (grad * R.dup[at, cols].astype(F32)).astype(BF16)
            R.dgate[at, cols] = (grad * R.dgate[at, cols].astype(F32)).astype(BF16)

    def back_term(chunk):
        backward_mlp(chunk)
        at = chunk_rows(chunk)
        for n, size in tiles(width, 512):
            some = slice(n, n + size)
            R.part[chunk, :, some] = (
                dot(R.dgate[at, :], R.wg[:, some]) + dot(R.dup[at, :], R.wu[:, some])
            ).astype(BF16)

    def down_term(chunk):
        at = chunk_rows(chunk)
        for n, size in tiles(width, 512):
            some = slice(n, n + size)
            R.part[chunk, :, some] = dot(R.hid[at, :], R.wd[:, some]).astype(BF16)

    def d_attended(chunk):
        at = chunk_rows(chunk)
        R.datt[at, :] = dot_rows(R.norm[at, :], R.wo[...]).astype(BF16)

    def backward_attend(chunk):
        at = chunk_rows(chunk)
        keys, values = R.kv[:, :head], R.kv[:, head:]
        cosine, sine = R.cos[at, :], R.sin[at, :]
        for h in range(heads):
            cols = slice(h * head, (h + 1) * head)
            weights = R.probs[h, at, :]
            probs = weights.astype(F32)
            grad = R.datt[at, cols]
            d_probs = dot_rows(grad, values)
            inner = jnp.sum(d_probs * probs, axis=1, keepdims=True)
            d_scores = (probs * (d_probs - inner)).astype(BF16)
            d_queries = dot(d_scores, keys) * scale
            R.dq[at, cols] = turn(d_queries, cosine, -sine).astype(BF16)
            R.dkv[:, :head] += dot_cols(d_scores, R.q[at, cols]) * scale
            R.dkv[:, head:] += dot_cols(weights, grad)

    def query_term(chunk):
        backward_attend(chunk)
        at = chunk_rows(chunk)
        for n, size in tiles(width, 512):
            some = slice(n, n + size)
            R.part[chunk, :, some] = dot_rows(R.dq[at, :], R.wq[some, :]).astype(BF16)

    def grad_send(name, yy, cc):
        quarter = 2 * yy + cc
        stage = R.stage[name].at[quarter]
        into_x, into_c = R.px[name].at[yy], R.pc[name].at[yy]

        @pl.when(jnp.logical_not(keeper))
        def _():
            send(
                stage,
                into_x,
                S.px + 4 * name + quarter,
                S.px + 4 * name + yy,
                (2 * y + cc, 2 * z + 1 - x),
            ).start()

        @pl.when(keeper & (c == cc))
        def _():
            pltpu.make_async_copy(stage, into_c, DR.at[S.pc + 4 * name + yy]).start()

        @pl.when(keeper & (c != cc))
        def _():
            send(
                stage, into_c, S.pc + 4 * name + quarter, S.pc + 4 * name + yy, sibling
            ).start()

    def grad_sent(name, yy, cc):
        quarter = 2 * yy + cc
        stage = R.stage[name].at[quarter]

        @pl.when(jnp.logical_not(keeper))
        def _():
            sent(stage, S.px + 4 * name + quarter)

        @pl.when(keeper & (c != cc))
        def _():
            sent(stage, S.pc + 4 * name + quarter)

    QUARTERS = [(0, 0), (0, 1), (1, 0), (1, 1)]

    def grad_make(name, left, right):
        split_left = name == QUERY
        quarter_cols = (left if split_left else right).shape[1] // 4
        tile = R.tile[name]
        for index, (yy, cc) in enumerate(QUARTERS):
            first = index * quarter_cols
            if index > 1:
                pltpu.make_async_copy(
                    tile.at[index % 2],
                    R.stage[name].at[index - 2],
                    DR.at[S.stage + 4 * name + index - 2],
                ).wait()
                grad_send(name, *QUARTERS[index - 2])
            if split_left:
                for m, size in tiles(quarter_cols, 256):
                    tile[index % 2, m : m + size, :] = dot_cols(
                        left[:, first + m : first + m + size], right[...]
                    ).astype(BF16)
            else:
                for m, size in tiles(left.shape[1], 256):
                    tile[index % 2, m : m + size, :] = dot_cols(
                        left[:, m : m + size], right[:, first : first + quarter_cols]
                    ).astype(BF16)
            pltpu.make_async_copy(
                tile.at[index % 2],
                R.stage[name].at[index],
                DR.at[S.stage + 4 * name + index],
            ).start()
        for index in (2, 3):
            pltpu.make_async_copy(
                tile.at[index % 2],
                R.stage[name].at[index],
                DR.at[S.stage + 4 * name + index],
            ).wait()
            grad_send(name, *QUARTERS[index])

    def sum_room(name):
        if name == QUERY:
            return R.wg.at[0 : width // 4, 0 : R.wq.shape[1]]
        cols = name * (width // 4)
        return R.wd.at[0 : R.tile[name].shape[1], cols : cols + width // 4]

    def grad_add(name):
        tile = R.tile[name]
        count, cols = tile.shape[1:]
        places = (
            (tile.at[0], tile.at[1]),
            (R.wu.at[0:count, 0:cols], R.wu.at[0:count, cols : 2 * cols]),
        )
        loads = []
        for turn_at, yy in enumerate((1 - y, y)):
            for k, (source, base) in enumerate(((R.px, S.px), (R.pc, S.pc))):
                arrived(source[name].at[yy], base + 4 * name + yy)
                load = pltpu.make_async_copy(
                    source[name].at[yy],
                    places[turn_at][k],
                    DR.at[S.ld + 4 * name + 2 * turn_at + k],
                )
                load.start()
                loads.append(load)
        for turn_at in range(2):
            loads[2 * turn_at].wait()
            loads[2 * turn_at + 1].wait()
            one, two = places[turn_at]
            into = sum_room(name) if turn_at == 0 else one

            @pl.loop(0, count // 32)
            def _(i):
                at = pl.ds(pl.multiple_of(i * 32, 32), 32)
                into[at, :] = (one[at, :].astype(F32) + two[at, :].astype(F32)).astype(BF16)

            if turn_at == 0:
                send(
                    into, R.other[name], S.py + name, S.py + name, across_y
                ).start()
            else:
                store = pltpu.make_async_copy(
                    into, R.mine[name], DR.at[S.st + name]
                )
                store.start()
                store.wait()

    swap_start(LEN, R.lens, R.len)
    swap_start(TOK, R.tokens, R.tok)
    swap_wait(LEN, R.len)
    swap_wait(TOK, R.tok)
    swap_start(WQ, R.w_query, R.wq)

    def norm_rows(first, count):
        at = pl.ds(first, count)
        value = R.tok[at, :].astype(F32)
        inverse = lax.rsqrt(jnp.mean(value * value, axis=1, keepdims=True) + EPSILON)
        R.norm[pl.ds(own_at + first, count), :] = (
            value * inverse * R.gain_attn[0:1, :]
        ).astype(BF16)

    each_rows(norm_rows)
    gather_start(GN, R.norm)
    swap_start(OG, R.out_grad, R.og)
    swap_start(KVG, R.kv_grad, R.kvg)
    rotary()
    swap_wait(WQ, R.wq)
    gather_own(GN, R.norm, project)
    for step in range(nz - 1):
        gather_pass(GN, R.norm, step)
        if step == 0:
            swap_start(WO, R.w_attn_out, R.wo)
            swap_wait(OG, R.og)
            swap_wait(KVG, R.kvg)

            def mask_rows(first, count):
                at = pl.ds(first, count)
                R.gmlp[pl.ds(own_at + first, count), :] = (
                    keep_of(first, count) * R.og[at, :].astype(F32)
                ).astype(BF16)

            each_rows(mask_rows)
        if step == 1:
            swap_start(WG, R.w_gate, R.wg)
        gather_use(GN, R.norm, step, project)
    gather_start(GG, R.gmlp)
    spill = pltpu.make_async_copy(R.norm, R.norm_store, DR.at[S.spill])
    spill.start()
    swap_wait(WO, R.wo)
    swap_start(WU, R.w_up, R.wu)

    for step in range(nz - 1):
        scatter_step(RO, step, out_term)
        gather_pass(GG, R.gmlp, step)
    scatter_term(RO, z, out_term)
    scatter_end(RO)
    for step in range(nz - 1):
        gather_use(GG, R.gmlp, step, None)
    gather_own(GG, R.gmlp, None)
    swap_start(WD, R.w_down, R.wd)

    def mid_rows(first, count):
        at = pl.ds(first, count)
        mid = R.tok[at, :].astype(F32) + R.acc[at, :]
        R.mid[at, :] = mid
        inverse = lax.rsqrt(jnp.mean(mid * mid, axis=1, keepdims=True) + EPSILON)
        R.nmlp[pl.ds(own_at + first, count), :] = (
            mid * inverse * R.gain_mlp[0:1, :]
        ).astype(BF16)

    each_rows(mid_rows)
    gather_start(GM, R.nmlp)
    scatter_sent(RO)
    gather_end(GN, R.norm)
    spill.wait()
    swap_wait(WG, R.wg)
    swap_wait(WU, R.wu)
    gather_own(GM, R.nmlp, forward_mlp)
    for step in range(nz - 1):
        gather_pass(GM, R.nmlp, step)
        gather_use(GM, R.nmlp, step, forward_mlp)
    swap_wait(WD, R.wd)

    for step in range(nz - 1):
        scatter_step(RB, step, back_term)
        if step == 0:
            grad_make(DOWN, R.hid, R.gmlp)
    scatter_term(RB, z, back_term)
    scatter_end(RB)
    R.gains[...] = jnp.zeros(R.gains.shape, F32)

    def fold(value):
        return jnp.sum(value.reshape(value.shape[0] // 8, 8, value.shape[1]), axis=0)

    def d_mid_rows(first, count):
        at = pl.ds(first, count)
        mid = R.mid[at, :]
        inverse = lax.rsqrt(jnp.mean(mid * mid, axis=1, keepdims=True) + EPSILON)
        unit = mid * inverse
        back = R.acc[at, :]
        R.gains[1] += fold(back * unit)
        e = back * R.gain_mlp[0:1, :]
        grad = keep_of(first, count) * R.og[at, :].astype(F32) + inverse * (
            e - unit * jnp.mean(e * unit, axis=1, keepdims=True)
        )
        R.dmid[at, :] = grad
        R.norm[pl.ds(own_at + first, count), :] = grad.astype(BF16)

    each_rows(d_mid_rows)
    gather_start(GA, R.norm)
    scatter_sent(RB)
    gather_end(GG, R.gmlp)
    back_norm = pltpu.make_async_copy(R.norm_store, R.gmlp, DR.at[S.spill + 1])
    back_norm.start()
    gather_own(GA, R.norm, d_attended)
    grad_make(GATE, R.dgate, R.nmlp)
    for step in range(nz - 1):
        gather_pass(GA, R.norm, step)
        scatter_step(RD, step, down_term)
        gather_use(GA, R.norm, step, d_attended)
        if step == 1:
            grad_make(UP, R.dup, R.nmlp)
    scatter_term(RD, z, down_term)
    scatter_end(RD)

    def out_rows(first, count):
        at = pl.ds(first, count)
        R.bo[at, :] = (keep_of(first, count) * (R.mid[at, :] + R.acc[at, :])).astype(BF16)

    each_rows(out_rows)
    swap_start(BO, R.bo, R.block_out)
    scatter_sent(RD)
    gather_end(GM, R.nmlp)
    R.dkv[...] = jnp.zeros(R.dkv.shape, F32)
    back_norm.wait()

    for step in range(nz - 1):
        scatter_step(RQ, step, query_term)
        if step == 0:
            grad_make(OUT, R.att, R.norm)
    scatter_term(RQ, z, query_term)

    R.dkvb[...] = R.dkv[...].astype(BF16)
    for zz in range(nz):
        send(
            piece(R.dkvb, zz, 1 - c),
            R.kc.at[zz],
            S.kc + zz,
            S.kc + zz,
            sibling,
        ).start()
    grad_make(QUERY, R.gmlp, R.dq)
    for zz in range(nz):
        arrived(R.kc.at[zz], S.kc + zz)
        R.ks[zz] = (
            R.dkv[pl.ds(pl.multiple_of((2 * zz + c) * rows, rows), rows), :]
            + R.kc[zz].astype(F32)
        ).astype(BF16)

        @pl.when(zz != z)
        def _():
            send(R.ks.at[zz], R.kz.at[z], S.kz + zz, S.kz + z, dev(y, c, zz, x)).start()

    R.kacc[...] = keep_of(0, rows) * R.kvg[...].astype(F32) + R.ks[z].astype(F32)
    for zz in range(nz):

        @pl.when(zz != z)
        def _():
            arrived(R.kz.at[zz], S.kz + zz)
            R.kacc[...] += R.kz[zz].astype(F32)

    own_rows = pl.ds(own_at, rows)
    R.dkva[own_rows, :head] = turn(
        R.kacc[:, :head], R.cos[own_rows, :], -R.sin[own_rows, :]
    ).astype(BF16)
    R.dkva[own_rows, head:] = R.kacc[:, head:].astype(BF16)
    own_kv = piece(R.dkva, z, c)
    for zz in range(nz):
        for cc in range(2):

            @pl.when((zz != z) | (cc != c))
            def _():
                send(
                    own_kv, own_kv, S.ka + 2 * zz + cc, S.ka + 2 * z + c, dev(y, cc, zz, x)
                ).start()

    grad_add(DOWN)
    for zz in range(nz):
        for cc in range(2):

            @pl.when((zz != z) | (cc != c))
            def _():
                arrived(piece(R.dkva, zz, cc), S.ka + 2 * zz + cc)

    first_col = c * (4 * nz * 32) + z * 128
    for yy in range(2):
        cols = pl.ds(pl.multiple_of(yy * (width // 2) + first_col, 128), 128)
        R.gkv[yy] = dot_cols(R.gmlp[:, cols], R.dkva[...])
    send(
        R.gkv.at[1 - y], R.kyb, S.kyx, S.kyx, across_y
    ).start()
    arrived(R.kyb, S.kyx)
    R.kysum[...] = R.gkv[y] + R.kyb[...]
    send(
        R.kysum.at[pl.ds(pl.multiple_of((1 - x) * 64, 64), 64)],
        R.kxb,
        S.kyx + 1,
        S.kyx + 1,
        across_x,
    ).start()
    arrived(R.kxb, S.kyx + 1)
    R.kfinal[...] = (
        R.kysum[pl.ds(pl.multiple_of(x * 64, 64), 64), :] + R.kxb[...]
    )
    kv_out = pltpu.make_async_copy(R.kfinal, R.grad_w_kv, DR.at[S.outs])
    kv_out.start()
    grad_add(GATE)

    scatter_end(RQ)
    for n, size in tiles(width, 512):
        some = slice(n, n + size)
        R.acc[:, some] += dot_rows(R.dkva[own_rows, :], R.wkv[some, :])

    def tail_rows(first, count):
        at = pl.ds(first, count)
        value = R.tok[at, :].astype(F32)
        inverse = lax.rsqrt(jnp.mean(value * value, axis=1, keepdims=True) + EPSILON)
        unit = value * inverse
        back = R.acc[at, :]
        R.gains[0] += fold(back * unit)
        e = back * R.gain_attn[0:1, :]
        R.gt[at, :] = (
            R.dmid[at, :]
            + inverse * (e - unit * jnp.mean(e * unit, axis=1, keepdims=True))
        ).astype(BF16)

    each_rows(tail_rows)
    swap_start(GT, R.gt, R.grad_tokens)

    line = lax.broadcasted_iota(jnp.int32, (8, width), 0)
    gain_first = jnp.sum(R.gains[0], axis=0, keepdims=True)
    gain_second = jnp.sum(R.gains[1], axis=0, keepdims=True)
    R.ga[...] = jnp.where(line == 0, gain_first, jnp.where(line == 1, gain_second, 0.0))
    part_y, part_c = width // 2, width // 4

    def cols_of(index, size):
        return pl.ds(pl.multiple_of(index * size, size), size)

    send(
        R.ga.at[:, cols_of(1 - y, part_y)], R.gb_y, S.gains, S.gains, across_y
    ).start()
    arrived(R.gb_y, S.gains)
    R.ga_y[...] = R.ga[:, cols_of(y, part_y)] + R.gb_y[...]
    send(
        R.ga_y.at[:, cols_of(1 - c, part_c)],
        R.gb_c,
        S.gains + 1,
        S.gains + 1,
        sibling,
    ).start()
    arrived(R.gb_c, S.gains + 1)
    R.ga_c[...] = R.ga_y[:, cols_of(c, part_c)] + R.gb_c[...]
    send(R.ga_c, R.gb_x, S.gains + 2, S.gains + 2, across_x).start()
    arrived(R.gb_x, S.gains + 2)
    R.ga_x[...] = R.ga_c[...] + R.gb_x[...]
    for zz in range(nz):

        @pl.when(zz != z)
        def _():
            send(
                R.ga_x.at[:, zz * 128 : (zz + 1) * 128],
                R.gb_z.at[z],
                S.gains + 3 + zz,
                S.gains + 3 + z,
                dev(y, c, zz, x),
            ).start()

    R.gfinal[...] = R.ga_x[:, cols_of(z, 128)]
    for zz in range(nz):

        @pl.when(zz != z)
        def _():
            arrived(R.gb_z.at[zz], S.gains + 3 + zz)
            R.gfinal[...] += R.gb_z[zz]

    gain_out = pltpu.make_async_copy(R.gfinal, R.grad_gains, DR.at[S.outs + 1])
    gain_out.start()

    for name in (UP, OUT, QUERY):
        grad_add(name)
    for name in GRADS:
        arrived(R.other[name], S.py + name)
        sent(sum_room(name), S.py + name)
        for yy, cc in QUARTERS:
            grad_sent(name, yy, cc)
    kv_out.wait()
    gain_out.wait()
    scatter_sent(RQ)
    gather_end(GA, R.norm)
    swap_wait(BO, R.block_out)
    swap_wait(GT, R.grad_tokens)
    for item, src in enumerate(
        (R.lens, R.tokens, R.w_query, R.out_grad, R.kv_grad, R.w_attn_out, R.w_gate, R.w_up,
         R.w_down, R.bo, R.gt)
    ):
        swap_sent(item, src)
    for zz in range(nz):
        sent(piece(R.dkvb, zz, 1 - c), S.kc + zz)

        @pl.when(zz != z)
        def _():
            sent(R.ks.at[zz], S.kz + zz)
            sent(R.ga_x.at[:, zz * 128 : (zz + 1) * 128], S.gains + 3 + zz)

        for cc in range(2):

            @pl.when((zz != z) | (cc != c))
            def _():
                sent(own_kv, S.ka + 2 * zz + cc)

    sent(R.gkv.at[1 - y], S.kyx)
    sent(R.kysum.at[pl.ds(pl.multiple_of((1 - x) * 64, 64), 64)], S.kyx + 1)
    sent(R.ga.at[:, cols_of(1 - y, part_y)], S.gains)
    sent(R.ga_y.at[:, cols_of(1 - c, part_c)], S.gains + 1)
    sent(R.ga_c, S.gains + 2)


def fused(nz, *args):
    (tokens, lengths, gain_attn, w_query, w_kv, w_attn_out, gain_mlp, w_gate, w_up, w_down,
     out_grad, kv_grad) = args
    rows, width = tokens.shape
    ff = w_gate.shape[1]
    qw = w_query.shape[1]
    total, pair = 2 * nz * rows, 2 * rows
    pieces = lengths.shape[1]
    head = w_kv.shape[1] // 2
    lens = jnp.broadcast_to(
        jnp.pad(lengths[0].astype(F32), (0, 8 - pieces))[:, None], (8, 128)
    )
    half_width = head // 2
    freqs = ROTARY_BASE ** (-jnp.arange(half_width, dtype=F32) / half_width)
    freq = jnp.broadcast_to(jnp.concatenate([freqs, freqs])[None, :], (8, 128))
    anywhere, vmem = pl.BlockSpec(memory_space=pl.ANY), pl.BlockSpec(memory_space=pltpu.VMEM)
    ins = dict(
        tokens=(tokens, anywhere),
        lens=(lens, vmem),
        freq=(freq, vmem),
        gain_attn=(jnp.broadcast_to(gain_attn[None], (8, width)), vmem),
        gain_mlp=(jnp.broadcast_to(gain_mlp[None], (8, width)), vmem),
        w_query=(w_query, anywhere),
        wkv=(w_kv, vmem),
        w_attn_out=(w_attn_out, anywhere),
        w_gate=(w_gate.T, anywhere),
        w_up=(w_up.T, anywhere),
        w_down=(w_down, anywhere),
        out_grad=(out_grad, anywhere),
        kv_grad=(kv_grad, anywhere),
    )
    quarter = width // 4
    grad_tiles = [(ff, quarter), (ff, quarter), (ff, quarter), (qw, quarter), (quarter, qw)]
    outs = dict(
        block_out=((rows, width), BF16),
        grad_tokens=((rows, width), BF16),
        grad_w_kv=((64, 2 * head), F32),
        grad_gains=((8, 128), F32),
        norm_store=((total, width), BF16),
    )
    moved = [
        (shape, BF16)
        for tile in grad_tiles
        for shape in (tile, tile, (4,) + tile, (2,) + tile, (2,) + tile)
    ]
    S, count = semaphores(nz)
    scratch = dict(
        len=((8, 128), F32),
        last=((8, 128), F32),
        tok=((rows, width), BF16),
        og=((rows, width), BF16),
        kvg=((rows, 2 * head), BF16),
        wq=((width, qw), BF16),
        wo=((qw, width), BF16),
        wg=((ff, width), BF16),
        wu=((ff, width), BF16),
        wd=((ff, width), BF16),
        norm=((total, width), BF16),
        nmlp=((total, width), BF16),
        gmlp=((total, width), BF16),
        cos=((total, 128), F32),
        sin=((total, 128), F32),
        start=((total, 128), F32),
        q=((total, qw), BF16),
        kv=((total, 2 * head), BF16),
        att=((total, qw), BF16),
        datt=((total, qw), BF16),
        dq=((total, qw), BF16),
        probs=((qw // head, total, total), BF16),
        hid=((total, ff), BF16),
        dgate=((total, ff), BF16),
        dup=((total, ff), BF16),
        part=((nz, pair, width), BF16),
        from_core=((nz, rows, width), BF16),
        from_z=((2, nz + 1, rows, width), BF16),
        acc=((rows, width), F32),
        mid=((rows, width), F32),
        dmid=((rows, width), F32),
        bo=((rows, width), BF16),
        gt=((rows, width), BF16),
        gains=((2, 8, width), F32),
        ga=((8, width), F32),
        ga_y=((8, width // 2), F32),
        gb_y=((8, width // 2), F32),
        ga_c=((8, width // 4), F32),
        gb_c=((8, width // 4), F32),
        ga_x=((8, width // 4), F32),
        gb_x=((8, width // 4), F32),
        gb_z=((nz, 8, 128), F32),
        gfinal=((8, 128), F32),
        dkv=((total, 2 * head), F32),
        dkvb=((total, 2 * head), BF16),
        dkva=((total, 2 * head), BF16),
        kc=((nz, rows, 2 * head), BF16),
        ks=((nz, rows, 2 * head), BF16),
        kz=((nz, rows, 2 * head), BF16),
        kacc=((rows, 2 * head), F32),
        gkv=((2, 128, 2 * head), F32),
        kyb=((128, 2 * head), F32),
        kysum=((128, 2 * head), F32),
        kxb=((64, 2 * head), F32),
        kfinal=((64, 2 * head), F32),
    )
    tile_shapes = (grad_tiles[DOWN], grad_tiles[OUT], grad_tiles[QUERY])
    out_shapes = list(outs.values()) + moved
    scratch_shapes = list(scratch.values()) + [((2,) + shape, BF16) for shape in tile_shapes]

    def body(*refs):
        refs = list(refs)

        def take(count):
            taken = refs[:count]
            del refs[:count]
            return taken

        R = types.SimpleNamespace(
            **dict(zip(ins, take(len(ins)))), **dict(zip(outs, take(len(outs))))
        )
        rest = take(len(moved))
        R.mine, R.other, R.stage, R.px, R.pc = (rest[k::5] for k in range(5))
        for key, ref in zip(scratch, take(len(scratch))):
            setattr(R, key, ref)
        big, out_tile, query_tile = take(3)
        R.tile = [big, big, big, out_tile, query_tile]
        R.send, R.recv = refs
        block_kernel(nz, pieces, S, R)

    results = pl.pallas_call(
        body,
        out_shape=[jax.ShapeDtypeStruct(shape, kind) for shape, kind in out_shapes],
        in_specs=[spec for _, spec in ins.values()],
        out_specs=[anywhere] * len(out_shapes),
        scratch_shapes=[pltpu.VMEM(shape, kind) for shape, kind in scratch_shapes]
        + [pltpu.SemaphoreType.DMA((count,))] * 2,
        compiler_params=pltpu.CompilerParams(
            collective_id=0, has_side_effects=True, vmem_limit_bytes=63 * MIB
        ),
        name="block",
    )(*[value for value, _ in ins.values()])
    block_out, grad_tokens, grad_w_kv, grad_gains = results[:4]
    mine, other = results[5::5], results[6::5]
    sums = [one.astype(F32) + two.astype(F32) for one, two in zip(mine, other)]
    gains = lax.dynamic_slice_in_dim(
        grad_gains, (lax.axis_index("tensor") % 2) * 64, 64, 1
    )
    return (
        block_out,
        grad_tokens,
        gains[0],
        sums[QUERY],
        grad_w_kv,
        sums[OUT],
        gains[1],
        sums[GATE].T,
        sums[UP].T,
        sums[DOWN],
    )


def solution(mesh):
    groups, parts = mesh.shape["dp"], mesh.shape["tensor"]
    paired = groups == 4 and parts == 8
    per_group = functools.partial(fused, parts // 2) if paired else per_device
    placed = (
        P(("dp", "tensor"), None),
        P("dp", None),
        P(),
        P(None, "tensor"),
        P(),
        P("tensor", None),
        P(),
        P(None, "tensor"),
        P(None, "tensor"),
        P("tensor", None),
        P(("dp", "tensor"), None),
        P(("dp", "tensor"), None),
    )
    return jax.shard_map(
        per_group,
        mesh=mesh,
        in_specs=placed,
        out_specs=(
            P(("dp", "tensor"), None),
            P(("dp", "tensor"), None),
            P(("dp", "tensor")),
            P("dp", "tensor"),
            P(("dp", "tensor"), None),
            P("tensor", "dp"),
            P(("dp", "tensor")),
            P("dp", "tensor"),
            P("dp", "tensor"),
            P("tensor", "dp"),
        ),
        check_vma=False,
    )
```

```python
import functools
import types

import jax
import jax.numpy as jnp
import numpy as np
from jax import lax
from jax.experimental import pallas as pl
from jax.experimental.pallas import tpu as pltpu
from jax.sharding import PartitionSpec as P

SPAN = 64


EPSILON = 1e-05
ROTARY_BASE = 10000.0
MASKED = -1e30


def rotary_tables(positions, width):
    half_width = width // 2
    freqs = ROTARY_BASE ** (-jnp.arange(half_width, dtype=jnp.float32) / half_width)
    angles = positions[:, None] * freqs[None, :]
    return (jnp.cos(angles), jnp.sin(angles))


def rotate(values, cosine, sine):
    half_width = values.shape[-1] // 2
    first_half = values[..., :half_width]
    second_half = values[..., half_width:]
    return jnp.concatenate(
        [first_half * cosine - second_half * sine, second_half * cosine + first_half * sine],
        axis=-1,
    )


def unrotate(values, cosine, sine):
    half_width = values.shape[-1] // 2
    first_half = values[..., :half_width]
    second_half = values[..., half_width:]
    return jnp.concatenate(
        [first_half * cosine + second_half * sine, second_half * cosine - first_half * sine],
        axis=-1,
    )


def layout(piece_units, rows):
    piece_rows = piece_units * SPAN
    ends = jnp.cumsum(piece_rows)
    starts = ends - piece_rows
    row_steps = jnp.arange(rows, dtype=jnp.int32)
    segment = jnp.sum((row_steps[:, None] >= ends[None, :]).astype(jnp.int32), axis=1)
    member = segment[:, None] == jnp.arange(piece_units.shape[0], dtype=jnp.int32)[None, :]
    row_start = jnp.sum(jnp.where(member, starts[None, :], 0), axis=1)
    positions = (row_steps - row_start).astype(jnp.float32)
    keep = (segment < piece_units.shape[0] - 1).astype(jnp.float32)
    return (segment, row_steps, positions, keep)


def permitted(block_segment, block_steps, segment, row_steps):
    return (block_segment[:, None] == segment[None, :]) & (
        row_steps[None, :] <= block_steps[:, None]
    )


def spread_rows(values):
    return lax.all_gather(values, "tensor", axis=0, tiled=True)


def spread_grads(values):
    return lax.all_gather(values, "tensor", axis=0, tiled=True)


def per_device(
    tokens,
    lengths,
    gain_attn,
    w_query,
    w_kv,
    w_attn_out,
    gain_mlp,
    w_gate,
    w_up,
    w_down,
    out_grad,
    kv_grad,
):
    local_rows = tokens.shape[0]
    parts = lax.axis_size("tensor")
    total_rows = local_rows * parts
    first_row = lax.axis_index("tensor") * local_rows
    segment, row_steps, positions, keep = layout(lengths[0], total_rows)
    head_dim = w_kv.shape[1] // 2
    local_heads = w_query.shape[1] // head_dim
    scale = head_dim ** (-0.5)
    cosine, sine = rotary_tables(positions, head_dim)
    row_keep = lax.dynamic_slice_in_dim(keep, first_row, local_rows, 0)[:, None]
    row_cosine = lax.dynamic_slice_in_dim(cosine, first_row, local_rows, 0)
    row_sine = lax.dynamic_slice_in_dim(sine, first_row, local_rows, 0)
    tokens_full = tokens.astype(jnp.float32)
    inv_first = lax.rsqrt(jnp.mean(tokens_full * tokens_full, axis=-1, keepdims=True) + EPSILON)
    unit_first = tokens_full * inv_first
    normed_rows = (unit_first * gain_attn).astype(jnp.bfloat16)
    normed = spread_rows(normed_rows)
    queries = jnp.dot(normed, w_query, preferred_element_type=jnp.float32).reshape(
        total_rows, local_heads, head_dim
    )
    queries = rotate(queries, cosine[:, None, :], sine[:, None, :]).astype(jnp.bfloat16)
    kv_raw = jnp.dot(normed, w_kv, preferred_element_type=jnp.float32)
    shared = jnp.concatenate(
        [rotate(kv_raw[:, :head_dim], cosine, sine), kv_raw[:, head_dim:]], axis=1
    ).astype(jnp.bfloat16)
    keys = shared[:, :head_dim]
    values = shared[:, head_dim:]
    block = min(512, total_rows)
    count = total_rows // block
    pieces = []
    log_totals = []
    for number in range(count):
        begin = number * block
        query_block = queries[begin : begin + block]
        allowed = permitted(
            segment[begin : begin + block], row_steps[begin : begin + block], segment, row_steps
        )
        scores = (
            jnp.einsum("qhd,kd->hqk", query_block, keys, preferred_element_type=jnp.float32) * scale
        )
        scores = jnp.where(allowed[None], scores, MASKED)
        row_max = jnp.max(scores, axis=-1, keepdims=True)
        exp_scores = jnp.exp(scores - row_max)
        row_total = jnp.sum(exp_scores, axis=-1, keepdims=True)
        log_totals.append(row_max + jnp.log(row_total))
        weights = (exp_scores / row_total).astype(jnp.bfloat16)
        pieces.append(
            jnp.einsum("hqk,kd->qhd", weights, values, preferred_element_type=jnp.float32).astype(
                jnp.bfloat16
            )
        )
    attended = jnp.concatenate(pieces, axis=0).reshape(total_rows, local_heads * head_dim)
    attn_rows = lax.psum_scatter(
        jnp.dot(attended, w_attn_out, preferred_element_type=jnp.float32).astype(jnp.bfloat16),
        "tensor",
        scatter_dimension=0,
        tiled=True,
    ).astype(jnp.float32)
    mid = tokens_full + attn_rows
    inv_second = lax.rsqrt(jnp.mean(mid * mid, axis=-1, keepdims=True) + EPSILON)
    unit_second = mid * inv_second
    normed_mlp = spread_rows((unit_second * gain_mlp).astype(jnp.bfloat16))
    gate = jnp.dot(normed_mlp, w_gate, preferred_element_type=jnp.float32)
    up = jnp.dot(normed_mlp, w_up, preferred_element_type=jnp.float32)
    sigma = jax.nn.sigmoid(gate)
    active = gate * sigma
    hidden = (active * up).astype(jnp.bfloat16)
    mlp_rows = lax.psum_scatter(
        jnp.dot(hidden, w_down, preferred_element_type=jnp.float32).astype(jnp.bfloat16),
        "tensor",
        scatter_dimension=0,
        tiled=True,
    ).astype(jnp.float32)
    block_out = (row_keep * (mid + mlp_rows)).astype(jnp.bfloat16)
    out_full = row_keep * out_grad.astype(jnp.float32)
    grad_mlp = spread_grads(out_full.astype(jnp.bfloat16))
    g_down = jnp.einsum("rf,rd->fd", hidden, grad_mlp, preferred_element_type=jnp.float32)
    g_hidden = jnp.einsum("rd,fd->rf", grad_mlp, w_down, preferred_element_type=jnp.float32)
    d_gate = (g_hidden * up * sigma * (1.0 + gate * (1.0 - sigma))).astype(jnp.bfloat16)
    d_up = (g_hidden * active).astype(jnp.bfloat16)
    g_gate = jnp.einsum("rd,rf->df", normed_mlp, d_gate, preferred_element_type=jnp.float32)
    g_up = jnp.einsum("rd,rf->df", normed_mlp, d_up, preferred_element_type=jnp.float32)
    back_mlp = lax.psum_scatter(
        (
            jnp.einsum("rf,df->rd", d_gate, w_gate, preferred_element_type=jnp.float32)
            + jnp.einsum("rf,df->rd", d_up, w_up, preferred_element_type=jnp.float32)
        ).astype(jnp.bfloat16),
        "tensor",
        scatter_dimension=0,
        tiled=True,
    ).astype(jnp.float32)
    e_mlp = back_mlp * gain_mlp
    g_gain_mlp = jnp.sum(back_mlp * unit_second, axis=0)
    d_mid = out_full + inv_second * (
        e_mlp - unit_second * jnp.mean(e_mlp * unit_second, axis=-1, keepdims=True)
    )
    grad_attn = spread_grads(d_mid.astype(jnp.bfloat16))
    g_attn_out = jnp.einsum("rh,rd->hd", attended, grad_attn, preferred_element_type=jnp.float32)
    d_att = jnp.einsum(
        "rd,hd->rh", grad_attn, w_attn_out, preferred_element_type=jnp.float32
    ).astype(jnp.bfloat16)
    d_att = d_att.reshape(total_rows, local_heads, head_dim)
    query_pieces = []
    d_keys = jnp.zeros((total_rows, head_dim), jnp.float32)
    d_values = jnp.zeros((total_rows, head_dim), jnp.float32)
    for number in range(count):
        begin = number * block
        query_block = queries[begin : begin + block]
        grad_block = d_att[begin : begin + block]
        allowed = permitted(
            segment[begin : begin + block], row_steps[begin : begin + block], segment, row_steps
        )
        scores = (
            jnp.einsum("qhd,kd->hqk", query_block, keys, preferred_element_type=jnp.float32) * scale
        )
        scores = jnp.where(allowed[None], scores, MASKED)
        probs = jnp.exp(scores - log_totals[number])
        weights = probs.astype(jnp.bfloat16)
        d_probs = jnp.einsum("qhd,kd->hqk", grad_block, values, preferred_element_type=jnp.float32)
        inner = jnp.sum(d_probs * probs, axis=-1, keepdims=True)
        d_scores = (probs * (d_probs - inner)).astype(jnp.bfloat16)
        query_pieces.append(
            jnp.einsum("hqk,kd->qhd", d_scores, keys, preferred_element_type=jnp.float32) * scale
        )
        d_keys = (
            d_keys
            + jnp.einsum("hqk,qhd->kd", d_scores, query_block, preferred_element_type=jnp.float32)
            * scale
        )
        d_values = d_values + jnp.einsum(
            "hqk,qhd->kd", weights, grad_block, preferred_element_type=jnp.float32
        )
    d_queries = jnp.concatenate(query_pieces, axis=0)
    d_queries = unrotate(d_queries, cosine[:, None, :], sine[:, None, :]).astype(jnp.bfloat16)
    d_queries = d_queries.reshape(total_rows, local_heads * head_dim)
    g_query = jnp.einsum("rd,rh->dh", normed, d_queries, preferred_element_type=jnp.float32)
    kv_rows = lax.psum_scatter(
        jnp.concatenate([d_keys, d_values], axis=1).astype(jnp.bfloat16),
        "tensor",
        scatter_dimension=0,
        tiled=True,
    ).astype(jnp.float32)
    kv_rows = kv_rows + row_keep * kv_grad.astype(jnp.float32)
    d_kv = jnp.concatenate(
        [unrotate(kv_rows[:, :head_dim], row_cosine, row_sine), kv_rows[:, head_dim:]], axis=1
    ).astype(jnp.bfloat16)
    d_kv_all = lax.all_gather(d_kv, "tensor", axis=0, tiled=True)
    width = normed.shape[1]
    groups = lax.axis_size("dp")
    own = lax.dynamic_index_in_dim(
        normed.reshape(total_rows, groups, parts, width // (groups * parts)),
        lax.axis_index("tensor"),
        2,
        False,
    ).reshape(total_rows, width // parts)
    g_kv = jnp.einsum("rd,rk->dk", own, d_kv_all, preferred_element_type=jnp.float32)
    back_attn = lax.psum_scatter(
        jnp.einsum("rh,dh->rd", d_queries, w_query, preferred_element_type=jnp.float32).astype(
            jnp.bfloat16
        ),
        "tensor",
        scatter_dimension=0,
        tiled=True,
    ).astype(jnp.float32)
    back_attn = back_attn + jnp.einsum("rk,dk->rd", d_kv, w_kv, preferred_element_type=jnp.float32)
    e_attn = back_attn * gain_attn
    g_gain_attn = jnp.sum(back_attn * unit_first, axis=0)
    grad_tokens = (
        d_mid
        + inv_first * (e_attn - unit_first * jnp.mean(e_attn * unit_first, axis=-1, keepdims=True))
    ).astype(jnp.bfloat16)
    kv_sum = lax.psum_scatter(g_kv, "dp", scatter_dimension=0, tiled=True)
    share = width // (groups * parts)
    first = (lax.axis_index("dp") * parts + lax.axis_index("tensor")) * share
    gain_all = lax.all_gather(jnp.stack([g_gain_attn, g_gain_mlp]), ("dp", "tensor"), axis=0)
    gain_sums = jnp.sum(lax.dynamic_slice_in_dim(gain_all, first, share, 2), axis=0)
    query_sum, out_sum, gate_sum, up_sum, down_sum = (
        lax.psum_scatter(
            g_query.astype(jnp.bfloat16), "dp", scatter_dimension=0, tiled=True
        ).astype(jnp.float32),
        lax.psum_scatter(
            g_attn_out.astype(jnp.bfloat16), "dp", scatter_dimension=1, tiled=True
        ).astype(jnp.float32),
        lax.psum_scatter(g_gate.astype(jnp.bfloat16), "dp", scatter_dimension=0, tiled=True).astype(
            jnp.float32
        ),
        lax.psum_scatter(g_up.astype(jnp.bfloat16), "dp", scatter_dimension=0, tiled=True).astype(
            jnp.float32
        ),
        lax.psum_scatter(g_down.astype(jnp.bfloat16), "dp", scatter_dimension=1, tiled=True).astype(
            jnp.float32
        ),
    )
    return (
        block_out,
        grad_tokens,
        gain_sums[0],
        query_sum,
        kv_sum,
        out_sum,
        gain_sums[1],
        gate_sum,
        up_sum,
        down_sum,
    )


F32, BF16 = jnp.float32, jnp.bfloat16
MESH = pl.DeviceIdType.MESH
MIB = 1 << 20


def dot(a, b):
    return jnp.dot(a, b, preferred_element_type=F32)


def dot_rows(a, b):
    return lax.dot_general(a, b, (((1,), (1,)), ((), ())), preferred_element_type=F32)


def dot_cols(a, b):
    return lax.dot_general(a, b, (((0,), (0,)), ((), ())), preferred_element_type=F32)


def tiles(width, step):
    return [(at, min(step, width - at)) for at in range(0, width, step)]


GN, GG, GM, GA = range(4)
RO, RB, RD, RQ = range(4)
LEN, TOK, WQ, OG, KVG, WO, WG, WU, WD, BO, GT = range(11)
DOWN, GATE, UP, OUT, QUERY = GRADS = range(5)


def semaphores(nz):
    counts = dict(
        swap=11,
        swap_y=11,
        gz=4 * 2 * nz,
        gc=4 * nz,
        rz=4 * 2 * nz,
        rc=4 * nz,
        stage=20,
        px=20,
        pc=20,
        py=5,
        ld=20,
        st=5,
        kc=nz,
        kz=nz,
        ka=2 * nz,
        kyx=2,
        gains=3 + nz,
        spill=2,
        outs=4,
    )
    firsts, total = {}, 0
    for name, count in counts.items():
        firsts[name] = total
        total += count
    return types.SimpleNamespace(**firsts), total


def block_kernel(nz, pieces, S, R):
    rows, width = R.tokens.shape
    ff = R.w_down.shape[0]
    total = 2 * nz * rows
    pair = 2 * rows
    head = 128
    heads = R.wq.shape[1] // head
    scale = head ** (-0.5)
    DS, DR = R.send, R.recv

    dp, tensor = lax.axis_index("dp"), lax.axis_index("tensor")
    y, c = dp // 2, dp % 2
    z, x = tensor // 2, tensor % 2
    keeper = c == x

    def dev(yy, cc, zz, xx):
        return (2 * yy + cc, 2 * zz + xx)

    sibling = dev(y, 1 - c, z, x)
    partner = dev(y, 1 - c, z, 1 - x)
    across_x = dev(y, c, z, 1 - x)
    across_y = dev(1 - y, c, z, x)

    def send(src, dst, s, r, to):
        return pltpu.make_async_remote_copy(
            src_ref=src,
            dst_ref=dst,
            send_sem=DS.at[s],
            recv_sem=DR.at[r],
            device_id=to,
            device_id_type=MESH,
        )

    def arrived(dst, r):
        pltpu.make_async_copy(dst, dst, DR.at[r]).wait()

    def sent(src, s):
        pltpu.make_async_copy(src, src, DS.at[s]).wait()

    barrier = pltpu.get_barrier_semaphore()
    for to in (across_x, across_y, partner):
        pl.semaphore_signal(barrier, inc=1, device_id=to, device_id_type=MESH)
    for zz in range(nz):
        for cc in range(2):

            @pl.when((zz != z) | (cc != c))
            def _():
                pl.semaphore_signal(
                    barrier, inc=1, device_id=dev(y, cc, zz, x), device_id_type=MESH
                )

    pl.semaphore_wait(barrier, 3 + 2 * nz - 1)

    def swap_start(item, src, dst):
        at = S.swap + item

        @pl.when(keeper)
        def _():
            pltpu.make_async_copy(src, dst, DR.at[at]).start()

        @pl.when(jnp.logical_not(keeper))
        def _():
            send(src, dst, at, at, partner).start()

    def swap_wait(item, dst):
        arrived(dst, S.swap + item)

    def swap_sent(item, src):
        @pl.when(jnp.logical_not(keeper))
        def _():
            sent(src, S.swap + item)

    def part_at(ref, which):
        count = ref.shape[0] // 2
        return ref.at[pl.ds(pl.multiple_of(which * count, count), count)]

    def weight_start(item, src, dst):
        at = S.swap + item

        @pl.when(keeper)
        def _():
            pltpu.make_async_copy(src, dst, DR.at[at]).start()

        @pl.when(jnp.logical_not(keeper))
        def _():
            send(part_at(src, y), part_at(dst, y), at, at, partner).start()

    def weight_pass(item, dst):
        @pl.when(jnp.logical_not(keeper))
        def _():
            half_here = part_at(dst, y)
            arrived(half_here, S.swap + item)
            send(half_here, half_here, S.swap_y + item, S.swap_y + item, across_y).start()

    def weight_wait(item, dst):
        @pl.when(keeper)
        def _():
            arrived(dst, S.swap + item)

        @pl.when(jnp.logical_not(keeper))
        def _():
            arrived(part_at(dst, 1 - y), S.swap_y + item)

    def weight_sent(item, src, dst):
        @pl.when(jnp.logical_not(keeper))
        def _():
            sent(part_at(src, y), S.swap + item)
            sent(part_at(dst, y), S.swap_y + item)

    def piece(ref, chunk, core):
        return ref.at[pl.ds(pl.multiple_of((2 * chunk + core) * rows, rows), rows)]

    def chunk_rows(chunk):
        return pl.ds(pl.multiple_of(chunk * pair, pair), pair)

    own_at = pl.multiple_of((2 * z + c) * rows, rows)

    def gather_start(name, ref):
        own = piece(ref, z, c)

        @pl.when(z < nz - 1)
        def _():
            send(own, own, S.gz + 2 * nz * name + z, S.gz + 2 * nz * name + z, dev(y, c, z + 1, x)).start()

        @pl.when(z > 0)
        def _():
            send(
                own, own, S.gz + 2 * nz * name + nz + z, S.gz + 2 * nz * name + z, dev(y, c, z - 1, x)
            ).start()

        send(own, own, S.gc + nz * name + z, S.gc + nz * name + z, sibling).start()

    def gather_pass(name, ref, step):
        for way in range(2):
            chunk = z - 1 - step if way == 0 else z + 1 + step

            @pl.when((chunk >= 0) & (chunk <= nz - 1))
            def _():
                part = piece(ref, chunk, c)
                arrived(part, S.gz + 2 * nz * name + chunk)
                further = z < nz - 1 if way == 0 else z > 0
                to = dev(y, c, z + 1 - 2 * way, x)

                @pl.when(further)
                def _():
                    send(
                        part,
                        part,
                        S.gz + 2 * nz * name + nz * way + chunk,
                        S.gz + 2 * nz * name + chunk,
                        to,
                    ).start()

                send(
                    part, part, S.gc + nz * name + chunk, S.gc + nz * name + chunk, sibling
                ).start()

    def gather_own(name, ref, work):
        arrived(piece(ref, z, 1 - c), S.gc + nz * name + z)
        if work is not None:
            work(z)

    def gather_use(name, ref, step, work):
        for way in range(2):
            chunk = z - 1 - step if way == 0 else z + 1 + step

            @pl.when((chunk >= 0) & (chunk <= nz - 1))
            def _():
                arrived(piece(ref, chunk, 1 - c), S.gc + nz * name + chunk)
                if work is not None:
                    work(chunk)

    def gather_end(name, ref):
        for chunk in range(nz):
            part = piece(ref, chunk, c)
            sent(part, S.gc + nz * name + chunk)

            @pl.when((z < nz - 1) & (chunk <= z))
            def _():
                sent(part, S.gz + 2 * nz * name + chunk)

            @pl.when((z > 0) & (chunk >= z))
            def _():
                sent(part, S.gz + 2 * nz * name + nz + chunk)

    def terms(name):
        return R.nmlp if name == RQ else R.part

    def half(name, chunk, core):
        return piece(terms(name), chunk, core)

    def core_room(name, chunk):
        room = R.wg if name == RQ else R.from_core
        return room.at[pl.ds(pl.multiple_of(chunk * rows, rows), rows)]

    def z_slot(name, way, chunk, at):
        slot = chunk if way == 0 else jnp.where(chunk == at, nz, chunk)
        return R.from_z.at[name % 2, slot]

    def add_rows(dst, src):
        @pl.loop(0, rows // 32)
        def _(i):
            at = pl.ds(pl.multiple_of(i * 32, 32), 32)
            dst[at, :] = (dst[at, :].astype(F32) + src[at, :].astype(F32)).astype(dst.dtype)

    def scatter_term(name, chunk, work):
        work(chunk)
        send(
            half(name, chunk, 1 - c),
            core_room(name, chunk),
            S.rc + nz * name + chunk,
            S.rc + nz * name + chunk,
            sibling,
        ).start()

    def scatter_slot(step, way):
        if way == 0:
            chunk = nz - 1 + z - step
            return chunk, (step >= z) & (z < nz - 1)
        chunk = step - (nz - 1 - z)
        return chunk, (chunk >= 0) & (z > 0)

    def scatter_step(name, step, work):
        for way in range(2):
            chunk, valid = scatter_slot(step, way)

            @pl.when(valid)
            def _():
                scatter_term(name, chunk, work)

        for way in range(2):
            chunk, valid = scatter_slot(step, way)

            @pl.when(valid)
            def _():
                arrived(core_room(name, chunk), S.rc + nz * name + chunk)
                mine = half(name, chunk, c)
                add_rows(mine, core_room(name, chunk))
                earlier = z > 0 if way == 0 else z < nz - 1

                @pl.when(earlier)
                def _():
                    arrived(z_slot(name, way, chunk, z), S.rz + 2 * nz * name + nz * way + chunk)
                    add_rows(mine, z_slot(name, way, chunk, z))

                send(
                    mine,
                    z_slot(name, way, chunk, z + 1 - 2 * way),
                    S.rz + 2 * nz * name + nz * way + chunk,
                    S.rz + 2 * nz * name + nz * way + chunk,
                    dev(y, c, z + 1 - 2 * way, x),
                ).start()

    def scatter_end(name, own_term=True):
        arrived(core_room(name, z), S.rc + nz * name + z)
        mine, theirs = half(name, z, c), core_room(name, z)
        acc = R.acc

        @pl.loop(0, rows // 32)
        def _(i):
            at = pl.ds(pl.multiple_of(i * 32, 32), 32)
            acc[at, :] = mine[at, :].astype(F32) + theirs[at, :].astype(F32)

        for way in range(2):

            @pl.when(z > 0 if way == 0 else z < nz - 1)
            def _():
                arrived(z_slot(name, way, z, z), S.rz + 2 * nz * name + nz * way + z)
                add_rows(acc, z_slot(name, way, z, z))

    def scatter_sent(name):
        for chunk in range(nz):
            sent(half(name, chunk, 1 - c), S.rc + nz * name + chunk)
            for way in range(2):

                @pl.when(z < chunk if way == 0 else z > chunk)
                def _():
                    sent(half(name, chunk, c), S.rz + 2 * nz * name + nz * way + chunk)

    def each_rows(body, step=32):
        @pl.loop(0, rows // step)
        def _(i):
            body(pl.multiple_of(i * step, step), step)

    def keep_of(first, count):
        index = lax.broadcasted_iota(jnp.int32, (count, 1), 0) + (own_at + first)
        return (index.astype(F32) < R.last[0:1, 0:1]).astype(F32)

    def rotary():
        units = R.len[...] * 64.0
        ends, end = [], jnp.zeros((1, 128), F32)
        for p in range(pieces):
            end = end + units[p : p + 1, :]
            ends.append((units[p : p + 1, :], end))
        R.last[...] = jnp.broadcast_to(ends[-2][1], (8, 128))

        @pl.loop(0, total // 128)
        def _(i):
            at = pl.ds(pl.multiple_of(i * 128, 128), 128)
            index = (lax.broadcasted_iota(jnp.int32, (128, 128), 0) + i * 128).astype(F32)
            start = jnp.zeros((128, 128), F32)
            for length, stop in ends[:-1]:
                start = start + jnp.where(stop <= index, length, 0.0)
            R.start[at, :] = start
            angle = (index - start) * R.freq[0:1, :]
            lane = lax.broadcasted_iota(jnp.int32, (128, 128), 1)
            R.cos[at, :] = jnp.cos(angle)
            R.sin[at, :] = jnp.where(lane < 64, -1.0, 1.0) * jnp.sin(angle)

    def turn(value, cosine, sine):
        swapped = jnp.concatenate([value[:, 64:], value[:, :64]], axis=1)
        return value * cosine + swapped * sine

    def project(chunk):
        at = chunk_rows(chunk)
        normed = R.norm[at, :]
        cosine, sine = R.cos[at, :], R.sin[at, :]
        queries = dot(normed, R.wq[...])
        for h in range(heads):
            cols = slice(h * head, (h + 1) * head)
            R.q[at, cols] = turn(queries[:, cols], cosine, sine).astype(BF16)
        kv = dot(normed, R.wkv[...])
        R.kv[at, :head] = turn(kv[:, :head], cosine, sine).astype(BF16)
        R.kv[at, head:] = kv[:, head:].astype(BF16)

    def attend(chunk):
        at = chunk_rows(chunk)
        keys, values = R.kv[:, :head], R.kv[:, head:]
        start = R.start[at, 0:1]
        column = lax.broadcasted_iota(jnp.int32, (pair, total), 1).astype(F32)
        row = (lax.broadcasted_iota(jnp.int32, (pair, 1), 0) + chunk * pair).astype(F32)
        allowed = (column >= start) & (column <= row)
        for h in range(heads):
            cols = slice(h * head, (h + 1) * head)
            scores = dot_rows(R.q[at, cols], keys) * scale
            scores = jnp.where(allowed, scores, -1e30)
            exps = jnp.exp(scores - jnp.max(scores, axis=1, keepdims=True))
            weights = exps * (1.0 / jnp.sum(exps, axis=1, keepdims=True))
            weights = weights.astype(BF16)
            R.probs[h, at, :] = weights
            R.att[at, cols] = dot(weights, values).astype(BF16)

    def out_term(chunk):
        attend(chunk)
        at = chunk_rows(chunk)
        for n, size in tiles(width, 512):
            R.part[at, n : n + size] = dot(
                R.att[at, :], R.wo[:, n : n + size]
            ).astype(BF16)

    def mlp(chunk):
        at = chunk_rows(chunk)
        for n, size in tiles(ff, 256):
            cols = slice(n, n + size)
            gate = dot_rows(R.nmlp[at, :], R.wg[cols, :])
            up = dot_rows(R.nmlp[at, :], R.wu[cols, :])
            grad = dot_rows(R.gmlp[at, :], R.wd[cols, :])
            sigma = 1.0 / (1.0 + jnp.exp(-gate))
            active = gate * sigma
            R.hid[at, cols] = (active * up).astype(BF16)
            R.dup[at, cols] = (grad * active).astype(BF16)
            R.dgate[at, cols] = (grad * up * (sigma * (1.0 + gate * (1.0 - sigma)))).astype(BF16)

    def back_term(chunk):
        at = chunk_rows(chunk)
        for n, size in tiles(width, 512):
            some = slice(n, n + size)
            R.part[at, some] = (
                dot(R.dgate[at, :], R.wg[:, some]) + dot(R.dup[at, :], R.wu[:, some])
            ).astype(BF16)

    def down_term(chunk):
        at = chunk_rows(chunk)
        for n, size in tiles(width, 512):
            some = slice(n, n + size)
            R.part[at, some] = dot(R.hid[at, :], R.wd[:, some]).astype(BF16)

    def d_attended(chunk):
        at = chunk_rows(chunk)
        R.datt[at, :] = dot_rows(R.norm[at, :], R.wo[...]).astype(BF16)
        backward_attend(chunk)

    def backward_attend(chunk):
        at = chunk_rows(chunk)
        keys, values = R.kv[:, :head], R.kv[:, head:]
        cosine, sine = R.cos[at, :], R.sin[at, :]
        for h in range(heads):
            cols = slice(h * head, (h + 1) * head)
            weights = R.probs[h, at, :]
            probs = weights.astype(F32)
            grad = R.datt[at, cols]
            d_probs = dot_rows(grad, values)
            inner = jnp.sum(d_probs * probs, axis=1, keepdims=True)
            d_scores = (probs * (d_probs - inner)).astype(BF16)
            d_queries = dot(d_scores, keys) * scale
            R.dq[at, cols] = turn(d_queries, cosine, -sine).astype(BF16)
            R.dkv[:, :head] += dot_cols(d_scores, R.q[at, cols]) * scale
            R.dkv[:, head:] += dot_cols(weights, grad)

    def query_term(chunk):
        at = chunk_rows(chunk)
        for n, size in tiles(width, 512):
            some = slice(n, n + size)
            terms(RQ)[at, some] = dot_rows(R.dq[at, :], R.wq[some, :]).astype(BF16)

    def grad_send(name, yy, cc):
        quarter = 2 * yy + cc
        stage = R.stage[name].at[quarter]
        into_x, into_c = R.px[name].at[yy], R.pc[name].at[yy]

        @pl.when(jnp.logical_not(keeper))
        def _():
            send(
                stage,
                into_x,
                S.px + 4 * name + quarter,
                S.px + 4 * name + yy,
                (2 * y + cc, 2 * z + 1 - x),
            ).start()

        @pl.when(keeper & (c == cc))
        def _():
            pltpu.make_async_copy(stage, into_c, DR.at[S.pc + 4 * name + yy]).start()

        @pl.when(keeper & (c != cc))
        def _():
            send(
                stage, into_c, S.pc + 4 * name + quarter, S.pc + 4 * name + yy, sibling
            ).start()

    def grad_sent(name, yy, cc):
        quarter = 2 * yy + cc
        stage = R.stage[name].at[quarter]

        @pl.when(jnp.logical_not(keeper))
        def _():
            sent(stage, S.px + 4 * name + quarter)

        @pl.when(keeper & (c != cc))
        def _():
            sent(stage, S.pc + 4 * name + quarter)

    QUARTERS = [(0, 0), (0, 1), (1, 0), (1, 1)]

    def grad_make(name, left, right):
        split_left = name == QUERY
        quarter_cols = (left if split_left else right).shape[1] // 4
        tile = R.tile[name]
        for index, (yy, cc) in enumerate(QUARTERS):
            first = index * quarter_cols
            if index > 1:
                pltpu.make_async_copy(
                    tile.at[index % 2],
                    R.stage[name].at[index - 2],
                    DR.at[S.stage + 4 * name + index - 2],
                ).wait()
                grad_send(name, *QUARTERS[index - 2])
            if split_left:
                for m, size in tiles(quarter_cols, 256):
                    tile[index % 2, m : m + size, :] = dot_cols(
                        left[:, first + m : first + m + size], right[...]
                    ).astype(BF16)
            else:
                for m, size in tiles(left.shape[1], 256):
                    tile[index % 2, m : m + size, :] = dot_cols(
                        left[:, m : m + size], right[:, first : first + quarter_cols]
                    ).astype(BF16)
            pltpu.make_async_copy(
                tile.at[index % 2],
                R.stage[name].at[index],
                DR.at[S.stage + 4 * name + index],
            ).start()
        for index in (2, 3):
            pltpu.make_async_copy(
                tile.at[index % 2],
                R.stage[name].at[index],
                DR.at[S.stage + 4 * name + index],
            ).wait()
            grad_send(name, *QUARTERS[index])

    def sum_room(name):
        if name == QUERY:
            return R.wu.at[0 : width // 4, 3 * (width // 4) : 3 * (width // 4) + R.wq.shape[1]]
        if name == DOWN:
            return R.wu.at[:, 2 * (width // 4) : 3 * (width // 4)]
        cols = name * (width // 4)
        return R.wd.at[0 : R.tile[name].shape[1], cols : cols + width // 4]

    def grad_add(name):
        tile = R.tile[name]
        count, cols = tile.shape[1:]
        places = (
            (tile.at[0], tile.at[1]),
            (R.wu.at[0:count, 0:cols], R.wu.at[0:count, cols : 2 * cols]),
        )
        loads = []
        for turn_at, yy in enumerate((1 - y, y)):
            for k, (source, base) in enumerate(((R.px, S.px), (R.pc, S.pc))):
                arrived(source[name].at[yy], base + 4 * name + yy)
                load = pltpu.make_async_copy(
                    source[name].at[yy],
                    places[turn_at][k],
                    DR.at[S.ld + 4 * name + 2 * turn_at + k],
                )
                load.start()
                loads.append(load)
        for turn_at in range(2):
            loads[2 * turn_at].wait()
            loads[2 * turn_at + 1].wait()
            one, two = places[turn_at]
            into = sum_room(name) if turn_at == 0 else one

            @pl.loop(0, count // 32)
            def _(i):
                at = pl.ds(pl.multiple_of(i * 32, 32), 32)
                into[at, :] = (one[at, :].astype(F32) + two[at, :].astype(F32)).astype(BF16)

            if turn_at == 0:
                send(
                    into, R.other[name], S.py + name, S.py + name, across_y
                ).start()
            else:
                store = pltpu.make_async_copy(
                    into, R.mine[name], DR.at[S.st + name]
                )
                store.start()
                store.wait()

    R.own_len[...] = jnp.zeros((8, 128), F32)
    for p in range(pieces):
        R.own_len[p : p + 1, :] = jnp.broadcast_to(R.lengths[0:1, p : p + 1].astype(F32), (1, 128))
    swap_start(LEN, R.own_len, R.len)
    swap_start(TOK, R.tokens, R.tok)
    swap_wait(LEN, R.len)
    swap_wait(TOK, R.tok)
    weight_start(WQ, R.w_query, R.wq)
    swap_start(OG, R.out_grad, R.og)
    swap_start(KVG, R.kv_grad, R.kvg)

    def norm_rows(first, count):
        at = pl.ds(first, count)
        value = R.tok[at, :].astype(F32)
        inverse = lax.rsqrt(jnp.mean(value * value, axis=1, keepdims=True) + EPSILON)
        R.norm[pl.ds(own_at + first, count), :] = (
            value * inverse * R.gain_attn[0:1, :]
        ).astype(BF16)

    each_rows(norm_rows)
    gather_start(GN, R.norm)
    weight_start(WO, R.w_attn_out, R.wo)
    rotary()
    weight_pass(WQ, R.wq)
    weight_start(WG, R.w_gate, R.wg)
    weight_wait(WQ, R.wq)
    gather_own(GN, R.norm, project)

    def mask_rows(first, count):
        at = pl.ds(first, count)
        R.gmlp[pl.ds(own_at + first, count), :] = (
            keep_of(first, count) * R.og[at, :].astype(F32)
        ).astype(BF16)

    for step in range(nz - 1):
        gather_pass(GN, R.norm, step)
        if step == 0:
            weight_pass(WO, R.wo)
            weight_start(WU, R.w_up, R.wu)
            swap_wait(OG, R.og)
            swap_wait(KVG, R.kvg)
            each_rows(mask_rows)
        if step == nz - 2:
            gather_start(GG, R.gmlp)
            weight_pass(WG, R.wg)
            weight_start(WD, R.w_down, R.wd)
        gather_use(GN, R.norm, step, project)
    spill = pltpu.make_async_copy(R.norm, R.norm_store, DR.at[S.spill])
    spill.start()
    weight_wait(WO, R.wo)

    for step in range(nz - 1):
        scatter_step(RO, step, out_term)
        gather_pass(GG, R.gmlp, step)
        if step == 0:
            weight_pass(WU, R.wu)
        if step == nz - 2:
            weight_pass(WD, R.wd)
    scatter_term(RO, z, out_term)
    scatter_end(RO)
    for step in range(nz - 1):
        gather_use(GG, R.gmlp, step, None)
    gather_own(GG, R.gmlp, None)

    def mid_rows(first, count):
        at = pl.ds(first, count)
        mid = R.tok[at, :].astype(F32) + R.acc[at, :]
        R.mid[at, :] = mid
        inverse = lax.rsqrt(jnp.mean(mid * mid, axis=1, keepdims=True) + EPSILON)
        R.nmlp[pl.ds(own_at + first, count), :] = (
            mid * inverse * R.gain_mlp[0:1, :]
        ).astype(BF16)

    each_rows(mid_rows)
    gather_start(GM, R.nmlp)
    scatter_sent(RO)
    gather_end(GN, R.norm)
    spill.wait()
    weight_wait(WG, R.wg)
    weight_wait(WU, R.wu)
    weight_wait(WD, R.wd)
    gather_own(GM, R.nmlp, mlp)
    for step in range(nz - 1):
        gather_pass(GM, R.nmlp, step)
        gather_use(GM, R.nmlp, step, mlp)

    for item, src, dst in (
        (WQ, R.w_query, R.wq),
        (WO, R.w_attn_out, R.wo),
        (WG, R.w_gate, R.wg),
        (WU, R.w_up, R.wu),
        (WD, R.w_down, R.wd),
    ):
        weight_sent(item, src, dst)

    mlp_grads = ((DOWN, R.hid, R.gmlp), (GATE, R.dgate, R.nmlp), (UP, R.dup, R.nmlp))
    for step in range(nz - 1):
        scatter_step(RB, step, back_term)
        if step < 3:
            grad_make(*mlp_grads[step])
    scatter_term(RB, z, back_term)
    for rest in mlp_grads[nz - 1 :]:
        grad_make(*rest)
    scatter_end(RB)
    R.gains[...] = jnp.zeros(R.gains.shape, F32)

    def fold(value):
        return jnp.sum(value.reshape(value.shape[0] // 8, 8, value.shape[1]), axis=0)

    def d_mid_rows(first, count):
        at = pl.ds(first, count)
        mid = R.mid[at, :]
        inverse = lax.rsqrt(jnp.mean(mid * mid, axis=1, keepdims=True) + EPSILON)
        unit = mid * inverse
        back = R.acc[at, :]
        R.gains[1] += fold(back * unit)
        e = back * R.gain_mlp[0:1, :]
        grad = keep_of(first, count) * R.og[at, :].astype(F32) + inverse * (
            e - unit * jnp.mean(e * unit, axis=1, keepdims=True)
        )
        R.dmid[at, :] = grad
        R.norm[pl.ds(own_at + first, count), :] = grad.astype(BF16)

    each_rows(d_mid_rows)
    gather_start(GA, R.norm)
    scatter_sent(RB)
    gather_end(GG, R.gmlp)
    gather_end(GM, R.nmlp)
    back_norm = pltpu.make_async_copy(R.norm_store, R.gmlp, DR.at[S.spill + 1])
    back_norm.start()
    R.dkv[...] = jnp.zeros(R.dkv.shape, F32)
    gather_own(GA, R.norm, d_attended)
    for step in range(nz - 1):
        gather_pass(GA, R.norm, step)
        scatter_step(RD, step, down_term)
        gather_use(GA, R.norm, step, d_attended)
        if step == 1:
            grad_add(DOWN)
    scatter_term(RD, z, down_term)

    R.dkvb[...] = R.dkv[...].astype(BF16)
    for zz in range(nz):
        send(piece(R.dkvb, zz, 1 - c), R.kc.at[zz], S.kc + zz, S.kc + zz, sibling).start()

    def kv_over_z():
        for zz in range(nz):
            arrived(R.kc.at[zz], S.kc + zz)
            R.ks[zz] = (
                R.dkv[pl.ds(pl.multiple_of((2 * zz + c) * rows, rows), rows), :]
                + R.kc[zz].astype(F32)
            ).astype(BF16)

            @pl.when(zz != z)
            def _():
                send(R.ks.at[zz], R.kz.at[z], S.kz + zz, S.kz + z, dev(y, c, zz, x)).start()

    own_rows = pl.ds(own_at, rows)
    own_kv = piece(R.dkva, z, c)

    def kv_own():
        R.kacc[...] = keep_of(0, rows) * R.kvg[...].astype(F32) + R.ks[z].astype(F32)
        for zz in range(nz):

            @pl.when(zz != z)
            def _():
                arrived(R.kz.at[zz], S.kz + zz)
                R.kacc[...] += R.kz[zz].astype(F32)

        R.dkva[own_rows, :head] = turn(
            R.kacc[:, :head], R.cos[own_rows, :], -R.sin[own_rows, :]
        ).astype(BF16)
        R.dkva[own_rows, head:] = R.kacc[:, head:].astype(BF16)
        for zz in range(nz):
            for cc in range(2):

                @pl.when((zz != z) | (cc != c))
                def _():
                    send(
                        own_kv, own_kv, S.ka + 2 * zz + cc, S.ka + 2 * z + c, dev(y, cc, zz, x)
                    ).start()

    def out_rows(first, count):
        at = pl.ds(first, count)
        R.bo[at, :] = (keep_of(first, count) * (R.mid[at, :] + R.acc[at, :])).astype(BF16)

    back_norm.wait()
    for step in range(nz - 1):
        scatter_step(RQ, step, query_term)
        if step == 0:
            scatter_end(RD)
            each_rows(out_rows)
            swap_start(BO, R.bo, R.block_out)
            kv_over_z()
            grad_make(OUT, R.att, R.norm)
        if step == 1:
            kv_own()
            grad_make(QUERY, R.gmlp, R.dq)
            grad_add(GATE)
    scatter_term(RQ, z, query_term)
    for zz in range(nz):
        for cc in range(2):

            @pl.when((zz != z) | (cc != c))
            def _():
                arrived(piece(R.dkva, zz, cc), S.ka + 2 * zz + cc)

    first_col = c * (4 * nz * 32) + z * 128
    for yy in range(2):
        cols = pl.ds(pl.multiple_of(yy * (width // 2) + first_col, 128), 128)
        R.gkv[yy] = dot_cols(R.gmlp[:, cols], R.dkva[...])
    send(
        R.gkv.at[1 - y], R.kyb, S.kyx, S.kyx, across_y
    ).start()
    arrived(R.kyb, S.kyx)
    R.kysum[...] = R.gkv[y] + R.kyb[...]
    send(
        R.kysum.at[pl.ds(pl.multiple_of((1 - x) * 64, 64), 64)],
        R.kxb,
        S.kyx + 1,
        S.kyx + 1,
        across_x,
    ).start()
    arrived(R.kxb, S.kyx + 1)
    R.kfinal[...] = (
        R.kysum[pl.ds(pl.multiple_of(x * 64, 64), 64), :] + R.kxb[...]
    )
    kv_out = pltpu.make_async_copy(R.kfinal, R.grad_w_kv, DR.at[S.outs])
    kv_out.start()
    grad_add(UP)

    scatter_end(RQ)
    for n, size in tiles(width, 512):
        some = slice(n, n + size)
        R.acc[:, some] += dot_rows(R.dkva[own_rows, :], R.wkv[some, :])

    def tail_rows(first, count):
        at = pl.ds(first, count)
        value = R.tok[at, :].astype(F32)
        inverse = lax.rsqrt(jnp.mean(value * value, axis=1, keepdims=True) + EPSILON)
        unit = value * inverse
        back = R.acc[at, :]
        R.gains[0] += fold(back * unit)
        e = back * R.gain_attn[0:1, :]
        R.gt[at, :] = (
            R.dmid[at, :]
            + inverse * (e - unit * jnp.mean(e * unit, axis=1, keepdims=True))
        ).astype(BF16)

    each_rows(tail_rows)
    swap_start(GT, R.gt, R.grad_tokens)

    line = lax.broadcasted_iota(jnp.int32, (8, width), 0)
    gain_first = jnp.sum(R.gains[0], axis=0, keepdims=True)
    gain_second = jnp.sum(R.gains[1], axis=0, keepdims=True)
    R.ga[...] = jnp.where(line == 0, gain_first, jnp.where(line == 1, gain_second, 0.0))
    part_y, part_c = width // 2, width // 4

    def cols_of(index, size):
        return pl.ds(pl.multiple_of(index * size, size), size)

    send(
        R.ga.at[:, cols_of(1 - y, part_y)], R.gb_y, S.gains, S.gains, across_y
    ).start()
    arrived(R.gb_y, S.gains)
    R.ga_y[...] = R.ga[:, cols_of(y, part_y)] + R.gb_y[...]
    send(
        R.ga_y.at[:, cols_of(1 - c, part_c)],
        R.gb_c,
        S.gains + 1,
        S.gains + 1,
        sibling,
    ).start()
    arrived(R.gb_c, S.gains + 1)
    R.ga_c[...] = R.ga_y[:, cols_of(c, part_c)] + R.gb_c[...]
    send(R.ga_c, R.gb_x, S.gains + 2, S.gains + 2, across_x).start()
    arrived(R.gb_x, S.gains + 2)
    R.ga_x[...] = R.ga_c[...] + R.gb_x[...]
    for zz in range(nz):

        @pl.when(zz != z)
        def _():
            send(
                R.ga_x.at[:, zz * 128 : (zz + 1) * 128],
                R.gb_z.at[z],
                S.gains + 3 + zz,
                S.gains + 3 + z,
                dev(y, c, zz, x),
            ).start()

    R.gfinal[...] = R.ga_x[:, cols_of(z, 128)]
    for zz in range(nz):

        @pl.when(zz != z)
        def _():
            arrived(R.gb_z.at[zz], S.gains + 3 + zz)
            R.gfinal[...] += R.gb_z[zz]

    gain_out = pltpu.make_async_copy(R.gfinal, R.grad_gains, DR.at[S.outs + 1])
    gain_out.start()

    for name in (OUT, QUERY):
        grad_add(name)
    for name in GRADS:
        arrived(R.other[name], S.py + name)
        sent(sum_room(name), S.py + name)
        for yy, cc in QUARTERS:
            grad_sent(name, yy, cc)
    kv_out.wait()
    gain_out.wait()
    scatter_sent(RD)
    scatter_sent(RQ)
    gather_end(GA, R.norm)
    swap_wait(BO, R.block_out)
    swap_wait(GT, R.grad_tokens)
    for item, src in (
        (LEN, R.own_len), (TOK, R.tokens), (OG, R.out_grad), (KVG, R.kv_grad), (BO, R.bo), (GT, R.gt)
    ):
        swap_sent(item, src)
    for zz in range(nz):
        sent(piece(R.dkvb, zz, 1 - c), S.kc + zz)

        @pl.when(zz != z)
        def _():
            sent(R.ks.at[zz], S.kz + zz)
            sent(R.ga_x.at[:, zz * 128 : (zz + 1) * 128], S.gains + 3 + zz)

        for cc in range(2):

            @pl.when((zz != z) | (cc != c))
            def _():
                sent(own_kv, S.ka + 2 * zz + cc)

    sent(R.gkv.at[1 - y], S.kyx)
    sent(R.kysum.at[pl.ds(pl.multiple_of((1 - x) * 64, 64), 64)], S.kyx + 1)
    sent(R.ga.at[:, cols_of(1 - y, part_y)], S.gains)
    sent(R.ga_y.at[:, cols_of(1 - c, part_c)], S.gains + 1)
    sent(R.ga_c, S.gains + 2)


def fused(nz, *args):
    (tokens, lengths, gain_attn, w_query, w_kv, w_attn_out, gain_mlp, w_gate, w_up, w_down,
     out_grad, kv_grad) = args
    rows, width = tokens.shape
    ff = w_gate.shape[1]
    qw = w_query.shape[1]
    total, pair = 2 * nz * rows, 2 * rows
    pieces = lengths.shape[1]
    head = w_kv.shape[1] // 2
    half_width = head // 2
    freqs = (ROTARY_BASE ** (-np.arange(half_width, dtype=np.float32) / half_width)).astype(np.float32)
    freq = np.tile(np.concatenate([freqs, freqs])[None, :], (8, 1))
    anywhere, vmem = pl.BlockSpec(memory_space=pl.ANY), pl.BlockSpec(memory_space=pltpu.VMEM)
    ins = dict(
        tokens=(tokens, anywhere),
        lengths=(lengths, vmem),
        freq=(freq, vmem),
        gain_attn=(gain_attn[None], vmem),
        gain_mlp=(gain_mlp[None], vmem),
        w_query=(w_query, anywhere),
        wkv=(w_kv, vmem),
        w_attn_out=(w_attn_out, anywhere),
        w_gate=(w_gate.T, anywhere),
        w_up=(w_up.T, anywhere),
        w_down=(w_down, anywhere),
        out_grad=(out_grad, anywhere),
        kv_grad=(kv_grad, anywhere),
    )
    quarter = width // 4
    grad_tiles = [(ff, quarter), (ff, quarter), (ff, quarter), (qw, quarter), (quarter, qw)]
    outs = dict(
        block_out=((rows, width), BF16),
        grad_tokens=((rows, width), BF16),
        grad_w_kv=((64, 2 * head), F32),
        grad_gains=((8, 128), F32),
        norm_store=((total, width), BF16),
    )
    moved = [
        (shape, BF16)
        for tile in grad_tiles
        for shape in (tile, tile, (4,) + tile, (2,) + tile, (2,) + tile)
    ]
    S, count = semaphores(nz)
    scratch = dict(
        own_len=((8, 128), F32),
        len=((8, 128), F32),
        last=((8, 128), F32),
        tok=((rows, width), BF16),
        og=((rows, width), BF16),
        kvg=((rows, 2 * head), BF16),
        wq=((width, qw), BF16),
        wo=((qw, width), BF16),
        wg=((ff, width), BF16),
        wu=((ff, width), BF16),
        wd=((ff, width), BF16),
        norm=((total, width), BF16),
        nmlp=((total, width), BF16),
        gmlp=((total, width), BF16),
        cos=((total, 128), F32),
        sin=((total, 128), F32),
        start=((total, 128), F32),
        q=((total, qw), BF16),
        kv=((total, 2 * head), BF16),
        att=((total, qw), BF16),
        datt=((total, qw), BF16),
        dq=((total, qw), BF16),
        probs=((qw // head, total, total), BF16),
        hid=((total, ff), BF16),
        dgate=((total, ff), BF16),
        dup=((total, ff), BF16),
        part=((total, width), BF16),
        from_core=((nz * rows, width), BF16),
        from_z=((2, nz + 1, rows, width), BF16),
        acc=((rows, width), F32),
        mid=((rows, width), F32),
        dmid=((rows, width), F32),
        bo=((rows, width), BF16),
        gt=((rows, width), BF16),
        gains=((2, 8, width), F32),
        ga=((8, width), F32),
        ga_y=((8, width // 2), F32),
        gb_y=((8, width // 2), F32),
        ga_c=((8, width // 4), F32),
        gb_c=((8, width // 4), F32),
        ga_x=((8, width // 4), F32),
        gb_x=((8, width // 4), F32),
        gb_z=((nz, 8, 128), F32),
        gfinal=((8, 128), F32),
        dkv=((total, 2 * head), F32),
        dkvb=((total, 2 * head), BF16),
        dkva=((total, 2 * head), BF16),
        kc=((nz, rows, 2 * head), BF16),
        ks=((nz, rows, 2 * head), BF16),
        kz=((nz, rows, 2 * head), BF16),
        kacc=((rows, 2 * head), F32),
        gkv=((2, 128, 2 * head), F32),
        kyb=((128, 2 * head), F32),
        kysum=((128, 2 * head), F32),
        kxb=((64, 2 * head), F32),
        kfinal=((64, 2 * head), F32),
    )
    tile_shapes = (grad_tiles[DOWN], grad_tiles[OUT], grad_tiles[QUERY])
    out_shapes = list(outs.values()) + moved
    scratch_shapes = list(scratch.values()) + [((2,) + shape, BF16) for shape in tile_shapes]

    def body(*refs):
        refs = list(refs)

        def take(count):
            taken = refs[:count]
            del refs[:count]
            return taken

        R = types.SimpleNamespace(
            **dict(zip(ins, take(len(ins)))), **dict(zip(outs, take(len(outs))))
        )
        rest = take(len(moved))
        R.mine, R.other, R.stage, R.px, R.pc = (rest[k::5] for k in range(5))
        for key, ref in zip(scratch, take(len(scratch))):
            setattr(R, key, ref)
        big, out_tile, query_tile = take(3)
        R.tile = [big, big, big, out_tile, query_tile]
        R.send, R.recv = refs
        block_kernel(nz, pieces, S, R)

    results = pl.pallas_call(
        body,
        out_shape=[jax.ShapeDtypeStruct(shape, kind) for shape, kind in out_shapes],
        in_specs=[spec for _, spec in ins.values()],
        out_specs=[anywhere] * len(out_shapes),
        scratch_shapes=[pltpu.VMEM(shape, kind) for shape, kind in scratch_shapes]
        + [pltpu.SemaphoreType.DMA((count,))] * 2,
        compiler_params=pltpu.CompilerParams(
            collective_id=0, has_side_effects=True, vmem_limit_bytes=63 * MIB
        ),
        name="block",
    )(*[value for value, _ in ins.values()])
    block_out, grad_tokens, grad_w_kv, grad_gains = results[:4]
    mine, other = results[5::5], results[6::5]
    sums = [one.astype(F32) + two.astype(F32) for one, two in zip(mine, other)]
    gains = lax.dynamic_slice_in_dim(
        grad_gains, (lax.axis_index("tensor") % 2) * 64, 64, 1
    )
    return (
        block_out,
        grad_tokens,
        gains[0],
        sums[QUERY],
        grad_w_kv,
        sums[OUT],
        gains[1],
        sums[GATE].T,
        sums[UP].T,
        sums[DOWN],
    )


def solution(mesh):
    groups, parts = mesh.shape["dp"], mesh.shape["tensor"]
    paired = groups == 4 and parts == 8
    per_group = functools.partial(fused, parts // 2) if paired else per_device
    placed = (
        P(("dp", "tensor"), None),
        P("dp", None),
        P(),
        P(None, "tensor"),
        P(),
        P("tensor", None),
        P(),
        P(None, "tensor"),
        P(None, "tensor"),
        P("tensor", None),
        P(("dp", "tensor"), None),
        P(("dp", "tensor"), None),
    )
    return jax.shard_map(
        per_group,
        mesh=mesh,
        in_specs=placed,
        out_specs=(
            P(("dp", "tensor"), None),
            P(("dp", "tensor"), None),
            P(("dp", "tensor")),
            P("dp", "tensor"),
            P(("dp", "tensor"), None),
            P("tensor", "dp"),
            P(("dp", "tensor")),
            P("dp", "tensor"),
            P("dp", "tensor"),
            P("tensor", "dp"),
        ),
        check_vma=False,
    )
```

```python
import functools
import types

import jax
import jax.numpy as jnp
import numpy as np
from jax import lax
from jax.experimental import pallas as pl
from jax.experimental.pallas import tpu as pltpu
from jax.sharding import PartitionSpec as P

SPAN = 64


EPSILON = 1e-05
ROTARY_BASE = 10000.0
MASKED = -1e30


def rotary_tables(positions, width):
    half_width = width // 2
    freqs = ROTARY_BASE ** (-jnp.arange(half_width, dtype=jnp.float32) / half_width)
    angles = positions[:, None] * freqs[None, :]
    return (jnp.cos(angles), jnp.sin(angles))


def rotate(values, cosine, sine):
    half_width = values.shape[-1] // 2
    first_half = values[..., :half_width]
    second_half = values[..., half_width:]
    return jnp.concatenate(
        [first_half * cosine - second_half * sine, second_half * cosine + first_half * sine],
        axis=-1,
    )


def unrotate(values, cosine, sine):
    half_width = values.shape[-1] // 2
    first_half = values[..., :half_width]
    second_half = values[..., half_width:]
    return jnp.concatenate(
        [first_half * cosine + second_half * sine, second_half * cosine - first_half * sine],
        axis=-1,
    )


def layout(piece_units, rows):
    piece_rows = piece_units * SPAN
    ends = jnp.cumsum(piece_rows)
    starts = ends - piece_rows
    row_steps = jnp.arange(rows, dtype=jnp.int32)
    segment = jnp.sum((row_steps[:, None] >= ends[None, :]).astype(jnp.int32), axis=1)
    member = segment[:, None] == jnp.arange(piece_units.shape[0], dtype=jnp.int32)[None, :]
    row_start = jnp.sum(jnp.where(member, starts[None, :], 0), axis=1)
    positions = (row_steps - row_start).astype(jnp.float32)
    keep = (segment < piece_units.shape[0] - 1).astype(jnp.float32)
    return (segment, row_steps, positions, keep)


def permitted(block_segment, block_steps, segment, row_steps):
    return (block_segment[:, None] == segment[None, :]) & (
        row_steps[None, :] <= block_steps[:, None]
    )


def spread_rows(values):
    return lax.all_gather(values, "tensor", axis=0, tiled=True)


def spread_grads(values):
    return lax.all_gather(values, "tensor", axis=0, tiled=True)


def per_device(
    tokens,
    lengths,
    gain_attn,
    w_query,
    w_kv,
    w_attn_out,
    gain_mlp,
    w_gate,
    w_up,
    w_down,
    out_grad,
    kv_grad,
):
    local_rows = tokens.shape[0]
    parts = lax.axis_size("tensor")
    total_rows = local_rows * parts
    first_row = lax.axis_index("tensor") * local_rows
    segment, row_steps, positions, keep = layout(lengths[0], total_rows)
    head_dim = w_kv.shape[1] // 2
    local_heads = w_query.shape[1] // head_dim
    scale = head_dim ** (-0.5)
    cosine, sine = rotary_tables(positions, head_dim)
    row_keep = lax.dynamic_slice_in_dim(keep, first_row, local_rows, 0)[:, None]
    row_cosine = lax.dynamic_slice_in_dim(cosine, first_row, local_rows, 0)
    row_sine = lax.dynamic_slice_in_dim(sine, first_row, local_rows, 0)
    tokens_full = tokens.astype(jnp.float32)
    inv_first = lax.rsqrt(jnp.mean(tokens_full * tokens_full, axis=-1, keepdims=True) + EPSILON)
    unit_first = tokens_full * inv_first
    normed_rows = (unit_first * gain_attn).astype(jnp.bfloat16)
    normed = spread_rows(normed_rows)
    queries = jnp.dot(normed, w_query, preferred_element_type=jnp.float32).reshape(
        total_rows, local_heads, head_dim
    )
    queries = rotate(queries, cosine[:, None, :], sine[:, None, :]).astype(jnp.bfloat16)
    kv_raw = jnp.dot(normed, w_kv, preferred_element_type=jnp.float32)
    shared = jnp.concatenate(
        [rotate(kv_raw[:, :head_dim], cosine, sine), kv_raw[:, head_dim:]], axis=1
    ).astype(jnp.bfloat16)
    keys = shared[:, :head_dim]
    values = shared[:, head_dim:]
    block = min(512, total_rows)
    count = total_rows // block
    pieces = []
    log_totals = []
    for number in range(count):
        begin = number * block
        query_block = queries[begin : begin + block]
        allowed = permitted(
            segment[begin : begin + block], row_steps[begin : begin + block], segment, row_steps
        )
        scores = (
            jnp.einsum("qhd,kd->hqk", query_block, keys, preferred_element_type=jnp.float32) * scale
        )
        scores = jnp.where(allowed[None], scores, MASKED)
        row_max = jnp.max(scores, axis=-1, keepdims=True)
        exp_scores = jnp.exp(scores - row_max)
        row_total = jnp.sum(exp_scores, axis=-1, keepdims=True)
        log_totals.append(row_max + jnp.log(row_total))
        weights = (exp_scores / row_total).astype(jnp.bfloat16)
        pieces.append(
            jnp.einsum("hqk,kd->qhd", weights, values, preferred_element_type=jnp.float32).astype(
                jnp.bfloat16
            )
        )
    attended = jnp.concatenate(pieces, axis=0).reshape(total_rows, local_heads * head_dim)
    attn_rows = lax.psum_scatter(
        jnp.dot(attended, w_attn_out, preferred_element_type=jnp.float32).astype(jnp.bfloat16),
        "tensor",
        scatter_dimension=0,
        tiled=True,
    ).astype(jnp.float32)
    mid = tokens_full + attn_rows
    inv_second = lax.rsqrt(jnp.mean(mid * mid, axis=-1, keepdims=True) + EPSILON)
    unit_second = mid * inv_second
    normed_mlp = spread_rows((unit_second * gain_mlp).astype(jnp.bfloat16))
    gate = jnp.dot(normed_mlp, w_gate, preferred_element_type=jnp.float32)
    up = jnp.dot(normed_mlp, w_up, preferred_element_type=jnp.float32)
    sigma = jax.nn.sigmoid(gate)
    active = gate * sigma
    hidden = (active * up).astype(jnp.bfloat16)
    mlp_rows = lax.psum_scatter(
        jnp.dot(hidden, w_down, preferred_element_type=jnp.float32).astype(jnp.bfloat16),
        "tensor",
        scatter_dimension=0,
        tiled=True,
    ).astype(jnp.float32)
    block_out = (row_keep * (mid + mlp_rows)).astype(jnp.bfloat16)
    out_full = row_keep * out_grad.astype(jnp.float32)
    grad_mlp = spread_grads(out_full.astype(jnp.bfloat16))
    g_down = jnp.einsum("rf,rd->fd", hidden, grad_mlp, preferred_element_type=jnp.float32)
    g_hidden = jnp.einsum("rd,fd->rf", grad_mlp, w_down, preferred_element_type=jnp.float32)
    d_gate = (g_hidden * up * sigma * (1.0 + gate * (1.0 - sigma))).astype(jnp.bfloat16)
    d_up = (g_hidden * active).astype(jnp.bfloat16)
    g_gate = jnp.einsum("rd,rf->df", normed_mlp, d_gate, preferred_element_type=jnp.float32)
    g_up = jnp.einsum("rd,rf->df", normed_mlp, d_up, preferred_element_type=jnp.float32)
    back_mlp = lax.psum_scatter(
        (
            jnp.einsum("rf,df->rd", d_gate, w_gate, preferred_element_type=jnp.float32)
            + jnp.einsum("rf,df->rd", d_up, w_up, preferred_element_type=jnp.float32)
        ).astype(jnp.bfloat16),
        "tensor",
        scatter_dimension=0,
        tiled=True,
    ).astype(jnp.float32)
    e_mlp = back_mlp * gain_mlp
    g_gain_mlp = jnp.sum(back_mlp * unit_second, axis=0)
    d_mid = out_full + inv_second * (
        e_mlp - unit_second * jnp.mean(e_mlp * unit_second, axis=-1, keepdims=True)
    )
    grad_attn = spread_grads(d_mid.astype(jnp.bfloat16))
    g_attn_out = jnp.einsum("rh,rd->hd", attended, grad_attn, preferred_element_type=jnp.float32)
    d_att = jnp.einsum(
        "rd,hd->rh", grad_attn, w_attn_out, preferred_element_type=jnp.float32
    ).astype(jnp.bfloat16)
    d_att = d_att.reshape(total_rows, local_heads, head_dim)
    query_pieces = []
    d_keys = jnp.zeros((total_rows, head_dim), jnp.float32)
    d_values = jnp.zeros((total_rows, head_dim), jnp.float32)
    for number in range(count):
        begin = number * block
        query_block = queries[begin : begin + block]
        grad_block = d_att[begin : begin + block]
        allowed = permitted(
            segment[begin : begin + block], row_steps[begin : begin + block], segment, row_steps
        )
        scores = (
            jnp.einsum("qhd,kd->hqk", query_block, keys, preferred_element_type=jnp.float32) * scale
        )
        scores = jnp.where(allowed[None], scores, MASKED)
        probs = jnp.exp(scores - log_totals[number])
        weights = probs.astype(jnp.bfloat16)
        d_probs = jnp.einsum("qhd,kd->hqk", grad_block, values, preferred_element_type=jnp.float32)
        inner = jnp.sum(d_probs * probs, axis=-1, keepdims=True)
        d_scores = (probs * (d_probs - inner)).astype(jnp.bfloat16)
        query_pieces.append(
            jnp.einsum("hqk,kd->qhd", d_scores, keys, preferred_element_type=jnp.float32) * scale
        )
        d_keys = (
            d_keys
            + jnp.einsum("hqk,qhd->kd", d_scores, query_block, preferred_element_type=jnp.float32)
            * scale
        )
        d_values = d_values + jnp.einsum(
            "hqk,qhd->kd", weights, grad_block, preferred_element_type=jnp.float32
        )
    d_queries = jnp.concatenate(query_pieces, axis=0)
    d_queries = unrotate(d_queries, cosine[:, None, :], sine[:, None, :]).astype(jnp.bfloat16)
    d_queries = d_queries.reshape(total_rows, local_heads * head_dim)
    g_query = jnp.einsum("rd,rh->dh", normed, d_queries, preferred_element_type=jnp.float32)
    kv_rows = lax.psum_scatter(
        jnp.concatenate([d_keys, d_values], axis=1).astype(jnp.bfloat16),
        "tensor",
        scatter_dimension=0,
        tiled=True,
    ).astype(jnp.float32)
    kv_rows = kv_rows + row_keep * kv_grad.astype(jnp.float32)
    d_kv = jnp.concatenate(
        [unrotate(kv_rows[:, :head_dim], row_cosine, row_sine), kv_rows[:, head_dim:]], axis=1
    ).astype(jnp.bfloat16)
    d_kv_all = lax.all_gather(d_kv, "tensor", axis=0, tiled=True)
    width = normed.shape[1]
    groups = lax.axis_size("dp")
    own = lax.dynamic_index_in_dim(
        normed.reshape(total_rows, groups, parts, width // (groups * parts)),
        lax.axis_index("tensor"),
        2,
        False,
    ).reshape(total_rows, width // parts)
    g_kv = jnp.einsum("rd,rk->dk", own, d_kv_all, preferred_element_type=jnp.float32)
    back_attn = lax.psum_scatter(
        jnp.einsum("rh,dh->rd", d_queries, w_query, preferred_element_type=jnp.float32).astype(
            jnp.bfloat16
        ),
        "tensor",
        scatter_dimension=0,
        tiled=True,
    ).astype(jnp.float32)
    back_attn = back_attn + jnp.einsum("rk,dk->rd", d_kv, w_kv, preferred_element_type=jnp.float32)
    e_attn = back_attn * gain_attn
    g_gain_attn = jnp.sum(back_attn * unit_first, axis=0)
    grad_tokens = (
        d_mid
        + inv_first * (e_attn - unit_first * jnp.mean(e_attn * unit_first, axis=-1, keepdims=True))
    ).astype(jnp.bfloat16)
    kv_sum = lax.psum_scatter(g_kv, "dp", scatter_dimension=0, tiled=True)
    share = width // (groups * parts)
    first = (lax.axis_index("dp") * parts + lax.axis_index("tensor")) * share
    gain_all = lax.all_gather(jnp.stack([g_gain_attn, g_gain_mlp]), ("dp", "tensor"), axis=0)
    gain_sums = jnp.sum(lax.dynamic_slice_in_dim(gain_all, first, share, 2), axis=0)
    query_sum, out_sum, gate_sum, up_sum, down_sum = (
        lax.psum_scatter(
            g_query.astype(jnp.bfloat16), "dp", scatter_dimension=0, tiled=True
        ).astype(jnp.float32),
        lax.psum_scatter(
            g_attn_out.astype(jnp.bfloat16), "dp", scatter_dimension=1, tiled=True
        ).astype(jnp.float32),
        lax.psum_scatter(g_gate.astype(jnp.bfloat16), "dp", scatter_dimension=0, tiled=True).astype(
            jnp.float32
        ),
        lax.psum_scatter(g_up.astype(jnp.bfloat16), "dp", scatter_dimension=0, tiled=True).astype(
            jnp.float32
        ),
        lax.psum_scatter(g_down.astype(jnp.bfloat16), "dp", scatter_dimension=1, tiled=True).astype(
            jnp.float32
        ),
    )
    return (
        block_out,
        grad_tokens,
        gain_sums[0],
        query_sum,
        kv_sum,
        out_sum,
        gain_sums[1],
        gate_sum,
        up_sum,
        down_sum,
    )


F32, BF16 = jnp.float32, jnp.bfloat16
MESH = pl.DeviceIdType.MESH
MIB = 1 << 20


def dot(a, b):
    return jnp.dot(a, b, preferred_element_type=F32)


def dot_rows(a, b):
    return lax.dot_general(a, b, (((1,), (1,)), ((), ())), preferred_element_type=F32)


def dot_cols(a, b):
    return lax.dot_general(a, b, (((0,), (0,)), ((), ())), preferred_element_type=F32)


def tiles(width, step):
    return [(at, min(step, width - at)) for at in range(0, width, step)]


GN, GG, GM, GA = range(4)
RO, RB, RD, RQ = range(4)
LEN, TOK, TOK2, WQ, OG, KVG, WO, WG, WU, WD, BO, GT, GT2 = range(13)
DOWN, GATE, UP, OUT, QUERY = GRADS = range(5)


def semaphores(nz):
    counts = dict(
        swap=13,
        swap_y=13,
        gz=4 * 4 * nz,
        gc=4 * 2 * nz,
        rz=4 * 4 * nz,
        rc=4 * nz,
        stage=20,
        px=20,
        pc=20,
        py=5,
        ld=20,
        st=5,
        kc=nz,
        kz=nz,
        ka=2 * nz,
        kyx=2,
        gains=8 + nz,
        spill=2,
        outs=4,
    )
    firsts, total = {}, 0
    for name, count in counts.items():
        firsts[name] = total
        total += count
    return types.SimpleNamespace(**firsts), total


def block_kernel(nz, pieces, S, R):
    rows, width = R.tokens.shape
    ff = R.w_down.shape[0]
    total = 2 * nz * rows
    pair = 2 * rows
    head = 128
    heads = R.wq.shape[1] // head
    scale = head ** (-0.5)
    DS, DR = R.send, R.recv

    dp, tensor = lax.axis_index("dp"), lax.axis_index("tensor")
    y, c = dp // 2, dp % 2
    z, x = tensor // 2, tensor % 2
    keeper = c == x

    def dev(yy, cc, zz, xx):
        return (2 * yy + cc, 2 * zz + xx)

    def flip(value, yes):
        return 1 - value if yes else value

    sibling = dev(y, 1 - c, z, x)
    partner = dev(y, 1 - c, z, 1 - x)
    across_x = dev(y, c, z, 1 - x)
    across_y = dev(1 - y, c, z, x)

    def send(src, dst, s, r, to):
        return pltpu.make_async_remote_copy(
            src_ref=src,
            dst_ref=dst,
            send_sem=DS.at[s],
            recv_sem=DR.at[r],
            device_id=to,
            device_id_type=MESH,
        )

    def arrived(dst, r):
        pltpu.make_async_copy(dst, dst, DR.at[r]).wait()

    def sent(src, s):
        pltpu.make_async_copy(src, src, DS.at[s]).wait()

    barrier = pltpu.get_barrier_semaphore()
    around = {
        (dy, dc, dx): dev(flip(y, dy), flip(c, dc), z, flip(x, dx))
        for dy in range(2)
        for dc in range(2)
        for dx in range(2)
        if dy + dc + dx
    }
    for (dy, dc, dx), to in around.items():
        if dy + dx:
            pl.semaphore_signal(barrier, inc=1, device_id=to, device_id_type=MESH)
    for zz in range(nz):
        for cc in range(2):

            @pl.when((zz != z) | (cc != c))
            def _():
                pl.semaphore_signal(
                    barrier, inc=1, device_id=dev(y, cc, zz, x), device_id_type=MESH
                )

    pl.semaphore_wait(barrier, 6 + 2 * nz - 1)

    def swap_start(item, src, dst):
        at = S.swap + item

        @pl.when(keeper)
        def _():
            pltpu.make_async_copy(src, dst, DR.at[at]).start()

        @pl.when(jnp.logical_not(keeper))
        def _():
            send(src, dst, at, at, partner).start()

    def swap_wait(item, dst):
        arrived(dst, S.swap + item)

    def swap_sent(item, src):
        @pl.when(jnp.logical_not(keeper))
        def _():
            sent(src, S.swap + item)

    def part_at(ref, which):
        count = ref.shape[0] // 2
        return ref.at[pl.ds(pl.multiple_of(which * count, count), count)]

    def weight_start(item, src, dst):
        at = S.swap + item

        @pl.when(keeper)
        def _():
            pltpu.make_async_copy(src, dst, DR.at[at]).start()

        @pl.when(jnp.logical_not(keeper))
        def _():
            send(part_at(src, y), part_at(dst, y), at, at, partner).start()

    def weight_pass(item, dst):
        @pl.when(jnp.logical_not(keeper))
        def _():
            half_here = part_at(dst, y)
            arrived(half_here, S.swap + item)
            send(half_here, half_here, S.swap_y + item, S.swap_y + item, across_y).start()

    def weight_wait(item, dst):
        @pl.when(keeper)
        def _():
            arrived(dst, S.swap + item)

        @pl.when(jnp.logical_not(keeper))
        def _():
            arrived(part_at(dst, 1 - y), S.swap_y + item)

    def weight_sent(item, src, dst):
        @pl.when(jnp.logical_not(keeper))
        def _():
            sent(part_at(src, y), S.swap + item)
            sent(part_at(dst, y), S.swap_y + item)

    def piece(ref, chunk, core):
        return ref.at[pl.ds(pl.multiple_of((2 * chunk + core) * rows, rows), rows)]

    def chunk_rows(chunk):
        return pl.ds(pl.multiple_of(chunk * pair, pair), pair)

    own_at = pl.multiple_of((2 * z + c) * rows, rows)

    def bit(ref, chunk, core, part):
        count = rows // 2
        first = (2 * chunk + core) * rows + part * count
        return ref.at[pl.ds(pl.multiple_of(first, count), count)]

    def gather_sem(base, name, way, chunk, part):
        return base + ((2 * name + way) * nz + chunk) * 2 + part

    def core_sem(name, chunk, part):
        return S.gc + (name * nz + chunk) * 2 + part

    def gather_hop(name, ref, way, chunk, part):
        some = bit(ref, chunk, c, part)
        to = dev(y, c, z + 1 - 2 * way, x)
        send(
            some,
            some,
            gather_sem(S.gz, name, way, chunk, part),
            gather_sem(S.gz, name, 0, chunk, part),
            to,
        ).start()

    def gather_share(name, ref, chunk, part):
        some = bit(ref, chunk, c, part)
        at = core_sem(name, chunk, part)
        send(some, some, at, at, sibling).start()

    def gather_start(name, ref, parts=(0, 1)):
        for part in parts:

            @pl.when(z < nz - 1)
            def _():
                gather_hop(name, ref, 0, z, part)

            @pl.when(z > 0)
            def _():
                gather_hop(name, ref, 1, z, part)

            gather_share(name, ref, z, part)

    def gather_pass(name, ref, step):
        for part in range(2):
            for way in range(2):
                chunk = z - 1 - step if way == 0 else z + 1 + step

                @pl.when((chunk >= 0) & (chunk <= nz - 1))
                def _():
                    arrived(bit(ref, chunk, c, part), gather_sem(S.gz, name, 0, chunk, part))

                    @pl.when(z < nz - 1 if way == 0 else z > 0)
                    def _():
                        gather_hop(name, ref, way, chunk, part)

                    gather_share(name, ref, chunk, part)

    def gather_theirs(name, ref, chunk):
        for part in range(2):
            arrived(bit(ref, chunk, 1 - c, part), core_sem(name, chunk, part))

    def gather_own(name, ref, work):
        gather_theirs(name, ref, z)
        if work is not None:
            work(z)

    def gather_use(name, ref, step, work):
        for way in range(2):
            chunk = z - 1 - step if way == 0 else z + 1 + step

            @pl.when((chunk >= 0) & (chunk <= nz - 1))
            def _():
                gather_theirs(name, ref, chunk)
                if work is not None:
                    work(chunk)

    def gather_end(name, ref):
        for chunk in range(nz):
            for part in range(2):
                some = bit(ref, chunk, c, part)
                sent(some, core_sem(name, chunk, part))

                @pl.when((z < nz - 1) & (chunk <= z))
                def _():
                    sent(some, gather_sem(S.gz, name, 0, chunk, part))

                @pl.when((z > 0) & (chunk >= z))
                def _():
                    sent(some, gather_sem(S.gz, name, 1, chunk, part))

    def terms(name):
        return R.nmlp if name == RQ else R.part

    def half(name, chunk, core):
        return piece(terms(name), chunk, core)

    def core_room(name, chunk):
        room = R.wg if name == RQ else R.from_core
        return room.at[pl.ds(pl.multiple_of(chunk * rows, rows), rows)]

    def z_slot(name, way, chunk, at, part):
        slot = chunk if way == 0 else jnp.where(chunk == at, nz, chunk)
        count = rows // 2
        return R.from_z.at[name % 2, slot, pl.ds(part * count, count)]

    def add_rows(dst, *sources):
        step = 32

        @pl.loop(0, dst.shape[0] // step)
        def _(i):
            at = pl.ds(pl.multiple_of(i * step, step), step)
            value = sources[0][at, :].astype(F32)
            for source in sources[1:]:
                value = value + source[at, :].astype(F32)
            dst[at, :] = value.astype(dst.dtype)

    def scatter_term(name, chunk, work):
        work(chunk)
        send(
            half(name, chunk, 1 - c),
            core_room(name, chunk),
            S.rc + nz * name + chunk,
            S.rc + nz * name + chunk,
            sibling,
        ).start()

    def scatter_slot(step, way):
        if way == 0:
            chunk = nz - 1 + z - step
            return chunk, (step >= z) & (z < nz - 1)
        chunk = step - (nz - 1 - z)
        return chunk, (chunk >= 0) & (z > 0)

    def scatter_step(name, step, work):
        for way in range(2):
            chunk, valid = scatter_slot(step, way)

            @pl.when(valid)
            def _():
                scatter_term(name, chunk, work)

        for way in range(2):
            chunk, valid = scatter_slot(step, way)

            @pl.when(valid)
            def _():
                arrived(core_room(name, chunk), S.rc + nz * name + chunk)
                earlier = z > 0 if way == 0 else z < nz - 1
                to = z + 1 - 2 * way
                for part in range(2):
                    mine = bit(terms(name), chunk, c, part)
                    theirs = core_room(name, chunk).at[part * (rows // 2) : (part + 1) * (rows // 2)]
                    before = z_slot(name, way, chunk, z, part)
                    at = gather_sem(S.rz, name, way, chunk, part)

                    @pl.when(earlier)
                    def _():
                        arrived(before, at)
                        add_rows(mine, mine, theirs, before)

                    @pl.when(jnp.logical_not(earlier))
                    def _():
                        add_rows(mine, mine, theirs)

                    send(
                        mine, z_slot(name, way, chunk, to, part), at, at, dev(y, c, to, x)
                    ).start()

    def scatter_end(name, finish):
        arrived(core_room(name, z), S.rc + nz * name + z)
        for part in range(2):
            some = pl.ds(part * (rows // 2), rows // 2)
            add_rows(R.acc.at[some], half(name, z, c).at[some], core_room(name, z).at[some])
            for way in range(2):

                @pl.when(z > 0 if way == 0 else z < nz - 1)
                def _():
                    before = z_slot(name, way, z, z, part)
                    arrived(before, gather_sem(S.rz, name, way, z, part))
                    add_rows(R.acc.at[some], R.acc.at[some], before)

            finish(part)

    def scatter_sent(name):
        for chunk in range(nz):
            sent(half(name, chunk, 1 - c), S.rc + nz * name + chunk)
            for way in range(2):
                for part in range(2):

                    @pl.when(z < chunk if way == 0 else z > chunk)
                    def _():
                        sent(
                            bit(terms(name), chunk, c, part),
                            gather_sem(S.rz, name, way, chunk, part),
                        )

    def each_rows(body, part, step=32):
        @pl.loop(0, rows // 2 // step)
        def _(i):
            body(pl.multiple_of(part * (rows // 2) + i * step, step), step)

    def keep_of(first, count):
        index = lax.broadcasted_iota(jnp.int32, (count, 1), 0) + (own_at + first)
        return (index.astype(F32) < R.last[0:1, 0:1]).astype(F32)

    def rotary():
        units = R.len[...] * 64.0
        ends, end = [], jnp.zeros((1, 128), F32)
        for p in range(pieces):
            end = end + units[p : p + 1, :]
            ends.append((units[p : p + 1, :], end))
        R.last[...] = jnp.broadcast_to(ends[-2][1], (8, 128))

        @pl.loop(0, total // 128)
        def _(i):
            at = pl.ds(pl.multiple_of(i * 128, 128), 128)
            index = (lax.broadcasted_iota(jnp.int32, (128, 128), 0) + i * 128).astype(F32)
            start = jnp.zeros((128, 128), F32)
            for length, stop in ends[:-1]:
                start = start + jnp.where(stop <= index, length, 0.0)
            R.start[at, :] = start
            angle = (index - start) * R.freq[0:1, :]
            lane = lax.broadcasted_iota(jnp.int32, (128, 128), 1)
            R.cos[at, :] = jnp.cos(angle)
            R.sin[at, :] = jnp.where(lane < 64, -1.0, 1.0) * jnp.sin(angle)

    def turn(value, cosine, sine):
        swapped = jnp.concatenate([value[:, 64:], value[:, :64]], axis=1)
        return value * cosine + swapped * sine

    def project(chunk):
        at = chunk_rows(chunk)
        normed = R.norm[at, :]
        cosine, sine = R.cos[at, :], R.sin[at, :]
        queries = dot(normed, R.wq[...])
        for h in range(heads):
            cols = slice(h * head, (h + 1) * head)
            R.q[at, cols] = turn(queries[:, cols], cosine, sine).astype(BF16)
        kv = dot(normed, R.wkv[...])
        R.kv[at, :head] = turn(kv[:, :head], cosine, sine).astype(BF16)
        R.kv[at, head:] = kv[:, head:].astype(BF16)

    def attend(chunk):
        at = chunk_rows(chunk)
        keys, values = R.kv[:, :head], R.kv[:, head:]
        start = R.start[at, 0:1]
        column = lax.broadcasted_iota(jnp.int32, (pair, total), 1).astype(F32)
        row = (lax.broadcasted_iota(jnp.int32, (pair, 1), 0) + chunk * pair).astype(F32)
        allowed = (column >= start) & (column <= row)
        for h in range(heads):
            cols = slice(h * head, (h + 1) * head)
            scores = dot_rows(R.q[at, cols], keys) * scale
            scores = jnp.where(allowed, scores, -1e30)
            exps = jnp.exp(scores - jnp.max(scores, axis=1, keepdims=True))
            weights = exps * (1.0 / jnp.sum(exps, axis=1, keepdims=True))
            weights = weights.astype(BF16)
            R.probs[h, at, :] = weights
            R.att[at, cols] = dot(weights, values).astype(BF16)

    def out_term(chunk):
        attend(chunk)
        at = chunk_rows(chunk)
        for n, size in tiles(width, 512):
            R.part[at, n : n + size] = dot(
                R.att[at, :], R.wo[:, n : n + size]
            ).astype(BF16)

    def mlp(chunk):
        at = chunk_rows(chunk)
        for n, size in tiles(ff, 256):
            cols = slice(n, n + size)
            gate = dot_rows(R.nmlp[at, :], R.wg[cols, :])
            up = dot_rows(R.nmlp[at, :], R.wu[cols, :])
            grad = dot_rows(R.gmlp[at, :], R.wd[cols, :])
            sigma = 1.0 / (1.0 + jnp.exp(-gate))
            active = gate * sigma
            R.hid[at, cols] = (active * up).astype(BF16)
            R.dup[at, cols] = (grad * active).astype(BF16)
            R.dgate[at, cols] = (grad * up * (sigma * (1.0 + gate * (1.0 - sigma)))).astype(BF16)

    def back_term(chunk):
        at = chunk_rows(chunk)
        for n, size in tiles(width, 512):
            some = slice(n, n + size)
            R.part[at, some] = (
                dot(R.dgate[at, :], R.wg[:, some]) + dot(R.dup[at, :], R.wu[:, some])
            ).astype(BF16)

    def down_term(chunk):
        at = chunk_rows(chunk)
        for n, size in tiles(width, 512):
            some = slice(n, n + size)
            R.part[at, some] = dot(R.hid[at, :], R.wd[:, some]).astype(BF16)

    def d_attended(chunk):
        at = chunk_rows(chunk)
        R.datt[at, :] = dot_rows(R.norm[at, :], R.wo[...]).astype(BF16)
        backward_attend(chunk)

    def backward_attend(chunk):
        at = chunk_rows(chunk)
        keys, values = R.kv[:, :head], R.kv[:, head:]
        cosine, sine = R.cos[at, :], R.sin[at, :]
        for h in range(heads):
            cols = slice(h * head, (h + 1) * head)
            weights = R.probs[h, at, :]
            probs = weights.astype(F32)
            grad = R.datt[at, cols]
            d_probs = dot_rows(grad, values)
            inner = jnp.sum(d_probs * probs, axis=1, keepdims=True)
            d_scores = (probs * (d_probs - inner)).astype(BF16)
            d_queries = dot(d_scores, keys) * scale
            R.dq[at, cols] = turn(d_queries, cosine, -sine).astype(BF16)
            R.dkv[:, :head] += dot_cols(d_scores, R.q[at, cols]) * scale
            R.dkv[:, head:] += dot_cols(weights, grad)

    def query_term(chunk):
        at = chunk_rows(chunk)
        for n, size in tiles(width, 512):
            some = slice(n, n + size)
            terms(RQ)[at, some] = dot_rows(R.dq[at, :], R.wq[some, :]).astype(BF16)

    Y_FIRST = (GATE, OUT)

    def grad_send(name, yy, cc):
        quarter = 2 * yy + cc
        stage = R.stage[name].at[quarter]
        if name in Y_FIRST:
            at = S.px + 4 * name + cc

            @pl.when(yy != y)
            def _():
                send(stage, R.px[name].at[cc], at, at, across_y).start()

            return
        into_x, into_c = R.px[name].at[yy], R.pc[name].at[yy]

        @pl.when(jnp.logical_not(keeper))
        def _():
            send(
                stage,
                into_x,
                S.px + 4 * name + quarter,
                S.px + 4 * name + yy,
                (2 * y + cc, 2 * z + 1 - x),
            ).start()

        @pl.when(keeper & (c == cc))
        def _():
            pltpu.make_async_copy(stage, into_c, DR.at[S.pc + 4 * name + yy]).start()

        @pl.when(keeper & (c != cc))
        def _():
            send(
                stage, into_c, S.pc + 4 * name + quarter, S.pc + 4 * name + yy, sibling
            ).start()

    def grad_sent(name, yy, cc):
        quarter = 2 * yy + cc
        stage = R.stage[name].at[quarter]
        if name in Y_FIRST:

            @pl.when(yy != y)
            def _():
                sent(stage, S.px + 4 * name + cc)

            return

        @pl.when(jnp.logical_not(keeper))
        def _():
            sent(stage, S.px + 4 * name + quarter)

        @pl.when(keeper & (c != cc))
        def _():
            sent(stage, S.pc + 4 * name + quarter)

    QUARTERS = [(0, 0), (0, 1), (1, 0), (1, 1)]

    def grad_make(name, left, right):
        split_left = name == QUERY
        quarter_cols = (left if split_left else right).shape[1] // 4
        tile = R.tile[name]
        for index, (yy, cc) in enumerate(QUARTERS):
            first = index * quarter_cols
            if index > 1:
                pltpu.make_async_copy(
                    tile.at[index % 2],
                    R.stage[name].at[index - 2],
                    DR.at[S.stage + 4 * name + index - 2],
                ).wait()
                grad_send(name, *QUARTERS[index - 2])
            if split_left:
                for m, size in tiles(quarter_cols, 256):
                    tile[index % 2, m : m + size, :] = dot_cols(
                        left[:, first + m : first + m + size], right[...]
                    ).astype(BF16)
            else:
                for m, size in tiles(left.shape[1], 256):
                    tile[index % 2, m : m + size, :] = dot_cols(
                        left[:, m : m + size], right[:, first : first + quarter_cols]
                    ).astype(BF16)
            pltpu.make_async_copy(
                tile.at[index % 2],
                R.stage[name].at[index],
                DR.at[S.stage + 4 * name + index],
            ).start()
        for index in (2, 3):
            pltpu.make_async_copy(
                tile.at[index % 2],
                R.stage[name].at[index],
                DR.at[S.stage + 4 * name + index],
            ).wait()
            grad_send(name, *QUARTERS[index])

    def sum_room(name, cc=0):
        cols = width // 4
        if name == QUERY:
            return R.wu.at[0:cols, 3 * cols : 3 * cols + R.wq.shape[1]]
        if name == DOWN:
            return R.wu.at[:, 2 * cols : 3 * cols]
        if name == UP:
            return R.wd.at[:, 2 * cols : 3 * cols]
        if name == GATE:
            return R.wd.at[:, cc * cols : (cc + 1) * cols]
        count = R.wo.shape[0]
        return R.wd.at[cc * count : (cc + 1) * count, 3 * cols :]

    def grad_places(name):
        count, cols = R.tile[name].shape[1:]
        return (
            (R.tile[name].at[0], R.tile[name].at[1]),
            (R.wu.at[0:count, 0:cols], R.wu.at[0:count, cols : 2 * cols]),
        )

    def grad_loads(name, turn_at, sources):
        loads = []
        for k, source in enumerate(sources):
            load = pltpu.make_async_copy(
                source,
                grad_places(name)[turn_at][k],
                DR.at[S.ld + 4 * name + 2 * turn_at + k],
            )
            load.start()
            loads.append(load)
        return loads

    def grad_mid(name):
        loads = []
        for cc in range(2):
            arrived(R.px[name].at[cc], S.px + 4 * name + cc)
            loads.append(
                grad_loads(name, cc, (R.px[name].at[cc], R.stage[name].at[2 * y + cc]))
            )
        for cc in range(2):
            for load in loads[cc]:
                load.wait()
            into = sum_room(name, cc)
            add_rows(into, *grad_places(name)[cc])
            at = S.pc + 4 * name + cc

            @pl.when(jnp.logical_not(keeper))
            def _():
                send(
                    into, R.other[name], at, S.py + name, (2 * y + cc, 2 * z + 1 - x)
                ).start()

            @pl.when(keeper & (c == cc))
            def _():
                pltpu.make_async_copy(into, R.mine[name], DR.at[S.st + name]).start()

            @pl.when(keeper & (c != cc))
            def _():
                send(into, R.mine[name], at, S.st + name, sibling).start()

    def grad_add(name):
        loads = []
        for turn_at, yy in enumerate((1 - y, y)):
            arrived(R.px[name].at[yy], S.px + 4 * name + yy)
            arrived(R.pc[name].at[yy], S.pc + 4 * name + yy)
            loads.append(grad_loads(name, turn_at, (R.px[name].at[yy], R.pc[name].at[yy])))
        for turn_at in range(2):
            for load in loads[turn_at]:
                load.wait()
            one, two = grad_places(name)[turn_at]
            if turn_at == 0:
                into = sum_room(name)
                add_rows(into, one, two)
                send(into, R.other[name], S.py + name, S.py + name, across_y).start()
            else:
                add_rows(one, one, two)
                store = pltpu.make_async_copy(one, R.mine[name], DR.at[S.st + name])
                store.start()
                store.wait()

    R.own_len[...] = jnp.zeros((8, 128), F32)
    for p in range(pieces):
        R.own_len[p : p + 1, :] = jnp.broadcast_to(R.lengths[0:1, p : p + 1].astype(F32), (1, 128))
    swap_start(LEN, R.own_len, R.len)
    for part in range(2):
        swap_start(TOK + part, part_at(R.tokens, part), part_at(R.tok, part))
    weight_start(WQ, R.w_query, R.wq)
    swap_start(OG, R.out_grad, R.og)
    swap_start(KVG, R.kv_grad, R.kvg)

    def norm_rows(first, count):
        at = pl.ds(first, count)
        value = R.tok[at, :].astype(F32)
        inverse = lax.rsqrt(jnp.mean(value * value, axis=1, keepdims=True) + EPSILON)
        R.norm[pl.ds(own_at + first, count), :] = (
            value * inverse * R.gain_attn[0:1, :]
        ).astype(BF16)

    for part in range(2):
        swap_wait(TOK + part, part_at(R.tok, part))
        each_rows(norm_rows, part)
        gather_start(GN, R.norm, (part,))
    swap_wait(LEN, R.len)
    weight_start(WO, R.w_attn_out, R.wo)
    rotary()
    weight_pass(WQ, R.wq)
    weight_start(WG, R.w_gate, R.wg)
    weight_wait(WQ, R.wq)
    gather_own(GN, R.norm, project)

    def mask_rows(first, count):
        at = pl.ds(first, count)
        R.gmlp[pl.ds(own_at + first, count), :] = (
            keep_of(first, count) * R.og[at, :].astype(F32)
        ).astype(BF16)

    for step in range(nz - 1):
        gather_pass(GN, R.norm, step)
        if step == 0:
            weight_pass(WO, R.wo)
            weight_start(WU, R.w_up, R.wu)
            swap_wait(OG, R.og)
            swap_wait(KVG, R.kvg)
            for part in range(2):
                each_rows(mask_rows, part)
        if step == nz - 2:
            gather_start(GG, R.gmlp)
        gather_use(GN, R.norm, step, project)
    spill = pltpu.make_async_copy(R.norm, R.norm_store, DR.at[S.spill])
    spill.start()
    weight_wait(WO, R.wo)

    for step in range(nz - 1):
        scatter_step(RO, step, out_term)
        gather_pass(GG, R.gmlp, step)
        if step == 0:
            weight_pass(WG, R.wg)
            weight_start(WD, R.w_down, R.wd)
        if step == 1:
            weight_pass(WU, R.wu)
    scatter_term(RO, z, out_term)
    weight_pass(WD, R.wd)

    def mid_rows(first, count):
        at = pl.ds(first, count)
        mid = R.tok[at, :].astype(F32) + R.acc[at, :]
        R.mid[at, :] = mid
        inverse = lax.rsqrt(jnp.mean(mid * mid, axis=1, keepdims=True) + EPSILON)
        R.nmlp[pl.ds(own_at + first, count), :] = (
            mid * inverse * R.gain_mlp[0:1, :]
        ).astype(BF16)

    def mid_done(part):
        each_rows(mid_rows, part)
        gather_start(GM, R.nmlp, (part,))

    scatter_end(RO, mid_done)
    for step in range(nz - 1):
        gather_use(GG, R.gmlp, step, None)
    gather_own(GG, R.gmlp, None)
    scatter_sent(RO)
    gather_end(GN, R.norm)
    spill.wait()
    weight_wait(WG, R.wg)
    weight_wait(WU, R.wu)
    weight_wait(WD, R.wd)
    gather_own(GM, R.nmlp, mlp)
    for step in range(nz - 1):
        gather_pass(GM, R.nmlp, step)
        gather_use(GM, R.nmlp, step, mlp)

    for item, src, dst in (
        (WQ, R.w_query, R.wq),
        (WO, R.w_attn_out, R.wo),
        (WG, R.w_gate, R.wg),
        (WU, R.w_up, R.wu),
        (WD, R.w_down, R.wd),
    ):
        weight_sent(item, src, dst)

    mlp_grads = ((DOWN, R.hid, R.gmlp), (GATE, R.dgate, R.nmlp), (UP, R.dup, R.nmlp))
    for step in range(nz - 1):
        scatter_step(RB, step, back_term)
        if step < 3:
            grad_make(*mlp_grads[step])
    scatter_term(RB, z, back_term)
    for rest in mlp_grads[nz - 1 :]:
        grad_make(*rest)
    R.gains[...] = jnp.zeros(R.gains.shape, F32)

    def fold(value):
        return jnp.sum(value.reshape(value.shape[0] // 8, 8, value.shape[1]), axis=0)

    def d_mid_rows(first, count):
        at = pl.ds(first, count)
        mid = R.mid[at, :]
        inverse = lax.rsqrt(jnp.mean(mid * mid, axis=1, keepdims=True) + EPSILON)
        unit = mid * inverse
        back = R.acc[at, :]
        R.gains[1] += fold(back * unit)
        e = back * R.gain_mlp[0:1, :]
        grad = keep_of(first, count) * R.og[at, :].astype(F32) + inverse * (
            e - unit * jnp.mean(e * unit, axis=1, keepdims=True)
        )
        R.dmid[at, :] = grad
        R.norm[pl.ds(own_at + first, count), :] = grad.astype(BF16)

    def d_mid_done(part):
        each_rows(d_mid_rows, part)
        gather_start(GA, R.norm, (part,))

    scatter_end(RB, d_mid_done)
    scatter_sent(RB)
    gather_end(GG, R.gmlp)
    gather_end(GM, R.nmlp)
    back_norm = pltpu.make_async_copy(R.norm_store, R.gmlp, DR.at[S.spill + 1])
    back_norm.start()
    R.dkv[...] = jnp.zeros(R.dkv.shape, F32)
    gather_own(GA, R.norm, d_attended)
    for step in range(nz - 1):
        gather_pass(GA, R.norm, step)
        scatter_step(RD, step, down_term)
        gather_use(GA, R.norm, step, d_attended)
        if step == 1:
            grad_add(DOWN)
    scatter_term(RD, z, down_term)

    R.dkvb[...] = R.dkv[...].astype(BF16)
    for zz in range(nz):
        send(piece(R.dkvb, zz, 1 - c), R.kc.at[zz], S.kc + zz, S.kc + zz, sibling).start()

    def kv_over_z():
        for zz in range(nz):
            arrived(R.kc.at[zz], S.kc + zz)
            R.ks[zz] = (
                R.dkv[pl.ds(pl.multiple_of((2 * zz + c) * rows, rows), rows), :]
                + R.kc[zz].astype(F32)
            ).astype(BF16)

            @pl.when(zz != z)
            def _():
                send(R.ks.at[zz], R.kz.at[z], S.kz + zz, S.kz + z, dev(y, c, zz, x)).start()

    own_rows = pl.ds(own_at, rows)
    own_kv = piece(R.dkva, z, c)

    def kv_own():
        R.kacc[...] = keep_of(0, rows) * R.kvg[...].astype(F32) + R.ks[z].astype(F32)
        for zz in range(nz):

            @pl.when(zz != z)
            def _():
                arrived(R.kz.at[zz], S.kz + zz)
                R.kacc[...] += R.kz[zz].astype(F32)

        R.dkva[own_rows, :head] = turn(
            R.kacc[:, :head], R.cos[own_rows, :], -R.sin[own_rows, :]
        ).astype(BF16)
        R.dkva[own_rows, head:] = R.kacc[:, head:].astype(BF16)
        for zz in range(nz):
            for cc in range(2):

                @pl.when((zz != z) | (cc != c))
                def _():
                    send(
                        own_kv, own_kv, S.ka + 2 * zz + cc, S.ka + 2 * z + c, dev(y, cc, zz, x)
                    ).start()

    def out_rows(first, count):
        at = pl.ds(first, count)
        R.bo[at, :] = (keep_of(first, count) * (R.mid[at, :] + R.acc[at, :])).astype(BF16)

    back_norm.wait()
    for step in range(nz - 1):
        scatter_step(RQ, step, query_term)
        if step == 0:
            scatter_end(RD, lambda part: each_rows(out_rows, part))
            swap_start(BO, R.bo, R.block_out)
            kv_over_z()
            grad_make(OUT, R.att, R.norm)
            grad_mid(GATE)
        if step == 1:
            kv_own()
            grad_make(QUERY, R.gmlp, R.dq)
            grad_add(UP)
    scatter_term(RQ, z, query_term)
    for zz in range(nz):
        for cc in range(2):

            @pl.when((zz != z) | (cc != c))
            def _():
                arrived(piece(R.dkva, zz, cc), S.ka + 2 * zz + cc)

    first_col = c * (4 * nz * 32) + z * 128
    for yy in range(2):
        cols = pl.ds(pl.multiple_of(yy * (width // 2) + first_col, 128), 128)
        R.gkv[yy] = dot_cols(R.gmlp[:, cols], R.dkva[...])
    send(
        R.gkv.at[1 - y], R.kyb, S.kyx, S.kyx, across_y
    ).start()
    arrived(R.kyb, S.kyx)
    R.kysum[...] = R.gkv[y] + R.kyb[...]
    send(
        R.kysum.at[pl.ds(pl.multiple_of((1 - x) * 64, 64), 64)],
        R.kxb,
        S.kyx + 1,
        S.kyx + 1,
        across_x,
    ).start()
    arrived(R.kxb, S.kyx + 1)
    R.kfinal[...] = (
        R.kysum[pl.ds(pl.multiple_of(x * 64, 64), 64), :] + R.kxb[...]
    )
    kv_out = pltpu.make_async_copy(R.kfinal, R.grad_w_kv, DR.at[S.outs])
    kv_out.start()
    for n, size in tiles(width, 512):
        some = slice(n, n + size)
        R.mid[:, some] = dot_rows(R.dkva[own_rows, :], R.wkv[some, :])
    grad_mid(OUT)

    def tail_rows(first, count):
        at = pl.ds(first, count)
        value = R.tok[at, :].astype(F32)
        inverse = lax.rsqrt(jnp.mean(value * value, axis=1, keepdims=True) + EPSILON)
        unit = value * inverse
        back = R.acc[at, :] + R.mid[at, :]
        R.gains[0] += fold(back * unit)
        e = back * R.gain_attn[0:1, :]
        R.gt[at, :] = (
            R.dmid[at, :]
            + inverse * (e - unit * jnp.mean(e * unit, axis=1, keepdims=True))
        ).astype(BF16)

    def tail_done(part):
        each_rows(tail_rows, part)
        swap_start(GT + part, part_at(R.gt, part), part_at(R.grad_tokens, part))

    scatter_end(RQ, tail_done)

    line = lax.broadcasted_iota(jnp.int32, (8, width), 0)
    gain_first = jnp.sum(R.gains[0], axis=0, keepdims=True)
    gain_second = jnp.sum(R.gains[1], axis=0, keepdims=True)
    R.ga[...] = jnp.where(line == 0, gain_first, jnp.where(line == 1, gain_second, 0.0))
    span = width // 4

    def gain_cols(yy, cc):
        return pl.ds(pl.multiple_of((2 * yy + cc) * span, span), span)

    def gain_send(index, offset):
        dy, dc, dx = offset
        return send(
            R.ga.at[:, gain_cols(flip(y, dy), flip(c, dc))],
            R.gb.at[index],
            S.gains + index,
            S.gains + index,
            around[offset],
        )

    for index, offset in enumerate(around):
        gain_send(index, offset).start()
    R.ga_x[...] = R.ga[:, gain_cols(y, c)]
    for index in range(len(around)):
        arrived(R.gb.at[index], S.gains + index)
        R.ga_x[...] += R.gb[index]
    for zz in range(nz):

        @pl.when(zz != z)
        def _():
            send(
                R.ga_x.at[:, zz * 128 : (zz + 1) * 128],
                R.gb_z.at[z],
                S.gains + 8 + zz,
                S.gains + 8 + z,
                dev(y, c, zz, x),
            ).start()

    R.gfinal[...] = R.ga_x[:, pl.ds(pl.multiple_of(z * 128, 128), 128)]
    for zz in range(nz):

        @pl.when(zz != z)
        def _():
            arrived(R.gb_z.at[zz], S.gains + 8 + zz)
            R.gfinal[...] += R.gb_z[zz]

    gain_out = pltpu.make_async_copy(R.gfinal, R.grad_gains, DR.at[S.outs + 1])
    gain_out.start()

    grad_add(QUERY)
    for name in GRADS:
        arrived(R.other[name], S.py + name)
        if name in Y_FIRST:
            arrived(R.mine[name], S.st + name)
            for cc in range(2):

                @pl.when(jnp.logical_not(keeper & (c == cc)))
                def _():
                    sent(sum_room(name, cc), S.pc + 4 * name + cc)
        else:
            sent(sum_room(name), S.py + name)
        for yy, cc in QUARTERS:
            grad_sent(name, yy, cc)
    kv_out.wait()
    gain_out.wait()
    scatter_sent(RD)
    scatter_sent(RQ)
    gather_end(GA, R.norm)
    swap_wait(BO, R.block_out)
    for part in range(2):
        swap_wait(GT + part, part_at(R.grad_tokens, part))
    for item, src in (
        (LEN, R.own_len),
        (TOK, part_at(R.tokens, 0)),
        (TOK2, part_at(R.tokens, 1)),
        (OG, R.out_grad),
        (KVG, R.kv_grad),
        (BO, R.bo),
        (GT, part_at(R.gt, 0)),
        (GT2, part_at(R.gt, 1)),
    ):
        swap_sent(item, src)
    for zz in range(nz):
        sent(piece(R.dkvb, zz, 1 - c), S.kc + zz)

        @pl.when(zz != z)
        def _():
            sent(R.ks.at[zz], S.kz + zz)
            sent(R.ga_x.at[:, zz * 128 : (zz + 1) * 128], S.gains + 8 + zz)

        for cc in range(2):

            @pl.when((zz != z) | (cc != c))
            def _():
                sent(own_kv, S.ka + 2 * zz + cc)

    sent(R.gkv.at[1 - y], S.kyx)
    sent(R.kysum.at[pl.ds(pl.multiple_of((1 - x) * 64, 64), 64)], S.kyx + 1)
    for index, offset in enumerate(around):
        gain_send(index, offset).wait_send()


def fused(nz, *args):
    (tokens, lengths, gain_attn, w_query, w_kv, w_attn_out, gain_mlp, w_gate, w_up, w_down,
     out_grad, kv_grad) = args
    rows, width = tokens.shape
    ff = w_gate.shape[1]
    qw = w_query.shape[1]
    total, pair = 2 * nz * rows, 2 * rows
    pieces = lengths.shape[1]
    head = w_kv.shape[1] // 2
    half_width = head // 2
    freqs = (ROTARY_BASE ** (-np.arange(half_width, dtype=np.float32) / half_width)).astype(np.float32)
    freq = np.tile(np.concatenate([freqs, freqs])[None, :], (8, 1))
    anywhere, vmem = pl.BlockSpec(memory_space=pl.ANY), pl.BlockSpec(memory_space=pltpu.VMEM)
    ins = dict(
        tokens=(tokens, anywhere),
        lengths=(lengths, vmem),
        freq=(freq, vmem),
        gain_attn=(gain_attn[None], vmem),
        gain_mlp=(gain_mlp[None], vmem),
        w_query=(w_query, anywhere),
        wkv=(w_kv, vmem),
        w_attn_out=(w_attn_out, anywhere),
        w_gate=(w_gate.T, anywhere),
        w_up=(w_up.T, anywhere),
        w_down=(w_down, anywhere),
        out_grad=(out_grad, anywhere),
        kv_grad=(kv_grad, anywhere),
    )
    quarter = width // 4
    grad_tiles = [(ff, quarter), (ff, quarter), (ff, quarter), (qw, quarter), (quarter, qw)]
    outs = dict(
        block_out=((rows, width), BF16),
        grad_tokens=((rows, width), BF16),
        grad_w_kv=((64, 2 * head), F32),
        grad_gains=((8, 128), F32),
        norm_store=((total, width), BF16),
    )
    moved = [
        (shape, BF16)
        for tile in grad_tiles
        for shape in (tile, tile, (4,) + tile, (2,) + tile, (2,) + tile)
    ]
    S, count = semaphores(nz)
    scratch = dict(
        own_len=((8, 128), F32),
        len=((8, 128), F32),
        last=((8, 128), F32),
        tok=((rows, width), BF16),
        og=((rows, width), BF16),
        kvg=((rows, 2 * head), BF16),
        wq=((width, qw), BF16),
        wo=((qw, width), BF16),
        wg=((ff, width), BF16),
        wu=((ff, width), BF16),
        wd=((ff, width), BF16),
        norm=((total, width), BF16),
        nmlp=((total, width), BF16),
        gmlp=((total, width), BF16),
        cos=((total, 128), F32),
        sin=((total, 128), F32),
        start=((total, 128), F32),
        q=((total, qw), BF16),
        kv=((total, 2 * head), BF16),
        att=((total, qw), BF16),
        datt=((total, qw), BF16),
        dq=((total, qw), BF16),
        probs=((qw // head, total, total), BF16),
        hid=((total, ff), BF16),
        dgate=((total, ff), BF16),
        dup=((total, ff), BF16),
        part=((total, width), BF16),
        from_core=((nz * rows, width), BF16),
        from_z=((2, nz + 1, rows, width), BF16),
        acc=((rows, width), F32),
        mid=((rows, width), F32),
        dmid=((rows, width), F32),
        bo=((rows, width), BF16),
        gt=((rows, width), BF16),
        gains=((2, 8, width), F32),
        ga=((8, width), F32),
        ga_x=((8, width // 4), F32),
        gb=((7, 8, width // 4), F32),
        gb_z=((nz, 8, 128), F32),
        gfinal=((8, 128), F32),
        dkv=((total, 2 * head), F32),
        dkvb=((total, 2 * head), BF16),
        dkva=((total, 2 * head), BF16),
        kc=((nz, rows, 2 * head), BF16),
        ks=((nz, rows, 2 * head), BF16),
        kz=((nz, rows, 2 * head), BF16),
        kacc=((rows, 2 * head), F32),
        gkv=((2, 128, 2 * head), F32),
        kyb=((128, 2 * head), F32),
        kysum=((128, 2 * head), F32),
        kxb=((64, 2 * head), F32),
        kfinal=((64, 2 * head), F32),
    )
    tile_shapes = (grad_tiles[DOWN], grad_tiles[OUT], grad_tiles[QUERY])
    out_shapes = list(outs.values()) + moved
    scratch_shapes = list(scratch.values()) + [((2,) + shape, BF16) for shape in tile_shapes]

    def body(*refs):
        refs = list(refs)

        def take(count):
            taken = refs[:count]
            del refs[:count]
            return taken

        R = types.SimpleNamespace(
            **dict(zip(ins, take(len(ins)))), **dict(zip(outs, take(len(outs))))
        )
        rest = take(len(moved))
        R.mine, R.other, R.stage, R.px, R.pc = (rest[k::5] for k in range(5))
        for key, ref in zip(scratch, take(len(scratch))):
            setattr(R, key, ref)
        big, out_tile, query_tile = take(3)
        R.tile = [big, big, big, out_tile, query_tile]
        R.send, R.recv = refs
        block_kernel(nz, pieces, S, R)

    results = pl.pallas_call(
        body,
        out_shape=[jax.ShapeDtypeStruct(shape, kind) for shape, kind in out_shapes],
        in_specs=[spec for _, spec in ins.values()],
        out_specs=[anywhere] * len(out_shapes),
        scratch_shapes=[pltpu.VMEM(shape, kind) for shape, kind in scratch_shapes]
        + [pltpu.SemaphoreType.DMA((count,))] * 2,
        compiler_params=pltpu.CompilerParams(
            collective_id=0, has_side_effects=True, vmem_limit_bytes=63 * MIB
        ),
        name="block",
    )(*[value for value, _ in ins.values()])
    first = list(results[:4])
    mine, other = list(results[5::5]), list(results[6::5])

    def finish(*refs):
        ends, refs = refs[:4], refs[4:]
        one, two, refs = refs[:5], refs[5:10], refs[10:]
        for k in range(3):
            refs[k][...] = ends[k][...]
        right = (lax.axis_index("tensor") % 2) == 1
        refs[3][...] = jnp.where(right, ends[3][:, 64:], ends[3][:, :64])
        for k in GRADS:
            refs[4 + k][...] = one[k][...].astype(F32) + two[k][...].astype(F32)

    cuts = 4

    def cut(array):
        count = array.shape[0] // cuts
        return pl.BlockSpec((count, array.shape[1]), lambda i: (i, 0))

    whole = pl.BlockSpec((8, 128), lambda i: (0, 0))
    block_out, grad_tokens, grad_w_kv, gains, *sums = pl.pallas_call(
        finish,
        grid=(cuts,),
        out_shape=[jax.ShapeDtypeStruct(array.shape, array.dtype) for array in first[:3]]
        + [jax.ShapeDtypeStruct((8, 64), F32)]
        + [jax.ShapeDtypeStruct(array.shape, F32) for array in mine],
        in_specs=[cut(array) for array in first[:3]] + [whole] + [cut(a) for a in mine + other],
        out_specs=[cut(array) for array in first[:3]]
        + [pl.BlockSpec((8, 64), lambda i: (0, 0))]
        + [cut(array) for array in mine],
        compiler_params=pltpu.CompilerParams(vmem_limit_bytes=32 * MIB),
        name="finish",
    )(*first, *mine, *other)
    return (
        block_out,
        grad_tokens,
        gains[0],
        sums[QUERY],
        grad_w_kv,
        sums[OUT],
        gains[1],
        sums[GATE].T,
        sums[UP].T,
        sums[DOWN],
    )


def solution(mesh):
    groups, parts = mesh.shape["dp"], mesh.shape["tensor"]
    paired = groups == 4 and parts == 8
    per_group = functools.partial(fused, parts // 2) if paired else per_device
    placed = (
        P(("dp", "tensor"), None),
        P("dp", None),
        P(),
        P(None, "tensor"),
        P(),
        P("tensor", None),
        P(),
        P(None, "tensor"),
        P(None, "tensor"),
        P("tensor", None),
        P(("dp", "tensor"), None),
        P(("dp", "tensor"), None),
    )
    return jax.shard_map(
        per_group,
        mesh=mesh,
        in_specs=placed,
        out_specs=(
            P(("dp", "tensor"), None),
            P(("dp", "tensor"), None),
            P(("dp", "tensor")),
            P("dp", "tensor"),
            P(("dp", "tensor"), None),
            P("tensor", "dp"),
            P(("dp", "tensor")),
            P("dp", "tensor"),
            P("dp", "tensor"),
            P("tensor", "dp"),
        ),
        check_vma=False,
    )
```

```python
import functools
import types

import jax
import jax.numpy as jnp
import numpy as np
from jax import lax
from jax.experimental import pallas as pl
from jax.experimental.pallas import tpu as pltpu
from jax.sharding import PartitionSpec as P

SPAN = 64


EPSILON = 1e-05
ROTARY_BASE = 10000.0
MASKED = -1e30


def rotary_tables(positions, width):
    half_width = width // 2
    freqs = ROTARY_BASE ** (-jnp.arange(half_width, dtype=jnp.float32) / half_width)
    angles = positions[:, None] * freqs[None, :]
    return (jnp.cos(angles), jnp.sin(angles))


def rotate(values, cosine, sine):
    half_width = values.shape[-1] // 2
    first_half = values[..., :half_width]
    second_half = values[..., half_width:]
    return jnp.concatenate(
        [first_half * cosine - second_half * sine, second_half * cosine + first_half * sine],
        axis=-1,
    )


def unrotate(values, cosine, sine):
    half_width = values.shape[-1] // 2
    first_half = values[..., :half_width]
    second_half = values[..., half_width:]
    return jnp.concatenate(
        [first_half * cosine + second_half * sine, second_half * cosine - first_half * sine],
        axis=-1,
    )


def layout(piece_units, rows):
    piece_rows = piece_units * SPAN
    ends = jnp.cumsum(piece_rows)
    starts = ends - piece_rows
    row_steps = jnp.arange(rows, dtype=jnp.int32)
    segment = jnp.sum((row_steps[:, None] >= ends[None, :]).astype(jnp.int32), axis=1)
    member = segment[:, None] == jnp.arange(piece_units.shape[0], dtype=jnp.int32)[None, :]
    row_start = jnp.sum(jnp.where(member, starts[None, :], 0), axis=1)
    positions = (row_steps - row_start).astype(jnp.float32)
    keep = (segment < piece_units.shape[0] - 1).astype(jnp.float32)
    return (segment, row_steps, positions, keep)


def permitted(block_segment, block_steps, segment, row_steps):
    return (block_segment[:, None] == segment[None, :]) & (
        row_steps[None, :] <= block_steps[:, None]
    )


def spread_rows(values):
    return lax.all_gather(values, "tensor", axis=0, tiled=True)


def spread_grads(values):
    return lax.all_gather(values, "tensor", axis=0, tiled=True)


def per_device(
    tokens,
    lengths,
    gain_attn,
    w_query,
    w_kv,
    w_attn_out,
    gain_mlp,
    w_gate,
    w_up,
    w_down,
    out_grad,
    kv_grad,
):
    local_rows = tokens.shape[0]
    parts = lax.axis_size("tensor")
    total_rows = local_rows * parts
    first_row = lax.axis_index("tensor") * local_rows
    segment, row_steps, positions, keep = layout(lengths[0], total_rows)
    head_dim = w_kv.shape[1] // 2
    local_heads = w_query.shape[1] // head_dim
    scale = head_dim ** (-0.5)
    cosine, sine = rotary_tables(positions, head_dim)
    row_keep = lax.dynamic_slice_in_dim(keep, first_row, local_rows, 0)[:, None]
    row_cosine = lax.dynamic_slice_in_dim(cosine, first_row, local_rows, 0)
    row_sine = lax.dynamic_slice_in_dim(sine, first_row, local_rows, 0)
    tokens_full = tokens.astype(jnp.float32)
    inv_first = lax.rsqrt(jnp.mean(tokens_full * tokens_full, axis=-1, keepdims=True) + EPSILON)
    unit_first = tokens_full * inv_first
    normed_rows = (unit_first * gain_attn).astype(jnp.bfloat16)
    normed = spread_rows(normed_rows)
    queries = jnp.dot(normed, w_query, preferred_element_type=jnp.float32).reshape(
        total_rows, local_heads, head_dim
    )
    queries = rotate(queries, cosine[:, None, :], sine[:, None, :]).astype(jnp.bfloat16)
    kv_raw = jnp.dot(normed, w_kv, preferred_element_type=jnp.float32)
    shared = jnp.concatenate(
        [rotate(kv_raw[:, :head_dim], cosine, sine), kv_raw[:, head_dim:]], axis=1
    ).astype(jnp.bfloat16)
    keys = shared[:, :head_dim]
    values = shared[:, head_dim:]
    block = min(512, total_rows)
    count = total_rows // block
    pieces = []
    log_totals = []
    for number in range(count):
        begin = number * block
        query_block = queries[begin : begin + block]
        allowed = permitted(
            segment[begin : begin + block], row_steps[begin : begin + block], segment, row_steps
        )
        scores = (
            jnp.einsum("qhd,kd->hqk", query_block, keys, preferred_element_type=jnp.float32) * scale
        )
        scores = jnp.where(allowed[None], scores, MASKED)
        row_max = jnp.max(scores, axis=-1, keepdims=True)
        exp_scores = jnp.exp(scores - row_max)
        row_total = jnp.sum(exp_scores, axis=-1, keepdims=True)
        log_totals.append(row_max + jnp.log(row_total))
        weights = (exp_scores / row_total).astype(jnp.bfloat16)
        pieces.append(
            jnp.einsum("hqk,kd->qhd", weights, values, preferred_element_type=jnp.float32).astype(
                jnp.bfloat16
            )
        )
    attended = jnp.concatenate(pieces, axis=0).reshape(total_rows, local_heads * head_dim)
    attn_rows = lax.psum_scatter(
        jnp.dot(attended, w_attn_out, preferred_element_type=jnp.float32).astype(jnp.bfloat16),
        "tensor",
        scatter_dimension=0,
        tiled=True,
    ).astype(jnp.float32)
    mid = tokens_full + attn_rows
    inv_second = lax.rsqrt(jnp.mean(mid * mid, axis=-1, keepdims=True) + EPSILON)
    unit_second = mid * inv_second
    normed_mlp = spread_rows((unit_second * gain_mlp).astype(jnp.bfloat16))
    gate = jnp.dot(normed_mlp, w_gate, preferred_element_type=jnp.float32)
    up = jnp.dot(normed_mlp, w_up, preferred_element_type=jnp.float32)
    sigma = jax.nn.sigmoid(gate)
    active = gate * sigma
    hidden = (active * up).astype(jnp.bfloat16)
    mlp_rows = lax.psum_scatter(
        jnp.dot(hidden, w_down, preferred_element_type=jnp.float32).astype(jnp.bfloat16),
        "tensor",
        scatter_dimension=0,
        tiled=True,
    ).astype(jnp.float32)
    block_out = (row_keep * (mid + mlp_rows)).astype(jnp.bfloat16)
    out_full = row_keep * out_grad.astype(jnp.float32)
    grad_mlp = spread_grads(out_full.astype(jnp.bfloat16))
    g_down = jnp.einsum("rf,rd->fd", hidden, grad_mlp, preferred_element_type=jnp.float32)
    g_hidden = jnp.einsum("rd,fd->rf", grad_mlp, w_down, preferred_element_type=jnp.float32)
    d_gate = (g_hidden * up * sigma * (1.0 + gate * (1.0 - sigma))).astype(jnp.bfloat16)
    d_up = (g_hidden * active).astype(jnp.bfloat16)
    g_gate = jnp.einsum("rd,rf->df", normed_mlp, d_gate, preferred_element_type=jnp.float32)
    g_up = jnp.einsum("rd,rf->df", normed_mlp, d_up, preferred_element_type=jnp.float32)
    back_mlp = lax.psum_scatter(
        (
            jnp.einsum("rf,df->rd", d_gate, w_gate, preferred_element_type=jnp.float32)
            + jnp.einsum("rf,df->rd", d_up, w_up, preferred_element_type=jnp.float32)
        ).astype(jnp.bfloat16),
        "tensor",
        scatter_dimension=0,
        tiled=True,
    ).astype(jnp.float32)
    e_mlp = back_mlp * gain_mlp
    g_gain_mlp = jnp.sum(back_mlp * unit_second, axis=0)
    d_mid = out_full + inv_second * (
        e_mlp - unit_second * jnp.mean(e_mlp * unit_second, axis=-1, keepdims=True)
    )
    grad_attn = spread_grads(d_mid.astype(jnp.bfloat16))
    g_attn_out = jnp.einsum("rh,rd->hd", attended, grad_attn, preferred_element_type=jnp.float32)
    d_att = jnp.einsum(
        "rd,hd->rh", grad_attn, w_attn_out, preferred_element_type=jnp.float32
    ).astype(jnp.bfloat16)
    d_att = d_att.reshape(total_rows, local_heads, head_dim)
    query_pieces = []
    d_keys = jnp.zeros((total_rows, head_dim), jnp.float32)
    d_values = jnp.zeros((total_rows, head_dim), jnp.float32)
    for number in range(count):
        begin = number * block
        query_block = queries[begin : begin + block]
        grad_block = d_att[begin : begin + block]
        allowed = permitted(
            segment[begin : begin + block], row_steps[begin : begin + block], segment, row_steps
        )
        scores = (
            jnp.einsum("qhd,kd->hqk", query_block, keys, preferred_element_type=jnp.float32) * scale
        )
        scores = jnp.where(allowed[None], scores, MASKED)
        probs = jnp.exp(scores - log_totals[number])
        weights = probs.astype(jnp.bfloat16)
        d_probs = jnp.einsum("qhd,kd->hqk", grad_block, values, preferred_element_type=jnp.float32)
        inner = jnp.sum(d_probs * probs, axis=-1, keepdims=True)
        d_scores = (probs * (d_probs - inner)).astype(jnp.bfloat16)
        query_pieces.append(
            jnp.einsum("hqk,kd->qhd", d_scores, keys, preferred_element_type=jnp.float32) * scale
        )
        d_keys = (
            d_keys
            + jnp.einsum("hqk,qhd->kd", d_scores, query_block, preferred_element_type=jnp.float32)
            * scale
        )
        d_values = d_values + jnp.einsum(
            "hqk,qhd->kd", weights, grad_block, preferred_element_type=jnp.float32
        )
    d_queries = jnp.concatenate(query_pieces, axis=0)
    d_queries = unrotate(d_queries, cosine[:, None, :], sine[:, None, :]).astype(jnp.bfloat16)
    d_queries = d_queries.reshape(total_rows, local_heads * head_dim)
    g_query = jnp.einsum("rd,rh->dh", normed, d_queries, preferred_element_type=jnp.float32)
    kv_rows = lax.psum_scatter(
        jnp.concatenate([d_keys, d_values], axis=1).astype(jnp.bfloat16),
        "tensor",
        scatter_dimension=0,
        tiled=True,
    ).astype(jnp.float32)
    kv_rows = kv_rows + row_keep * kv_grad.astype(jnp.float32)
    d_kv = jnp.concatenate(
        [unrotate(kv_rows[:, :head_dim], row_cosine, row_sine), kv_rows[:, head_dim:]], axis=1
    ).astype(jnp.bfloat16)
    d_kv_all = lax.all_gather(d_kv, "tensor", axis=0, tiled=True)
    width = normed.shape[1]
    groups = lax.axis_size("dp")
    own = lax.dynamic_index_in_dim(
        normed.reshape(total_rows, groups, parts, width // (groups * parts)),
        lax.axis_index("tensor"),
        2,
        False,
    ).reshape(total_rows, width // parts)
    g_kv = jnp.einsum("rd,rk->dk", own, d_kv_all, preferred_element_type=jnp.float32)
    back_attn = lax.psum_scatter(
        jnp.einsum("rh,dh->rd", d_queries, w_query, preferred_element_type=jnp.float32).astype(
            jnp.bfloat16
        ),
        "tensor",
        scatter_dimension=0,
        tiled=True,
    ).astype(jnp.float32)
    back_attn = back_attn + jnp.einsum("rk,dk->rd", d_kv, w_kv, preferred_element_type=jnp.float32)
    e_attn = back_attn * gain_attn
    g_gain_attn = jnp.sum(back_attn * unit_first, axis=0)
    grad_tokens = (
        d_mid
        + inv_first * (e_attn - unit_first * jnp.mean(e_attn * unit_first, axis=-1, keepdims=True))
    ).astype(jnp.bfloat16)
    kv_sum = lax.psum_scatter(g_kv, "dp", scatter_dimension=0, tiled=True)
    share = width // (groups * parts)
    first = (lax.axis_index("dp") * parts + lax.axis_index("tensor")) * share
    gain_all = lax.all_gather(jnp.stack([g_gain_attn, g_gain_mlp]), ("dp", "tensor"), axis=0)
    gain_sums = jnp.sum(lax.dynamic_slice_in_dim(gain_all, first, share, 2), axis=0)
    query_sum, out_sum, gate_sum, up_sum, down_sum = (
        lax.psum_scatter(
            g_query.astype(jnp.bfloat16), "dp", scatter_dimension=0, tiled=True
        ).astype(jnp.float32),
        lax.psum_scatter(
            g_attn_out.astype(jnp.bfloat16), "dp", scatter_dimension=1, tiled=True
        ).astype(jnp.float32),
        lax.psum_scatter(g_gate.astype(jnp.bfloat16), "dp", scatter_dimension=0, tiled=True).astype(
            jnp.float32
        ),
        lax.psum_scatter(g_up.astype(jnp.bfloat16), "dp", scatter_dimension=0, tiled=True).astype(
            jnp.float32
        ),
        lax.psum_scatter(g_down.astype(jnp.bfloat16), "dp", scatter_dimension=1, tiled=True).astype(
            jnp.float32
        ),
    )
    return (
        block_out,
        grad_tokens,
        gain_sums[0],
        query_sum,
        kv_sum,
        out_sum,
        gain_sums[1],
        gate_sum,
        up_sum,
        down_sum,
    )


F32, BF16 = jnp.float32, jnp.bfloat16
MESH = pl.DeviceIdType.MESH
MIB = 1 << 20


def dot(a, b):
    return jnp.dot(a, b, preferred_element_type=F32)


def dot_rows(a, b):
    return lax.dot_general(a, b, (((1,), (1,)), ((), ())), preferred_element_type=F32)


def dot_cols(a, b):
    return lax.dot_general(a, b, (((0,), (0,)), ((), ())), preferred_element_type=F32)


def tiles(width, step):
    return [(at, min(step, width - at)) for at in range(0, width, step)]


GN, GG, GM, GA = range(4)
RO, RB, RD, RQ = range(4)
LEN, TOK, TOK2, WQ, OG, KVG, WO, WG, WU, WD, BO, GT, GT2 = range(13)
DOWN, GATE, UP, OUT, QUERY = GRADS = range(5)


def semaphores(nz):
    counts = dict(
        swap=13,
        swap_y=13,
        gz=4 * 4 * nz,
        gc=4 * 2 * nz,
        rz=4 * 4 * nz,
        rc=4 * nz,
        stage=20,
        px=20,
        pc=20,
        py=5,
        ld=20,
        st=5,
        kc=nz,
        kz=nz,
        ka=2 * nz,
        kyx=2,
        gains=8 + nz,
        spill=2,
        outs=4,
    )
    firsts, total = {}, 0
    for name, count in counts.items():
        firsts[name] = total
        total += count
    return types.SimpleNamespace(**firsts), total


def block_kernel(nz, pieces, S, R):
    rows, width = R.tokens.shape
    ff = R.w_down.shape[0]
    total = 2 * nz * rows
    pair = 2 * rows
    head = 128
    heads = R.wq.shape[1] // head
    scale = head ** (-0.5)
    DS, DR = R.send, R.recv

    dp, tensor = lax.axis_index("dp"), lax.axis_index("tensor")
    y, c = dp // 2, dp % 2
    z, x = tensor // 2, tensor % 2
    keeper = c == x

    def dev(yy, cc, zz, xx):
        return (2 * yy + cc, 2 * zz + xx)

    def flip(value, yes):
        return 1 - value if yes else value

    sibling = dev(y, 1 - c, z, x)
    partner = dev(y, 1 - c, z, 1 - x)
    across_x = dev(y, c, z, 1 - x)
    across_y = dev(1 - y, c, z, x)

    def send(src, dst, s, r, to):
        return pltpu.make_async_remote_copy(
            src_ref=src,
            dst_ref=dst,
            send_sem=DS.at[s],
            recv_sem=DR.at[r],
            device_id=to,
            device_id_type=MESH,
        )

    def arrived(dst, r):
        pltpu.make_async_copy(dst, dst, DR.at[r]).wait()

    def sent(src, s):
        pltpu.make_async_copy(src, src, DS.at[s]).wait()

    barrier = pltpu.get_barrier_semaphore()
    around = {
        (dy, dc, dx): dev(flip(y, dy), flip(c, dc), z, flip(x, dx))
        for dy in range(2)
        for dc in range(2)
        for dx in range(2)
        if dy + dc + dx
    }
    for (dy, dc, dx), to in around.items():
        if dy + dx:
            pl.semaphore_signal(barrier, inc=1, device_id=to, device_id_type=MESH)
    for zz in range(nz):
        for cc in range(2):

            @pl.when((zz != z) | (cc != c))
            def _():
                pl.semaphore_signal(
                    barrier, inc=1, device_id=dev(y, cc, zz, x), device_id_type=MESH
                )

    pl.semaphore_wait(barrier, 6 + 2 * nz - 1)

    def swap_start(item, src, dst):
        at = S.swap + item

        @pl.when(keeper)
        def _():
            pltpu.make_async_copy(src, dst, DR.at[at]).start()

        @pl.when(jnp.logical_not(keeper))
        def _():
            send(src, dst, at, at, partner).start()

    def swap_wait(item, dst):
        arrived(dst, S.swap + item)

    def swap_sent(item, src):
        @pl.when(jnp.logical_not(keeper))
        def _():
            sent(src, S.swap + item)

    def part_at(ref, which):
        count = ref.shape[0] // 2
        return ref.at[pl.ds(pl.multiple_of(which * count, count), count)]

    def weight_start(item, src, dst):
        at = S.swap + item

        @pl.when(keeper)
        def _():
            pltpu.make_async_copy(src, dst, DR.at[at]).start()

        @pl.when(jnp.logical_not(keeper))
        def _():
            send(part_at(src, y), part_at(dst, y), at, at, partner).start()

    def weight_pass(item, dst):
        @pl.when(jnp.logical_not(keeper))
        def _():
            half_here = part_at(dst, y)
            arrived(half_here, S.swap + item)
            send(half_here, half_here, S.swap_y + item, S.swap_y + item, across_y).start()

    def weight_wait(item, dst):
        @pl.when(keeper)
        def _():
            arrived(dst, S.swap + item)

        @pl.when(jnp.logical_not(keeper))
        def _():
            arrived(part_at(dst, 1 - y), S.swap_y + item)

    def weight_sent(item, src, dst):
        @pl.when(jnp.logical_not(keeper))
        def _():
            sent(part_at(src, y), S.swap + item)
            sent(part_at(dst, y), S.swap_y + item)

    def piece(ref, chunk, core):
        return ref.at[pl.ds(pl.multiple_of((2 * chunk + core) * rows, rows), rows)]

    def chunk_rows(chunk):
        return pl.ds(pl.multiple_of(chunk * pair, pair), pair)

    own_at = pl.multiple_of((2 * z + c) * rows, rows)

    def bit(ref, chunk, core, part):
        count = rows // 2
        first = (2 * chunk + core) * rows + part * count
        return ref.at[pl.ds(pl.multiple_of(first, count), count)]

    def gather_sem(base, name, way, chunk, part):
        return base + ((2 * name + way) * nz + chunk) * 2 + part

    def core_sem(name, chunk, part):
        return S.gc + (name * nz + chunk) * 2 + part

    def gather_hop(name, ref, way, chunk, part):
        some = bit(ref, chunk, c, part)
        to = dev(y, c, z + 1 - 2 * way, x)
        send(
            some,
            some,
            gather_sem(S.gz, name, way, chunk, part),
            gather_sem(S.gz, name, 0, chunk, part),
            to,
        ).start()

    def gather_share(name, ref, chunk, part):
        some = bit(ref, chunk, c, part)
        at = core_sem(name, chunk, part)
        send(some, some, at, at, sibling).start()

    def gather_start(name, ref, parts=(0, 1)):
        for part in parts:

            @pl.when(z < nz - 1)
            def _():
                gather_hop(name, ref, 0, z, part)

            @pl.when(z > 0)
            def _():
                gather_hop(name, ref, 1, z, part)

            gather_share(name, ref, z, part)

    def gather_pass(name, ref, step):
        for part in range(2):
            for way in range(2):
                chunk = z - 1 - step if way == 0 else z + 1 + step

                @pl.when((chunk >= 0) & (chunk <= nz - 1))
                def _():
                    arrived(bit(ref, chunk, c, part), gather_sem(S.gz, name, 0, chunk, part))

                    @pl.when(z < nz - 1 if way == 0 else z > 0)
                    def _():
                        gather_hop(name, ref, way, chunk, part)

                    gather_share(name, ref, chunk, part)

    def gather_theirs(name, ref, chunk):
        for part in range(2):
            arrived(bit(ref, chunk, 1 - c, part), core_sem(name, chunk, part))

    def gather_own(name, ref, work):
        gather_theirs(name, ref, z)
        if work is not None:
            work(z)

    def gather_use(name, ref, step, work):
        for way in range(2):
            chunk = z - 1 - step if way == 0 else z + 1 + step

            @pl.when((chunk >= 0) & (chunk <= nz - 1))
            def _():
                gather_theirs(name, ref, chunk)
                if work is not None:
                    work(chunk)

    def gather_end(name, ref):
        for chunk in range(nz):
            for part in range(2):
                some = bit(ref, chunk, c, part)
                sent(some, core_sem(name, chunk, part))

                @pl.when((z < nz - 1) & (chunk <= z))
                def _():
                    sent(some, gather_sem(S.gz, name, 0, chunk, part))

                @pl.when((z > 0) & (chunk >= z))
                def _():
                    sent(some, gather_sem(S.gz, name, 1, chunk, part))

    def terms(name):
        return R.nmlp if name == RQ else R.part

    def half(name, chunk, core):
        return piece(terms(name), chunk, core)

    def core_room(name, chunk):
        room = R.wg if name == RQ else R.from_core
        return room.at[pl.ds(pl.multiple_of(chunk * rows, rows), rows)]

    def z_slot(name, way, chunk, at, part):
        slot = jnp.where((way == 1) & (chunk == at), nz, chunk)
        count = rows // 2
        return R.from_z.at[name % 2, slot, pl.ds(part * count, count)]

    def add_rows(dst, *sources):
        step = 32

        @pl.loop(0, dst.shape[0] // step)
        def _(i):
            at = pl.ds(pl.multiple_of(i * step, step), step)
            value = sources[0][at, :].astype(F32)
            for source in sources[1:]:
                value = value + source[at, :].astype(F32)
            dst[at, :] = value.astype(dst.dtype)

    def scatter_term(name, chunk, work):
        work(chunk)
        send(
            half(name, chunk, 1 - c),
            core_room(name, chunk),
            S.rc + nz * name + chunk,
            S.rc + nz * name + chunk,
            sibling,
        ).start()

    def scatter_forward(name, way, chunk):
        arrived(core_room(name, chunk), S.rc + nz * name + chunk)
        earlier = ((way == 0) & (z > 0)) | ((way == 1) & (z < nz - 1))
        to = z + 1 - 2 * way
        for part in range(2):
            mine = bit(terms(name), chunk, c, part)
            theirs = core_room(name, chunk).at[part * (rows // 2) : (part + 1) * (rows // 2)]
            before = z_slot(name, way, chunk, z, part)
            at = gather_sem(S.rz, name, way, chunk, part)

            @pl.when(earlier)
            def _():
                arrived(before, at)
                add_rows(mine, mine, theirs, before)

            @pl.when(jnp.logical_not(earlier))
            def _():
                add_rows(mine, mine, theirs)

            send(mine, z_slot(name, way, chunk, to, part), at, at, dev(y, c, to, x)).start()

    def between(index):
        way, chunk, valid = 0, 0, False
        for at in range(1, nz - 1):
            hops = [(other + at / 2, 0, other) for other in range(at + 1, nz)]
            hops += [(nz - 1 - other + (nz - 1 - at) / 2, 1, other) for other in range(at)]
            _, this_way, this_chunk = sorted(hops)[index]
            way = jnp.where(z == at, this_way, way)
            chunk = jnp.where(z == at, this_chunk, chunk)
            valid = valid | (z == at)
        return way, chunk, valid

    def scatter_slot(step, way):
        if way == 0:
            chunk = nz - 1 + z - step
            return chunk, (step >= z) & (z < nz - 1)
        chunk = step - (nz - 1 - z)
        return chunk, (chunk >= 0) & (z > 0)

    def scatter_step(name, step, work):
        for way in range(2):
            chunk, valid = scatter_slot(step, way)

            @pl.when(valid)
            def _():
                scatter_term(name, chunk, work)

        for way in range(2):
            chunk, valid = scatter_slot(step, way)

            @pl.when(valid)
            def _():
                scatter_forward(name, way, chunk)

    def scatter_end(name, finish):
        arrived(core_room(name, z), S.rc + nz * name + z)
        for part in range(2):
            some = pl.ds(part * (rows // 2), rows // 2)
            add_rows(R.acc.at[some], half(name, z, c).at[some], core_room(name, z).at[some])
            for way in range(2):

                @pl.when(z > 0 if way == 0 else z < nz - 1)
                def _():
                    before = z_slot(name, way, z, z, part)
                    arrived(before, gather_sem(S.rz, name, way, z, part))
                    add_rows(R.acc.at[some], R.acc.at[some], before)

            finish(part)

    def scatter_sent(name):
        for chunk in range(nz):
            sent(half(name, chunk, 1 - c), S.rc + nz * name + chunk)
            for way in range(2):
                for part in range(2):

                    @pl.when(z < chunk if way == 0 else z > chunk)
                    def _():
                        sent(
                            bit(terms(name), chunk, c, part),
                            gather_sem(S.rz, name, way, chunk, part),
                        )

    def each_rows(body, part, step=32):
        @pl.loop(0, rows // 2 // step)
        def _(i):
            body(pl.multiple_of(part * (rows // 2) + i * step, step), step)

    def keep_of(first, count):
        index = lax.broadcasted_iota(jnp.int32, (count, 1), 0) + (own_at + first)
        return (index.astype(F32) < R.last[0:1, 0:1]).astype(F32)

    def rotary():
        units = R.len[...] * 64.0
        ends, end = [], jnp.zeros((1, 128), F32)
        for p in range(pieces):
            end = end + units[p : p + 1, :]
            ends.append((units[p : p + 1, :], end))
        R.last[...] = jnp.broadcast_to(ends[-2][1], (8, 128))

        @pl.loop(0, total // 128)
        def _(i):
            at = pl.ds(pl.multiple_of(i * 128, 128), 128)
            index = (lax.broadcasted_iota(jnp.int32, (128, 128), 0) + i * 128).astype(F32)
            start = jnp.zeros((128, 128), F32)
            for length, stop in ends[:-1]:
                start = start + jnp.where(stop <= index, length, 0.0)
            R.start[at, :] = start
            angle = (index - start) * R.freq[0:1, :]
            lane = lax.broadcasted_iota(jnp.int32, (128, 128), 1)
            R.cos[at, :] = jnp.cos(angle)
            R.sin[at, :] = jnp.where(lane < 64, -1.0, 1.0) * jnp.sin(angle)

    def turn(value, cosine, sine):
        swapped = jnp.concatenate([value[:, 64:], value[:, :64]], axis=1)
        return value * cosine + swapped * sine

    def project(chunk):
        at = chunk_rows(chunk)
        normed = R.norm[at, :]
        cosine, sine = R.cos[at, :], R.sin[at, :]
        queries = dot(normed, R.wq[...])
        for h in range(heads):
            cols = slice(h * head, (h + 1) * head)
            R.q[at, cols] = turn(queries[:, cols], cosine, sine).astype(BF16)
        kv = dot(normed, R.wkv[...])
        R.kv[at, :head] = turn(kv[:, :head], cosine, sine).astype(BF16)
        R.kv[at, head:] = kv[:, head:].astype(BF16)

    def attend(chunk):
        at = chunk_rows(chunk)
        keys, values = R.kv[:, :head], R.kv[:, head:]
        start = R.start[at, 0:1]
        column = lax.broadcasted_iota(jnp.int32, (pair, total), 1).astype(F32)
        row = (lax.broadcasted_iota(jnp.int32, (pair, 1), 0) + chunk * pair).astype(F32)
        allowed = (column >= start) & (column <= row)
        for h in range(heads):
            cols = slice(h * head, (h + 1) * head)
            scores = dot_rows(R.q[at, cols], keys) * scale
            scores = jnp.where(allowed, scores, -1e30)
            exps = jnp.exp(scores - jnp.max(scores, axis=1, keepdims=True))
            weights = exps * (1.0 / jnp.sum(exps, axis=1, keepdims=True))
            weights = weights.astype(BF16)
            R.probs[h, at, :] = weights
            R.att[at, cols] = dot(weights, values).astype(BF16)

    def out_term(chunk):
        attend(chunk)
        at = chunk_rows(chunk)
        for n, size in tiles(width, 512):
            R.part[at, n : n + size] = dot(
                R.att[at, :], R.wo[:, n : n + size]
            ).astype(BF16)

    def mlp(chunk):
        at = chunk_rows(chunk)
        for n, size in tiles(ff, 256):
            cols = slice(n, n + size)
            gate = dot_rows(R.nmlp[at, :], R.wg[cols, :])
            up = dot_rows(R.nmlp[at, :], R.wu[cols, :])
            grad = dot_rows(R.gmlp[at, :], R.wd[cols, :])
            sigma = 1.0 / (1.0 + jnp.exp(-gate))
            active = gate * sigma
            R.hid[at, cols] = (active * up).astype(BF16)
            R.dup[at, cols] = (grad * active).astype(BF16)
            R.dgate[at, cols] = (grad * up * (sigma * (1.0 + gate * (1.0 - sigma)))).astype(BF16)

    def back_term(chunk):
        at = chunk_rows(chunk)
        for n, size in tiles(width, 512):
            some = slice(n, n + size)
            R.part[at, some] = (
                dot(R.dgate[at, :], R.wg[:, some]) + dot(R.dup[at, :], R.wu[:, some])
            ).astype(BF16)

    def down_term(chunk):
        at = chunk_rows(chunk)
        for n, size in tiles(width, 512):
            some = slice(n, n + size)
            R.part[at, some] = dot(R.hid[at, :], R.wd[:, some]).astype(BF16)

    def d_attended(chunk):
        at = chunk_rows(chunk)
        R.datt[at, :] = dot_rows(R.norm[at, :], R.wo[...]).astype(BF16)
        backward_attend(chunk)

    def backward_attend(chunk):
        at = chunk_rows(chunk)
        keys, values = R.kv[:, :head], R.kv[:, head:]
        cosine, sine = R.cos[at, :], R.sin[at, :]
        for h in range(heads):
            cols = slice(h * head, (h + 1) * head)
            weights = R.probs[h, at, :]
            probs = weights.astype(F32)
            grad = R.datt[at, cols]
            d_probs = dot_rows(grad, values)
            inner = jnp.sum(d_probs * probs, axis=1, keepdims=True)
            d_scores = (probs * (d_probs - inner)).astype(BF16)
            d_queries = dot(d_scores, keys) * scale
            R.dq[at, cols] = turn(d_queries, cosine, -sine).astype(BF16)
            R.dkv[:, :head] += dot_cols(d_scores, R.q[at, cols]) * scale
            R.dkv[:, head:] += dot_cols(weights, grad)

    def query_term(chunk):
        at = chunk_rows(chunk)
        for n, size in tiles(width, 512):
            some = slice(n, n + size)
            terms(RQ)[at, some] = dot_rows(R.dq[at, :], R.wq[some, :]).astype(BF16)

    Y_FIRST = (GATE, OUT)

    def grad_send(name, yy, cc):
        quarter = 2 * yy + cc
        stage = R.stage[name].at[quarter]
        if name in Y_FIRST:
            at = S.px + 4 * name + cc

            @pl.when(yy != y)
            def _():
                send(stage, R.px[name].at[cc], at, at, across_y).start()

            return
        into_x, into_c = R.px[name].at[yy], R.pc[name].at[yy]

        @pl.when(jnp.logical_not(keeper))
        def _():
            send(
                stage,
                into_x,
                S.px + 4 * name + quarter,
                S.px + 4 * name + yy,
                (2 * y + cc, 2 * z + 1 - x),
            ).start()

        @pl.when(keeper & (c == cc))
        def _():
            pltpu.make_async_copy(stage, into_c, DR.at[S.pc + 4 * name + yy]).start()

        @pl.when(keeper & (c != cc))
        def _():
            send(
                stage, into_c, S.pc + 4 * name + quarter, S.pc + 4 * name + yy, sibling
            ).start()

    def grad_sent(name, yy, cc):
        quarter = 2 * yy + cc
        stage = R.stage[name].at[quarter]
        if name in Y_FIRST:

            @pl.when(yy != y)
            def _():
                sent(stage, S.px + 4 * name + cc)

            return

        @pl.when(jnp.logical_not(keeper))
        def _():
            sent(stage, S.px + 4 * name + quarter)

        @pl.when(keeper & (c != cc))
        def _():
            sent(stage, S.pc + 4 * name + quarter)

    QUARTERS = [(0, 0), (0, 1), (1, 0), (1, 1)]

    def grad_make(name, left, right):
        split_left = name == QUERY
        quarter_cols = (left if split_left else right).shape[1] // 4
        tile = R.tile[name]
        for index, (yy, cc) in enumerate(QUARTERS):
            first = index * quarter_cols
            if index > 1:
                pltpu.make_async_copy(
                    tile.at[index % 2],
                    R.stage[name].at[index - 2],
                    DR.at[S.stage + 4 * name + index - 2],
                ).wait()
                grad_send(name, *QUARTERS[index - 2])
            if split_left:
                for m, size in tiles(quarter_cols, 256):
                    tile[index % 2, m : m + size, :] = dot_cols(
                        left[:, first + m : first + m + size], right[...]
                    ).astype(BF16)
            else:
                for m, size in tiles(left.shape[1], 256):
                    tile[index % 2, m : m + size, :] = dot_cols(
                        left[:, m : m + size], right[:, first : first + quarter_cols]
                    ).astype(BF16)
            pltpu.make_async_copy(
                tile.at[index % 2],
                R.stage[name].at[index],
                DR.at[S.stage + 4 * name + index],
            ).start()
        for index in (2, 3):
            pltpu.make_async_copy(
                tile.at[index % 2],
                R.stage[name].at[index],
                DR.at[S.stage + 4 * name + index],
            ).wait()
            grad_send(name, *QUARTERS[index])

    def sum_room(name, cc=0):
        cols = width // 4
        if name == QUERY:
            return R.wu.at[0:cols, 3 * cols : 3 * cols + R.wq.shape[1]]
        if name == DOWN:
            return R.wu.at[:, 2 * cols : 3 * cols]
        if name == UP:
            return R.wd.at[:, 2 * cols : 3 * cols]
        if name == GATE:
            return R.wd.at[:, cc * cols : (cc + 1) * cols]
        count = R.wo.shape[0]
        return R.wd.at[cc * count : (cc + 1) * count, 3 * cols :]

    def grad_places(name):
        count, cols = R.tile[name].shape[1:]
        return (
            (R.tile[name].at[0], R.tile[name].at[1]),
            (R.wu.at[0:count, 0:cols], R.wu.at[0:count, cols : 2 * cols]),
        )

    def grad_loads(name, turn_at, sources):
        loads = []
        for k, source in enumerate(sources):
            load = pltpu.make_async_copy(
                source,
                grad_places(name)[turn_at][k],
                DR.at[S.ld + 4 * name + 2 * turn_at + k],
            )
            load.start()
            loads.append(load)
        return loads

    def grad_mid(name):
        loads = []
        for cc in range(2):
            arrived(R.px[name].at[cc], S.px + 4 * name + cc)
            loads.append(
                grad_loads(name, cc, (R.px[name].at[cc], R.stage[name].at[2 * y + cc]))
            )
        for cc in range(2):
            for load in loads[cc]:
                load.wait()
            into = sum_room(name, cc)
            add_rows(into, *grad_places(name)[cc])
            at = S.pc + 4 * name + cc

            @pl.when(jnp.logical_not(keeper))
            def _():
                send(
                    into, R.other[name], at, S.py + name, (2 * y + cc, 2 * z + 1 - x)
                ).start()

            @pl.when(keeper & (c == cc))
            def _():
                pltpu.make_async_copy(into, R.mine[name], DR.at[S.st + name]).start()

            @pl.when(keeper & (c != cc))
            def _():
                send(into, R.mine[name], at, S.st + name, sibling).start()

    def grad_add(name):
        loads = []
        for turn_at, yy in enumerate((1 - y, y)):
            arrived(R.px[name].at[yy], S.px + 4 * name + yy)
            arrived(R.pc[name].at[yy], S.pc + 4 * name + yy)
            loads.append(grad_loads(name, turn_at, (R.px[name].at[yy], R.pc[name].at[yy])))
        for turn_at in range(2):
            for load in loads[turn_at]:
                load.wait()
            one, two = grad_places(name)[turn_at]
            if turn_at == 0:
                into = sum_room(name)
                add_rows(into, one, two)
                send(into, R.other[name], S.py + name, S.py + name, across_y).start()
            else:
                add_rows(one, one, two)
                store = pltpu.make_async_copy(one, R.mine[name], DR.at[S.st + name])
                store.start()
                store.wait()

    R.own_len[...] = jnp.zeros((8, 128), F32)
    for p in range(pieces):
        R.own_len[p : p + 1, :] = jnp.broadcast_to(R.lengths[0:1, p : p + 1].astype(F32), (1, 128))
    swap_start(LEN, R.own_len, R.len)
    for part in range(2):
        swap_start(TOK + part, part_at(R.tokens, part), part_at(R.tok, part))
    weight_start(WQ, R.w_query, R.wq)
    swap_start(OG, R.out_grad, R.og)
    swap_start(KVG, R.kv_grad, R.kvg)

    def norm_rows(first, count):
        at = pl.ds(first, count)
        value = R.tok[at, :].astype(F32)
        inverse = lax.rsqrt(jnp.mean(value * value, axis=1, keepdims=True) + EPSILON)
        R.norm[pl.ds(own_at + first, count), :] = (
            value * inverse * R.gain_attn[0:1, :]
        ).astype(BF16)

    for part in range(2):
        swap_wait(TOK + part, part_at(R.tok, part))
        each_rows(norm_rows, part)
        gather_start(GN, R.norm, (part,))
    swap_wait(LEN, R.len)
    weight_start(WO, R.w_attn_out, R.wo)
    rotary()
    weight_pass(WQ, R.wq)
    weight_wait(WQ, R.wq)
    gather_own(GN, R.norm, project)

    def mask_rows(first, count):
        at = pl.ds(first, count)
        R.gmlp[pl.ds(own_at + first, count), :] = (
            keep_of(first, count) * R.og[at, :].astype(F32)
        ).astype(BF16)

    for step in range(nz - 1):
        gather_pass(GN, R.norm, step)
        if step == 0:
            weight_pass(WO, R.wo)
            weight_start(WG, R.w_gate, R.wg)
            swap_wait(OG, R.og)
            swap_wait(KVG, R.kvg)
            for part in range(2):
                each_rows(mask_rows, part)
        if step == 1:
            weight_start(WU, R.w_up, R.wu)
        if step == nz - 2:
            gather_start(GG, R.gmlp)
            weight_pass(WG, R.wg)
            weight_start(WD, R.w_down, R.wd)
        gather_use(GN, R.norm, step, project)
    spill = pltpu.make_async_copy(R.norm, R.norm_store, DR.at[S.spill])
    spill.start()
    weight_wait(WO, R.wo)

    for step in range(nz - 1):
        scatter_step(RO, step, out_term)
        gather_pass(GG, R.gmlp, step)
        if step == 0:
            weight_pass(WU, R.wu)
        if step == 1:
            weight_pass(WD, R.wd)
    scatter_term(RO, z, out_term)

    def mid_rows(first, count):
        at = pl.ds(first, count)
        mid = R.tok[at, :].astype(F32) + R.acc[at, :]
        R.mid[at, :] = mid
        inverse = lax.rsqrt(jnp.mean(mid * mid, axis=1, keepdims=True) + EPSILON)
        R.nmlp[pl.ds(own_at + first, count), :] = (
            mid * inverse * R.gain_mlp[0:1, :]
        ).astype(BF16)

    def mid_done(part):
        each_rows(mid_rows, part)
        gather_start(GM, R.nmlp, (part,))

    scatter_end(RO, mid_done)
    for step in range(nz - 1):
        gather_use(GG, R.gmlp, step, None)
    gather_own(GG, R.gmlp, None)
    scatter_sent(RO)
    gather_end(GN, R.norm)
    spill.wait()
    weight_wait(WG, R.wg)
    weight_wait(WU, R.wu)
    weight_wait(WD, R.wd)
    def mlp_and_back(chunk):
        mlp(chunk)
        scatter_term(RB, chunk, back_term)

    gather_own(GM, R.nmlp, mlp_and_back)
    for step in range(nz - 1):
        gather_pass(GM, R.nmlp, step)
        gather_use(GM, R.nmlp, step, mlp_and_back)

        @pl.when(z == 0)
        def _():
            scatter_forward(RB, 0, step + 1)

        @pl.when(z == nz - 1)
        def _():
            scatter_forward(RB, 1, nz - 2 - step)

    for item, src, dst in (
        (WQ, R.w_query, R.wq),
        (WO, R.w_attn_out, R.wo),
        (WG, R.w_gate, R.wg),
        (WU, R.w_up, R.wu),
        (WD, R.w_down, R.wd),
    ):
        weight_sent(item, src, dst)

    mlp_grads = ((DOWN, R.hid, R.gmlp), (GATE, R.dgate, R.nmlp), (UP, R.dup, R.nmlp))
    for index in range(nz - 1):
        if index < 2:
            grad_make(*mlp_grads[index])
        way, chunk, valid = between(index)

        @pl.when(valid)
        def _():
            scatter_forward(RB, way, chunk)

    grad_make(*mlp_grads[2])
    R.gains[...] = jnp.zeros(R.gains.shape, F32)

    def fold(value):
        return jnp.sum(value.reshape(value.shape[0] // 8, 8, value.shape[1]), axis=0)

    def d_mid_rows(first, count):
        at = pl.ds(first, count)
        mid = R.mid[at, :]
        inverse = lax.rsqrt(jnp.mean(mid * mid, axis=1, keepdims=True) + EPSILON)
        unit = mid * inverse
        back = R.acc[at, :]
        R.gains[1] += fold(back * unit)
        e = back * R.gain_mlp[0:1, :]
        grad = keep_of(first, count) * R.og[at, :].astype(F32) + inverse * (
            e - unit * jnp.mean(e * unit, axis=1, keepdims=True)
        )
        R.dmid[at, :] = grad
        R.norm[pl.ds(own_at + first, count), :] = grad.astype(BF16)

    def d_mid_done(part):
        each_rows(d_mid_rows, part)
        gather_start(GA, R.norm, (part,))

    scatter_end(RB, d_mid_done)
    scatter_sent(RB)
    gather_end(GG, R.gmlp)
    gather_end(GM, R.nmlp)
    back_norm = pltpu.make_async_copy(R.norm_store, R.gmlp, DR.at[S.spill + 1])
    back_norm.start()
    R.dkv[...] = jnp.zeros(R.dkv.shape, F32)
    gather_own(GA, R.norm, d_attended)
    for step in range(nz - 1):
        gather_pass(GA, R.norm, step)
        scatter_step(RD, step, down_term)
        gather_use(GA, R.norm, step, d_attended)
        if step == 1:
            grad_add(DOWN)
    scatter_term(RD, z, down_term)

    R.dkvb[...] = R.dkv[...].astype(BF16)
    for zz in range(nz):
        send(piece(R.dkvb, zz, 1 - c), R.kc.at[zz], S.kc + zz, S.kc + zz, sibling).start()

    def kv_over_z():
        for zz in range(nz):
            arrived(R.kc.at[zz], S.kc + zz)
            R.ks[zz] = (
                R.dkv[pl.ds(pl.multiple_of((2 * zz + c) * rows, rows), rows), :]
                + R.kc[zz].astype(F32)
            ).astype(BF16)

            @pl.when(zz != z)
            def _():
                send(R.ks.at[zz], R.kz.at[z], S.kz + zz, S.kz + z, dev(y, c, zz, x)).start()

    own_rows = pl.ds(own_at, rows)
    own_kv = piece(R.dkva, z, c)

    def kv_own():
        R.kacc[...] = keep_of(0, rows) * R.kvg[...].astype(F32) + R.ks[z].astype(F32)
        for zz in range(nz):

            @pl.when(zz != z)
            def _():
                arrived(R.kz.at[zz], S.kz + zz)
                R.kacc[...] += R.kz[zz].astype(F32)

        R.dkva[own_rows, :head] = turn(
            R.kacc[:, :head], R.cos[own_rows, :], -R.sin[own_rows, :]
        ).astype(BF16)
        R.dkva[own_rows, head:] = R.kacc[:, head:].astype(BF16)
        for zz in range(nz):
            for cc in range(2):

                @pl.when((zz != z) | (cc != c))
                def _():
                    send(
                        own_kv, own_kv, S.ka + 2 * zz + cc, S.ka + 2 * z + c, dev(y, cc, zz, x)
                    ).start()

    def out_rows(first, count):
        at = pl.ds(first, count)
        R.bo[at, :] = (keep_of(first, count) * (R.mid[at, :] + R.acc[at, :])).astype(BF16)

    back_norm.wait()
    for step in range(nz - 1):
        scatter_step(RQ, step, query_term)
        if step == 0:
            scatter_end(RD, lambda part: each_rows(out_rows, part))
            swap_start(BO, R.bo, R.block_out)
            kv_over_z()
            grad_make(OUT, R.att, R.norm)
            grad_mid(GATE)
        if step == 1:
            kv_own()
            grad_make(QUERY, R.gmlp, R.dq)
            grad_add(UP)
    scatter_term(RQ, z, query_term)
    for zz in range(nz):
        for cc in range(2):

            @pl.when((zz != z) | (cc != c))
            def _():
                arrived(piece(R.dkva, zz, cc), S.ka + 2 * zz + cc)

    first_col = c * (4 * nz * 32) + z * 128
    for yy in range(2):
        cols = pl.ds(pl.multiple_of(yy * (width // 2) + first_col, 128), 128)
        R.gkv[yy] = dot_cols(R.gmlp[:, cols], R.dkva[...])
    send(
        R.gkv.at[1 - y], R.kyb, S.kyx, S.kyx, across_y
    ).start()
    arrived(R.kyb, S.kyx)
    R.kysum[...] = R.gkv[y] + R.kyb[...]
    send(
        R.kysum.at[pl.ds(pl.multiple_of((1 - x) * 64, 64), 64)],
        R.kxb,
        S.kyx + 1,
        S.kyx + 1,
        across_x,
    ).start()
    arrived(R.kxb, S.kyx + 1)
    R.kfinal[...] = (
        R.kysum[pl.ds(pl.multiple_of(x * 64, 64), 64), :] + R.kxb[...]
    )
    kv_out = pltpu.make_async_copy(R.kfinal, R.grad_w_kv, DR.at[S.outs])
    kv_out.start()
    for n, size in tiles(width, 512):
        some = slice(n, n + size)
        R.mid[:, some] = dot_rows(R.dkva[own_rows, :], R.wkv[some, :])
    grad_mid(OUT)

    def tail_rows(first, count):
        at = pl.ds(first, count)
        value = R.tok[at, :].astype(F32)
        inverse = lax.rsqrt(jnp.mean(value * value, axis=1, keepdims=True) + EPSILON)
        unit = value * inverse
        back = R.acc[at, :] + R.mid[at, :]
        R.gains[0] += fold(back * unit)
        e = back * R.gain_attn[0:1, :]
        R.gt[at, :] = (
            R.dmid[at, :]
            + inverse * (e - unit * jnp.mean(e * unit, axis=1, keepdims=True))
        ).astype(BF16)

    def tail_done(part):
        each_rows(tail_rows, part)
        swap_start(GT + part, part_at(R.gt, part), part_at(R.grad_tokens, part))

    scatter_end(RQ, tail_done)

    line = lax.broadcasted_iota(jnp.int32, (8, width), 0)
    gain_first = jnp.sum(R.gains[0], axis=0, keepdims=True)
    gain_second = jnp.sum(R.gains[1], axis=0, keepdims=True)
    R.ga[...] = jnp.where(line == 0, gain_first, jnp.where(line == 1, gain_second, 0.0))
    span = width // 4

    def gain_cols(yy, cc):
        return pl.ds(pl.multiple_of((2 * yy + cc) * span, span), span)

    def gain_send(index, offset):
        dy, dc, dx = offset
        return send(
            R.ga.at[:, gain_cols(flip(y, dy), flip(c, dc))],
            R.gb.at[index],
            S.gains + index,
            S.gains + index,
            around[offset],
        )

    for index, offset in enumerate(around):
        gain_send(index, offset).start()
    R.ga_x[...] = R.ga[:, gain_cols(y, c)]
    for index in range(len(around)):
        arrived(R.gb.at[index], S.gains + index)
        R.ga_x[...] += R.gb[index]
    for zz in range(nz):

        @pl.when(zz != z)
        def _():
            send(
                R.ga_x.at[:, zz * 128 : (zz + 1) * 128],
                R.gb_z.at[z],
                S.gains + 8 + zz,
                S.gains + 8 + z,
                dev(y, c, zz, x),
            ).start()

    R.gfinal[...] = R.ga_x[:, pl.ds(pl.multiple_of(z * 128, 128), 128)]
    for zz in range(nz):

        @pl.when(zz != z)
        def _():
            arrived(R.gb_z.at[zz], S.gains + 8 + zz)
            R.gfinal[...] += R.gb_z[zz]

    gain_out = pltpu.make_async_copy(R.gfinal, R.grad_gains, DR.at[S.outs + 1])
    gain_out.start()

    grad_add(QUERY)
    for name in GRADS:
        arrived(R.other[name], S.py + name)
        if name in Y_FIRST:
            arrived(R.mine[name], S.st + name)
            for cc in range(2):

                @pl.when(jnp.logical_not(keeper & (c == cc)))
                def _():
                    sent(sum_room(name, cc), S.pc + 4 * name + cc)
        else:
            sent(sum_room(name), S.py + name)
        for yy, cc in QUARTERS:
            grad_sent(name, yy, cc)
    kv_out.wait()
    gain_out.wait()
    scatter_sent(RD)
    scatter_sent(RQ)
    gather_end(GA, R.norm)
    swap_wait(BO, R.block_out)
    for part in range(2):
        swap_wait(GT + part, part_at(R.grad_tokens, part))
    for item, src in (
        (LEN, R.own_len),
        (TOK, part_at(R.tokens, 0)),
        (TOK2, part_at(R.tokens, 1)),
        (OG, R.out_grad),
        (KVG, R.kv_grad),
        (BO, R.bo),
        (GT, part_at(R.gt, 0)),
        (GT2, part_at(R.gt, 1)),
    ):
        swap_sent(item, src)
    for zz in range(nz):
        sent(piece(R.dkvb, zz, 1 - c), S.kc + zz)

        @pl.when(zz != z)
        def _():
            sent(R.ks.at[zz], S.kz + zz)
            sent(R.ga_x.at[:, zz * 128 : (zz + 1) * 128], S.gains + 8 + zz)

        for cc in range(2):

            @pl.when((zz != z) | (cc != c))
            def _():
                sent(own_kv, S.ka + 2 * zz + cc)

    sent(R.gkv.at[1 - y], S.kyx)
    sent(R.kysum.at[pl.ds(pl.multiple_of((1 - x) * 64, 64), 64)], S.kyx + 1)
    for index, offset in enumerate(around):
        gain_send(index, offset).wait_send()


def fused(nz, *args):
    (tokens, lengths, gain_attn, w_query, w_kv, w_attn_out, gain_mlp, w_gate, w_up, w_down,
     out_grad, kv_grad) = args
    rows, width = tokens.shape
    ff = w_gate.shape[1]
    qw = w_query.shape[1]
    total, pair = 2 * nz * rows, 2 * rows
    pieces = lengths.shape[1]
    head = w_kv.shape[1] // 2
    half_width = head // 2
    freqs = (ROTARY_BASE ** (-np.arange(half_width, dtype=np.float32) / half_width)).astype(np.float32)
    freq = np.tile(np.concatenate([freqs, freqs])[None, :], (8, 1))
    anywhere, vmem = pl.BlockSpec(memory_space=pl.ANY), pl.BlockSpec(memory_space=pltpu.VMEM)
    ins = dict(
        tokens=(tokens, anywhere),
        lengths=(lengths, vmem),
        freq=(freq, vmem),
        gain_attn=(gain_attn[None], vmem),
        gain_mlp=(gain_mlp[None], vmem),
        w_query=(w_query, anywhere),
        wkv=(w_kv, vmem),
        w_attn_out=(w_attn_out, anywhere),
        w_gate=(w_gate.T, anywhere),
        w_up=(w_up.T, anywhere),
        w_down=(w_down, anywhere),
        out_grad=(out_grad, anywhere),
        kv_grad=(kv_grad, anywhere),
    )
    quarter = width // 4
    grad_tiles = [(ff, quarter), (ff, quarter), (ff, quarter), (qw, quarter), (quarter, qw)]
    outs = dict(
        block_out=((rows, width), BF16),
        grad_tokens=((rows, width), BF16),
        grad_w_kv=((64, 2 * head), F32),
        grad_gains=((8, 128), F32),
        norm_store=((total, width), BF16),
    )
    moved = [
        (shape, BF16)
        for tile in grad_tiles
        for shape in (tile, tile, (4,) + tile, (2,) + tile, (2,) + tile)
    ]
    S, count = semaphores(nz)
    scratch = dict(
        own_len=((8, 128), F32),
        len=((8, 128), F32),
        last=((8, 128), F32),
        tok=((rows, width), BF16),
        og=((rows, width), BF16),
        kvg=((rows, 2 * head), BF16),
        wq=((width, qw), BF16),
        wo=((qw, width), BF16),
        wg=((ff, width), BF16),
        wu=((ff, width), BF16),
        wd=((ff, width), BF16),
        norm=((total, width), BF16),
        nmlp=((total, width), BF16),
        gmlp=((total, width), BF16),
        cos=((total, 128), F32),
        sin=((total, 128), F32),
        start=((total, 128), F32),
        q=((total, qw), BF16),
        kv=((total, 2 * head), BF16),
        att=((total, qw), BF16),
        datt=((total, qw), BF16),
        dq=((total, qw), BF16),
        probs=((qw // head, total, total), BF16),
        hid=((total, ff), BF16),
        dgate=((total, ff), BF16),
        dup=((total, ff), BF16),
        part=((total, width), BF16),
        from_core=((nz * rows, width), BF16),
        from_z=((2, nz + 1, rows, width), BF16),
        acc=((rows, width), F32),
        mid=((rows, width), F32),
        dmid=((rows, width), F32),
        bo=((rows, width), BF16),
        gt=((rows, width), BF16),
        gains=((2, 8, width), F32),
        ga=((8, width), F32),
        ga_x=((8, width // 4), F32),
        gb=((7, 8, width // 4), F32),
        gb_z=((nz, 8, 128), F32),
        gfinal=((8, 128), F32),
        dkv=((total, 2 * head), F32),
        dkvb=((total, 2 * head), BF16),
        dkva=((total, 2 * head), BF16),
        kc=((nz, rows, 2 * head), BF16),
        ks=((nz, rows, 2 * head), BF16),
        kz=((nz, rows, 2 * head), BF16),
        kacc=((rows, 2 * head), F32),
        gkv=((2, 128, 2 * head), F32),
        kyb=((128, 2 * head), F32),
        kysum=((128, 2 * head), F32),
        kxb=((64, 2 * head), F32),
        kfinal=((64, 2 * head), F32),
    )
    tile_shapes = (grad_tiles[DOWN], grad_tiles[OUT], grad_tiles[QUERY])
    out_shapes = list(outs.values()) + moved
    scratch_shapes = list(scratch.values()) + [((2,) + shape, BF16) for shape in tile_shapes]

    def body(*refs):
        refs = list(refs)

        def take(count):
            taken = refs[:count]
            del refs[:count]
            return taken

        R = types.SimpleNamespace(
            **dict(zip(ins, take(len(ins)))), **dict(zip(outs, take(len(outs))))
        )
        rest = take(len(moved))
        R.mine, R.other, R.stage, R.px, R.pc = (rest[k::5] for k in range(5))
        for key, ref in zip(scratch, take(len(scratch))):
            setattr(R, key, ref)
        big, out_tile, query_tile = take(3)
        R.tile = [big, big, big, out_tile, query_tile]
        R.send, R.recv = refs
        block_kernel(nz, pieces, S, R)

    results = pl.pallas_call(
        body,
        out_shape=[jax.ShapeDtypeStruct(shape, kind) for shape, kind in out_shapes],
        in_specs=[spec for _, spec in ins.values()],
        out_specs=[anywhere] * len(out_shapes),
        scratch_shapes=[pltpu.VMEM(shape, kind) for shape, kind in scratch_shapes]
        + [pltpu.SemaphoreType.DMA((count,))] * 2,
        compiler_params=pltpu.CompilerParams(
            collective_id=0, has_side_effects=True, vmem_limit_bytes=63 * MIB
        ),
        name="block",
    )(*[value for value, _ in ins.values()])
    first = list(results[:4])
    mine, other = list(results[5::5]), list(results[6::5])

    def finish(*refs):
        ends, refs = refs[:4], refs[4:]
        one, two, refs = refs[:5], refs[5:10], refs[10:]
        for k in range(3):
            refs[k][...] = ends[k][...]
        right = (lax.axis_index("tensor") % 2) == 1
        refs[3][...] = jnp.where(right, ends[3][:, 64:], ends[3][:, :64])
        for k in GRADS:
            refs[4 + k][...] = one[k][...].astype(F32) + two[k][...].astype(F32)

    cuts = 4

    def cut(array):
        count = array.shape[0] // cuts
        return pl.BlockSpec((count, array.shape[1]), lambda i: (i, 0))

    whole = pl.BlockSpec((8, 128), lambda i: (0, 0))
    block_out, grad_tokens, grad_w_kv, gains, *sums = pl.pallas_call(
        finish,
        grid=(cuts,),
        out_shape=[jax.ShapeDtypeStruct(array.shape, array.dtype) for array in first[:3]]
        + [jax.ShapeDtypeStruct((8, 64), F32)]
        + [jax.ShapeDtypeStruct(array.shape, F32) for array in mine],
        in_specs=[cut(array) for array in first[:3]] + [whole] + [cut(a) for a in mine + other],
        out_specs=[cut(array) for array in first[:3]]
        + [pl.BlockSpec((8, 64), lambda i: (0, 0))]
        + [cut(array) for array in mine],
        compiler_params=pltpu.CompilerParams(vmem_limit_bytes=63 * MIB),
        name="finish",
    )(*first, *mine, *other)
    return (
        block_out,
        grad_tokens,
        gains[0],
        sums[QUERY],
        grad_w_kv,
        sums[OUT],
        gains[1],
        sums[GATE].T,
        sums[UP].T,
        sums[DOWN],
    )


def solution(mesh):
    groups, parts = mesh.shape["dp"], mesh.shape["tensor"]
    paired = groups == 4 and parts == 8
    per_group = functools.partial(fused, parts // 2) if paired else per_device
    placed = (
        P(("dp", "tensor"), None),
        P("dp", None),
        P(),
        P(None, "tensor"),
        P(),
        P("tensor", None),
        P(),
        P(None, "tensor"),
        P(None, "tensor"),
        P("tensor", None),
        P(("dp", "tensor"), None),
        P(("dp", "tensor"), None),
    )
    return jax.shard_map(
        per_group,
        mesh=mesh,
        in_specs=placed,
        out_specs=(
            P(("dp", "tensor"), None),
            P(("dp", "tensor"), None),
            P(("dp", "tensor")),
            P("dp", "tensor"),
            P(("dp", "tensor"), None),
            P("tensor", "dp"),
            P(("dp", "tensor")),
            P("dp", "tensor"),
            P("dp", "tensor"),
            P("tensor", "dp"),
        ),
        check_vma=False,
    )
```

```python
import functools
import types

import jax
import jax.numpy as jnp
import numpy as np
from jax import lax
from jax.experimental import pallas as pl
from jax.experimental.pallas import tpu as pltpu
from jax.sharding import PartitionSpec as P

SPAN = 64


EPSILON = 1e-05
ROTARY_BASE = 10000.0
MASKED = -1e30


def rotary_tables(positions, width):
    half_width = width // 2
    freqs = ROTARY_BASE ** (-jnp.arange(half_width, dtype=jnp.float32) / half_width)
    angles = positions[:, None] * freqs[None, :]
    return (jnp.cos(angles), jnp.sin(angles))


def rotate(values, cosine, sine):
    half_width = values.shape[-1] // 2
    first_half = values[..., :half_width]
    second_half = values[..., half_width:]
    return jnp.concatenate(
        [first_half * cosine - second_half * sine, second_half * cosine + first_half * sine],
        axis=-1,
    )


def unrotate(values, cosine, sine):
    half_width = values.shape[-1] // 2
    first_half = values[..., :half_width]
    second_half = values[..., half_width:]
    return jnp.concatenate(
        [first_half * cosine + second_half * sine, second_half * cosine - first_half * sine],
        axis=-1,
    )


def layout(piece_units, rows):
    piece_rows = piece_units * SPAN
    ends = jnp.cumsum(piece_rows)
    starts = ends - piece_rows
    row_steps = jnp.arange(rows, dtype=jnp.int32)
    segment = jnp.sum((row_steps[:, None] >= ends[None, :]).astype(jnp.int32), axis=1)
    member = segment[:, None] == jnp.arange(piece_units.shape[0], dtype=jnp.int32)[None, :]
    row_start = jnp.sum(jnp.where(member, starts[None, :], 0), axis=1)
    positions = (row_steps - row_start).astype(jnp.float32)
    keep = (segment < piece_units.shape[0] - 1).astype(jnp.float32)
    return (segment, row_steps, positions, keep)


def permitted(block_segment, block_steps, segment, row_steps):
    return (block_segment[:, None] == segment[None, :]) & (
        row_steps[None, :] <= block_steps[:, None]
    )


def spread_rows(values):
    return lax.all_gather(values, "tensor", axis=0, tiled=True)


def spread_grads(values):
    return lax.all_gather(values, "tensor", axis=0, tiled=True)


def per_device(
    tokens,
    lengths,
    gain_attn,
    w_query,
    w_kv,
    w_attn_out,
    gain_mlp,
    w_gate,
    w_up,
    w_down,
    out_grad,
    kv_grad,
):
    local_rows = tokens.shape[0]
    parts = lax.axis_size("tensor")
    total_rows = local_rows * parts
    first_row = lax.axis_index("tensor") * local_rows
    segment, row_steps, positions, keep = layout(lengths[0], total_rows)
    head_dim = w_kv.shape[1] // 2
    local_heads = w_query.shape[1] // head_dim
    scale = head_dim ** (-0.5)
    cosine, sine = rotary_tables(positions, head_dim)
    row_keep = lax.dynamic_slice_in_dim(keep, first_row, local_rows, 0)[:, None]
    row_cosine = lax.dynamic_slice_in_dim(cosine, first_row, local_rows, 0)
    row_sine = lax.dynamic_slice_in_dim(sine, first_row, local_rows, 0)
    tokens_full = tokens.astype(jnp.float32)
    inv_first = lax.rsqrt(jnp.mean(tokens_full * tokens_full, axis=-1, keepdims=True) + EPSILON)
    unit_first = tokens_full * inv_first
    normed_rows = (unit_first * gain_attn).astype(jnp.bfloat16)
    normed = spread_rows(normed_rows)
    queries = jnp.dot(normed, w_query, preferred_element_type=jnp.float32).reshape(
        total_rows, local_heads, head_dim
    )
    queries = rotate(queries, cosine[:, None, :], sine[:, None, :]).astype(jnp.bfloat16)
    kv_raw = jnp.dot(normed, w_kv, preferred_element_type=jnp.float32)
    shared = jnp.concatenate(
        [rotate(kv_raw[:, :head_dim], cosine, sine), kv_raw[:, head_dim:]], axis=1
    ).astype(jnp.bfloat16)
    keys = shared[:, :head_dim]
    values = shared[:, head_dim:]
    block = min(512, total_rows)
    count = total_rows // block
    pieces = []
    log_totals = []
    for number in range(count):
        begin = number * block
        query_block = queries[begin : begin + block]
        allowed = permitted(
            segment[begin : begin + block], row_steps[begin : begin + block], segment, row_steps
        )
        scores = (
            jnp.einsum("qhd,kd->hqk", query_block, keys, preferred_element_type=jnp.float32) * scale
        )
        scores = jnp.where(allowed[None], scores, MASKED)
        row_max = jnp.max(scores, axis=-1, keepdims=True)
        exp_scores = jnp.exp(scores - row_max)
        row_total = jnp.sum(exp_scores, axis=-1, keepdims=True)
        log_totals.append(row_max + jnp.log(row_total))
        weights = (exp_scores / row_total).astype(jnp.bfloat16)
        pieces.append(
            jnp.einsum("hqk,kd->qhd", weights, values, preferred_element_type=jnp.float32).astype(
                jnp.bfloat16
            )
        )
    attended = jnp.concatenate(pieces, axis=0).reshape(total_rows, local_heads * head_dim)
    attn_rows = lax.psum_scatter(
        jnp.dot(attended, w_attn_out, preferred_element_type=jnp.float32).astype(jnp.bfloat16),
        "tensor",
        scatter_dimension=0,
        tiled=True,
    ).astype(jnp.float32)
    mid = tokens_full + attn_rows
    inv_second = lax.rsqrt(jnp.mean(mid * mid, axis=-1, keepdims=True) + EPSILON)
    unit_second = mid * inv_second
    normed_mlp = spread_rows((unit_second * gain_mlp).astype(jnp.bfloat16))
    gate = jnp.dot(normed_mlp, w_gate, preferred_element_type=jnp.float32)
    up = jnp.dot(normed_mlp, w_up, preferred_element_type=jnp.float32)
    sigma = jax.nn.sigmoid(gate)
    active = gate * sigma
    hidden = (active * up).astype(jnp.bfloat16)
    mlp_rows = lax.psum_scatter(
        jnp.dot(hidden, w_down, preferred_element_type=jnp.float32).astype(jnp.bfloat16),
        "tensor",
        scatter_dimension=0,
        tiled=True,
    ).astype(jnp.float32)
    block_out = (row_keep * (mid + mlp_rows)).astype(jnp.bfloat16)
    out_full = row_keep * out_grad.astype(jnp.float32)
    grad_mlp = spread_grads(out_full.astype(jnp.bfloat16))
    g_down = jnp.einsum("rf,rd->fd", hidden, grad_mlp, preferred_element_type=jnp.float32)
    g_hidden = jnp.einsum("rd,fd->rf", grad_mlp, w_down, preferred_element_type=jnp.float32)
    d_gate = (g_hidden * up * sigma * (1.0 + gate * (1.0 - sigma))).astype(jnp.bfloat16)
    d_up = (g_hidden * active).astype(jnp.bfloat16)
    g_gate = jnp.einsum("rd,rf->df", normed_mlp, d_gate, preferred_element_type=jnp.float32)
    g_up = jnp.einsum("rd,rf->df", normed_mlp, d_up, preferred_element_type=jnp.float32)
    back_mlp = lax.psum_scatter(
        (
            jnp.einsum("rf,df->rd", d_gate, w_gate, preferred_element_type=jnp.float32)
            + jnp.einsum("rf,df->rd", d_up, w_up, preferred_element_type=jnp.float32)
        ).astype(jnp.bfloat16),
        "tensor",
        scatter_dimension=0,
        tiled=True,
    ).astype(jnp.float32)
    e_mlp = back_mlp * gain_mlp
    g_gain_mlp = jnp.sum(back_mlp * unit_second, axis=0)
    d_mid = out_full + inv_second * (
        e_mlp - unit_second * jnp.mean(e_mlp * unit_second, axis=-1, keepdims=True)
    )
    grad_attn = spread_grads(d_mid.astype(jnp.bfloat16))
    g_attn_out = jnp.einsum("rh,rd->hd", attended, grad_attn, preferred_element_type=jnp.float32)
    d_att = jnp.einsum(
        "rd,hd->rh", grad_attn, w_attn_out, preferred_element_type=jnp.float32
    ).astype(jnp.bfloat16)
    d_att = d_att.reshape(total_rows, local_heads, head_dim)
    query_pieces = []
    d_keys = jnp.zeros((total_rows, head_dim), jnp.float32)
    d_values = jnp.zeros((total_rows, head_dim), jnp.float32)
    for number in range(count):
        begin = number * block
        query_block = queries[begin : begin + block]
        grad_block = d_att[begin : begin + block]
        allowed = permitted(
            segment[begin : begin + block], row_steps[begin : begin + block], segment, row_steps
        )
        scores = (
            jnp.einsum("qhd,kd->hqk", query_block, keys, preferred_element_type=jnp.float32) * scale
        )
        scores = jnp.where(allowed[None], scores, MASKED)
        probs = jnp.exp(scores - log_totals[number])
        weights = probs.astype(jnp.bfloat16)
        d_probs = jnp.einsum("qhd,kd->hqk", grad_block, values, preferred_element_type=jnp.float32)
        inner = jnp.sum(d_probs * probs, axis=-1, keepdims=True)
        d_scores = (probs * (d_probs - inner)).astype(jnp.bfloat16)
        query_pieces.append(
            jnp.einsum("hqk,kd->qhd", d_scores, keys, preferred_element_type=jnp.float32) * scale
        )
        d_keys = (
            d_keys
            + jnp.einsum("hqk,qhd->kd", d_scores, query_block, preferred_element_type=jnp.float32)
            * scale
        )
        d_values = d_values + jnp.einsum(
            "hqk,qhd->kd", weights, grad_block, preferred_element_type=jnp.float32
        )
    d_queries = jnp.concatenate(query_pieces, axis=0)
    d_queries = unrotate(d_queries, cosine[:, None, :], sine[:, None, :]).astype(jnp.bfloat16)
    d_queries = d_queries.reshape(total_rows, local_heads * head_dim)
    g_query = jnp.einsum("rd,rh->dh", normed, d_queries, preferred_element_type=jnp.float32)
    kv_rows = lax.psum_scatter(
        jnp.concatenate([d_keys, d_values], axis=1).astype(jnp.bfloat16),
        "tensor",
        scatter_dimension=0,
        tiled=True,
    ).astype(jnp.float32)
    kv_rows = kv_rows + row_keep * kv_grad.astype(jnp.float32)
    d_kv = jnp.concatenate(
        [unrotate(kv_rows[:, :head_dim], row_cosine, row_sine), kv_rows[:, head_dim:]], axis=1
    ).astype(jnp.bfloat16)
    d_kv_all = lax.all_gather(d_kv, "tensor", axis=0, tiled=True)
    width = normed.shape[1]
    groups = lax.axis_size("dp")
    own = lax.dynamic_index_in_dim(
        normed.reshape(total_rows, groups, parts, width // (groups * parts)),
        lax.axis_index("tensor"),
        2,
        False,
    ).reshape(total_rows, width // parts)
    g_kv = jnp.einsum("rd,rk->dk", own, d_kv_all, preferred_element_type=jnp.float32)
    back_attn = lax.psum_scatter(
        jnp.einsum("rh,dh->rd", d_queries, w_query, preferred_element_type=jnp.float32).astype(
            jnp.bfloat16
        ),
        "tensor",
        scatter_dimension=0,
        tiled=True,
    ).astype(jnp.float32)
    back_attn = back_attn + jnp.einsum("rk,dk->rd", d_kv, w_kv, preferred_element_type=jnp.float32)
    e_attn = back_attn * gain_attn
    g_gain_attn = jnp.sum(back_attn * unit_first, axis=0)
    grad_tokens = (
        d_mid
        + inv_first * (e_attn - unit_first * jnp.mean(e_attn * unit_first, axis=-1, keepdims=True))
    ).astype(jnp.bfloat16)
    kv_sum = lax.psum_scatter(g_kv, "dp", scatter_dimension=0, tiled=True)
    share = width // (groups * parts)
    first = (lax.axis_index("dp") * parts + lax.axis_index("tensor")) * share
    gain_all = lax.all_gather(jnp.stack([g_gain_attn, g_gain_mlp]), ("dp", "tensor"), axis=0)
    gain_sums = jnp.sum(lax.dynamic_slice_in_dim(gain_all, first, share, 2), axis=0)
    query_sum, out_sum, gate_sum, up_sum, down_sum = (
        lax.psum_scatter(
            g_query.astype(jnp.bfloat16), "dp", scatter_dimension=0, tiled=True
        ).astype(jnp.float32),
        lax.psum_scatter(
            g_attn_out.astype(jnp.bfloat16), "dp", scatter_dimension=1, tiled=True
        ).astype(jnp.float32),
        lax.psum_scatter(g_gate.astype(jnp.bfloat16), "dp", scatter_dimension=0, tiled=True).astype(
            jnp.float32
        ),
        lax.psum_scatter(g_up.astype(jnp.bfloat16), "dp", scatter_dimension=0, tiled=True).astype(
            jnp.float32
        ),
        lax.psum_scatter(g_down.astype(jnp.bfloat16), "dp", scatter_dimension=1, tiled=True).astype(
            jnp.float32
        ),
    )
    return (
        block_out,
        grad_tokens,
        gain_sums[0],
        query_sum,
        kv_sum,
        out_sum,
        gain_sums[1],
        gate_sum,
        up_sum,
        down_sum,
    )


F32, BF16 = jnp.float32, jnp.bfloat16
MESH = pl.DeviceIdType.MESH
MIB = 1 << 20


def dot(a, b):
    return jnp.dot(a, b, preferred_element_type=F32)


def dot_rows(a, b):
    return lax.dot_general(a, b, (((1,), (1,)), ((), ())), preferred_element_type=F32)


def dot_cols(a, b):
    return lax.dot_general(a, b, (((0,), (0,)), ((), ())), preferred_element_type=F32)


def tiles(width, step):
    return [(at, min(step, width - at)) for at in range(0, width, step)]


GN, GG, GM, GA = range(4)
RO, RB, RD, RQ = range(4)
LEN, TOK, TOK2, WQ, OG, KVG, WO, WG, WU, WD, BO, GT, GT2 = range(13)
DOWN, GATE, UP, OUT, QUERY = GRADS = range(5)


def semaphores(nz):
    counts = dict(
        swap=13,
        swap_y=13,
        gz=4 * 4 * nz,
        gc=4 * 2 * nz,
        rz=4 * 4 * nz,
        rc=4 * nz,
        stage=20,
        px=20,
        pc=20,
        py=5,
        ld=20,
        st=5,
        kc=nz,
        kz=nz,
        ka=2 * nz,
        kyx=2,
        gains=8 + nz,
        spill=2,
        outs=4,
    )
    firsts, total = {}, 0
    for name, count in counts.items():
        firsts[name] = total
        total += count
    return types.SimpleNamespace(**firsts), total


def block_kernel(nz, pieces, S, R):
    rows, width = R.tokens.shape
    ff = R.w_down.shape[0]
    total = 2 * nz * rows
    pair = 2 * rows
    head = 128
    heads = R.wq.shape[1] // head
    scale = head ** (-0.5)
    DS, DR = R.send, R.recv

    dp, tensor = lax.axis_index("dp"), lax.axis_index("tensor")
    y, c = dp // 2, dp % 2
    z, x = tensor // 2, tensor % 2
    keeper = c == x

    def dev(yy, cc, zz, xx):
        return (2 * yy + cc, 2 * zz + xx)

    def flip(value, yes):
        return 1 - value if yes else value

    sibling = dev(y, 1 - c, z, x)
    partner = dev(y, 1 - c, z, 1 - x)
    across_x = dev(y, c, z, 1 - x)
    across_y = dev(1 - y, c, z, x)

    def send(src, dst, s, r, to):
        return pltpu.make_async_remote_copy(
            src_ref=src,
            dst_ref=dst,
            send_sem=DS.at[s],
            recv_sem=DR.at[r],
            device_id=to,
            device_id_type=MESH,
        )

    def arrived(dst, r):
        pltpu.make_async_copy(dst, dst, DR.at[r]).wait()

    def sent(src, s):
        pltpu.make_async_copy(src, src, DS.at[s]).wait()

    barrier = pltpu.get_barrier_semaphore()
    around = {
        (dy, dc, dx): dev(flip(y, dy), flip(c, dc), z, flip(x, dx))
        for dy in range(2)
        for dc in range(2)
        for dx in range(2)
        if dy + dc + dx
    }
    for (dy, dc, dx), to in around.items():
        if dy + dx:
            pl.semaphore_signal(barrier, inc=1, device_id=to, device_id_type=MESH)
    for zz in range(nz):
        for cc in range(2):

            @pl.when((zz != z) | (cc != c))
            def _():
                pl.semaphore_signal(
                    barrier, inc=1, device_id=dev(y, cc, zz, x), device_id_type=MESH
                )

    pl.semaphore_wait(barrier, 6 + 2 * nz - 1)

    def swap_start(item, src, dst):
        at = S.swap + item

        @pl.when(keeper)
        def _():
            pltpu.make_async_copy(src, dst, DR.at[at]).start()

        @pl.when(jnp.logical_not(keeper))
        def _():
            send(src, dst, at, at, partner).start()

    def swap_wait(item, dst):
        arrived(dst, S.swap + item)

    def swap_sent(item, src):
        @pl.when(jnp.logical_not(keeper))
        def _():
            sent(src, S.swap + item)

    def part_at(ref, which):
        count = ref.shape[0] // 2
        return ref.at[pl.ds(pl.multiple_of(which * count, count), count)]

    def weight_start(item, src, dst):
        at = S.swap + item

        @pl.when(keeper)
        def _():
            pltpu.make_async_copy(src, dst, DR.at[at]).start()

        @pl.when(jnp.logical_not(keeper))
        def _():
            send(part_at(src, y), part_at(dst, y), at, at, partner).start()

    def weight_pass(item, dst):
        @pl.when(jnp.logical_not(keeper))
        def _():
            half_here = part_at(dst, y)
            arrived(half_here, S.swap + item)
            send(half_here, half_here, S.swap_y + item, S.swap_y + item, across_y).start()

    def weight_wait(item, dst):
        @pl.when(keeper)
        def _():
            arrived(dst, S.swap + item)

        @pl.when(jnp.logical_not(keeper))
        def _():
            arrived(part_at(dst, 1 - y), S.swap_y + item)

    def weight_sent(item, src, dst):
        @pl.when(jnp.logical_not(keeper))
        def _():
            sent(part_at(src, y), S.swap + item)
            sent(part_at(dst, y), S.swap_y + item)

    def piece(ref, chunk, core):
        return ref.at[pl.ds(pl.multiple_of((2 * chunk + core) * rows, rows), rows)]

    def chunk_rows(chunk):
        return pl.ds(pl.multiple_of(chunk * pair, pair), pair)

    own_at = pl.multiple_of((2 * z + c) * rows, rows)

    def bit(ref, chunk, core, part):
        count = rows // 2
        first = (2 * chunk + core) * rows + part * count
        return ref.at[pl.ds(pl.multiple_of(first, count), count)]

    def gather_sem(base, name, way, chunk, part):
        return base + ((2 * name + way) * nz + chunk) * 2 + part

    def core_sem(name, chunk, part):
        return S.gc + (name * nz + chunk) * 2 + part

    def gather_hop(name, ref, way, chunk, part):
        some = bit(ref, chunk, c, part)
        to = dev(y, c, z + 1 - 2 * way, x)
        send(
            some,
            some,
            gather_sem(S.gz, name, way, chunk, part),
            gather_sem(S.gz, name, 0, chunk, part),
            to,
        ).start()

    def gather_share(name, ref, chunk, part):
        some = bit(ref, chunk, c, part)
        at = core_sem(name, chunk, part)
        send(some, some, at, at, sibling).start()

    def gather_start(name, ref, parts=(0, 1)):
        for part in parts:

            @pl.when(z < nz - 1)
            def _():
                gather_hop(name, ref, 0, z, part)

            @pl.when(z > 0)
            def _():
                gather_hop(name, ref, 1, z, part)

            gather_share(name, ref, z, part)

    def gather_pass(name, ref, step):
        for part in range(2):
            for way in range(2):
                chunk = z - 1 - step if way == 0 else z + 1 + step

                @pl.when((chunk >= 0) & (chunk <= nz - 1))
                def _():
                    arrived(bit(ref, chunk, c, part), gather_sem(S.gz, name, 0, chunk, part))

                    @pl.when(z < nz - 1 if way == 0 else z > 0)
                    def _():
                        gather_hop(name, ref, way, chunk, part)

                    gather_share(name, ref, chunk, part)

    def gather_theirs(name, ref, chunk):
        for part in range(2):
            arrived(bit(ref, chunk, 1 - c, part), core_sem(name, chunk, part))

    def gather_own(name, ref, work):
        gather_theirs(name, ref, z)
        if work is not None:
            work(z)

    def gather_use(name, ref, step, work):
        for way in range(2):
            chunk = z - 1 - step if way == 0 else z + 1 + step

            @pl.when((chunk >= 0) & (chunk <= nz - 1))
            def _():
                gather_theirs(name, ref, chunk)
                if work is not None:
                    work(chunk)

    def gather_end(name, ref):
        for chunk in range(nz):
            for part in range(2):
                some = bit(ref, chunk, c, part)
                sent(some, core_sem(name, chunk, part))

                @pl.when((z < nz - 1) & (chunk <= z))
                def _():
                    sent(some, gather_sem(S.gz, name, 0, chunk, part))

                @pl.when((z > 0) & (chunk >= z))
                def _():
                    sent(some, gather_sem(S.gz, name, 1, chunk, part))

    def terms(name):
        return R.nmlp if name == RQ else R.part

    def half(name, chunk, core):
        return piece(terms(name), chunk, core)

    def core_room(name, chunk):
        room = R.wg if name == RQ else R.from_core
        return room.at[pl.ds(pl.multiple_of(chunk * rows, rows), rows)]

    def z_slot(name, way, chunk, at, part):
        slot = jnp.where((way == 1) & (chunk == at), nz, chunk)
        count = rows // 2
        return R.from_z.at[name % 2, slot, pl.ds(part * count, count)]

    def add_rows(dst, *sources):
        step = 32

        @pl.loop(0, dst.shape[0] // step)
        def _(i):
            at = pl.ds(pl.multiple_of(i * step, step), step)
            value = sources[0][at, :].astype(F32)
            for source in sources[1:]:
                value = value + source[at, :].astype(F32)
            dst[at, :] = value.astype(dst.dtype)

    def scatter_term(name, chunk, work):
        work(chunk)
        send(
            half(name, chunk, 1 - c),
            core_room(name, chunk),
            S.rc + nz * name + chunk,
            S.rc + nz * name + chunk,
            sibling,
        ).start()

    def scatter_forward(name, way, chunk):
        arrived(core_room(name, chunk), S.rc + nz * name + chunk)
        earlier = ((way == 0) & (z > 0)) | ((way == 1) & (z < nz - 1))
        to = z + 1 - 2 * way
        for part in range(2):
            mine = bit(terms(name), chunk, c, part)
            theirs = core_room(name, chunk).at[part * (rows // 2) : (part + 1) * (rows // 2)]
            before = z_slot(name, way, chunk, z, part)
            at = gather_sem(S.rz, name, way, chunk, part)

            @pl.when(earlier)
            def _():
                arrived(before, at)
                add_rows(mine, mine, theirs, before)

            @pl.when(jnp.logical_not(earlier))
            def _():
                add_rows(mine, mine, theirs)

            send(mine, z_slot(name, way, chunk, to, part), at, at, dev(y, c, to, x)).start()

    def between(index):
        way, chunk, valid = 0, 0, False
        for at in range(1, nz - 1):
            hops = [(other + at / 2, 0, other) for other in range(at + 1, nz)]
            hops += [(nz - 1 - other + (nz - 1 - at) / 2, 1, other) for other in range(at)]
            _, this_way, this_chunk = sorted(hops)[index]
            way = jnp.where(z == at, this_way, way)
            chunk = jnp.where(z == at, this_chunk, chunk)
            valid = valid | (z == at)
        return way, chunk, valid

    def scatter_slot(step, way):
        if way == 0:
            chunk = nz - 1 + z - step
            return chunk, (step >= z) & (z < nz - 1)
        chunk = step - (nz - 1 - z)
        return chunk, (chunk >= 0) & (z > 0)

    def scatter_step(name, step, work):
        for way in range(2):
            chunk, valid = scatter_slot(step, way)

            @pl.when(valid)
            def _():
                scatter_term(name, chunk, work)

        for way in range(2):
            chunk, valid = scatter_slot(step, way)

            @pl.when(valid)
            def _():
                scatter_forward(name, way, chunk)

    def scatter_end(name, finish):
        arrived(core_room(name, z), S.rc + nz * name + z)
        for part in range(2):
            some = pl.ds(part * (rows // 2), rows // 2)
            add_rows(R.acc.at[some], half(name, z, c).at[some], core_room(name, z).at[some])
            for way in range(2):

                @pl.when(z > 0 if way == 0 else z < nz - 1)
                def _():
                    before = z_slot(name, way, z, z, part)
                    arrived(before, gather_sem(S.rz, name, way, z, part))
                    add_rows(R.acc.at[some], R.acc.at[some], before)

            finish(part)

    def scatter_sent(name):
        for chunk in range(nz):
            sent(half(name, chunk, 1 - c), S.rc + nz * name + chunk)
            for way in range(2):
                for part in range(2):

                    @pl.when(z < chunk if way == 0 else z > chunk)
                    def _():
                        sent(
                            bit(terms(name), chunk, c, part),
                            gather_sem(S.rz, name, way, chunk, part),
                        )

    def each_rows(body, part, step=32):
        @pl.loop(0, rows // 2 // step)
        def _(i):
            body(pl.multiple_of(part * (rows // 2) + i * step, step), step)

    def keep_of(first, count):
        index = lax.broadcasted_iota(jnp.int32, (count, 1), 0) + (own_at + first)
        return (index.astype(F32) < R.last[0:1, 0:1]).astype(F32)

    def rotary():
        units = R.len[...] * 64.0
        ends, end = [], jnp.zeros((1, 128), F32)
        for p in range(pieces):
            end = end + units[p : p + 1, :]
            ends.append((units[p : p + 1, :], end))
        R.last[...] = jnp.broadcast_to(ends[-2][1], (8, 128))

        @pl.loop(0, total // 128)
        def _(i):
            at = pl.ds(pl.multiple_of(i * 128, 128), 128)
            index = (lax.broadcasted_iota(jnp.int32, (128, 128), 0) + i * 128).astype(F32)
            start = jnp.zeros((128, 128), F32)
            for length, stop in ends[:-1]:
                start = start + jnp.where(stop <= index, length, 0.0)
            R.start[at, :] = start
            angle = (index - start) * R.freq[0:1, :]
            lane = lax.broadcasted_iota(jnp.int32, (128, 128), 1)
            R.cos[at, :] = jnp.cos(angle)
            R.sin[at, :] = jnp.where(lane < 64, -1.0, 1.0) * jnp.sin(angle)

    def turn(value, cosine, sine):
        swapped = jnp.concatenate([value[:, 64:], value[:, :64]], axis=1)
        return value * cosine + swapped * sine

    def project(chunk):
        at = chunk_rows(chunk)
        normed = R.norm[at, :]
        cosine, sine = R.cos[at, :], R.sin[at, :]
        queries = dot(normed, R.wq[...])
        for h in range(heads):
            cols = slice(h * head, (h + 1) * head)
            R.q[at, cols] = turn(queries[:, cols], cosine, sine).astype(BF16)
        kv = dot(normed, R.wkv[...])
        R.kv[at, :head] = turn(kv[:, :head], cosine, sine).astype(BF16)
        R.kv[at, head:] = kv[:, head:].astype(BF16)

    def attend(chunk):
        at = chunk_rows(chunk)
        keys, values = R.kv[:, :head], R.kv[:, head:]
        start = R.start[at, 0:1]
        column = lax.broadcasted_iota(jnp.int32, (pair, total), 1).astype(F32)
        row = (lax.broadcasted_iota(jnp.int32, (pair, 1), 0) + chunk * pair).astype(F32)
        allowed = (column >= start) & (column <= row)
        for h in range(heads):
            cols = slice(h * head, (h + 1) * head)
            scores = dot_rows(R.q[at, cols], keys) * scale
            scores = jnp.where(allowed, scores, -1e30)
            exps = jnp.exp(scores - jnp.max(scores, axis=1, keepdims=True))
            weights = exps * (1.0 / jnp.sum(exps, axis=1, keepdims=True))
            weights = weights.astype(BF16)
            R.probs[h, at, :] = weights
            R.att[at, cols] = dot(weights, values).astype(BF16)

    def out_term(chunk):
        attend(chunk)
        at = chunk_rows(chunk)
        for n, size in tiles(width, 512):
            R.part[at, n : n + size] = dot(
                R.att[at, :], R.wo[:, n : n + size]
            ).astype(BF16)

    def mlp(chunk):
        at = chunk_rows(chunk)
        for n, size in tiles(ff, 256):
            cols = slice(n, n + size)
            gate = dot_rows(R.nmlp[at, :], R.wg[cols, :])
            up = dot_rows(R.nmlp[at, :], R.wu[cols, :])
            grad = dot_rows(R.gmlp[at, :], R.wd[cols, :])
            sigma = 1.0 / (1.0 + jnp.exp(-gate))
            active = gate * sigma
            R.hid[at, cols] = (active * up).astype(BF16)
            R.dup[at, cols] = (grad * active).astype(BF16)
            R.dgate[at, cols] = (grad * up * (sigma * (1.0 + gate * (1.0 - sigma)))).astype(BF16)

    def back_term(chunk):
        at = chunk_rows(chunk)
        for n, size in tiles(width, 512):
            some = slice(n, n + size)
            R.part[at, some] = (
                dot(R.dgate[at, :], R.wg[:, some]) + dot(R.dup[at, :], R.wu[:, some])
            ).astype(BF16)

    def down_term(chunk):
        at = chunk_rows(chunk)
        for n, size in tiles(width, 512):
            some = slice(n, n + size)
            R.part[at, some] = dot(R.hid[at, :], R.wd[:, some]).astype(BF16)

    def d_attended(chunk):
        at = chunk_rows(chunk)
        R.datt[at, :] = dot_rows(R.norm[at, :], R.wo[...]).astype(BF16)
        backward_attend(chunk)

    def backward_attend(chunk):
        at = chunk_rows(chunk)
        keys, values = R.kv[:, :head], R.kv[:, head:]
        cosine, sine = R.cos[at, :], R.sin[at, :]
        for h in range(heads):
            cols = slice(h * head, (h + 1) * head)
            weights = R.probs[h, at, :]
            probs = weights.astype(F32)
            grad = R.datt[at, cols]
            d_probs = dot_rows(grad, values)
            inner = jnp.sum(d_probs * probs, axis=1, keepdims=True)
            d_scores = (probs * (d_probs - inner)).astype(BF16)
            d_queries = dot(d_scores, keys) * scale
            R.dq[at, cols] = turn(d_queries, cosine, -sine).astype(BF16)
            R.dkv[:, :head] += dot_cols(d_scores, R.q[at, cols]) * scale
            R.dkv[:, head:] += dot_cols(weights, grad)

    def query_term(chunk):
        at = chunk_rows(chunk)
        for n, size in tiles(width, 512):
            some = slice(n, n + size)
            terms(RQ)[at, some] = dot_rows(R.dq[at, :], R.wq[some, :]).astype(BF16)

    Y_FIRST = (GATE, OUT)

    def grad_send(name, yy, cc):
        quarter = 2 * yy + cc
        stage = R.stage[name].at[quarter]
        if name in Y_FIRST:
            at = S.px + 4 * name + cc

            @pl.when(yy != y)
            def _():
                send(stage, R.px[name].at[cc], at, at, across_y).start()

            return
        into_x, into_c = R.px[name].at[yy], R.pc[name].at[yy]

        @pl.when(jnp.logical_not(keeper))
        def _():
            send(
                stage,
                into_x,
                S.px + 4 * name + quarter,
                S.px + 4 * name + yy,
                (2 * y + cc, 2 * z + 1 - x),
            ).start()

        @pl.when(keeper & (c == cc))
        def _():
            pltpu.make_async_copy(stage, into_c, DR.at[S.pc + 4 * name + yy]).start()

        @pl.when(keeper & (c != cc))
        def _():
            send(
                stage, into_c, S.pc + 4 * name + quarter, S.pc + 4 * name + yy, sibling
            ).start()

    def grad_sent(name, yy, cc):
        quarter = 2 * yy + cc
        stage = R.stage[name].at[quarter]
        if name in Y_FIRST:

            @pl.when(yy != y)
            def _():
                sent(stage, S.px + 4 * name + cc)

            return

        @pl.when(jnp.logical_not(keeper))
        def _():
            sent(stage, S.px + 4 * name + quarter)

        @pl.when(keeper & (c != cc))
        def _():
            sent(stage, S.pc + 4 * name + quarter)

    QUARTERS = [(0, 0), (0, 1), (1, 0), (1, 1)]

    def grad_make(name, left, right):
        split_left = name == QUERY
        quarter_cols = (left if split_left else right).shape[1] // 4
        tile = R.tile[name]
        for index, (yy, cc) in enumerate(QUARTERS):
            first = index * quarter_cols
            if index > 1:
                pltpu.make_async_copy(
                    tile.at[index % 2],
                    R.stage[name].at[index - 2],
                    DR.at[S.stage + 4 * name + index - 2],
                ).wait()
                grad_send(name, *QUARTERS[index - 2])
            if split_left:
                for m, size in tiles(quarter_cols, 256):
                    tile[index % 2, m : m + size, :] = dot_cols(
                        left[:, first + m : first + m + size], right[...]
                    ).astype(BF16)
            else:
                for m, size in tiles(left.shape[1], 256):
                    tile[index % 2, m : m + size, :] = dot_cols(
                        left[:, m : m + size], right[:, first : first + quarter_cols]
                    ).astype(BF16)
            pltpu.make_async_copy(
                tile.at[index % 2],
                R.stage[name].at[index],
                DR.at[S.stage + 4 * name + index],
            ).start()
        for index in (2, 3):
            pltpu.make_async_copy(
                tile.at[index % 2],
                R.stage[name].at[index],
                DR.at[S.stage + 4 * name + index],
            ).wait()
            grad_send(name, *QUARTERS[index])

    def sum_room(name, cc=0):
        cols = width // 4
        if name == QUERY:
            return R.wd.at[0:cols, 2 * cols : 2 * cols + R.wq.shape[1]]
        if name == DOWN:
            return R.wu.at[:, 2 * cols : 3 * cols]
        if name == UP:
            return R.wu.at[:, 3 * cols :]
        if name == GATE:
            return R.wd.at[:, cc * cols : (cc + 1) * cols]
        count = R.wo.shape[0]
        return R.wd.at[cc * count : (cc + 1) * count, 3 * cols :]

    def grad_places(name):
        count, cols = R.tile[name].shape[1:]
        return (
            (R.tile[name].at[0], R.tile[name].at[1]),
            (R.wu.at[0:count, 0:cols], R.wu.at[0:count, cols : 2 * cols]),
        )

    def grad_loads(name, turn_at, sources):
        loads = []
        for k, source in enumerate(sources):
            load = pltpu.make_async_copy(
                source,
                grad_places(name)[turn_at][k],
                DR.at[S.ld + 4 * name + 2 * turn_at + k],
            )
            load.start()
            loads.append(load)
        return loads

    def grad_mid(name):
        loads = []
        for cc in range(2):
            arrived(R.px[name].at[cc], S.px + 4 * name + cc)
            loads.append(
                grad_loads(name, cc, (R.px[name].at[cc], R.stage[name].at[2 * y + cc]))
            )
        for cc in range(2):
            for load in loads[cc]:
                load.wait()
            into = sum_room(name, cc)
            add_rows(into, *grad_places(name)[cc])
            at = S.pc + 4 * name + cc

            @pl.when(jnp.logical_not(keeper))
            def _():
                send(
                    into, R.other[name], at, S.py + name, (2 * y + cc, 2 * z + 1 - x)
                ).start()

            @pl.when(keeper & (c == cc))
            def _():
                pltpu.make_async_copy(into, R.mine[name], DR.at[S.st + name]).start()

            @pl.when(keeper & (c != cc))
            def _():
                send(into, R.mine[name], at, S.st + name, sibling).start()

    def grad_add(name):
        loads = []
        for turn_at, yy in enumerate((1 - y, y)):
            arrived(R.px[name].at[yy], S.px + 4 * name + yy)
            arrived(R.pc[name].at[yy], S.pc + 4 * name + yy)
            loads.append(grad_loads(name, turn_at, (R.px[name].at[yy], R.pc[name].at[yy])))
        for turn_at in range(2):
            for load in loads[turn_at]:
                load.wait()
            one, two = grad_places(name)[turn_at]
            if turn_at == 0:
                into = sum_room(name)
                add_rows(into, one, two)
                send(into, R.other[name], S.py + name, S.py + name, across_y).start()
            else:
                add_rows(one, one, two)
                store = pltpu.make_async_copy(one, R.mine[name], DR.at[S.st + name])
                store.start()
                store.wait()

    R.own_len[...] = jnp.zeros((8, 128), F32)
    for p in range(pieces):
        R.own_len[p : p + 1, :] = jnp.broadcast_to(R.lengths[0:1, p : p + 1].astype(F32), (1, 128))
    swap_start(LEN, R.own_len, R.len)
    for part in range(2):
        swap_start(TOK + part, part_at(R.tokens, part), part_at(R.tok, part))
    weight_start(WQ, R.w_query, R.wq)
    swap_start(OG, R.out_grad, R.og)
    swap_start(KVG, R.kv_grad, R.kvg)

    def norm_rows(first, count):
        at = pl.ds(first, count)
        value = R.tok[at, :].astype(F32)
        inverse = lax.rsqrt(jnp.mean(value * value, axis=1, keepdims=True) + EPSILON)
        R.norm[pl.ds(own_at + first, count), :] = (
            value * inverse * R.gain_attn[0:1, :]
        ).astype(BF16)

    for part in range(2):
        swap_wait(TOK + part, part_at(R.tok, part))
        each_rows(norm_rows, part)
        gather_start(GN, R.norm, (part,))
    swap_wait(LEN, R.len)
    weight_start(WO, R.w_attn_out, R.wo)
    rotary()
    weight_pass(WQ, R.wq)
    weight_wait(WQ, R.wq)
    gather_own(GN, R.norm, project)

    def mask_rows(first, count):
        at = pl.ds(first, count)
        R.gmlp[pl.ds(own_at + first, count), :] = (
            keep_of(first, count) * R.og[at, :].astype(F32)
        ).astype(BF16)

    for step in range(nz - 1):
        gather_pass(GN, R.norm, step)
        if step == 0:
            weight_pass(WO, R.wo)
            weight_start(WG, R.w_gate, R.wg)
            swap_wait(OG, R.og)
            swap_wait(KVG, R.kvg)
            for part in range(2):
                each_rows(mask_rows, part)
        if step == 1:
            weight_start(WU, R.w_up, R.wu)
        if step == nz - 2:
            gather_start(GG, R.gmlp)
            weight_pass(WG, R.wg)
            weight_start(WD, R.w_down, R.wd)
        gather_use(GN, R.norm, step, project)
    spill = pltpu.make_async_copy(R.norm, R.norm_store, DR.at[S.spill])
    spill.start()
    weight_wait(WO, R.wo)

    for step in range(nz - 1):
        scatter_step(RO, step, out_term)
        gather_pass(GG, R.gmlp, step)
        if step == 0:
            weight_pass(WU, R.wu)
        if step == 1:
            weight_pass(WD, R.wd)
    scatter_term(RO, z, out_term)

    def mid_rows(first, count):
        at = pl.ds(first, count)
        mid = R.tok[at, :].astype(F32) + R.acc[at, :]
        R.mid[at, :] = mid
        inverse = lax.rsqrt(jnp.mean(mid * mid, axis=1, keepdims=True) + EPSILON)
        R.nmlp[pl.ds(own_at + first, count), :] = (
            mid * inverse * R.gain_mlp[0:1, :]
        ).astype(BF16)

    def mid_done(part):
        each_rows(mid_rows, part)
        gather_start(GM, R.nmlp, (part,))

    scatter_end(RO, mid_done)
    for step in range(nz - 1):
        gather_use(GG, R.gmlp, step, None)
    gather_own(GG, R.gmlp, None)
    scatter_sent(RO)
    gather_end(GN, R.norm)
    spill.wait()
    weight_wait(WG, R.wg)
    weight_wait(WU, R.wu)
    weight_wait(WD, R.wd)
    def mlp_and_back(chunk):
        mlp(chunk)
        scatter_term(RB, chunk, back_term)

    gather_own(GM, R.nmlp, mlp_and_back)
    for step in range(nz - 1):
        gather_pass(GM, R.nmlp, step)
        gather_use(GM, R.nmlp, step, mlp_and_back)

        @pl.when(z == 0)
        def _():
            scatter_forward(RB, 0, step + 1)

        @pl.when(z == nz - 1)
        def _():
            scatter_forward(RB, 1, nz - 2 - step)

    for item, src, dst in (
        (WQ, R.w_query, R.wq),
        (WO, R.w_attn_out, R.wo),
        (WG, R.w_gate, R.wg),
        (WU, R.w_up, R.wu),
        (WD, R.w_down, R.wd),
    ):
        weight_sent(item, src, dst)

    mlp_grads = ((DOWN, R.hid, R.gmlp), (GATE, R.dgate, R.nmlp), (UP, R.dup, R.nmlp))
    for index in range(nz - 1):
        if index < 2:
            grad_make(*mlp_grads[index])
        way, chunk, valid = between(index)

        @pl.when(valid)
        def _():
            scatter_forward(RB, way, chunk)

    grad_make(*mlp_grads[2])
    R.gains[...] = jnp.zeros(R.gains.shape, F32)

    def fold(value):
        return jnp.sum(value.reshape(value.shape[0] // 8, 8, value.shape[1]), axis=0)

    def d_mid_rows(first, count):
        at = pl.ds(first, count)
        mid = R.mid[at, :]
        inverse = lax.rsqrt(jnp.mean(mid * mid, axis=1, keepdims=True) + EPSILON)
        unit = mid * inverse
        back = R.acc[at, :]
        R.gains[1] += fold(back * unit)
        e = back * R.gain_mlp[0:1, :]
        grad = keep_of(first, count) * R.og[at, :].astype(F32) + inverse * (
            e - unit * jnp.mean(e * unit, axis=1, keepdims=True)
        )
        R.dmid[at, :] = grad
        R.norm[pl.ds(own_at + first, count), :] = grad.astype(BF16)

    def d_mid_done(part):
        each_rows(d_mid_rows, part)
        gather_start(GA, R.norm, (part,))

    scatter_end(RB, d_mid_done)
    scatter_sent(RB)
    gather_end(GG, R.gmlp)
    gather_end(GM, R.nmlp)
    back_norm = pltpu.make_async_copy(R.norm_store, R.gmlp, DR.at[S.spill + 1])
    back_norm.start()
    R.dkv[...] = jnp.zeros(R.dkv.shape, F32)
    def attend_and_query(chunk):
        d_attended(chunk)
        scatter_term(RQ, chunk, query_term)

    def down_forward(step):
        for way in range(2):
            chunk, valid = scatter_slot(step, way)

            @pl.when(valid)
            def _():
                scatter_forward(RD, way, chunk)

    gather_theirs(GA, R.norm, z)
    for chunk in range(nz):
        scatter_term(RD, chunk, down_term)
    down_forward(0)
    attend_and_query(z)
    for step in range(nz - 1):
        gather_pass(GA, R.norm, step)
        gather_use(GA, R.norm, step, attend_and_query)

        @pl.when(z == 0)
        def _():
            scatter_forward(RQ, 0, step + 1)

        @pl.when(z == nz - 1)
        def _():
            scatter_forward(RQ, 1, nz - 2 - step)

        if step == 1:
            grad_add(DOWN)

    R.dkvb[...] = R.dkv[...].astype(BF16)
    for zz in range(nz):
        send(piece(R.dkvb, zz, 1 - c), R.kc.at[zz], S.kc + zz, S.kc + zz, sibling).start()

    def kv_over_z():
        for zz in range(nz):
            arrived(R.kc.at[zz], S.kc + zz)
            R.ks[zz] = (
                R.dkv[pl.ds(pl.multiple_of((2 * zz + c) * rows, rows), rows), :]
                + R.kc[zz].astype(F32)
            ).astype(BF16)

            @pl.when(zz != z)
            def _():
                send(R.ks.at[zz], R.kz.at[z], S.kz + zz, S.kz + z, dev(y, c, zz, x)).start()

    own_rows = pl.ds(own_at, rows)
    own_kv = piece(R.dkva, z, c)

    def kv_own():
        R.kacc[...] = keep_of(0, rows) * R.kvg[...].astype(F32) + R.ks[z].astype(F32)
        for zz in range(nz):

            @pl.when(zz != z)
            def _():
                arrived(R.kz.at[zz], S.kz + zz)
                R.kacc[...] += R.kz[zz].astype(F32)

        R.dkva[own_rows, :head] = turn(
            R.kacc[:, :head], R.cos[own_rows, :], -R.sin[own_rows, :]
        ).astype(BF16)
        R.dkva[own_rows, head:] = R.kacc[:, head:].astype(BF16)
        for zz in range(nz):
            for cc in range(2):

                @pl.when((zz != z) | (cc != c))
                def _():
                    send(
                        own_kv, own_kv, S.ka + 2 * zz + cc, S.ka + 2 * z + c, dev(y, cc, zz, x)
                    ).start()

    def out_rows(first, count):
        at = pl.ds(first, count)
        R.bo[at, :] = (keep_of(first, count) * (R.mid[at, :] + R.acc[at, :])).astype(BF16)

    for step in range(1, nz - 2):
        down_forward(step)
    grad_make(OUT, R.att, R.norm)
    back_norm.wait()
    for index in range(nz - 1):
        way, chunk, valid = between(index)

        @pl.when(valid)
        def _():
            scatter_forward(RQ, way, chunk)

        if index == 0:
            kv_over_z()
            grad_add(UP)
            grad_make(QUERY, R.gmlp, R.dq)
        if index == 1:
            kv_own()
            grad_mid(GATE)
    down_forward(nz - 2)
    for zz in range(nz):
        for cc in range(2):

            @pl.when((zz != z) | (cc != c))
            def _():
                arrived(piece(R.dkva, zz, cc), S.ka + 2 * zz + cc)

    first_col = c * (4 * nz * 32) + z * 128
    for yy in range(2):
        cols = pl.ds(pl.multiple_of(yy * (width // 2) + first_col, 128), 128)
        R.gkv[yy] = dot_cols(R.gmlp[:, cols], R.dkva[...])
    send(
        R.gkv.at[1 - y], R.kyb, S.kyx, S.kyx, across_y
    ).start()
    arrived(R.kyb, S.kyx)
    R.kysum[...] = R.gkv[y] + R.kyb[...]
    send(
        R.kysum.at[pl.ds(pl.multiple_of((1 - x) * 64, 64), 64)],
        R.kxb,
        S.kyx + 1,
        S.kyx + 1,
        across_x,
    ).start()
    arrived(R.kxb, S.kyx + 1)
    R.kfinal[...] = (
        R.kysum[pl.ds(pl.multiple_of(x * 64, 64), 64), :] + R.kxb[...]
    )
    kv_out = pltpu.make_async_copy(R.kfinal, R.grad_w_kv, DR.at[S.outs])
    kv_out.start()
    for n, size in tiles(width, 512):
        some = slice(n, n + size)
        extra = dot_rows(R.dkva[own_rows, :], R.wkv[some, :])
        for m in range(n, n + size, 2 * head):
            at = m // (2 * head) * rows
            R.dkv[at : at + rows, :] = extra[:, m - n : m - n + 2 * head]
    grad_mid(OUT)
    grad_add(QUERY)

    def tail_rows(first, count):
        at = pl.ds(first, count)
        value = R.tok[at, :].astype(F32)
        inverse = lax.rsqrt(jnp.mean(value * value, axis=1, keepdims=True) + EPSILON)
        unit = value * inverse
        extra = [
            R.dkv[pl.ds(pl.multiple_of(m * rows + first, 32), count), :]
            for m in range(width // (2 * head))
        ]
        back = R.acc[at, :] + jnp.concatenate(extra, axis=1)
        R.gains[0] += fold(back * unit)
        e = back * R.gain_attn[0:1, :]
        R.gt[at, :] = (
            R.dmid[at, :]
            + inverse * (e - unit * jnp.mean(e * unit, axis=1, keepdims=True))
        ).astype(BF16)

    def tail_done(part):
        each_rows(tail_rows, part)
        swap_start(GT + part, part_at(R.gt, part), part_at(R.grad_tokens, part))

    scatter_end(RQ, tail_done)

    line = lax.broadcasted_iota(jnp.int32, (8, width), 0)
    gain_first = jnp.sum(R.gains[0], axis=0, keepdims=True)
    gain_second = jnp.sum(R.gains[1], axis=0, keepdims=True)
    R.ga[...] = jnp.where(line == 0, gain_first, jnp.where(line == 1, gain_second, 0.0))
    span = width // 4

    def gain_cols(yy, cc):
        return pl.ds(pl.multiple_of((2 * yy + cc) * span, span), span)

    def gain_send(index, offset):
        dy, dc, dx = offset
        return send(
            R.ga.at[:, gain_cols(flip(y, dy), flip(c, dc))],
            R.gb.at[index],
            S.gains + index,
            S.gains + index,
            around[offset],
        )

    for index, offset in enumerate(around):
        gain_send(index, offset).start()
    scatter_end(RD, lambda part: each_rows(out_rows, part))
    swap_start(BO, R.bo, R.block_out)
    R.ga_x[...] = R.ga[:, gain_cols(y, c)]
    for index in range(len(around)):
        arrived(R.gb.at[index], S.gains + index)
        R.ga_x[...] += R.gb[index]
    for zz in range(nz):

        @pl.when(zz != z)
        def _():
            send(
                R.ga_x.at[:, zz * 128 : (zz + 1) * 128],
                R.gb_z.at[z],
                S.gains + 8 + zz,
                S.gains + 8 + z,
                dev(y, c, zz, x),
            ).start()

    R.gfinal[...] = R.ga_x[:, pl.ds(pl.multiple_of(z * 128, 128), 128)]
    for zz in range(nz):

        @pl.when(zz != z)
        def _():
            arrived(R.gb_z.at[zz], S.gains + 8 + zz)
            R.gfinal[...] += R.gb_z[zz]

    gain_out = pltpu.make_async_copy(R.gfinal, R.grad_gains, DR.at[S.outs + 1])
    gain_out.start()

    for name in GRADS:
        arrived(R.other[name], S.py + name)
        if name in Y_FIRST:
            arrived(R.mine[name], S.st + name)
            for cc in range(2):

                @pl.when(jnp.logical_not(keeper & (c == cc)))
                def _():
                    sent(sum_room(name, cc), S.pc + 4 * name + cc)
        else:
            sent(sum_room(name), S.py + name)
        for yy, cc in QUARTERS:
            grad_sent(name, yy, cc)
    kv_out.wait()
    gain_out.wait()
    scatter_sent(RD)
    scatter_sent(RQ)
    gather_end(GA, R.norm)
    swap_wait(BO, R.block_out)
    for part in range(2):
        swap_wait(GT + part, part_at(R.grad_tokens, part))
    for item, src in (
        (LEN, R.own_len),
        (TOK, part_at(R.tokens, 0)),
        (TOK2, part_at(R.tokens, 1)),
        (OG, R.out_grad),
        (KVG, R.kv_grad),
        (BO, R.bo),
        (GT, part_at(R.gt, 0)),
        (GT2, part_at(R.gt, 1)),
    ):
        swap_sent(item, src)
    for zz in range(nz):
        sent(piece(R.dkvb, zz, 1 - c), S.kc + zz)

        @pl.when(zz != z)
        def _():
            sent(R.ks.at[zz], S.kz + zz)
            sent(R.ga_x.at[:, zz * 128 : (zz + 1) * 128], S.gains + 8 + zz)

        for cc in range(2):

            @pl.when((zz != z) | (cc != c))
            def _():
                sent(own_kv, S.ka + 2 * zz + cc)

    sent(R.gkv.at[1 - y], S.kyx)
    sent(R.kysum.at[pl.ds(pl.multiple_of((1 - x) * 64, 64), 64)], S.kyx + 1)
    for index, offset in enumerate(around):
        gain_send(index, offset).wait_send()


def fused(nz, *args):
    (tokens, lengths, gain_attn, w_query, w_kv, w_attn_out, gain_mlp, w_gate, w_up, w_down,
     out_grad, kv_grad) = args
    rows, width = tokens.shape
    ff = w_gate.shape[1]
    qw = w_query.shape[1]
    total, pair = 2 * nz * rows, 2 * rows
    pieces = lengths.shape[1]
    head = w_kv.shape[1] // 2
    half_width = head // 2
    freqs = (ROTARY_BASE ** (-np.arange(half_width, dtype=np.float32) / half_width)).astype(np.float32)
    freq = np.tile(np.concatenate([freqs, freqs])[None, :], (8, 1))
    anywhere, vmem = pl.BlockSpec(memory_space=pl.ANY), pl.BlockSpec(memory_space=pltpu.VMEM)
    ins = dict(
        tokens=(tokens, anywhere),
        lengths=(lengths, vmem),
        freq=(freq, vmem),
        gain_attn=(gain_attn[None], vmem),
        gain_mlp=(gain_mlp[None], vmem),
        w_query=(w_query, anywhere),
        wkv=(w_kv, vmem),
        w_attn_out=(w_attn_out, anywhere),
        w_gate=(w_gate.T, anywhere),
        w_up=(w_up.T, anywhere),
        w_down=(w_down, anywhere),
        out_grad=(out_grad, anywhere),
        kv_grad=(kv_grad, anywhere),
    )
    quarter = width // 4
    grad_tiles = [(ff, quarter), (ff, quarter), (ff, quarter), (qw, quarter), (quarter, qw)]
    outs = dict(
        block_out=((rows, width), BF16),
        grad_tokens=((rows, width), BF16),
        grad_w_kv=((64, 2 * head), F32),
        grad_gains=((8, 128), F32),
        norm_store=((total, width), BF16),
    )
    moved = [
        (shape, BF16)
        for tile in grad_tiles
        for shape in (tile, tile, (4,) + tile, (2,) + tile, (2,) + tile)
    ]
    S, count = semaphores(nz)
    scratch = dict(
        own_len=((8, 128), F32),
        len=((8, 128), F32),
        last=((8, 128), F32),
        tok=((rows, width), BF16),
        og=((rows, width), BF16),
        kvg=((rows, 2 * head), BF16),
        wq=((width, qw), BF16),
        wo=((qw, width), BF16),
        wg=((ff, width), BF16),
        wu=((ff, width), BF16),
        wd=((ff, width), BF16),
        norm=((total, width), BF16),
        nmlp=((total, width), BF16),
        gmlp=((total, width), BF16),
        cos=((total, 128), F32),
        sin=((total, 128), F32),
        start=((total, 128), F32),
        q=((total, qw), BF16),
        kv=((total, 2 * head), BF16),
        att=((total, qw), BF16),
        datt=((total, qw), BF16),
        dq=((total, qw), BF16),
        probs=((qw // head, total, total), BF16),
        hid=((total, ff), BF16),
        dgate=((total, ff), BF16),
        dup=((total, ff), BF16),
        part=((total, width), BF16),
        from_core=((nz * rows, width), BF16),
        from_z=((2, nz + 1, rows, width), BF16),
        acc=((rows, width), F32),
        mid=((rows, width), F32),
        dmid=((rows, width), F32),
        bo=((rows, width), BF16),
        gt=((rows, width), BF16),
        gains=((2, 8, width), F32),
        ga=((8, width), F32),
        ga_x=((8, width // 4), F32),
        gb=((7, 8, width // 4), F32),
        gb_z=((nz, 8, 128), F32),
        gfinal=((8, 128), F32),
        dkv=((total, 2 * head), F32),
        dkvb=((total, 2 * head), BF16),
        dkva=((total, 2 * head), BF16),
        kc=((nz, rows, 2 * head), BF16),
        ks=((nz, rows, 2 * head), BF16),
        kz=((nz, rows, 2 * head), BF16),
        kacc=((rows, 2 * head), F32),
        gkv=((2, 128, 2 * head), F32),
        kyb=((128, 2 * head), F32),
        kysum=((128, 2 * head), F32),
        kxb=((64, 2 * head), F32),
        kfinal=((64, 2 * head), F32),
    )
    tile_shapes = (grad_tiles[DOWN], grad_tiles[OUT], grad_tiles[QUERY])
    out_shapes = list(outs.values()) + moved
    scratch_shapes = list(scratch.values()) + [((2,) + shape, BF16) for shape in tile_shapes]

    def body(*refs):
        refs = list(refs)

        def take(count):
            taken = refs[:count]
            del refs[:count]
            return taken

        R = types.SimpleNamespace(
            **dict(zip(ins, take(len(ins)))), **dict(zip(outs, take(len(outs))))
        )
        rest = take(len(moved))
        R.mine, R.other, R.stage, R.px, R.pc = (rest[k::5] for k in range(5))
        for key, ref in zip(scratch, take(len(scratch))):
            setattr(R, key, ref)
        big, out_tile, query_tile = take(3)
        R.tile = [big, big, big, out_tile, query_tile]
        R.send, R.recv = refs
        block_kernel(nz, pieces, S, R)

    results = pl.pallas_call(
        body,
        out_shape=[jax.ShapeDtypeStruct(shape, kind) for shape, kind in out_shapes],
        in_specs=[spec for _, spec in ins.values()],
        out_specs=[anywhere] * len(out_shapes),
        scratch_shapes=[pltpu.VMEM(shape, kind) for shape, kind in scratch_shapes]
        + [pltpu.SemaphoreType.DMA((count,))] * 2,
        compiler_params=pltpu.CompilerParams(
            collective_id=0, has_side_effects=True, vmem_limit_bytes=63 * MIB
        ),
        name="block",
    )(*[value for value, _ in ins.values()])
    first = list(results[:4])
    mine, other = list(results[5::5]), list(results[6::5])

    def finish(*refs):
        ends, refs = refs[:4], refs[4:]
        one, two, refs = refs[:5], refs[5:10], refs[10:]
        for k in range(3):
            refs[k][...] = ends[k][...]
        right = (lax.axis_index("tensor") % 2) == 1
        refs[3][...] = jnp.where(right, ends[3][:, 64:], ends[3][:, :64])
        for k in GRADS:
            refs[4 + k][...] = one[k][...].astype(F32) + two[k][...].astype(F32)

    cuts = 4

    def cut(array):
        count = array.shape[0] // cuts
        return pl.BlockSpec((count, array.shape[1]), lambda i: (i, 0))

    whole = pl.BlockSpec((8, 128), lambda i: (0, 0))
    block_out, grad_tokens, grad_w_kv, gains, *sums = pl.pallas_call(
        finish,
        grid=(cuts,),
        out_shape=[jax.ShapeDtypeStruct(array.shape, array.dtype) for array in first[:3]]
        + [jax.ShapeDtypeStruct((8, 64), F32)]
        + [jax.ShapeDtypeStruct(array.shape, F32) for array in mine],
        in_specs=[cut(array) for array in first[:3]] + [whole] + [cut(a) for a in mine + other],
        out_specs=[cut(array) for array in first[:3]]
        + [pl.BlockSpec((8, 64), lambda i: (0, 0))]
        + [cut(array) for array in mine],
        compiler_params=pltpu.CompilerParams(vmem_limit_bytes=63 * MIB),
        name="finish",
    )(*first, *mine, *other)
    return (
        block_out,
        grad_tokens,
        gains[0],
        sums[QUERY],
        grad_w_kv,
        sums[OUT],
        gains[1],
        sums[GATE].T,
        sums[UP].T,
        sums[DOWN],
    )


def solution(mesh):
    groups, parts = mesh.shape["dp"], mesh.shape["tensor"]
    paired = groups == 4 and parts == 8
    per_group = functools.partial(fused, parts // 2) if paired else per_device
    placed = (
        P(("dp", "tensor"), None),
        P("dp", None),
        P(),
        P(None, "tensor"),
        P(),
        P("tensor", None),
        P(),
        P(None, "tensor"),
        P(None, "tensor"),
        P("tensor", None),
        P(("dp", "tensor"), None),
        P(("dp", "tensor"), None),
    )
    return jax.shard_map(
        per_group,
        mesh=mesh,
        in_specs=placed,
        out_specs=(
            P(("dp", "tensor"), None),
            P(("dp", "tensor"), None),
            P(("dp", "tensor")),
            P("dp", "tensor"),
            P(("dp", "tensor"), None),
            P("tensor", "dp"),
            P(("dp", "tensor")),
            P("dp", "tensor"),
            P("dp", "tensor"),
            P("tensor", "dp"),
        ),
        check_vma=False,
    )
```

```python
import functools
import types

import jax
import jax.numpy as jnp
import numpy as np
from jax import lax
from jax.experimental import pallas as pl
from jax.experimental.pallas import tpu as pltpu
from jax.sharding import PartitionSpec as P

SPAN = 64


EPSILON = 1e-05
ROTARY_BASE = 10000.0
MASKED = -1e30


def rotary_tables(positions, width):
    half_width = width // 2
    freqs = ROTARY_BASE ** (-jnp.arange(half_width, dtype=jnp.float32) / half_width)
    angles = positions[:, None] * freqs[None, :]
    return (jnp.cos(angles), jnp.sin(angles))


def rotate(values, cosine, sine):
    half_width = values.shape[-1] // 2
    first_half = values[..., :half_width]
    second_half = values[..., half_width:]
    return jnp.concatenate(
        [first_half * cosine - second_half * sine, second_half * cosine + first_half * sine],
        axis=-1,
    )


def unrotate(values, cosine, sine):
    half_width = values.shape[-1] // 2
    first_half = values[..., :half_width]
    second_half = values[..., half_width:]
    return jnp.concatenate(
        [first_half * cosine + second_half * sine, second_half * cosine - first_half * sine],
        axis=-1,
    )


def layout(piece_units, rows):
    piece_rows = piece_units * SPAN
    ends = jnp.cumsum(piece_rows)
    starts = ends - piece_rows
    row_steps = jnp.arange(rows, dtype=jnp.int32)
    segment = jnp.sum((row_steps[:, None] >= ends[None, :]).astype(jnp.int32), axis=1)
    member = segment[:, None] == jnp.arange(piece_units.shape[0], dtype=jnp.int32)[None, :]
    row_start = jnp.sum(jnp.where(member, starts[None, :], 0), axis=1)
    positions = (row_steps - row_start).astype(jnp.float32)
    keep = (segment < piece_units.shape[0] - 1).astype(jnp.float32)
    return (segment, row_steps, positions, keep)


def permitted(block_segment, block_steps, segment, row_steps):
    return (block_segment[:, None] == segment[None, :]) & (
        row_steps[None, :] <= block_steps[:, None]
    )


def spread_rows(values):
    return lax.all_gather(values, "tensor", axis=0, tiled=True)


def spread_grads(values):
    return lax.all_gather(values, "tensor", axis=0, tiled=True)


def per_device(
    tokens,
    lengths,
    gain_attn,
    w_query,
    w_kv,
    w_attn_out,
    gain_mlp,
    w_gate,
    w_up,
    w_down,
    out_grad,
    kv_grad,
):
    local_rows = tokens.shape[0]
    parts = lax.axis_size("tensor")
    total_rows = local_rows * parts
    first_row = lax.axis_index("tensor") * local_rows
    segment, row_steps, positions, keep = layout(lengths[0], total_rows)
    head_dim = w_kv.shape[1] // 2
    local_heads = w_query.shape[1] // head_dim
    scale = head_dim ** (-0.5)
    cosine, sine = rotary_tables(positions, head_dim)
    row_keep = lax.dynamic_slice_in_dim(keep, first_row, local_rows, 0)[:, None]
    row_cosine = lax.dynamic_slice_in_dim(cosine, first_row, local_rows, 0)
    row_sine = lax.dynamic_slice_in_dim(sine, first_row, local_rows, 0)
    tokens_full = tokens.astype(jnp.float32)
    inv_first = lax.rsqrt(jnp.mean(tokens_full * tokens_full, axis=-1, keepdims=True) + EPSILON)
    unit_first = tokens_full * inv_first
    normed_rows = (unit_first * gain_attn).astype(jnp.bfloat16)
    normed = spread_rows(normed_rows)
    queries = jnp.dot(normed, w_query, preferred_element_type=jnp.float32).reshape(
        total_rows, local_heads, head_dim
    )
    queries = rotate(queries, cosine[:, None, :], sine[:, None, :]).astype(jnp.bfloat16)
    kv_raw = jnp.dot(normed, w_kv, preferred_element_type=jnp.float32)
    shared = jnp.concatenate(
        [rotate(kv_raw[:, :head_dim], cosine, sine), kv_raw[:, head_dim:]], axis=1
    ).astype(jnp.bfloat16)
    keys = shared[:, :head_dim]
    values = shared[:, head_dim:]
    block = min(512, total_rows)
    count = total_rows // block
    pieces = []
    log_totals = []
    for number in range(count):
        begin = number * block
        query_block = queries[begin : begin + block]
        allowed = permitted(
            segment[begin : begin + block], row_steps[begin : begin + block], segment, row_steps
        )
        scores = (
            jnp.einsum("qhd,kd->hqk", query_block, keys, preferred_element_type=jnp.float32) * scale
        )
        scores = jnp.where(allowed[None], scores, MASKED)
        row_max = jnp.max(scores, axis=-1, keepdims=True)
        exp_scores = jnp.exp(scores - row_max)
        row_total = jnp.sum(exp_scores, axis=-1, keepdims=True)
        log_totals.append(row_max + jnp.log(row_total))
        weights = (exp_scores / row_total).astype(jnp.bfloat16)
        pieces.append(
            jnp.einsum("hqk,kd->qhd", weights, values, preferred_element_type=jnp.float32).astype(
                jnp.bfloat16
            )
        )
    attended = jnp.concatenate(pieces, axis=0).reshape(total_rows, local_heads * head_dim)
    attn_rows = lax.psum_scatter(
        jnp.dot(attended, w_attn_out, preferred_element_type=jnp.float32).astype(jnp.bfloat16),
        "tensor",
        scatter_dimension=0,
        tiled=True,
    ).astype(jnp.float32)
    mid = tokens_full + attn_rows
    inv_second = lax.rsqrt(jnp.mean(mid * mid, axis=-1, keepdims=True) + EPSILON)
    unit_second = mid * inv_second
    normed_mlp = spread_rows((unit_second * gain_mlp).astype(jnp.bfloat16))
    gate = jnp.dot(normed_mlp, w_gate, preferred_element_type=jnp.float32)
    up = jnp.dot(normed_mlp, w_up, preferred_element_type=jnp.float32)
    sigma = jax.nn.sigmoid(gate)
    active = gate * sigma
    hidden = (active * up).astype(jnp.bfloat16)
    mlp_rows = lax.psum_scatter(
        jnp.dot(hidden, w_down, preferred_element_type=jnp.float32).astype(jnp.bfloat16),
        "tensor",
        scatter_dimension=0,
        tiled=True,
    ).astype(jnp.float32)
    block_out = (row_keep * (mid + mlp_rows)).astype(jnp.bfloat16)
    out_full = row_keep * out_grad.astype(jnp.float32)
    grad_mlp = spread_grads(out_full.astype(jnp.bfloat16))
    g_down = jnp.einsum("rf,rd->fd", hidden, grad_mlp, preferred_element_type=jnp.float32)
    g_hidden = jnp.einsum("rd,fd->rf", grad_mlp, w_down, preferred_element_type=jnp.float32)
    d_gate = (g_hidden * up * sigma * (1.0 + gate * (1.0 - sigma))).astype(jnp.bfloat16)
    d_up = (g_hidden * active).astype(jnp.bfloat16)
    g_gate = jnp.einsum("rd,rf->df", normed_mlp, d_gate, preferred_element_type=jnp.float32)
    g_up = jnp.einsum("rd,rf->df", normed_mlp, d_up, preferred_element_type=jnp.float32)
    back_mlp = lax.psum_scatter(
        (
            jnp.einsum("rf,df->rd", d_gate, w_gate, preferred_element_type=jnp.float32)
            + jnp.einsum("rf,df->rd", d_up, w_up, preferred_element_type=jnp.float32)
        ).astype(jnp.bfloat16),
        "tensor",
        scatter_dimension=0,
        tiled=True,
    ).astype(jnp.float32)
    e_mlp = back_mlp * gain_mlp
    g_gain_mlp = jnp.sum(back_mlp * unit_second, axis=0)
    d_mid = out_full + inv_second * (
        e_mlp - unit_second * jnp.mean(e_mlp * unit_second, axis=-1, keepdims=True)
    )
    grad_attn = spread_grads(d_mid.astype(jnp.bfloat16))
    g_attn_out = jnp.einsum("rh,rd->hd", attended, grad_attn, preferred_element_type=jnp.float32)
    d_att = jnp.einsum(
        "rd,hd->rh", grad_attn, w_attn_out, preferred_element_type=jnp.float32
    ).astype(jnp.bfloat16)
    d_att = d_att.reshape(total_rows, local_heads, head_dim)
    query_pieces = []
    d_keys = jnp.zeros((total_rows, head_dim), jnp.float32)
    d_values = jnp.zeros((total_rows, head_dim), jnp.float32)
    for number in range(count):
        begin = number * block
        query_block = queries[begin : begin + block]
        grad_block = d_att[begin : begin + block]
        allowed = permitted(
            segment[begin : begin + block], row_steps[begin : begin + block], segment, row_steps
        )
        scores = (
            jnp.einsum("qhd,kd->hqk", query_block, keys, preferred_element_type=jnp.float32) * scale
        )
        scores = jnp.where(allowed[None], scores, MASKED)
        probs = jnp.exp(scores - log_totals[number])
        weights = probs.astype(jnp.bfloat16)
        d_probs = jnp.einsum("qhd,kd->hqk", grad_block, values, preferred_element_type=jnp.float32)
        inner = jnp.sum(d_probs * probs, axis=-1, keepdims=True)
        d_scores = (probs * (d_probs - inner)).astype(jnp.bfloat16)
        query_pieces.append(
            jnp.einsum("hqk,kd->qhd", d_scores, keys, preferred_element_type=jnp.float32) * scale
        )
        d_keys = (
            d_keys
            + jnp.einsum("hqk,qhd->kd", d_scores, query_block, preferred_element_type=jnp.float32)
            * scale
        )
        d_values = d_values + jnp.einsum(
            "hqk,qhd->kd", weights, grad_block, preferred_element_type=jnp.float32
        )
    d_queries = jnp.concatenate(query_pieces, axis=0)
    d_queries = unrotate(d_queries, cosine[:, None, :], sine[:, None, :]).astype(jnp.bfloat16)
    d_queries = d_queries.reshape(total_rows, local_heads * head_dim)
    g_query = jnp.einsum("rd,rh->dh", normed, d_queries, preferred_element_type=jnp.float32)
    kv_rows = lax.psum_scatter(
        jnp.concatenate([d_keys, d_values], axis=1).astype(jnp.bfloat16),
        "tensor",
        scatter_dimension=0,
        tiled=True,
    ).astype(jnp.float32)
    kv_rows = kv_rows + row_keep * kv_grad.astype(jnp.float32)
    d_kv = jnp.concatenate(
        [unrotate(kv_rows[:, :head_dim], row_cosine, row_sine), kv_rows[:, head_dim:]], axis=1
    ).astype(jnp.bfloat16)
    d_kv_all = lax.all_gather(d_kv, "tensor", axis=0, tiled=True)
    width = normed.shape[1]
    groups = lax.axis_size("dp")
    own = lax.dynamic_index_in_dim(
        normed.reshape(total_rows, groups, parts, width // (groups * parts)),
        lax.axis_index("tensor"),
        2,
        False,
    ).reshape(total_rows, width // parts)
    g_kv = jnp.einsum("rd,rk->dk", own, d_kv_all, preferred_element_type=jnp.float32)
    back_attn = lax.psum_scatter(
        jnp.einsum("rh,dh->rd", d_queries, w_query, preferred_element_type=jnp.float32).astype(
            jnp.bfloat16
        ),
        "tensor",
        scatter_dimension=0,
        tiled=True,
    ).astype(jnp.float32)
    back_attn = back_attn + jnp.einsum("rk,dk->rd", d_kv, w_kv, preferred_element_type=jnp.float32)
    e_attn = back_attn * gain_attn
    g_gain_attn = jnp.sum(back_attn * unit_first, axis=0)
    grad_tokens = (
        d_mid
        + inv_first * (e_attn - unit_first * jnp.mean(e_attn * unit_first, axis=-1, keepdims=True))
    ).astype(jnp.bfloat16)
    kv_sum = lax.psum_scatter(g_kv, "dp", scatter_dimension=0, tiled=True)
    share = width // (groups * parts)
    first = (lax.axis_index("dp") * parts + lax.axis_index("tensor")) * share
    gain_all = lax.all_gather(jnp.stack([g_gain_attn, g_gain_mlp]), ("dp", "tensor"), axis=0)
    gain_sums = jnp.sum(lax.dynamic_slice_in_dim(gain_all, first, share, 2), axis=0)
    query_sum, out_sum, gate_sum, up_sum, down_sum = (
        lax.psum_scatter(
            g_query.astype(jnp.bfloat16), "dp", scatter_dimension=0, tiled=True
        ).astype(jnp.float32),
        lax.psum_scatter(
            g_attn_out.astype(jnp.bfloat16), "dp", scatter_dimension=1, tiled=True
        ).astype(jnp.float32),
        lax.psum_scatter(g_gate.astype(jnp.bfloat16), "dp", scatter_dimension=0, tiled=True).astype(
            jnp.float32
        ),
        lax.psum_scatter(g_up.astype(jnp.bfloat16), "dp", scatter_dimension=0, tiled=True).astype(
            jnp.float32
        ),
        lax.psum_scatter(g_down.astype(jnp.bfloat16), "dp", scatter_dimension=1, tiled=True).astype(
            jnp.float32
        ),
    )
    return (
        block_out,
        grad_tokens,
        gain_sums[0],
        query_sum,
        kv_sum,
        out_sum,
        gain_sums[1],
        gate_sum,
        up_sum,
        down_sum,
    )


F32, BF16 = jnp.float32, jnp.bfloat16
MESH = pl.DeviceIdType.MESH
MIB = 1 << 20


def dot(a, b):
    return jnp.dot(a, b, preferred_element_type=F32)


def dot_rows(a, b):
    return lax.dot_general(a, b, (((1,), (1,)), ((), ())), preferred_element_type=F32)


def dot_cols(a, b):
    return lax.dot_general(a, b, (((0,), (0,)), ((), ())), preferred_element_type=F32)


def tiles(width, step):
    return [(at, min(step, width - at)) for at in range(0, width, step)]


GN, GG, GM, GA = range(4)
RO, RB, RD, RQ = range(4)
LEN, TOK, TOK2, WQ, OG, KVG, WO, WG, WU, WD, BO, BO2, GT, GT2 = range(14)
DOWN, GATE, UP, OUT, QUERY = GRADS = range(5)


def semaphores(nz):
    counts = dict(
        swap=14,
        swap_y=14,
        gz=4 * 4 * nz,
        gc=4 * 2 * nz,
        rz=4 * 4 * nz,
        rc=4 * nz,
        stage=20,
        px=20,
        pc=20,
        py=5,
        ld=20,
        st=5,
        kc=nz,
        kz=nz,
        ka=2 * nz,
        kyx=2,
        gains=8 + nz,
        spill=2,
        outs=4,
    )
    firsts, total = {}, 0
    for name, count in counts.items():
        firsts[name] = total
        total += count
    return types.SimpleNamespace(**firsts), total


def block_kernel(nz, pieces, S, R):
    rows, width = R.tokens.shape
    ff = R.w_down.shape[0]
    total = 2 * nz * rows
    pair = 2 * rows
    head = 128
    heads = R.wq.shape[1] // head
    scale = head ** (-0.5)
    DS, DR = R.send, R.recv

    dp, tensor = lax.axis_index("dp"), lax.axis_index("tensor")
    y, c = dp // 2, dp % 2
    z, x = tensor // 2, tensor % 2
    keeper = c == x

    def dev(yy, cc, zz, xx):
        return (2 * yy + cc, 2 * zz + xx)

    def flip(value, yes):
        return 1 - value if yes else value

    sibling = dev(y, 1 - c, z, x)
    partner = dev(y, 1 - c, z, 1 - x)
    across_x = dev(y, c, z, 1 - x)
    across_y = dev(1 - y, c, z, x)

    def send(src, dst, s, r, to):
        return pltpu.make_async_remote_copy(
            src_ref=src,
            dst_ref=dst,
            send_sem=DS.at[s],
            recv_sem=DR.at[r],
            device_id=to,
            device_id_type=MESH,
        )

    def arrived(dst, r):
        pltpu.make_async_copy(dst, dst, DR.at[r]).wait()

    def sent(src, s):
        pltpu.make_async_copy(src, src, DS.at[s]).wait()

    barrier = pltpu.get_barrier_semaphore()
    around = {
        (dy, dc, dx): dev(flip(y, dy), flip(c, dc), z, flip(x, dx))
        for dy in range(2)
        for dc in range(2)
        for dx in range(2)
        if dy + dc + dx
    }
    for (dy, dc, dx), to in around.items():
        if dy + dx:
            pl.semaphore_signal(barrier, inc=1, device_id=to, device_id_type=MESH)
    for zz in range(nz):
        for cc in range(2):

            @pl.when((zz != z) | (cc != c))
            def _():
                pl.semaphore_signal(
                    barrier, inc=1, device_id=dev(y, cc, zz, x), device_id_type=MESH
                )

    pl.semaphore_wait(barrier, 6 + 2 * nz - 1)

    def swap_start(item, src, dst):
        at = S.swap + item

        @pl.when(keeper)
        def _():
            pltpu.make_async_copy(src, dst, DR.at[at]).start()

        @pl.when(jnp.logical_not(keeper))
        def _():
            send(src, dst, at, at, partner).start()

    def swap_wait(item, dst):
        arrived(dst, S.swap + item)

    def swap_sent(item, src):
        @pl.when(jnp.logical_not(keeper))
        def _():
            sent(src, S.swap + item)

    def part_at(ref, which):
        count = ref.shape[0] // 2
        return ref.at[pl.ds(pl.multiple_of(which * count, count), count)]

    def weight_start(item, src, dst):
        at = S.swap + item

        @pl.when(keeper)
        def _():
            pltpu.make_async_copy(src, dst, DR.at[at]).start()

        @pl.when(jnp.logical_not(keeper))
        def _():
            send(part_at(src, y), part_at(dst, y), at, at, partner).start()

    def weight_pass(item, dst):
        @pl.when(jnp.logical_not(keeper))
        def _():
            half_here = part_at(dst, y)
            arrived(half_here, S.swap + item)
            send(half_here, half_here, S.swap_y + item, S.swap_y + item, across_y).start()

    def weight_wait(item, dst):
        @pl.when(keeper)
        def _():
            arrived(dst, S.swap + item)

        @pl.when(jnp.logical_not(keeper))
        def _():
            arrived(part_at(dst, 1 - y), S.swap_y + item)

    def weight_sent(item, src, dst):
        @pl.when(jnp.logical_not(keeper))
        def _():
            sent(part_at(src, y), S.swap + item)
            sent(part_at(dst, y), S.swap_y + item)

    def piece(ref, chunk, core):
        return ref.at[pl.ds(pl.multiple_of((2 * chunk + core) * rows, rows), rows)]

    def chunk_rows(chunk):
        return pl.ds(pl.multiple_of(chunk * pair, pair), pair)

    own_at = pl.multiple_of((2 * z + c) * rows, rows)

    def bit(ref, chunk, core, part):
        count = rows // 2
        first = (2 * chunk + core) * rows + part * count
        return ref.at[pl.ds(pl.multiple_of(first, count), count)]

    def gather_sem(base, name, way, chunk, part):
        return base + ((2 * name + way) * nz + chunk) * 2 + part

    def core_sem(name, chunk, part):
        return S.gc + (name * nz + chunk) * 2 + part

    def gather_hop(name, ref, way, chunk, part):
        some = bit(ref, chunk, c, part)
        to = dev(y, c, z + 1 - 2 * way, x)
        send(
            some,
            some,
            gather_sem(S.gz, name, way, chunk, part),
            gather_sem(S.gz, name, 0, chunk, part),
            to,
        ).start()

    def gather_share(name, ref, chunk, part):
        some = bit(ref, chunk, c, part)
        at = core_sem(name, chunk, part)
        send(some, some, at, at, sibling).start()

    def gather_start(name, ref, parts=(0, 1)):
        for part in parts:

            @pl.when(z < nz - 1)
            def _():
                gather_hop(name, ref, 0, z, part)

            @pl.when(z > 0)
            def _():
                gather_hop(name, ref, 1, z, part)

            gather_share(name, ref, z, part)

    def gather_pass(name, ref, step):
        for part in range(2):
            for way in range(2):
                chunk = z - 1 - step if way == 0 else z + 1 + step

                @pl.when((chunk >= 0) & (chunk <= nz - 1))
                def _():
                    arrived(bit(ref, chunk, c, part), gather_sem(S.gz, name, 0, chunk, part))

                    @pl.when(z < nz - 1 if way == 0 else z > 0)
                    def _():
                        gather_hop(name, ref, way, chunk, part)

                    gather_share(name, ref, chunk, part)

    def gather_theirs(name, ref, chunk):
        for part in range(2):
            arrived(bit(ref, chunk, 1 - c, part), core_sem(name, chunk, part))

    def gather_own(name, ref, work):
        gather_theirs(name, ref, z)
        if work is not None:
            work(z)

    def gather_use(name, ref, step, work):
        for way in range(2):
            chunk = z - 1 - step if way == 0 else z + 1 + step

            @pl.when((chunk >= 0) & (chunk <= nz - 1))
            def _():
                gather_theirs(name, ref, chunk)
                if work is not None:
                    work(chunk)

    def gather_end(name, ref):
        for chunk in range(nz):
            for part in range(2):
                some = bit(ref, chunk, c, part)
                sent(some, core_sem(name, chunk, part))

                @pl.when((z < nz - 1) & (chunk <= z))
                def _():
                    sent(some, gather_sem(S.gz, name, 0, chunk, part))

                @pl.when((z > 0) & (chunk >= z))
                def _():
                    sent(some, gather_sem(S.gz, name, 1, chunk, part))

    def terms(name):
        return R.nmlp if name == RQ else R.part

    def half(name, chunk, core):
        return piece(terms(name), chunk, core)

    def core_room(name, chunk):
        room = R.wg if name == RQ else R.from_core
        return room.at[pl.ds(pl.multiple_of(chunk * rows, rows), rows)]

    def z_slot(name, way, chunk, at, part):
        slot = jnp.where((way == 1) & (chunk == at), nz, chunk)
        count = rows // 2
        return R.from_z.at[name % 2, slot, pl.ds(part * count, count)]

    def add_rows(dst, *sources):
        step = 32

        @pl.loop(0, dst.shape[0] // step)
        def _(i):
            at = pl.ds(pl.multiple_of(i * step, step), step)
            value = sources[0][at, :].astype(F32)
            for source in sources[1:]:
                value = value + source[at, :].astype(F32)
            dst[at, :] = value.astype(dst.dtype)

    def scatter_term(name, chunk, work):
        work(chunk)
        send(
            half(name, chunk, 1 - c),
            core_room(name, chunk),
            S.rc + nz * name + chunk,
            S.rc + nz * name + chunk,
            sibling,
        ).start()

    def scatter_forward(name, way, chunk):
        arrived(core_room(name, chunk), S.rc + nz * name + chunk)
        earlier = ((way == 0) & (z > 0)) | ((way == 1) & (z < nz - 1))
        to = z + 1 - 2 * way
        for part in range(2):
            mine = bit(terms(name), chunk, c, part)
            theirs = core_room(name, chunk).at[part * (rows // 2) : (part + 1) * (rows // 2)]
            before = z_slot(name, way, chunk, z, part)
            at = gather_sem(S.rz, name, way, chunk, part)

            @pl.when(earlier)
            def _():
                arrived(before, at)
                add_rows(mine, mine, theirs, before)

            @pl.when(jnp.logical_not(earlier))
            def _():
                add_rows(mine, mine, theirs)

            send(mine, z_slot(name, way, chunk, to, part), at, at, dev(y, c, to, x)).start()

    def between(index):
        way, chunk, valid = 0, 0, False
        for at in range(1, nz - 1):
            hops = [(other + at / 2, 0, other) for other in range(at + 1, nz)]
            hops += [(nz - 1 - other + (nz - 1 - at) / 2, 1, other) for other in range(at)]
            _, this_way, this_chunk = sorted(hops)[index]
            way = jnp.where(z == at, this_way, way)
            chunk = jnp.where(z == at, this_chunk, chunk)
            valid = valid | (z == at)
        return way, chunk, valid

    def scatter_slot(step, way):
        if way == 0:
            chunk = nz - 1 + z - step
            return chunk, (step >= z) & (z < nz - 1)
        chunk = step - (nz - 1 - z)
        return chunk, (chunk >= 0) & (z > 0)

    def scatter_step(name, step, work):
        for way in range(2):
            chunk, valid = scatter_slot(step, way)

            @pl.when(valid)
            def _():
                scatter_term(name, chunk, work)

        for way in range(2):
            chunk, valid = scatter_slot(step, way)

            @pl.when(valid)
            def _():
                scatter_forward(name, way, chunk)

    def scatter_end(name, finish):
        arrived(core_room(name, z), S.rc + nz * name + z)
        for part in range(2):
            some = pl.ds(part * (rows // 2), rows // 2)
            add_rows(R.acc.at[some], half(name, z, c).at[some], core_room(name, z).at[some])
            for way in range(2):

                @pl.when(z > 0 if way == 0 else z < nz - 1)
                def _():
                    before = z_slot(name, way, z, z, part)
                    arrived(before, gather_sem(S.rz, name, way, z, part))
                    add_rows(R.acc.at[some], R.acc.at[some], before)

            finish(part)

    def scatter_sent(name):
        for chunk in range(nz):
            sent(half(name, chunk, 1 - c), S.rc + nz * name + chunk)
            for way in range(2):
                for part in range(2):

                    @pl.when(z < chunk if way == 0 else z > chunk)
                    def _():
                        sent(
                            bit(terms(name), chunk, c, part),
                            gather_sem(S.rz, name, way, chunk, part),
                        )

    def each_rows(body, part, step=32):
        @pl.loop(0, rows // 2 // step)
        def _(i):
            body(pl.multiple_of(part * (rows // 2) + i * step, step), step)

    def keep_of(first, count):
        index = lax.broadcasted_iota(jnp.int32, (count, 1), 0) + (own_at + first)
        return (index.astype(F32) < R.last[0:1, 0:1]).astype(F32)

    def rotary():
        units = R.len[...] * 64.0
        ends, end = [], jnp.zeros((1, 128), F32)
        for p in range(pieces):
            end = end + units[p : p + 1, :]
            ends.append((units[p : p + 1, :], end))
        R.last[...] = jnp.broadcast_to(ends[-2][1], (8, 128))

        @pl.loop(0, total // 128)
        def _(i):
            at = pl.ds(pl.multiple_of(i * 128, 128), 128)
            index = (lax.broadcasted_iota(jnp.int32, (128, 128), 0) + i * 128).astype(F32)
            start = jnp.zeros((128, 128), F32)
            for length, stop in ends[:-1]:
                start = start + jnp.where(stop <= index, length, 0.0)
            R.start[at, :] = start
            angle = (index - start) * R.freq[0:1, :]
            lane = lax.broadcasted_iota(jnp.int32, (128, 128), 1)
            R.cos[at, :] = jnp.cos(angle)
            R.sin[at, :] = jnp.where(lane < 64, -1.0, 1.0) * jnp.sin(angle)

    def turn(value, cosine, sine):
        swapped = jnp.concatenate([value[:, 64:], value[:, :64]], axis=1)
        return value * cosine + swapped * sine

    def project(chunk):
        at = chunk_rows(chunk)
        normed = R.norm[at, :]
        cosine, sine = R.cos[at, :], R.sin[at, :]
        queries = dot(normed, R.wq[...])
        for h in range(heads):
            cols = slice(h * head, (h + 1) * head)
            R.q[at, cols] = turn(queries[:, cols], cosine, sine).astype(BF16)
        kv = dot(normed, R.wkv[...])
        R.kv[at, :head] = turn(kv[:, :head], cosine, sine).astype(BF16)
        R.kv[at, head:] = kv[:, head:].astype(BF16)

    def attend(chunk):
        at = chunk_rows(chunk)
        keys, values = R.kv[:, :head], R.kv[:, head:]
        start = R.start[at, 0:1]
        column = lax.broadcasted_iota(jnp.int32, (pair, total), 1).astype(F32)
        row = (lax.broadcasted_iota(jnp.int32, (pair, 1), 0) + chunk * pair).astype(F32)
        allowed = (column >= start) & (column <= row)
        for h in range(heads):
            cols = slice(h * head, (h + 1) * head)
            scores = dot_rows(R.q[at, cols], keys) * scale
            scores = jnp.where(allowed, scores, -1e30)
            exps = jnp.exp(scores - jnp.max(scores, axis=1, keepdims=True))
            weights = exps * (1.0 / jnp.sum(exps, axis=1, keepdims=True))
            weights = weights.astype(BF16)
            R.probs[h, at, :] = weights
            R.att[at, cols] = dot(weights, values).astype(BF16)

    def out_term(chunk):
        attend(chunk)
        at = chunk_rows(chunk)
        for n, size in tiles(width, 512):
            R.part[at, n : n + size] = dot(
                R.att[at, :], R.wo[:, n : n + size]
            ).astype(BF16)

    def mlp(chunk):
        at = chunk_rows(chunk)
        for n, size in tiles(ff, 256):
            cols = slice(n, n + size)
            gate = dot_rows(R.nmlp[at, :], R.wg[cols, :])
            up = dot_rows(R.nmlp[at, :], R.wu[cols, :])
            grad = dot_rows(R.gmlp[at, :], R.wd[cols, :])
            sigma = 1.0 / (1.0 + jnp.exp(-gate))
            active = gate * sigma
            R.hid[at, cols] = (active * up).astype(BF16)
            R.dup[at, cols] = (grad * active).astype(BF16)
            R.dgate[at, cols] = (grad * up * (sigma * (1.0 + gate * (1.0 - sigma)))).astype(BF16)

    def back_term(chunk):
        at = chunk_rows(chunk)
        for n, size in tiles(width, 512):
            some = slice(n, n + size)
            R.part[at, some] = (
                dot(R.dgate[at, :], R.wg[:, some]) + dot(R.dup[at, :], R.wu[:, some])
            ).astype(BF16)

    def down_term(chunk):
        at = chunk_rows(chunk)
        for n, size in tiles(width, 512):
            some = slice(n, n + size)
            R.part[at, some] = dot(R.hid[at, :], R.wd[:, some]).astype(BF16)

    def d_attended(chunk):
        at = chunk_rows(chunk)
        R.datt[at, :] = dot_rows(R.norm[at, :], R.wo[...]).astype(BF16)
        backward_attend(chunk)

    def backward_attend(chunk):
        at = chunk_rows(chunk)
        keys, values = R.kv[:, :head], R.kv[:, head:]
        cosine, sine = R.cos[at, :], R.sin[at, :]
        for h in range(heads):
            cols = slice(h * head, (h + 1) * head)
            weights = R.probs[h, at, :]
            probs = weights.astype(F32)
            grad = R.datt[at, cols]
            d_probs = dot_rows(grad, values)
            inner = jnp.sum(d_probs * probs, axis=1, keepdims=True)
            d_scores = (probs * (d_probs - inner)).astype(BF16)
            d_queries = dot(d_scores, keys) * scale
            R.dq[at, cols] = turn(d_queries, cosine, -sine).astype(BF16)
            R.dkv[:, :head] += dot_cols(d_scores, R.q[at, cols]) * scale
            R.dkv[:, head:] += dot_cols(weights, grad)

    def query_term(chunk):
        at = chunk_rows(chunk)
        for n, size in tiles(width, 512):
            some = slice(n, n + size)
            terms(RQ)[at, some] = dot_rows(R.dq[at, :], R.wq[some, :]).astype(BF16)

    Y_FIRST = (GATE, OUT)

    def grad_send(name, yy, cc):
        quarter = 2 * yy + cc
        stage = R.stage[name].at[quarter]
        if name in Y_FIRST:
            at = S.px + 4 * name + cc

            @pl.when(yy != y)
            def _():
                send(stage, R.px[name].at[cc], at, at, across_y).start()

            return
        into_x, into_c = R.px[name].at[yy], R.pc[name].at[yy]

        @pl.when(jnp.logical_not(keeper))
        def _():
            send(
                stage,
                into_x,
                S.px + 4 * name + quarter,
                S.px + 4 * name + yy,
                (2 * y + cc, 2 * z + 1 - x),
            ).start()

        @pl.when(keeper & (c == cc))
        def _():
            pltpu.make_async_copy(stage, into_c, DR.at[S.pc + 4 * name + yy]).start()

        @pl.when(keeper & (c != cc))
        def _():
            send(
                stage, into_c, S.pc + 4 * name + quarter, S.pc + 4 * name + yy, sibling
            ).start()

    def grad_sent(name, yy, cc):
        quarter = 2 * yy + cc
        stage = R.stage[name].at[quarter]
        if name in Y_FIRST:

            @pl.when(yy != y)
            def _():
                sent(stage, S.px + 4 * name + cc)

            return

        @pl.when(jnp.logical_not(keeper))
        def _():
            sent(stage, S.px + 4 * name + quarter)

        @pl.when(keeper & (c != cc))
        def _():
            sent(stage, S.pc + 4 * name + quarter)

    QUARTERS = [(0, 0), (0, 1), (1, 0), (1, 1)]

    def grad_make(name, left, right):
        split_left = name == QUERY
        quarter_cols = (left if split_left else right).shape[1] // 4
        tile = R.tile[name]
        for index, (yy, cc) in enumerate(QUARTERS):
            first = index * quarter_cols
            if index > 1:
                pltpu.make_async_copy(
                    tile.at[index % 2],
                    R.stage[name].at[index - 2],
                    DR.at[S.stage + 4 * name + index - 2],
                ).wait()
                grad_send(name, *QUARTERS[index - 2])
            if split_left:
                for m, size in tiles(quarter_cols, 256):
                    tile[index % 2, m : m + size, :] = dot_cols(
                        left[:, first + m : first + m + size], right[...]
                    ).astype(BF16)
            else:
                for m, size in tiles(left.shape[1], 256):
                    tile[index % 2, m : m + size, :] = dot_cols(
                        left[:, m : m + size], right[:, first : first + quarter_cols]
                    ).astype(BF16)
            pltpu.make_async_copy(
                tile.at[index % 2],
                R.stage[name].at[index],
                DR.at[S.stage + 4 * name + index],
            ).start()
        for index in (2, 3):
            pltpu.make_async_copy(
                tile.at[index % 2],
                R.stage[name].at[index],
                DR.at[S.stage + 4 * name + index],
            ).wait()
            grad_send(name, *QUARTERS[index])

    def sum_room(name, cc=0):
        cols = width // 4
        if name == QUERY:
            return R.wd.at[0:cols, 2 * cols : 2 * cols + R.wq.shape[1]]
        if name == DOWN:
            return R.wu.at[:, 2 * cols : 3 * cols]
        if name == UP:
            return R.wu.at[:, 3 * cols :]
        if name == GATE:
            return R.wd.at[:, cc * cols : (cc + 1) * cols]
        count = R.wo.shape[0]
        return R.wd.at[cc * count : (cc + 1) * count, 3 * cols :]

    def grad_places(name):
        count, cols = R.tile[name].shape[1:]
        return (
            (R.tile[name].at[0], R.tile[name].at[1]),
            (R.wu.at[0:count, 0:cols], R.wu.at[0:count, cols : 2 * cols]),
        )

    def grad_loads(name, turn_at, sources):
        loads = []
        for k, source in enumerate(sources):
            load = pltpu.make_async_copy(
                source,
                grad_places(name)[turn_at][k],
                DR.at[S.ld + 4 * name + 2 * turn_at + k],
            )
            load.start()
            loads.append(load)
        return loads

    def grad_mid(name):
        loads = []
        for cc in range(2):
            arrived(R.px[name].at[cc], S.px + 4 * name + cc)
            loads.append(
                grad_loads(name, cc, (R.px[name].at[cc], R.stage[name].at[2 * y + cc]))
            )
        for cc in range(2):
            for load in loads[cc]:
                load.wait()
            into = sum_room(name, cc)
            add_rows(into, *grad_places(name)[cc])
            at = S.pc + 4 * name + cc

            @pl.when(jnp.logical_not(keeper))
            def _():
                send(
                    into, R.other[name], at, S.py + name, (2 * y + cc, 2 * z + 1 - x)
                ).start()

            @pl.when(keeper & (c == cc))
            def _():
                pltpu.make_async_copy(into, R.mine[name], DR.at[S.st + name]).start()

            @pl.when(keeper & (c != cc))
            def _():
                send(into, R.mine[name], at, S.st + name, sibling).start()

    def grad_add(name):
        loads = []
        for turn_at, yy in enumerate((1 - y, y)):
            arrived(R.px[name].at[yy], S.px + 4 * name + yy)
            arrived(R.pc[name].at[yy], S.pc + 4 * name + yy)
            loads.append(grad_loads(name, turn_at, (R.px[name].at[yy], R.pc[name].at[yy])))
        for turn_at in range(2):
            for load in loads[turn_at]:
                load.wait()
            one, two = grad_places(name)[turn_at]
            if turn_at == 0:
                into = sum_room(name)
                add_rows(into, one, two)
                send(into, R.other[name], S.py + name, S.py + name, across_y).start()
            else:
                add_rows(one, one, two)
                store = pltpu.make_async_copy(one, R.mine[name], DR.at[S.st + name])
                store.start()
                store.wait()

    R.own_len[...] = jnp.zeros((8, 128), F32)
    for p in range(pieces):
        R.own_len[p : p + 1, :] = jnp.broadcast_to(R.lengths[0:1, p : p + 1].astype(F32), (1, 128))
    swap_start(LEN, R.own_len, R.len)
    for part in range(2):
        swap_start(TOK + part, part_at(R.tokens, part), part_at(R.tok, part))
    weight_start(WQ, R.w_query, R.wq)
    swap_start(OG, R.out_grad, R.og)
    swap_start(KVG, R.kv_grad, R.kvg)

    def norm_rows(first, count):
        at = pl.ds(first, count)
        value = R.tok[at, :].astype(F32)
        inverse = lax.rsqrt(jnp.mean(value * value, axis=1, keepdims=True) + EPSILON)
        R.norm[pl.ds(own_at + first, count), :] = (
            value * inverse * R.gain_attn[0:1, :]
        ).astype(BF16)

    for part in range(2):
        swap_wait(TOK + part, part_at(R.tok, part))
        each_rows(norm_rows, part)
        gather_start(GN, R.norm, (part,))
    swap_wait(LEN, R.len)
    weight_start(WO, R.w_attn_out, R.wo)
    rotary()
    weight_pass(WQ, R.wq)
    weight_wait(WQ, R.wq)
    gather_own(GN, R.norm, project)

    def mask_rows(first, count):
        at = pl.ds(first, count)
        R.gmlp[pl.ds(own_at + first, count), :] = (
            keep_of(first, count) * R.og[at, :].astype(F32)
        ).astype(BF16)

    for step in range(nz - 1):
        gather_pass(GN, R.norm, step)
        if step == 0:
            weight_pass(WO, R.wo)
            weight_start(WG, R.w_gate, R.wg)
            swap_wait(OG, R.og)
            swap_wait(KVG, R.kvg)
            for part in range(2):
                each_rows(mask_rows, part)
        if step == 1:
            weight_start(WU, R.w_up, R.wu)
        if step == nz - 2:
            gather_start(GG, R.gmlp)
            weight_pass(WG, R.wg)
            weight_start(WD, R.w_down, R.wd)
        gather_use(GN, R.norm, step, project)
    spill = pltpu.make_async_copy(R.norm, R.norm_store, DR.at[S.spill])
    spill.start()
    weight_wait(WO, R.wo)

    for step in range(nz - 1):
        scatter_step(RO, step, out_term)
        gather_pass(GG, R.gmlp, step)
        if step == 0:
            weight_pass(WU, R.wu)
        if step == 1:
            weight_pass(WD, R.wd)
    scatter_term(RO, z, out_term)

    def mid_rows(first, count):
        at = pl.ds(first, count)
        mid = R.tok[at, :].astype(F32) + R.acc[at, :]
        R.mid[at, :] = mid
        inverse = lax.rsqrt(jnp.mean(mid * mid, axis=1, keepdims=True) + EPSILON)
        R.nmlp[pl.ds(own_at + first, count), :] = (
            mid * inverse * R.gain_mlp[0:1, :]
        ).astype(BF16)

    def mid_done(part):
        each_rows(mid_rows, part)
        gather_start(GM, R.nmlp, (part,))

    scatter_end(RO, mid_done)
    for step in range(nz - 1):
        gather_use(GG, R.gmlp, step, None)
    gather_own(GG, R.gmlp, None)
    scatter_sent(RO)
    gather_end(GN, R.norm)
    spill.wait()
    weight_wait(WG, R.wg)
    weight_wait(WU, R.wu)
    weight_wait(WD, R.wd)
    def mlp_and_back(chunk):
        mlp(chunk)
        scatter_term(RB, chunk, back_term)

    gather_own(GM, R.nmlp, mlp_and_back)
    for step in range(nz - 1):
        gather_pass(GM, R.nmlp, step)
        gather_use(GM, R.nmlp, step, mlp_and_back)

        @pl.when(z == 0)
        def _():
            scatter_forward(RB, 0, step + 1)

        @pl.when(z == nz - 1)
        def _():
            scatter_forward(RB, 1, nz - 2 - step)

    for item, src, dst in (
        (WQ, R.w_query, R.wq),
        (WO, R.w_attn_out, R.wo),
        (WG, R.w_gate, R.wg),
        (WU, R.w_up, R.wu),
        (WD, R.w_down, R.wd),
    ):
        weight_sent(item, src, dst)

    mlp_grads = ((DOWN, R.hid, R.gmlp), (GATE, R.dgate, R.nmlp), (UP, R.dup, R.nmlp))
    for index in range(nz - 1):
        if index < 2:
            grad_make(*mlp_grads[index])
        way, chunk, valid = between(index)

        @pl.when(valid)
        def _():
            scatter_forward(RB, way, chunk)

    grad_make(*mlp_grads[2])
    R.gains[...] = jnp.zeros(R.gains.shape, F32)

    def fold(value):
        return jnp.sum(value.reshape(value.shape[0] // 8, 8, value.shape[1]), axis=0)

    def d_mid_rows(first, count):
        at = pl.ds(first, count)
        mid = R.mid[at, :]
        inverse = lax.rsqrt(jnp.mean(mid * mid, axis=1, keepdims=True) + EPSILON)
        unit = mid * inverse
        back = R.acc[at, :]
        R.gains[1] += fold(back * unit)
        e = back * R.gain_mlp[0:1, :]
        grad = keep_of(first, count) * R.og[at, :].astype(F32) + inverse * (
            e - unit * jnp.mean(e * unit, axis=1, keepdims=True)
        )
        R.dmid[at, :] = grad
        R.norm[pl.ds(own_at + first, count), :] = grad.astype(BF16)

    def d_mid_done(part):
        each_rows(d_mid_rows, part)
        gather_start(GA, R.norm, (part,))

    scatter_end(RB, d_mid_done)
    scatter_sent(RB)
    gather_end(GG, R.gmlp)
    gather_end(GM, R.nmlp)
    back_norm = pltpu.make_async_copy(R.norm_store, R.gmlp, DR.at[S.spill + 1])
    back_norm.start()
    R.dkv[...] = jnp.zeros(R.dkv.shape, F32)
    def attend_and_query(chunk):
        d_attended(chunk)
        scatter_term(RQ, chunk, query_term)

    def down_forward(step):
        for way in range(2):
            chunk, valid = scatter_slot(step, way)

            @pl.when(valid)
            def _():
                scatter_forward(RD, way, chunk)

    gather_theirs(GA, R.norm, z)
    for chunk in range(nz):
        scatter_term(RD, chunk, down_term)
    down_forward(0)
    attend_and_query(z)
    for step in range(nz - 1):
        gather_pass(GA, R.norm, step)
        gather_use(GA, R.norm, step, attend_and_query)

        @pl.when(z == 0)
        def _():
            scatter_forward(RQ, 0, step + 1)

        @pl.when(z == nz - 1)
        def _():
            scatter_forward(RQ, 1, nz - 2 - step)

        if step == 1:
            grad_add(DOWN)

    R.dkvb[...] = R.dkv[...].astype(BF16)
    for zz in range(nz):
        send(piece(R.dkvb, zz, 1 - c), R.kc.at[zz], S.kc + zz, S.kc + zz, sibling).start()

    def kv_over_z():
        for zz in range(nz):
            arrived(R.kc.at[zz], S.kc + zz)
            R.ks[zz] = (
                R.dkv[pl.ds(pl.multiple_of((2 * zz + c) * rows, rows), rows), :]
                + R.kc[zz].astype(F32)
            ).astype(BF16)

            @pl.when(zz != z)
            def _():
                send(R.ks.at[zz], R.kz.at[z], S.kz + zz, S.kz + z, dev(y, c, zz, x)).start()

    own_rows = pl.ds(own_at, rows)
    own_kv = piece(R.dkva, z, c)

    def kv_own():
        R.kacc[...] = keep_of(0, rows) * R.kvg[...].astype(F32) + R.ks[z].astype(F32)
        for zz in range(nz):

            @pl.when(zz != z)
            def _():
                arrived(R.kz.at[zz], S.kz + zz)
                R.kacc[...] += R.kz[zz].astype(F32)

        R.dkva[own_rows, :head] = turn(
            R.kacc[:, :head], R.cos[own_rows, :], -R.sin[own_rows, :]
        ).astype(BF16)
        R.dkva[own_rows, head:] = R.kacc[:, head:].astype(BF16)
        for zz in range(nz):
            for cc in range(2):

                @pl.when((zz != z) | (cc != c))
                def _():
                    send(
                        own_kv, own_kv, S.ka + 2 * zz + cc, S.ka + 2 * z + c, dev(y, cc, zz, x)
                    ).start()

    def out_rows(first, count):
        at = pl.ds(first, count)
        R.bo[at, :] = (keep_of(first, count) * (R.mid[at, :] + R.acc[at, :])).astype(BF16)

    for step in range(1, nz - 2):
        down_forward(step)
    grad_make(OUT, R.att, R.norm)
    grad_mid(GATE)
    back_norm.wait()
    for index in range(nz - 1):
        way, chunk, valid = between(index)

        @pl.when(valid)
        def _():
            scatter_forward(RQ, way, chunk)

        if index == 0:
            kv_over_z()
            grad_add(UP)
            grad_make(QUERY, R.gmlp, R.dq)
        if index == 1:
            kv_own()
    down_forward(nz - 2)
    for zz in range(nz):
        for cc in range(2):

            @pl.when((zz != z) | (cc != c))
            def _():
                arrived(piece(R.dkva, zz, cc), S.ka + 2 * zz + cc)

    first_col = c * (4 * nz * 32) + z * 128
    for yy in range(2):
        cols = pl.ds(pl.multiple_of(yy * (width // 2) + first_col, 128), 128)
        R.gkv[yy] = dot_cols(R.gmlp[:, cols], R.dkva[...])
    send(
        R.gkv.at[1 - y], R.kyb, S.kyx, S.kyx, across_y
    ).start()
    arrived(R.kyb, S.kyx)
    R.kysum[...] = R.gkv[y] + R.kyb[...]
    send(
        R.kysum.at[pl.ds(pl.multiple_of((1 - x) * 64, 64), 64)],
        R.kxb,
        S.kyx + 1,
        S.kyx + 1,
        across_x,
    ).start()
    arrived(R.kxb, S.kyx + 1)
    R.kfinal[...] = (
        R.kysum[pl.ds(pl.multiple_of(x * 64, 64), 64), :] + R.kxb[...]
    )
    kv_out = pltpu.make_async_copy(R.kfinal, R.grad_w_kv, DR.at[S.outs])
    kv_out.start()
    for n, size in tiles(width, 512):
        some = slice(n, n + size)
        extra = dot_rows(R.dkva[own_rows, :], R.wkv[some, :])
        for m in range(n, n + size, 2 * head):
            at = m // (2 * head) * rows
            R.dkv[at : at + rows, :] = extra[:, m - n : m - n + 2 * head]
    grad_mid(OUT)
    grad_add(QUERY)

    def tail_rows(first, count):
        at = pl.ds(first, count)
        value = R.tok[at, :].astype(F32)
        inverse = lax.rsqrt(jnp.mean(value * value, axis=1, keepdims=True) + EPSILON)
        unit = value * inverse
        extra = [
            R.dkv[pl.ds(pl.multiple_of(m * rows + first, 32), count), :]
            for m in range(width // (2 * head))
        ]
        back = R.acc[at, :] + jnp.concatenate(extra, axis=1)
        R.gains[0] += fold(back * unit)
        e = back * R.gain_attn[0:1, :]
        R.gt[at, :] = (
            R.dmid[at, :]
            + inverse * (e - unit * jnp.mean(e * unit, axis=1, keepdims=True))
        ).astype(BF16)

    def tail_done(part):
        each_rows(tail_rows, part)
        swap_start(GT + part, part_at(R.gt, part), part_at(R.grad_tokens, part))

    scatter_end(RQ, tail_done)

    line = lax.broadcasted_iota(jnp.int32, (8, width), 0)
    gain_first = jnp.sum(R.gains[0], axis=0, keepdims=True)
    gain_second = jnp.sum(R.gains[1], axis=0, keepdims=True)
    R.ga[...] = jnp.where(line == 0, gain_first, jnp.where(line == 1, gain_second, 0.0))
    span = width // 4

    def gain_cols(yy, cc):
        return pl.ds(pl.multiple_of((2 * yy + cc) * span, span), span)

    def gain_send(index, offset):
        dy, dc, dx = offset
        return send(
            R.ga.at[:, gain_cols(flip(y, dy), flip(c, dc))],
            R.gb.at[index],
            S.gains + index,
            S.gains + index,
            around[offset],
        )

    for index, offset in enumerate(around):
        gain_send(index, offset).start()

    def out_done(part):
        each_rows(out_rows, part)
        swap_start(BO + part, part_at(R.bo, part), part_at(R.block_out, part))

    scatter_end(RD, out_done)
    R.ga_x[...] = R.ga[:, gain_cols(y, c)]
    for index in range(len(around)):
        arrived(R.gb.at[index], S.gains + index)
        R.ga_x[...] += R.gb[index]
    for zz in range(nz):

        @pl.when(zz != z)
        def _():
            send(
                R.ga_x.at[:, zz * 128 : (zz + 1) * 128],
                R.gb_z.at[z],
                S.gains + 8 + zz,
                S.gains + 8 + z,
                dev(y, c, zz, x),
            ).start()

    R.gfinal[...] = R.ga_x[:, pl.ds(pl.multiple_of(z * 128, 128), 128)]
    for zz in range(nz):

        @pl.when(zz != z)
        def _():
            arrived(R.gb_z.at[zz], S.gains + 8 + zz)
            R.gfinal[...] += R.gb_z[zz]

    gain_out = pltpu.make_async_copy(R.gfinal, R.grad_gains, DR.at[S.outs + 1])
    gain_out.start()

    for name in GRADS:
        arrived(R.other[name], S.py + name)
        if name in Y_FIRST:
            arrived(R.mine[name], S.st + name)
            for cc in range(2):

                @pl.when(jnp.logical_not(keeper & (c == cc)))
                def _():
                    sent(sum_room(name, cc), S.pc + 4 * name + cc)
        else:
            sent(sum_room(name), S.py + name)
        for yy, cc in QUARTERS:
            grad_sent(name, yy, cc)
    kv_out.wait()
    gain_out.wait()
    scatter_sent(RD)
    scatter_sent(RQ)
    gather_end(GA, R.norm)
    for part in range(2):
        swap_wait(BO + part, part_at(R.block_out, part))
        swap_wait(GT + part, part_at(R.grad_tokens, part))
    for item, src in (
        (LEN, R.own_len),
        (TOK, part_at(R.tokens, 0)),
        (TOK2, part_at(R.tokens, 1)),
        (OG, R.out_grad),
        (KVG, R.kv_grad),
        (BO, part_at(R.bo, 0)),
        (BO2, part_at(R.bo, 1)),
        (GT, part_at(R.gt, 0)),
        (GT2, part_at(R.gt, 1)),
    ):
        swap_sent(item, src)
    for zz in range(nz):
        sent(piece(R.dkvb, zz, 1 - c), S.kc + zz)

        @pl.when(zz != z)
        def _():
            sent(R.ks.at[zz], S.kz + zz)
            sent(R.ga_x.at[:, zz * 128 : (zz + 1) * 128], S.gains + 8 + zz)

        for cc in range(2):

            @pl.when((zz != z) | (cc != c))
            def _():
                sent(own_kv, S.ka + 2 * zz + cc)

    sent(R.gkv.at[1 - y], S.kyx)
    sent(R.kysum.at[pl.ds(pl.multiple_of((1 - x) * 64, 64), 64)], S.kyx + 1)
    for index, offset in enumerate(around):
        gain_send(index, offset).wait_send()


def fused(nz, *args):
    (tokens, lengths, gain_attn, w_query, w_kv, w_attn_out, gain_mlp, w_gate, w_up, w_down,
     out_grad, kv_grad) = args
    rows, width = tokens.shape
    ff = w_gate.shape[1]
    qw = w_query.shape[1]
    total, pair = 2 * nz * rows, 2 * rows
    pieces = lengths.shape[1]
    head = w_kv.shape[1] // 2
    half_width = head // 2
    freqs = (ROTARY_BASE ** (-np.arange(half_width, dtype=np.float32) / half_width)).astype(np.float32)
    freq = np.tile(np.concatenate([freqs, freqs])[None, :], (8, 1))
    anywhere, vmem = pl.BlockSpec(memory_space=pl.ANY), pl.BlockSpec(memory_space=pltpu.VMEM)
    ins = dict(
        tokens=(tokens, anywhere),
        lengths=(lengths, vmem),
        freq=(freq, vmem),
        gain_attn=(gain_attn[None], vmem),
        gain_mlp=(gain_mlp[None], vmem),
        w_query=(w_query, anywhere),
        wkv=(w_kv, vmem),
        w_attn_out=(w_attn_out, anywhere),
        w_gate=(w_gate.T, anywhere),
        w_up=(w_up.T, anywhere),
        w_down=(w_down, anywhere),
        out_grad=(out_grad, anywhere),
        kv_grad=(kv_grad, anywhere),
    )
    quarter = width // 4
    grad_tiles = [(ff, quarter), (ff, quarter), (ff, quarter), (qw, quarter), (quarter, qw)]
    outs = dict(
        block_out=((rows, width), BF16),
        grad_tokens=((rows, width), BF16),
        grad_w_kv=((64, 2 * head), F32),
        grad_gains=((8, 128), F32),
        norm_store=((total, width), BF16),
    )
    moved = [
        (shape, BF16)
        for tile in grad_tiles
        for shape in (tile, tile, (4,) + tile, (2,) + tile, (2,) + tile)
    ]
    S, count = semaphores(nz)
    scratch = dict(
        own_len=((8, 128), F32),
        len=((8, 128), F32),
        last=((8, 128), F32),
        tok=((rows, width), BF16),
        og=((rows, width), BF16),
        kvg=((rows, 2 * head), BF16),
        wq=((width, qw), BF16),
        wo=((qw, width), BF16),
        wg=((ff, width), BF16),
        wu=((ff, width), BF16),
        wd=((ff, width), BF16),
        norm=((total, width), BF16),
        nmlp=((total, width), BF16),
        gmlp=((total, width), BF16),
        cos=((total, 128), F32),
        sin=((total, 128), F32),
        start=((total, 128), F32),
        q=((total, qw), BF16),
        kv=((total, 2 * head), BF16),
        att=((total, qw), BF16),
        datt=((total, qw), BF16),
        dq=((total, qw), BF16),
        probs=((qw // head, total, total), BF16),
        hid=((total, ff), BF16),
        dgate=((total, ff), BF16),
        dup=((total, ff), BF16),
        part=((total, width), BF16),
        from_core=((nz * rows, width), BF16),
        from_z=((2, nz + 1, rows, width), BF16),
        acc=((rows, width), F32),
        mid=((rows, width), F32),
        dmid=((rows, width), F32),
        bo=((rows, width), BF16),
        gt=((rows, width), BF16),
        gains=((2, 8, width), F32),
        ga=((8, width), F32),
        ga_x=((8, width // 4), F32),
        gb=((7, 8, width // 4), F32),
        gb_z=((nz, 8, 128), F32),
        gfinal=((8, 128), F32),
        dkv=((total, 2 * head), F32),
        dkvb=((total, 2 * head), BF16),
        dkva=((total, 2 * head), BF16),
        kc=((nz, rows, 2 * head), BF16),
        ks=((nz, rows, 2 * head), BF16),
        kz=((nz, rows, 2 * head), BF16),
        kacc=((rows, 2 * head), F32),
        gkv=((2, 128, 2 * head), F32),
        kyb=((128, 2 * head), F32),
        kysum=((128, 2 * head), F32),
        kxb=((64, 2 * head), F32),
        kfinal=((64, 2 * head), F32),
    )
    tile_shapes = (grad_tiles[DOWN], grad_tiles[OUT], grad_tiles[QUERY])
    out_shapes = list(outs.values()) + moved
    scratch_shapes = list(scratch.values()) + [((2,) + shape, BF16) for shape in tile_shapes]

    def body(*refs):
        refs = list(refs)

        def take(count):
            taken = refs[:count]
            del refs[:count]
            return taken

        R = types.SimpleNamespace(
            **dict(zip(ins, take(len(ins)))), **dict(zip(outs, take(len(outs))))
        )
        rest = take(len(moved))
        R.mine, R.other, R.stage, R.px, R.pc = (rest[k::5] for k in range(5))
        for key, ref in zip(scratch, take(len(scratch))):
            setattr(R, key, ref)
        big, out_tile, query_tile = take(3)
        R.tile = [big, big, big, out_tile, query_tile]
        R.send, R.recv = refs
        block_kernel(nz, pieces, S, R)

    results = pl.pallas_call(
        body,
        out_shape=[jax.ShapeDtypeStruct(shape, kind) for shape, kind in out_shapes],
        in_specs=[spec for _, spec in ins.values()],
        out_specs=[anywhere] * len(out_shapes),
        scratch_shapes=[pltpu.VMEM(shape, kind) for shape, kind in scratch_shapes]
        + [pltpu.SemaphoreType.DMA((count,))] * 2,
        compiler_params=pltpu.CompilerParams(
            collective_id=0, has_side_effects=True, vmem_limit_bytes=63 * MIB
        ),
        name="block",
    )(*[value for value, _ in ins.values()])
    first = list(results[:4])
    mine, other = list(results[5::5]), list(results[6::5])

    def finish(*refs):
        ends, refs = refs[:4], refs[4:]
        one, two, refs = refs[:5], refs[5:10], refs[10:]
        for k in range(3):
            refs[k][...] = ends[k][...]
        right = (lax.axis_index("tensor") % 2) == 1
        for k in range(2):
            line = ends[3][k : k + 1, :]
            refs[3 + k][...] = jnp.where(right, line[:, 64:], line[:, :64])
        for k in GRADS:
            refs[5 + k][...] = one[k][...].astype(F32) + two[k][...].astype(F32)

    cuts = 4

    def cut(array):
        count = array.shape[0] // cuts
        return pl.BlockSpec((count, array.shape[1]), lambda i: (i, 0))

    whole = pl.BlockSpec((8, 128), lambda i: (0, 0))
    block_out, grad_tokens, grad_w_kv, gain_first, gain_second, *sums = pl.pallas_call(
        finish,
        grid=(cuts,),
        out_shape=[jax.ShapeDtypeStruct(array.shape, array.dtype) for array in first[:3]]
        + [jax.ShapeDtypeStruct((1, 64), F32)] * 2
        + [jax.ShapeDtypeStruct(array.shape, F32) for array in mine],
        in_specs=[cut(array) for array in first[:3]] + [whole] + [cut(a) for a in mine + other],
        out_specs=[cut(array) for array in first[:3]]
        + [pl.BlockSpec((1, 64), lambda i: (0, 0))] * 2
        + [cut(array) for array in mine],
        compiler_params=pltpu.CompilerParams(vmem_limit_bytes=63 * MIB),
        name="finish",
    )(*first, *mine, *other)
    return (
        block_out,
        grad_tokens,
        gain_first[0],
        sums[QUERY],
        grad_w_kv,
        sums[OUT],
        gain_second[0],
        sums[GATE].T,
        sums[UP].T,
        sums[DOWN],
    )


def solution(mesh):
    groups, parts = mesh.shape["dp"], mesh.shape["tensor"]
    paired = groups == 4 and parts == 8
    per_group = functools.partial(fused, parts // 2) if paired else per_device
    placed = (
        P(("dp", "tensor"), None),
        P("dp", None),
        P(),
        P(None, "tensor"),
        P(),
        P("tensor", None),
        P(),
        P(None, "tensor"),
        P(None, "tensor"),
        P("tensor", None),
        P(("dp", "tensor"), None),
        P(("dp", "tensor"), None),
    )
    return jax.shard_map(
        per_group,
        mesh=mesh,
        in_specs=placed,
        out_specs=(
            P(("dp", "tensor"), None),
            P(("dp", "tensor"), None),
            P(("dp", "tensor")),
            P("dp", "tensor"),
            P(("dp", "tensor"), None),
            P("tensor", "dp"),
            P(("dp", "tensor")),
            P("dp", "tensor"),
            P("dp", "tensor"),
            P("tensor", "dp"),
        ),
        check_vma=False,
    )
```

```python
import functools
import types

import jax
import jax.numpy as jnp
import numpy as np
from jax import lax
from jax.experimental import pallas as pl
from jax.experimental.pallas import tpu as pltpu
from jax.sharding import PartitionSpec as P

SPAN = 64


EPSILON = 1e-05
ROTARY_BASE = 10000.0
MASKED = -1e30


def rotary_tables(positions, width):
    half_width = width // 2
    freqs = ROTARY_BASE ** (-jnp.arange(half_width, dtype=jnp.float32) / half_width)
    angles = positions[:, None] * freqs[None, :]
    return (jnp.cos(angles), jnp.sin(angles))


def rotate(values, cosine, sine):
    half_width = values.shape[-1] // 2
    first_half = values[..., :half_width]
    second_half = values[..., half_width:]
    return jnp.concatenate(
        [first_half * cosine - second_half * sine, second_half * cosine + first_half * sine],
        axis=-1,
    )


def unrotate(values, cosine, sine):
    half_width = values.shape[-1] // 2
    first_half = values[..., :half_width]
    second_half = values[..., half_width:]
    return jnp.concatenate(
        [first_half * cosine + second_half * sine, second_half * cosine - first_half * sine],
        axis=-1,
    )


def layout(piece_units, rows):
    piece_rows = piece_units * SPAN
    ends = jnp.cumsum(piece_rows)
    starts = ends - piece_rows
    row_steps = jnp.arange(rows, dtype=jnp.int32)
    segment = jnp.sum((row_steps[:, None] >= ends[None, :]).astype(jnp.int32), axis=1)
    member = segment[:, None] == jnp.arange(piece_units.shape[0], dtype=jnp.int32)[None, :]
    row_start = jnp.sum(jnp.where(member, starts[None, :], 0), axis=1)
    positions = (row_steps - row_start).astype(jnp.float32)
    keep = (segment < piece_units.shape[0] - 1).astype(jnp.float32)
    return (segment, row_steps, positions, keep)


def permitted(block_segment, block_steps, segment, row_steps):
    return (block_segment[:, None] == segment[None, :]) & (
        row_steps[None, :] <= block_steps[:, None]
    )


def spread_rows(values):
    return lax.all_gather(values, "tensor", axis=0, tiled=True)


def spread_grads(values):
    return lax.all_gather(values, "tensor", axis=0, tiled=True)


def per_device(
    tokens,
    lengths,
    gain_attn,
    w_query,
    w_kv,
    w_attn_out,
    gain_mlp,
    w_gate,
    w_up,
    w_down,
    out_grad,
    kv_grad,
):
    local_rows = tokens.shape[0]
    parts = lax.axis_size("tensor")
    total_rows = local_rows * parts
    first_row = lax.axis_index("tensor") * local_rows
    segment, row_steps, positions, keep = layout(lengths[0], total_rows)
    head_dim = w_kv.shape[1] // 2
    local_heads = w_query.shape[1] // head_dim
    scale = head_dim ** (-0.5)
    cosine, sine = rotary_tables(positions, head_dim)
    row_keep = lax.dynamic_slice_in_dim(keep, first_row, local_rows, 0)[:, None]
    row_cosine = lax.dynamic_slice_in_dim(cosine, first_row, local_rows, 0)
    row_sine = lax.dynamic_slice_in_dim(sine, first_row, local_rows, 0)
    tokens_full = tokens.astype(jnp.float32)
    inv_first = lax.rsqrt(jnp.mean(tokens_full * tokens_full, axis=-1, keepdims=True) + EPSILON)
    unit_first = tokens_full * inv_first
    normed_rows = (unit_first * gain_attn).astype(jnp.bfloat16)
    normed = spread_rows(normed_rows)
    queries = jnp.dot(normed, w_query, preferred_element_type=jnp.float32).reshape(
        total_rows, local_heads, head_dim
    )
    queries = rotate(queries, cosine[:, None, :], sine[:, None, :]).astype(jnp.bfloat16)
    kv_raw = jnp.dot(normed, w_kv, preferred_element_type=jnp.float32)
    shared = jnp.concatenate(
        [rotate(kv_raw[:, :head_dim], cosine, sine), kv_raw[:, head_dim:]], axis=1
    ).astype(jnp.bfloat16)
    keys = shared[:, :head_dim]
    values = shared[:, head_dim:]
    block = min(512, total_rows)
    count = total_rows // block
    pieces = []
    log_totals = []
    for number in range(count):
        begin = number * block
        query_block = queries[begin : begin + block]
        allowed = permitted(
            segment[begin : begin + block], row_steps[begin : begin + block], segment, row_steps
        )
        scores = (
            jnp.einsum("qhd,kd->hqk", query_block, keys, preferred_element_type=jnp.float32) * scale
        )
        scores = jnp.where(allowed[None], scores, MASKED)
        row_max = jnp.max(scores, axis=-1, keepdims=True)
        exp_scores = jnp.exp(scores - row_max)
        row_total = jnp.sum(exp_scores, axis=-1, keepdims=True)
        log_totals.append(row_max + jnp.log(row_total))
        weights = (exp_scores / row_total).astype(jnp.bfloat16)
        pieces.append(
            jnp.einsum("hqk,kd->qhd", weights, values, preferred_element_type=jnp.float32).astype(
                jnp.bfloat16
            )
        )
    attended = jnp.concatenate(pieces, axis=0).reshape(total_rows, local_heads * head_dim)
    attn_rows = lax.psum_scatter(
        jnp.dot(attended, w_attn_out, preferred_element_type=jnp.float32).astype(jnp.bfloat16),
        "tensor",
        scatter_dimension=0,
        tiled=True,
    ).astype(jnp.float32)
    mid = tokens_full + attn_rows
    inv_second = lax.rsqrt(jnp.mean(mid * mid, axis=-1, keepdims=True) + EPSILON)
    unit_second = mid * inv_second
    normed_mlp = spread_rows((unit_second * gain_mlp).astype(jnp.bfloat16))
    gate = jnp.dot(normed_mlp, w_gate, preferred_element_type=jnp.float32)
    up = jnp.dot(normed_mlp, w_up, preferred_element_type=jnp.float32)
    sigma = jax.nn.sigmoid(gate)
    active = gate * sigma
    hidden = (active * up).astype(jnp.bfloat16)
    mlp_rows = lax.psum_scatter(
        jnp.dot(hidden, w_down, preferred_element_type=jnp.float32).astype(jnp.bfloat16),
        "tensor",
        scatter_dimension=0,
        tiled=True,
    ).astype(jnp.float32)
    block_out = (row_keep * (mid + mlp_rows)).astype(jnp.bfloat16)
    out_full = row_keep * out_grad.astype(jnp.float32)
    grad_mlp = spread_grads(out_full.astype(jnp.bfloat16))
    g_down = jnp.einsum("rf,rd->fd", hidden, grad_mlp, preferred_element_type=jnp.float32)
    g_hidden = jnp.einsum("rd,fd->rf", grad_mlp, w_down, preferred_element_type=jnp.float32)
    d_gate = (g_hidden * up * sigma * (1.0 + gate * (1.0 - sigma))).astype(jnp.bfloat16)
    d_up = (g_hidden * active).astype(jnp.bfloat16)
    g_gate = jnp.einsum("rd,rf->df", normed_mlp, d_gate, preferred_element_type=jnp.float32)
    g_up = jnp.einsum("rd,rf->df", normed_mlp, d_up, preferred_element_type=jnp.float32)
    back_mlp = lax.psum_scatter(
        (
            jnp.einsum("rf,df->rd", d_gate, w_gate, preferred_element_type=jnp.float32)
            + jnp.einsum("rf,df->rd", d_up, w_up, preferred_element_type=jnp.float32)
        ).astype(jnp.bfloat16),
        "tensor",
        scatter_dimension=0,
        tiled=True,
    ).astype(jnp.float32)
    e_mlp = back_mlp * gain_mlp
    g_gain_mlp = jnp.sum(back_mlp * unit_second, axis=0)
    d_mid = out_full + inv_second * (
        e_mlp - unit_second * jnp.mean(e_mlp * unit_second, axis=-1, keepdims=True)
    )
    grad_attn = spread_grads(d_mid.astype(jnp.bfloat16))
    g_attn_out = jnp.einsum("rh,rd->hd", attended, grad_attn, preferred_element_type=jnp.float32)
    d_att = jnp.einsum(
        "rd,hd->rh", grad_attn, w_attn_out, preferred_element_type=jnp.float32
    ).astype(jnp.bfloat16)
    d_att = d_att.reshape(total_rows, local_heads, head_dim)
    query_pieces = []
    d_keys = jnp.zeros((total_rows, head_dim), jnp.float32)
    d_values = jnp.zeros((total_rows, head_dim), jnp.float32)
    for number in range(count):
        begin = number * block
        query_block = queries[begin : begin + block]
        grad_block = d_att[begin : begin + block]
        allowed = permitted(
            segment[begin : begin + block], row_steps[begin : begin + block], segment, row_steps
        )
        scores = (
            jnp.einsum("qhd,kd->hqk", query_block, keys, preferred_element_type=jnp.float32) * scale
        )
        scores = jnp.where(allowed[None], scores, MASKED)
        probs = jnp.exp(scores - log_totals[number])
        weights = probs.astype(jnp.bfloat16)
        d_probs = jnp.einsum("qhd,kd->hqk", grad_block, values, preferred_element_type=jnp.float32)
        inner = jnp.sum(d_probs * probs, axis=-1, keepdims=True)
        d_scores = (probs * (d_probs - inner)).astype(jnp.bfloat16)
        query_pieces.append(
            jnp.einsum("hqk,kd->qhd", d_scores, keys, preferred_element_type=jnp.float32) * scale
        )
        d_keys = (
            d_keys
            + jnp.einsum("hqk,qhd->kd", d_scores, query_block, preferred_element_type=jnp.float32)
            * scale
        )
        d_values = d_values + jnp.einsum(
            "hqk,qhd->kd", weights, grad_block, preferred_element_type=jnp.float32
        )
    d_queries = jnp.concatenate(query_pieces, axis=0)
    d_queries = unrotate(d_queries, cosine[:, None, :], sine[:, None, :]).astype(jnp.bfloat16)
    d_queries = d_queries.reshape(total_rows, local_heads * head_dim)
    g_query = jnp.einsum("rd,rh->dh", normed, d_queries, preferred_element_type=jnp.float32)
    kv_rows = lax.psum_scatter(
        jnp.concatenate([d_keys, d_values], axis=1).astype(jnp.bfloat16),
        "tensor",
        scatter_dimension=0,
        tiled=True,
    ).astype(jnp.float32)
    kv_rows = kv_rows + row_keep * kv_grad.astype(jnp.float32)
    d_kv = jnp.concatenate(
        [unrotate(kv_rows[:, :head_dim], row_cosine, row_sine), kv_rows[:, head_dim:]], axis=1
    ).astype(jnp.bfloat16)
    d_kv_all = lax.all_gather(d_kv, "tensor", axis=0, tiled=True)
    width = normed.shape[1]
    groups = lax.axis_size("dp")
    own = lax.dynamic_index_in_dim(
        normed.reshape(total_rows, groups, parts, width // (groups * parts)),
        lax.axis_index("tensor"),
        2,
        False,
    ).reshape(total_rows, width // parts)
    g_kv = jnp.einsum("rd,rk->dk", own, d_kv_all, preferred_element_type=jnp.float32)
    back_attn = lax.psum_scatter(
        jnp.einsum("rh,dh->rd", d_queries, w_query, preferred_element_type=jnp.float32).astype(
            jnp.bfloat16
        ),
        "tensor",
        scatter_dimension=0,
        tiled=True,
    ).astype(jnp.float32)
    back_attn = back_attn + jnp.einsum("rk,dk->rd", d_kv, w_kv, preferred_element_type=jnp.float32)
    e_attn = back_attn * gain_attn
    g_gain_attn = jnp.sum(back_attn * unit_first, axis=0)
    grad_tokens = (
        d_mid
        + inv_first * (e_attn - unit_first * jnp.mean(e_attn * unit_first, axis=-1, keepdims=True))
    ).astype(jnp.bfloat16)
    kv_sum = lax.psum_scatter(g_kv, "dp", scatter_dimension=0, tiled=True)
    share = width // (groups * parts)
    first = (lax.axis_index("dp") * parts + lax.axis_index("tensor")) * share
    gain_all = lax.all_gather(jnp.stack([g_gain_attn, g_gain_mlp]), ("dp", "tensor"), axis=0)
    gain_sums = jnp.sum(lax.dynamic_slice_in_dim(gain_all, first, share, 2), axis=0)
    query_sum, out_sum, gate_sum, up_sum, down_sum = (
        lax.psum_scatter(
            g_query.astype(jnp.bfloat16), "dp", scatter_dimension=0, tiled=True
        ).astype(jnp.float32),
        lax.psum_scatter(
            g_attn_out.astype(jnp.bfloat16), "dp", scatter_dimension=1, tiled=True
        ).astype(jnp.float32),
        lax.psum_scatter(g_gate.astype(jnp.bfloat16), "dp", scatter_dimension=0, tiled=True).astype(
            jnp.float32
        ),
        lax.psum_scatter(g_up.astype(jnp.bfloat16), "dp", scatter_dimension=0, tiled=True).astype(
            jnp.float32
        ),
        lax.psum_scatter(g_down.astype(jnp.bfloat16), "dp", scatter_dimension=1, tiled=True).astype(
            jnp.float32
        ),
    )
    return (
        block_out,
        grad_tokens,
        gain_sums[0],
        query_sum,
        kv_sum,
        out_sum,
        gain_sums[1],
        gate_sum,
        up_sum,
        down_sum,
    )


F32, BF16 = jnp.float32, jnp.bfloat16
MESH = pl.DeviceIdType.MESH
MIB = 1 << 20


def dot(a, b):
    return jnp.dot(a, b, preferred_element_type=F32)


def dot_rows(a, b):
    return lax.dot_general(a, b, (((1,), (1,)), ((), ())), preferred_element_type=F32)


def dot_cols(a, b):
    return lax.dot_general(a, b, (((0,), (0,)), ((), ())), preferred_element_type=F32)


def tiles(width, step):
    return [(at, min(step, width - at)) for at in range(0, width, step)]


GN, GG, GM, GA = range(4)
RO, RB, RD, RQ = range(4)
LEN, TOK, TOK2, WQ, OG, KVG, WO, WG, WU, WD, BO, BO2, GT, GT2 = range(14)
DOWN, GATE, UP, OUT, QUERY = GRADS = range(5)


def semaphores(nz):
    counts = dict(
        swap=14,
        swap_y=14,
        gz=4 * 4 * nz,
        gc=4 * 2 * nz,
        rz=4 * 4 * nz,
        rc=4 * nz,
        stage=20,
        px=20,
        pc=20,
        py=5,
        ld=20,
        st=5,
        kc=nz,
        kz=nz,
        ka=2 * nz,
        kyx=2,
        gains=8 + nz,
        spill=2,
        outs=4,
    )
    firsts, total = {}, 0
    for name, count in counts.items():
        firsts[name] = total
        total += count
    return types.SimpleNamespace(**firsts), total


def block_kernel(nz, pieces, S, R):
    rows, width = R.tokens.shape
    ff = R.w_down.shape[0]
    total = 2 * nz * rows
    pair = 2 * rows
    head = 128
    heads = R.wq.shape[1] // head
    scale = head ** (-0.5)
    DS, DR = R.send, R.recv

    dp, tensor = lax.axis_index("dp"), lax.axis_index("tensor")
    y, c = dp // 2, dp % 2
    z, x = tensor // 2, tensor % 2
    keeper = c == x

    def dev(yy, cc, zz, xx):
        return (2 * yy + cc, 2 * zz + xx)

    def flip(value, yes):
        return 1 - value if yes else value

    sibling = dev(y, 1 - c, z, x)
    partner = dev(y, 1 - c, z, 1 - x)
    across_x = dev(y, c, z, 1 - x)
    across_y = dev(1 - y, c, z, x)

    def send(src, dst, s, r, to):
        return pltpu.make_async_remote_copy(
            src_ref=src,
            dst_ref=dst,
            send_sem=DS.at[s],
            recv_sem=DR.at[r],
            device_id=to,
            device_id_type=MESH,
        )

    def arrived(dst, r):
        pltpu.make_async_copy(dst, dst, DR.at[r]).wait()

    def sent(src, s):
        pltpu.make_async_copy(src, src, DS.at[s]).wait()

    barrier = pltpu.get_barrier_semaphore()
    around = {
        (dy, dc, dx): dev(flip(y, dy), flip(c, dc), z, flip(x, dx))
        for dy in range(2)
        for dc in range(2)
        for dx in range(2)
        if dy + dc + dx
    }
    for (dy, dc, dx), to in around.items():
        if dy + dx:
            pl.semaphore_signal(barrier, inc=1, device_id=to, device_id_type=MESH)
    for zz in range(nz):
        for cc in range(2):

            @pl.when((zz != z) | (cc != c))
            def _():
                pl.semaphore_signal(
                    barrier, inc=1, device_id=dev(y, cc, zz, x), device_id_type=MESH
                )

    pl.semaphore_wait(barrier, 6 + 2 * nz - 1)

    def swap_start(item, src, dst):
        at = S.swap + item

        @pl.when(keeper)
        def _():
            pltpu.make_async_copy(src, dst, DR.at[at]).start()

        @pl.when(jnp.logical_not(keeper))
        def _():
            send(src, dst, at, at, partner).start()

    def swap_wait(item, dst):
        arrived(dst, S.swap + item)

    def swap_sent(item, src):
        @pl.when(jnp.logical_not(keeper))
        def _():
            sent(src, S.swap + item)

    def part_at(ref, which):
        count = ref.shape[0] // 2
        return ref.at[pl.ds(pl.multiple_of(which * count, count), count)]

    def weight_start(item, src, dst):
        at = S.swap + item

        @pl.when(keeper)
        def _():
            pltpu.make_async_copy(src, dst, DR.at[at]).start()

        @pl.when(jnp.logical_not(keeper))
        def _():
            send(part_at(src, y), part_at(dst, y), at, at, partner).start()

    def weight_pass(item, dst):
        @pl.when(jnp.logical_not(keeper))
        def _():
            half_here = part_at(dst, y)
            arrived(half_here, S.swap + item)
            send(half_here, half_here, S.swap_y + item, S.swap_y + item, across_y).start()

    def weight_wait(item, dst):
        @pl.when(keeper)
        def _():
            arrived(dst, S.swap + item)

        @pl.when(jnp.logical_not(keeper))
        def _():
            arrived(part_at(dst, 1 - y), S.swap_y + item)

    def weight_sent(item, src, dst):
        @pl.when(jnp.logical_not(keeper))
        def _():
            sent(part_at(src, y), S.swap + item)
            sent(part_at(dst, y), S.swap_y + item)

    def piece(ref, chunk, core):
        return ref.at[pl.ds(pl.multiple_of((2 * chunk + core) * rows, rows), rows)]

    def chunk_rows(chunk):
        return pl.ds(pl.multiple_of(chunk * pair, pair), pair)

    own_at = pl.multiple_of((2 * z + c) * rows, rows)

    def bit(ref, chunk, core, part):
        count = rows // 2
        first = (2 * chunk + core) * rows + part * count
        return ref.at[pl.ds(pl.multiple_of(first, count), count)]

    def gather_sem(base, name, way, chunk, part):
        return base + ((2 * name + way) * nz + chunk) * 2 + part

    def core_sem(name, chunk, part):
        return S.gc + (name * nz + chunk) * 2 + part

    def gather_hop(name, ref, way, chunk, part):
        some = bit(ref, chunk, c, part)
        to = dev(y, c, z + 1 - 2 * way, x)
        send(
            some,
            some,
            gather_sem(S.gz, name, way, chunk, part),
            gather_sem(S.gz, name, 0, chunk, part),
            to,
        ).start()

    def gather_share(name, ref, chunk, part):
        some = bit(ref, chunk, c, part)
        at = core_sem(name, chunk, part)
        send(some, some, at, at, sibling).start()

    def gather_start(name, ref, parts=(0, 1)):
        for part in parts:

            @pl.when(z < nz - 1)
            def _():
                gather_hop(name, ref, 0, z, part)

            @pl.when(z > 0)
            def _():
                gather_hop(name, ref, 1, z, part)

            gather_share(name, ref, z, part)

    def gather_pass(name, ref, step):
        for part in range(2):
            for way in range(2):
                chunk = z - 1 - step if way == 0 else z + 1 + step

                @pl.when((chunk >= 0) & (chunk <= nz - 1))
                def _():
                    arrived(bit(ref, chunk, c, part), gather_sem(S.gz, name, 0, chunk, part))

                    @pl.when(z < nz - 1 if way == 0 else z > 0)
                    def _():
                        gather_hop(name, ref, way, chunk, part)

                    gather_share(name, ref, chunk, part)

    def gather_theirs(name, ref, chunk):
        for part in range(2):
            arrived(bit(ref, chunk, 1 - c, part), core_sem(name, chunk, part))

    def gather_own(name, ref, work):
        gather_theirs(name, ref, z)
        if work is not None:
            work(z)

    def gather_use(name, ref, step, work):
        for way in range(2):
            chunk = z - 1 - step if way == 0 else z + 1 + step

            @pl.when((chunk >= 0) & (chunk <= nz - 1))
            def _():
                gather_theirs(name, ref, chunk)
                if work is not None:
                    work(chunk)

    def gather_end(name, ref):
        for chunk in range(nz):
            for part in range(2):
                some = bit(ref, chunk, c, part)
                sent(some, core_sem(name, chunk, part))

                @pl.when((z < nz - 1) & (chunk <= z))
                def _():
                    sent(some, gather_sem(S.gz, name, 0, chunk, part))

                @pl.when((z > 0) & (chunk >= z))
                def _():
                    sent(some, gather_sem(S.gz, name, 1, chunk, part))

    def terms(name):
        return R.nmlp if name == RQ else R.part

    def half(name, chunk, core):
        return piece(terms(name), chunk, core)

    def core_room(name, chunk):
        room = R.wg if name == RQ else R.from_core
        return room.at[pl.ds(pl.multiple_of(chunk * rows, rows), rows)]

    def z_slot(name, way, chunk, at, part):
        slot = jnp.where((way == 1) & (chunk == at), nz, chunk)
        count = rows // 2
        return R.from_z.at[name % 2, slot, pl.ds(part * count, count)]

    def add_rows(dst, *sources):
        step = 32

        @pl.loop(0, dst.shape[0] // step)
        def _(i):
            at = pl.ds(pl.multiple_of(i * step, step), step)
            value = sources[0][at, :].astype(F32)
            for source in sources[1:]:
                value = value + source[at, :].astype(F32)
            dst[at, :] = value.astype(dst.dtype)

    def scatter_term(name, chunk, work):
        work(chunk)
        send(
            half(name, chunk, 1 - c),
            core_room(name, chunk),
            S.rc + nz * name + chunk,
            S.rc + nz * name + chunk,
            sibling,
        ).start()

    def scatter_forward(name, way, chunk):
        arrived(core_room(name, chunk), S.rc + nz * name + chunk)
        earlier = ((way == 0) & (z > 0)) | ((way == 1) & (z < nz - 1))
        to = z + 1 - 2 * way
        for part in range(2):
            mine = bit(terms(name), chunk, c, part)
            theirs = core_room(name, chunk).at[part * (rows // 2) : (part + 1) * (rows // 2)]
            before = z_slot(name, way, chunk, z, part)
            at = gather_sem(S.rz, name, way, chunk, part)

            @pl.when(earlier)
            def _():
                arrived(before, at)
                add_rows(mine, mine, theirs, before)

            @pl.when(jnp.logical_not(earlier))
            def _():
                add_rows(mine, mine, theirs)

            send(mine, z_slot(name, way, chunk, to, part), at, at, dev(y, c, to, x)).start()

    def between(index):
        way, chunk, valid = 0, 0, False
        for at in range(1, nz - 1):
            hops = [(other + at / 2, 0, other) for other in range(at + 1, nz)]
            hops += [(nz - 1 - other + (nz - 1 - at) / 2, 1, other) for other in range(at)]
            _, this_way, this_chunk = sorted(hops)[index]
            way = jnp.where(z == at, this_way, way)
            chunk = jnp.where(z == at, this_chunk, chunk)
            valid = valid | (z == at)
        return way, chunk, valid

    def scatter_slot(step, way):
        if way == 0:
            chunk = nz - 1 + z - step
            return chunk, (step >= z) & (z < nz - 1)
        chunk = step - (nz - 1 - z)
        return chunk, (chunk >= 0) & (z > 0)

    def scatter_step(name, step, work):
        for way in range(2):
            chunk, valid = scatter_slot(step, way)

            @pl.when(valid)
            def _():
                scatter_term(name, chunk, work)

        for way in range(2):
            chunk, valid = scatter_slot(step, way)

            @pl.when(valid)
            def _():
                scatter_forward(name, way, chunk)

    def scatter_end(name, finish):
        arrived(core_room(name, z), S.rc + nz * name + z)
        for part in range(2):
            some = pl.ds(part * (rows // 2), rows // 2)
            add_rows(R.acc.at[some], half(name, z, c).at[some], core_room(name, z).at[some])
            for way in range(2):

                @pl.when(z > 0 if way == 0 else z < nz - 1)
                def _():
                    before = z_slot(name, way, z, z, part)
                    arrived(before, gather_sem(S.rz, name, way, z, part))
                    add_rows(R.acc.at[some], R.acc.at[some], before)

            finish(part)

    def scatter_sent(name):
        for chunk in range(nz):
            sent(half(name, chunk, 1 - c), S.rc + nz * name + chunk)
            for way in range(2):
                for part in range(2):

                    @pl.when(z < chunk if way == 0 else z > chunk)
                    def _():
                        sent(
                            bit(terms(name), chunk, c, part),
                            gather_sem(S.rz, name, way, chunk, part),
                        )

    def each_rows(body, part, step=32):
        @pl.loop(0, rows // 2 // step)
        def _(i):
            body(pl.multiple_of(part * (rows // 2) + i * step, step), step)

    def keep_of(first, count):
        index = lax.broadcasted_iota(jnp.int32, (count, 1), 0) + (own_at + first)
        return (index.astype(F32) < R.last[0:1, 0:1]).astype(F32)

    def rotary():
        units = R.len[...] * 64.0
        ends, end = [], jnp.zeros((1, 128), F32)
        for p in range(pieces):
            end = end + units[p : p + 1, :]
            ends.append((units[p : p + 1, :], end))
        R.last[...] = jnp.broadcast_to(ends[-2][1], (8, 128))

        @pl.loop(0, total // 128)
        def _(i):
            at = pl.ds(pl.multiple_of(i * 128, 128), 128)
            index = (lax.broadcasted_iota(jnp.int32, (128, 128), 0) + i * 128).astype(F32)
            start = jnp.zeros((128, 128), F32)
            for length, stop in ends[:-1]:
                start = start + jnp.where(stop <= index, length, 0.0)
            R.start[at, :] = start
            angle = (index - start) * R.freq[0:1, :]
            lane = lax.broadcasted_iota(jnp.int32, (128, 128), 1)
            R.cos[at, :] = jnp.cos(angle)
            R.sin[at, :] = jnp.where(lane < 64, -1.0, 1.0) * jnp.sin(angle)

    def turn(value, cosine, sine):
        swapped = jnp.concatenate([value[:, 64:], value[:, :64]], axis=1)
        return value * cosine + swapped * sine

    def project(chunk):
        at = chunk_rows(chunk)
        normed = R.norm[at, :]
        cosine, sine = R.cos[at, :], R.sin[at, :]
        queries = dot(normed, R.wq[...])
        for h in range(heads):
            cols = slice(h * head, (h + 1) * head)
            R.q[at, cols] = turn(queries[:, cols], cosine, sine).astype(BF16)
        kv = dot(normed, R.wkv[...])
        R.kv[at, :head] = turn(kv[:, :head], cosine, sine).astype(BF16)
        R.kv[at, head:] = kv[:, head:].astype(BF16)

    def attend(chunk):
        at = chunk_rows(chunk)
        keys, values = R.kv[:, :head], R.kv[:, head:]
        start = R.start[at, 0:1]
        column = lax.broadcasted_iota(jnp.int32, (pair, total), 1).astype(F32)
        row = (lax.broadcasted_iota(jnp.int32, (pair, 1), 0) + chunk * pair).astype(F32)
        allowed = (column >= start) & (column <= row)
        for h in range(heads):
            cols = slice(h * head, (h + 1) * head)
            scores = dot_rows(R.q[at, cols], keys) * scale
            scores = jnp.where(allowed, scores, -1e30)
            exps = jnp.exp(scores - jnp.max(scores, axis=1, keepdims=True))
            weights = exps * (1.0 / jnp.sum(exps, axis=1, keepdims=True))
            weights = weights.astype(BF16)
            R.probs[h, at, :] = weights
            R.att[at, cols] = dot(weights, values).astype(BF16)

    def out_term(chunk):
        attend(chunk)
        at = chunk_rows(chunk)
        for n, size in tiles(width, 512):
            R.part[at, n : n + size] = dot(
                R.att[at, :], R.wo[:, n : n + size]
            ).astype(BF16)

    def mlp(chunk):
        at = chunk_rows(chunk)
        for n, size in tiles(ff, 256):
            cols = slice(n, n + size)
            gate = dot_rows(R.nmlp[at, :], R.wg[cols, :])
            up = dot_rows(R.nmlp[at, :], R.wu[cols, :])
            grad = dot_rows(R.gmlp[at, :], R.wd[cols, :])
            sigma = 1.0 / (1.0 + jnp.exp(-gate))
            active = gate * sigma
            R.hid[at, cols] = (active * up).astype(BF16)
            R.dup[at, cols] = (grad * active).astype(BF16)
            R.dgate[at, cols] = (grad * up * (sigma * (1.0 + gate * (1.0 - sigma)))).astype(BF16)

    def back_term(chunk):
        at = chunk_rows(chunk)
        for n, size in tiles(width, 512):
            some = slice(n, n + size)
            R.part[at, some] = (
                dot(R.dgate[at, :], R.wg[:, some]) + dot(R.dup[at, :], R.wu[:, some])
            ).astype(BF16)

    def down_term(chunk):
        at = chunk_rows(chunk)
        for n, size in tiles(width, 512):
            some = slice(n, n + size)
            R.part[at, some] = dot(R.hid[at, :], R.wd[:, some]).astype(BF16)

    def d_attended(chunk):
        at = chunk_rows(chunk)
        R.datt[at, :] = dot_rows(R.norm[at, :], R.wo[...]).astype(BF16)
        backward_attend(chunk)

    def backward_attend(chunk):
        at = chunk_rows(chunk)
        cosine, sine = R.cos[at, :], R.sin[at, :]
        for h in range(heads):
            cols = slice(h * head, (h + 1) * head)
            grad, queries = R.datt[at, cols], R.q[at, cols]
            inner = jnp.sum(
                grad.astype(F32) * R.att[at, cols].astype(F32), axis=1, keepdims=True
            )

            def block(number, d_queries):
                some = pl.ds(pl.multiple_of(number * pair, pair), pair)
                weights = R.probs[h, at, some]
                d_probs = dot_rows(grad, R.kv[some, head:])
                d_scores = (weights.astype(F32) * (d_probs - inner)).astype(BF16)
                R.dkv[some, :head] += dot_cols(d_scores, queries) * scale
                R.dkv[some, head:] += dot_cols(weights, grad)
                return d_queries + dot(d_scores, R.kv[some, :head])

            d_queries = lax.fori_loop(0, chunk + 1, block, jnp.zeros((pair, head), F32)) * scale
            R.dq[at, cols] = turn(d_queries, cosine, -sine).astype(BF16)

    def query_term(chunk):
        at = chunk_rows(chunk)
        for n, size in tiles(width, 512):
            some = slice(n, n + size)
            terms(RQ)[at, some] = dot_rows(R.dq[at, :], R.wq[some, :]).astype(BF16)

    Y_FIRST = (GATE, OUT)

    def grad_send(name, yy, cc):
        quarter = 2 * yy + cc
        stage = R.stage[name].at[quarter]
        if name in Y_FIRST:
            at = S.px + 4 * name + cc

            @pl.when(yy != y)
            def _():
                send(stage, R.px[name].at[cc], at, at, across_y).start()

            return
        into_x, into_c = R.px[name].at[yy], R.pc[name].at[yy]

        @pl.when(jnp.logical_not(keeper))
        def _():
            send(
                stage,
                into_x,
                S.px + 4 * name + quarter,
                S.px + 4 * name + yy,
                (2 * y + cc, 2 * z + 1 - x),
            ).start()

        @pl.when(keeper & (c == cc))
        def _():
            pltpu.make_async_copy(stage, into_c, DR.at[S.pc + 4 * name + yy]).start()

        @pl.when(keeper & (c != cc))
        def _():
            send(
                stage, into_c, S.pc + 4 * name + quarter, S.pc + 4 * name + yy, sibling
            ).start()

    def grad_sent(name, yy, cc):
        quarter = 2 * yy + cc
        stage = R.stage[name].at[quarter]
        if name in Y_FIRST:

            @pl.when(yy != y)
            def _():
                sent(stage, S.px + 4 * name + cc)

            return

        @pl.when(jnp.logical_not(keeper))
        def _():
            sent(stage, S.px + 4 * name + quarter)

        @pl.when(keeper & (c != cc))
        def _():
            sent(stage, S.pc + 4 * name + quarter)

    QUARTERS = [(0, 0), (0, 1), (1, 0), (1, 1)]

    def grad_make(name, left, right):
        split_left = name == QUERY
        quarter_cols = (left if split_left else right).shape[1] // 4
        tile = R.tile[name]
        for index, (yy, cc) in enumerate(QUARTERS):
            first = index * quarter_cols
            if index > 1:
                pltpu.make_async_copy(
                    tile.at[index % 2],
                    R.stage[name].at[index - 2],
                    DR.at[S.stage + 4 * name + index - 2],
                ).wait()
                grad_send(name, *QUARTERS[index - 2])
            if split_left:
                for m, size in tiles(quarter_cols, 256):
                    tile[index % 2, m : m + size, :] = dot_cols(
                        left[:, first + m : first + m + size], right[...]
                    ).astype(BF16)
            else:
                for m, size in tiles(left.shape[1], 256):
                    tile[index % 2, m : m + size, :] = dot_cols(
                        left[:, m : m + size], right[:, first : first + quarter_cols]
                    ).astype(BF16)
            pltpu.make_async_copy(
                tile.at[index % 2],
                R.stage[name].at[index],
                DR.at[S.stage + 4 * name + index],
            ).start()
        for index in (2, 3):
            pltpu.make_async_copy(
                tile.at[index % 2],
                R.stage[name].at[index],
                DR.at[S.stage + 4 * name + index],
            ).wait()
            grad_send(name, *QUARTERS[index])

    def sum_room(name, cc=0):
        cols = width // 4
        if name == QUERY:
            return R.wd.at[0:cols, 2 * cols : 2 * cols + R.wq.shape[1]]
        if name == DOWN:
            return R.wu.at[:, 2 * cols : 3 * cols]
        if name == UP:
            return R.wu.at[:, 3 * cols :]
        if name == GATE:
            return R.wd.at[:, cc * cols : (cc + 1) * cols]
        count = R.wo.shape[0]
        return R.wd.at[cc * count : (cc + 1) * count, 3 * cols :]

    def grad_places(name):
        count, cols = R.tile[name].shape[1:]
        return (
            (R.tile[name].at[0], R.tile[name].at[1]),
            (R.wu.at[0:count, 0:cols], R.wu.at[0:count, cols : 2 * cols]),
        )

    def grad_loads(name, turn_at, sources):
        loads = []
        for k, source in enumerate(sources):
            load = pltpu.make_async_copy(
                source,
                grad_places(name)[turn_at][k],
                DR.at[S.ld + 4 * name + 2 * turn_at + k],
            )
            load.start()
            loads.append(load)
        return loads

    def grad_mid(name):
        loads = []
        for cc in range(2):
            arrived(R.px[name].at[cc], S.px + 4 * name + cc)
            loads.append(
                grad_loads(name, cc, (R.px[name].at[cc], R.stage[name].at[2 * y + cc]))
            )
        for cc in range(2):
            for load in loads[cc]:
                load.wait()
            into = sum_room(name, cc)
            add_rows(into, *grad_places(name)[cc])
            at = S.pc + 4 * name + cc

            @pl.when(jnp.logical_not(keeper))
            def _():
                send(
                    into, R.other[name], at, S.py + name, (2 * y + cc, 2 * z + 1 - x)
                ).start()

            @pl.when(keeper & (c == cc))
            def _():
                pltpu.make_async_copy(into, R.mine[name], DR.at[S.st + name]).start()

            @pl.when(keeper & (c != cc))
            def _():
                send(into, R.mine[name], at, S.st + name, sibling).start()

    def grad_add(name):
        loads = []
        for turn_at, yy in enumerate((1 - y, y)):
            arrived(R.px[name].at[yy], S.px + 4 * name + yy)
            arrived(R.pc[name].at[yy], S.pc + 4 * name + yy)
            loads.append(grad_loads(name, turn_at, (R.px[name].at[yy], R.pc[name].at[yy])))
        for turn_at in range(2):
            for load in loads[turn_at]:
                load.wait()
            one, two = grad_places(name)[turn_at]
            if turn_at == 0:
                into = sum_room(name)
                add_rows(into, one, two)
                send(into, R.other[name], S.py + name, S.py + name, across_y).start()
            else:
                add_rows(one, one, two)
                store = pltpu.make_async_copy(one, R.mine[name], DR.at[S.st + name])
                store.start()
                store.wait()

    R.own_len[...] = jnp.zeros((8, 128), F32)
    for p in range(pieces):
        R.own_len[p : p + 1, :] = jnp.broadcast_to(R.lengths[0:1, p : p + 1].astype(F32), (1, 128))
    swap_start(LEN, R.own_len, R.len)
    for part in range(2):
        swap_start(TOK + part, part_at(R.tokens, part), part_at(R.tok, part))
    weight_start(WQ, R.w_query, R.wq)
    swap_start(OG, R.out_grad, R.og)
    swap_start(KVG, R.kv_grad, R.kvg)

    def norm_rows(first, count):
        at = pl.ds(first, count)
        value = R.tok[at, :].astype(F32)
        inverse = lax.rsqrt(jnp.mean(value * value, axis=1, keepdims=True) + EPSILON)
        R.norm[pl.ds(own_at + first, count), :] = (
            value * inverse * R.gain_attn[0:1, :]
        ).astype(BF16)

    for part in range(2):
        swap_wait(TOK + part, part_at(R.tok, part))
        each_rows(norm_rows, part)
        gather_start(GN, R.norm, (part,))
    swap_wait(LEN, R.len)
    weight_start(WO, R.w_attn_out, R.wo)
    rotary()
    weight_pass(WQ, R.wq)
    weight_wait(WQ, R.wq)
    gather_own(GN, R.norm, project)

    def mask_rows(first, count):
        at = pl.ds(first, count)
        R.gmlp[pl.ds(own_at + first, count), :] = (
            keep_of(first, count) * R.og[at, :].astype(F32)
        ).astype(BF16)

    for step in range(nz - 1):
        gather_pass(GN, R.norm, step)
        if step == 0:
            weight_pass(WO, R.wo)
            weight_start(WG, R.w_gate, R.wg)
            swap_wait(OG, R.og)
            swap_wait(KVG, R.kvg)
            for part in range(2):
                each_rows(mask_rows, part)
        if step == 1:
            weight_start(WU, R.w_up, R.wu)
        if step == nz - 2:
            gather_start(GG, R.gmlp)
            weight_pass(WG, R.wg)
            weight_start(WD, R.w_down, R.wd)
        gather_use(GN, R.norm, step, project)
    spill = pltpu.make_async_copy(R.norm, R.norm_store, DR.at[S.spill])
    spill.start()
    weight_wait(WO, R.wo)

    for step in range(nz - 1):
        scatter_step(RO, step, out_term)
        gather_pass(GG, R.gmlp, step)
        if step == 0:
            weight_pass(WU, R.wu)
        if step == 1:
            weight_pass(WD, R.wd)
    scatter_term(RO, z, out_term)

    def mid_rows(first, count):
        at = pl.ds(first, count)
        mid = R.tok[at, :].astype(F32) + R.acc[at, :]
        R.mid[at, :] = mid
        inverse = lax.rsqrt(jnp.mean(mid * mid, axis=1, keepdims=True) + EPSILON)
        R.nmlp[pl.ds(own_at + first, count), :] = (
            mid * inverse * R.gain_mlp[0:1, :]
        ).astype(BF16)

    def mid_done(part):
        each_rows(mid_rows, part)
        gather_start(GM, R.nmlp, (part,))

    scatter_end(RO, mid_done)
    for step in range(nz - 1):
        gather_use(GG, R.gmlp, step, None)
    gather_own(GG, R.gmlp, None)
    scatter_sent(RO)
    gather_end(GN, R.norm)
    spill.wait()
    weight_wait(WG, R.wg)
    weight_wait(WU, R.wu)
    weight_wait(WD, R.wd)
    def mlp_and_back(chunk):
        mlp(chunk)
        scatter_term(RB, chunk, back_term)

    gather_own(GM, R.nmlp, mlp_and_back)
    for step in range(nz - 1):
        gather_pass(GM, R.nmlp, step)
        gather_use(GM, R.nmlp, step, mlp_and_back)

        @pl.when(z == 0)
        def _():
            scatter_forward(RB, 0, step + 1)

        @pl.when(z == nz - 1)
        def _():
            scatter_forward(RB, 1, nz - 2 - step)

    for item, src, dst in (
        (WQ, R.w_query, R.wq),
        (WO, R.w_attn_out, R.wo),
        (WG, R.w_gate, R.wg),
        (WU, R.w_up, R.wu),
        (WD, R.w_down, R.wd),
    ):
        weight_sent(item, src, dst)

    mlp_grads = ((DOWN, R.hid, R.gmlp), (GATE, R.dgate, R.nmlp), (UP, R.dup, R.nmlp))
    for index in range(nz - 1):
        if index < 2:
            grad_make(*mlp_grads[index])
        way, chunk, valid = between(index)

        @pl.when(valid)
        def _():
            scatter_forward(RB, way, chunk)

    grad_make(*mlp_grads[2])
    R.gains[...] = jnp.zeros(R.gains.shape, F32)

    def fold(value):
        return jnp.sum(value.reshape(value.shape[0] // 8, 8, value.shape[1]), axis=0)

    def d_mid_rows(first, count):
        at = pl.ds(first, count)
        mid = R.mid[at, :]
        inverse = lax.rsqrt(jnp.mean(mid * mid, axis=1, keepdims=True) + EPSILON)
        unit = mid * inverse
        back = R.acc[at, :]
        R.gains[1] += fold(back * unit)
        e = back * R.gain_mlp[0:1, :]
        grad = keep_of(first, count) * R.og[at, :].astype(F32) + inverse * (
            e - unit * jnp.mean(e * unit, axis=1, keepdims=True)
        )
        R.dmid[at, :] = grad
        R.norm[pl.ds(own_at + first, count), :] = grad.astype(BF16)

    def d_mid_done(part):
        each_rows(d_mid_rows, part)
        gather_start(GA, R.norm, (part,))

    scatter_end(RB, d_mid_done)
    scatter_sent(RB)
    gather_end(GG, R.gmlp)
    gather_end(GM, R.nmlp)
    back_norm = pltpu.make_async_copy(R.norm_store, R.gmlp, DR.at[S.spill + 1])
    back_norm.start()
    R.dkv[...] = jnp.zeros(R.dkv.shape, F32)
    def attend_and_query(chunk):
        d_attended(chunk)
        scatter_term(RQ, chunk, query_term)

    def down_forward(step):
        for way in range(2):
            chunk, valid = scatter_slot(step, way)

            @pl.when(valid)
            def _():
                scatter_forward(RD, way, chunk)

    gather_theirs(GA, R.norm, z)
    for chunk in range(nz):
        scatter_term(RD, chunk, down_term)
    down_forward(0)
    attend_and_query(z)
    for step in range(nz - 1):
        gather_pass(GA, R.norm, step)
        gather_use(GA, R.norm, step, attend_and_query)

        @pl.when(z == 0)
        def _():
            scatter_forward(RQ, 0, step + 1)

        @pl.when(z == nz - 1)
        def _():
            scatter_forward(RQ, 1, nz - 2 - step)

        if step == 1:
            grad_add(DOWN)

    R.dkvb[...] = R.dkv[...].astype(BF16)
    for zz in range(nz):
        send(piece(R.dkvb, zz, 1 - c), R.kc.at[zz], S.kc + zz, S.kc + zz, sibling).start()

    def kv_over_z():
        for zz in range(nz):
            arrived(R.kc.at[zz], S.kc + zz)
            R.ks[zz] = (
                R.dkv[pl.ds(pl.multiple_of((2 * zz + c) * rows, rows), rows), :]
                + R.kc[zz].astype(F32)
            ).astype(BF16)

            @pl.when(zz != z)
            def _():
                send(R.ks.at[zz], R.kz.at[z], S.kz + zz, S.kz + z, dev(y, c, zz, x)).start()

    own_rows = pl.ds(own_at, rows)
    own_kv = piece(R.dkva, z, c)

    def kv_own():
        R.kacc[...] = keep_of(0, rows) * R.kvg[...].astype(F32) + R.ks[z].astype(F32)
        for zz in range(nz):

            @pl.when(zz != z)
            def _():
                arrived(R.kz.at[zz], S.kz + zz)
                R.kacc[...] += R.kz[zz].astype(F32)

        R.dkva[own_rows, :head] = turn(
            R.kacc[:, :head], R.cos[own_rows, :], -R.sin[own_rows, :]
        ).astype(BF16)
        R.dkva[own_rows, head:] = R.kacc[:, head:].astype(BF16)
        for zz in range(nz):
            for cc in range(2):

                @pl.when((zz != z) | (cc != c))
                def _():
                    send(
                        own_kv, own_kv, S.ka + 2 * zz + cc, S.ka + 2 * z + c, dev(y, cc, zz, x)
                    ).start()

    def out_rows(first, count):
        at = pl.ds(first, count)
        R.bo[at, :] = (keep_of(first, count) * (R.mid[at, :] + R.acc[at, :])).astype(BF16)

    for step in range(1, nz - 2):
        down_forward(step)
    grad_make(OUT, R.att, R.norm)
    grad_mid(GATE)
    back_norm.wait()
    for index in range(nz - 1):
        way, chunk, valid = between(index)

        @pl.when(valid)
        def _():
            scatter_forward(RQ, way, chunk)

        if index == 0:
            kv_over_z()
            grad_add(UP)
            grad_make(QUERY, R.gmlp, R.dq)
        if index == 1:
            kv_own()
    down_forward(nz - 2)
    for zz in range(nz):
        for cc in range(2):

            @pl.when((zz != z) | (cc != c))
            def _():
                arrived(piece(R.dkva, zz, cc), S.ka + 2 * zz + cc)

    first_col = c * (4 * nz * 32) + z * 128
    for yy in range(2):
        cols = pl.ds(pl.multiple_of(yy * (width // 2) + first_col, 128), 128)
        R.gkv[yy] = dot_cols(R.gmlp[:, cols], R.dkva[...])
    send(
        R.gkv.at[1 - y], R.kyb, S.kyx, S.kyx, across_y
    ).start()
    arrived(R.kyb, S.kyx)
    R.kysum[...] = R.gkv[y] + R.kyb[...]
    send(
        R.kysum.at[pl.ds(pl.multiple_of((1 - x) * 64, 64), 64)],
        R.kxb,
        S.kyx + 1,
        S.kyx + 1,
        across_x,
    ).start()
    arrived(R.kxb, S.kyx + 1)
    R.kfinal[...] = (
        R.kysum[pl.ds(pl.multiple_of(x * 64, 64), 64), :] + R.kxb[...]
    )
    kv_out = pltpu.make_async_copy(R.kfinal, R.grad_w_kv, DR.at[S.outs])
    kv_out.start()
    for n, size in tiles(width, 512):
        some = slice(n, n + size)
        extra = dot_rows(R.dkva[own_rows, :], R.wkv[some, :])
        for m in range(n, n + size, 2 * head):
            at = m // (2 * head) * rows
            R.dkv[at : at + rows, :] = extra[:, m - n : m - n + 2 * head]
    grad_mid(OUT)
    grad_add(QUERY)

    def tail_rows(first, count):
        at = pl.ds(first, count)
        value = R.tok[at, :].astype(F32)
        inverse = lax.rsqrt(jnp.mean(value * value, axis=1, keepdims=True) + EPSILON)
        unit = value * inverse
        extra = [
            R.dkv[pl.ds(pl.multiple_of(m * rows + first, 32), count), :]
            for m in range(width // (2 * head))
        ]
        back = R.acc[at, :] + jnp.concatenate(extra, axis=1)
        R.gains[0] += fold(back * unit)
        e = back * R.gain_attn[0:1, :]
        R.gt[at, :] = (
            R.dmid[at, :]
            + inverse * (e - unit * jnp.mean(e * unit, axis=1, keepdims=True))
        ).astype(BF16)

    def tail_done(part):
        each_rows(tail_rows, part)
        swap_start(GT + part, part_at(R.gt, part), part_at(R.grad_tokens, part))

    scatter_end(RQ, tail_done)

    line = lax.broadcasted_iota(jnp.int32, (8, width), 0)
    gain_first = jnp.sum(R.gains[0], axis=0, keepdims=True)
    gain_second = jnp.sum(R.gains[1], axis=0, keepdims=True)
    R.ga[...] = jnp.where(line == 0, gain_first, jnp.where(line == 1, gain_second, 0.0))
    span = width // 4

    def gain_cols(yy, cc):
        return pl.ds(pl.multiple_of((2 * yy + cc) * span, span), span)

    def gain_send(index, offset):
        dy, dc, dx = offset
        return send(
            R.ga.at[:, gain_cols(flip(y, dy), flip(c, dc))],
            R.gb.at[index],
            S.gains + index,
            S.gains + index,
            around[offset],
        )

    for index, offset in enumerate(around):
        gain_send(index, offset).start()

    def out_done(part):
        each_rows(out_rows, part)
        swap_start(BO + part, part_at(R.bo, part), part_at(R.block_out, part))

    scatter_end(RD, out_done)
    R.ga_x[...] = R.ga[:, gain_cols(y, c)]
    for index in range(len(around)):
        arrived(R.gb.at[index], S.gains + index)
        R.ga_x[...] += R.gb[index]
    for zz in range(nz):

        @pl.when(zz != z)
        def _():
            send(
                R.ga_x.at[:, zz * 128 : (zz + 1) * 128],
                R.gb_z.at[z],
                S.gains + 8 + zz,
                S.gains + 8 + z,
                dev(y, c, zz, x),
            ).start()

    R.gfinal[...] = R.ga_x[:, pl.ds(pl.multiple_of(z * 128, 128), 128)]
    for zz in range(nz):

        @pl.when(zz != z)
        def _():
            arrived(R.gb_z.at[zz], S.gains + 8 + zz)
            R.gfinal[...] += R.gb_z[zz]

    gain_out = pltpu.make_async_copy(R.gfinal, R.grad_gains, DR.at[S.outs + 1])
    gain_out.start()

    for name in GRADS:
        arrived(R.other[name], S.py + name)
        if name in Y_FIRST:
            arrived(R.mine[name], S.st + name)
            for cc in range(2):

                @pl.when(jnp.logical_not(keeper & (c == cc)))
                def _():
                    sent(sum_room(name, cc), S.pc + 4 * name + cc)
        else:
            sent(sum_room(name), S.py + name)
        for yy, cc in QUARTERS:
            grad_sent(name, yy, cc)
    kv_out.wait()
    gain_out.wait()
    scatter_sent(RD)
    scatter_sent(RQ)
    gather_end(GA, R.norm)
    for part in range(2):
        swap_wait(BO + part, part_at(R.block_out, part))
        swap_wait(GT + part, part_at(R.grad_tokens, part))
    for item, src in (
        (LEN, R.own_len),
        (TOK, part_at(R.tokens, 0)),
        (TOK2, part_at(R.tokens, 1)),
        (OG, R.out_grad),
        (KVG, R.kv_grad),
        (BO, part_at(R.bo, 0)),
        (BO2, part_at(R.bo, 1)),
        (GT, part_at(R.gt, 0)),
        (GT2, part_at(R.gt, 1)),
    ):
        swap_sent(item, src)
    for zz in range(nz):
        sent(piece(R.dkvb, zz, 1 - c), S.kc + zz)

        @pl.when(zz != z)
        def _():
            sent(R.ks.at[zz], S.kz + zz)
            sent(R.ga_x.at[:, zz * 128 : (zz + 1) * 128], S.gains + 8 + zz)

        for cc in range(2):

            @pl.when((zz != z) | (cc != c))
            def _():
                sent(own_kv, S.ka + 2 * zz + cc)

    sent(R.gkv.at[1 - y], S.kyx)
    sent(R.kysum.at[pl.ds(pl.multiple_of((1 - x) * 64, 64), 64)], S.kyx + 1)
    for index, offset in enumerate(around):
        gain_send(index, offset).wait_send()


def fused(nz, *args):
    (tokens, lengths, gain_attn, w_query, w_kv, w_attn_out, gain_mlp, w_gate, w_up, w_down,
     out_grad, kv_grad) = args
    rows, width = tokens.shape
    ff = w_gate.shape[1]
    qw = w_query.shape[1]
    total, pair = 2 * nz * rows, 2 * rows
    pieces = lengths.shape[1]
    head = w_kv.shape[1] // 2
    half_width = head // 2
    freqs = (ROTARY_BASE ** (-np.arange(half_width, dtype=np.float32) / half_width)).astype(np.float32)
    freq = np.tile(np.concatenate([freqs, freqs])[None, :], (8, 1))
    anywhere, vmem = pl.BlockSpec(memory_space=pl.ANY), pl.BlockSpec(memory_space=pltpu.VMEM)
    ins = dict(
        tokens=(tokens, anywhere),
        lengths=(lengths, vmem),
        freq=(freq, vmem),
        gain_attn=(gain_attn[None], vmem),
        gain_mlp=(gain_mlp[None], vmem),
        w_query=(w_query, anywhere),
        wkv=(w_kv, vmem),
        w_attn_out=(w_attn_out, anywhere),
        w_gate=(w_gate.T, anywhere),
        w_up=(w_up.T, anywhere),
        w_down=(w_down, anywhere),
        out_grad=(out_grad, anywhere),
        kv_grad=(kv_grad, anywhere),
    )
    quarter = width // 4
    grad_tiles = [(ff, quarter), (ff, quarter), (ff, quarter), (qw, quarter), (quarter, qw)]
    outs = dict(
        block_out=((rows, width), BF16),
        grad_tokens=((rows, width), BF16),
        grad_w_kv=((64, 2 * head), F32),
        grad_gains=((8, 128), F32),
        norm_store=((total, width), BF16),
    )
    moved = [
        (shape, BF16)
        for tile in grad_tiles
        for shape in (tile, tile, (4,) + tile, (2,) + tile, (2,) + tile)
    ]
    S, count = semaphores(nz)
    scratch = dict(
        own_len=((8, 128), F32),
        len=((8, 128), F32),
        last=((8, 128), F32),
        tok=((rows, width), BF16),
        og=((rows, width), BF16),
        kvg=((rows, 2 * head), BF16),
        wq=((width, qw), BF16),
        wo=((qw, width), BF16),
        wg=((ff, width), BF16),
        wu=((ff, width), BF16),
        wd=((ff, width), BF16),
        norm=((total, width), BF16),
        nmlp=((total, width), BF16),
        gmlp=((total, width), BF16),
        cos=((total, 128), F32),
        sin=((total, 128), F32),
        start=((total, 128), F32),
        q=((total, qw), BF16),
        kv=((total, 2 * head), BF16),
        att=((total, qw), BF16),
        datt=((total, qw), BF16),
        dq=((total, qw), BF16),
        probs=((qw // head, total, total), BF16),
        hid=((total, ff), BF16),
        dgate=((total, ff), BF16),
        dup=((total, ff), BF16),
        part=((total, width), BF16),
        from_core=((nz * rows, width), BF16),
        from_z=((2, nz + 1, rows, width), BF16),
        acc=((rows, width), F32),
        mid=((rows, width), F32),
        dmid=((rows, width), F32),
        bo=((rows, width), BF16),
        gt=((rows, width), BF16),
        gains=((2, 8, width), F32),
        ga=((8, width), F32),
        ga_x=((8, width // 4), F32),
        gb=((7, 8, width // 4), F32),
        gb_z=((nz, 8, 128), F32),
        gfinal=((8, 128), F32),
        dkv=((total, 2 * head), F32),
        dkvb=((total, 2 * head), BF16),
        dkva=((total, 2 * head), BF16),
        kc=((nz, rows, 2 * head), BF16),
        ks=((nz, rows, 2 * head), BF16),
        kz=((nz, rows, 2 * head), BF16),
        kacc=((rows, 2 * head), F32),
        gkv=((2, 128, 2 * head), F32),
        kyb=((128, 2 * head), F32),
        kysum=((128, 2 * head), F32),
        kxb=((64, 2 * head), F32),
        kfinal=((64, 2 * head), F32),
    )
    tile_shapes = (grad_tiles[DOWN], grad_tiles[OUT], grad_tiles[QUERY])
    out_shapes = list(outs.values()) + moved
    scratch_shapes = list(scratch.values()) + [((2,) + shape, BF16) for shape in tile_shapes]

    def body(*refs):
        refs = list(refs)

        def take(count):
            taken = refs[:count]
            del refs[:count]
            return taken

        R = types.SimpleNamespace(
            **dict(zip(ins, take(len(ins)))), **dict(zip(outs, take(len(outs))))
        )
        rest = take(len(moved))
        R.mine, R.other, R.stage, R.px, R.pc = (rest[k::5] for k in range(5))
        for key, ref in zip(scratch, take(len(scratch))):
            setattr(R, key, ref)
        big, out_tile, query_tile = take(3)
        R.tile = [big, big, big, out_tile, query_tile]
        R.send, R.recv = refs
        block_kernel(nz, pieces, S, R)

    results = pl.pallas_call(
        body,
        out_shape=[jax.ShapeDtypeStruct(shape, kind) for shape, kind in out_shapes],
        in_specs=[spec for _, spec in ins.values()],
        out_specs=[anywhere] * len(out_shapes),
        scratch_shapes=[pltpu.VMEM(shape, kind) for shape, kind in scratch_shapes]
        + [pltpu.SemaphoreType.DMA((count,))] * 2,
        compiler_params=pltpu.CompilerParams(
            collective_id=0, has_side_effects=True, vmem_limit_bytes=63 * MIB
        ),
        name="block",
    )(*[value for value, _ in ins.values()])
    first = list(results[:4])
    mine, other = list(results[5::5]), list(results[6::5])

    def finish(*refs):
        ends, refs = refs[:4], refs[4:]
        one, two, refs = refs[:5], refs[5:10], refs[10:]
        for k in range(3):
            refs[k][...] = ends[k][...]
        right = (lax.axis_index("tensor") % 2) == 1
        for k in range(2):
            line = ends[3][k : k + 1, :]
            refs[3 + k][...] = jnp.where(right, line[:, 64:], line[:, :64])
        for k in GRADS:
            refs[5 + k][...] = one[k][...].astype(F32) + two[k][...].astype(F32)

    cuts = 4

    def cut(array):
        count = array.shape[0] // cuts
        return pl.BlockSpec((count, array.shape[1]), lambda i: (i, 0))

    whole = pl.BlockSpec((8, 128), lambda i: (0, 0))
    block_out, grad_tokens, grad_w_kv, gain_first, gain_second, *sums = pl.pallas_call(
        finish,
        grid=(cuts,),
        out_shape=[jax.ShapeDtypeStruct(array.shape, array.dtype) for array in first[:3]]
        + [jax.ShapeDtypeStruct((1, 64), F32)] * 2
        + [jax.ShapeDtypeStruct(array.shape, F32) for array in mine],
        in_specs=[cut(array) for array in first[:3]] + [whole] + [cut(a) for a in mine + other],
        out_specs=[cut(array) for array in first[:3]]
        + [pl.BlockSpec((1, 64), lambda i: (0, 0))] * 2
        + [cut(array) for array in mine],
        compiler_params=pltpu.CompilerParams(vmem_limit_bytes=63 * MIB),
        name="finish",
    )(*first, *mine, *other)
    return (
        block_out,
        grad_tokens,
        gain_first[0],
        sums[QUERY],
        grad_w_kv,
        sums[OUT],
        gain_second[0],
        sums[GATE].T,
        sums[UP].T,
        sums[DOWN],
    )


def solution(mesh):
    groups, parts = mesh.shape["dp"], mesh.shape["tensor"]
    paired = groups == 4 and parts == 8
    per_group = functools.partial(fused, parts // 2) if paired else per_device
    placed = (
        P(("dp", "tensor"), None),
        P("dp", None),
        P(),
        P(None, "tensor"),
        P(),
        P("tensor", None),
        P(),
        P(None, "tensor"),
        P(None, "tensor"),
        P("tensor", None),
        P(("dp", "tensor"), None),
        P(("dp", "tensor"), None),
    )
    return jax.shard_map(
        per_group,
        mesh=mesh,
        in_specs=placed,
        out_specs=(
            P(("dp", "tensor"), None),
            P(("dp", "tensor"), None),
            P(("dp", "tensor")),
            P("dp", "tensor"),
            P(("dp", "tensor"), None),
            P("tensor", "dp"),
            P(("dp", "tensor")),
            P("dp", "tensor"),
            P("dp", "tensor"),
            P("tensor", "dp"),
        ),
        check_vma=False,
    )
```
